32 devices in a mesh: member: 1, gx: 4 (over z), gy: 8 (over y, x, core).
Axes of the slice: x: 2, y: 2, z: 4, core: 2. Of those that a mesh axis runs over, the one named last changes fastest.
Arguments:
- couplings: float32 [6, 4, 32, 64, 128], P('member', None, 'gx', 'gy'), may hold values from -0.4 to 0.1
- diagonal_blocks: float32 [4, 32, 64, 128], P('member', 'gx', 'gy'), may hold values from -1 to 12
- well_vectors: float32 [4, 32, 64, 128], P('member', 'gx', 'gy'), may hold values from -3 to 3, as said below
- well_ids: int32 [32, 64, 128], P('gx', 'gy'), may hold values from 0 to 40, as said below
- right_side: float32 [4, 2, 32, 64, 128], P('member', None, 'gx', 'gy'), may hold values from -24 to 24
- initial_guess: float32 [4, 2, 32, 64, 128], P('member', None, 'gx', 'gy'), may hold values from -3 to 3
Outputs:
- solution: float32 [4, 2, 32, 64, 128], P('member', None, 'gx', 'gy')
The draws below stay inside these ranges and needn't reach their ends.
Inputs may be any that keep to these rules, and one draw needn't show every extreme that they name: `well_ids`: A value below 40 names the well perforating the cell; 40 marks a cell without a perforation. `well_vectors`: entries 0 and 1 lie within -1 to 1, entries 2 and 3 within -3 to 3.
All inputs are finite; a program needn't handle non-finite values.
Results may differ from the reference program's by a relative error of at most 0.0003.
Values sent between devices are 32-bit elements; how exact they have to be, the bound alone decides.
No kernel may reach another device: no remote copies, remote signals or barrier semaphores. Data moves between devices by JAX's collectives and lax.ppermute only.
A program may use at most 64 MiB of HBM per device.

```python
import jax
import jax.numpy as jnp
from jax import lax

CX = 8
CY = 8
NZ = 128
NRHS = 4
WELLS = 40
ITERS = 3
NX = 32
NY = 64


def draw_diagonal_blocks(key, part):
    key = jax.random.fold_in(key, 5)
    first_key, second_key = jax.random.split(key)
    extent = (2, NX, NY, NZ)
    leading = jax.random.uniform(first_key, extent, minval=6.0, maxval=12.0)
    across = jax.random.uniform(second_key, extent, minval=-1.0, maxval=1.0)
    return jnp.stack([leading[0], across[0], across[1], leading[1]])


def draw_well_vectors(key, part):
    key = jax.random.fold_in(key, 29)
    first_key, second_key = jax.random.split(key)
    extent = (2, NX, NY, NZ)
    unknown = jax.random.uniform(first_key, extent, minval=-1.0, maxval=1.0)
    equation = jax.random.uniform(second_key, extent, minval=-1.0, maxval=1.0)
    return jnp.stack([unknown[0], unknown[1], 3.0 * equation[0], 3.0 * equation[1]])


def draw_well_ids(key, part):
    key = jax.random.fold_in(key, 17)
    subkeys = jax.random.split(key, 5)
    row_blocks = jax.random.randint(subkeys[0], (WELLS,), 0, NY // CY).astype(jnp.int32)
    row_leads = jax.random.randint(subkeys[4], (WELLS,), 0, 2).astype(jnp.int32)
    base_rows = row_blocks * CY + CY - 1 - row_leads
    well_spans = jax.random.randint(subkeys[1], (WELLS,), CX + 1, 3 * CX + 1).astype(jnp.int32)
    starts = jax.random.randint(subkeys[2], (WELLS,), 0, NX - 3 * CX + 1).astype(jnp.int32)
    depths = jax.random.randint(subkeys[3], (WELLS,), 0, NZ - 3 * CX // 2).astype(jnp.int32)
    across = jnp.arange(NX, dtype=jnp.int32)[:, None, None]
    second = jnp.arange(NY, dtype=jnp.int32)[None, :, None]
    height = jnp.arange(NZ, dtype=jnp.int32)[None, None, :]

    def place(number, current):
        offset = across - starts[number]
        row_here = (base_rows[number] + offset // 2) % NY
        matched = (second == row_here) & (offset >= 0) & (offset < well_spans[number]) & (height == depths[number] + offset // 2)
        return jnp.where(matched, number, current)
    return lax.fori_loop(0, WELLS, place, jnp.full((NX, NY, NZ), WELLS, jnp.int32))


def steps_of(key, shape, cuts, low, high):
    def one(axis_at, shards_of):
        steps = jax.random.uniform(jax.random.fold_in(jax.random.fold_in(key, 6), axis_at), (shards_of,), jnp.float32, low / len(cuts), high / len(cuts))
        return jnp.repeat(jnp.exp(steps), shape[axis_at] // shards_of).reshape((-1,) + (1,) * (len(shape) - axis_at - 1))

    loudness = one(*cuts[0])
    for cut in cuts[1:]:
        loudness = loudness * one(*cut)
    return loudness


def gaussian(stream_key, shape, deviation, limit, shards=(), kind=jnp.bfloat16):
    factor_of = steps_of(stream_key, shape, shards, -0.22, 0.18) if shards else 1.0
    values = jax.random.normal(stream_key, shape, jnp.float32) * deviation * factor_of
    return jnp.minimum(jnp.maximum(values, -limit), limit).astype(kind)


def setup_inputs(seed: int = 0, part: int = 0) -> dict:
    keys = jax.random.split(jax.random.key(seed), 7)
    part_keys = jax.random.split(jax.random.fold_in(keys[6], part), 7)
    couplings = jnp.clip(-0.4 + 0.5 * jax.random.uniform(part_keys[0], (6, 4, NX, NY, NZ), jnp.float32) ** steps_of(part_keys[0], (6, 4, NX, NY, NZ), ((2, 4), (3, 8)), -0.2, 0.2), -0.4, 0.1)
    diagonal_blocks = draw_diagonal_blocks(jax.random.fold_in(jax.random.fold_in(keys[6], part), 71), part)
    well_vectors = draw_well_vectors(jax.random.fold_in(jax.random.fold_in(keys[6], part), 71), part)
    well_ids = draw_well_ids(jax.random.fold_in(keys[6], 71), part)
    right_side = gaussian(part_keys[4], (NRHS, 2, NX, NY, NZ), 4.0, 24.0, ((2, 4), (3, 8)), jnp.float32)
    initial_guess = gaussian(part_keys[5], (NRHS, 2, NX, NY, NZ), 0.5, 3.0, ((2, 4), (3, 8)), jnp.float32)
    return {"couplings": couplings, "diagonal_blocks": diagonal_blocks, "well_vectors": well_vectors, "well_ids": well_ids, "right_side": right_side, "initial_guess": initial_guess}


def block_product(blocks, vectors):
    first = blocks[0] * vectors[:, 0] + blocks[2] * vectors[:, 1]
    second = blocks[1] * vectors[:, 0] + blocks[3] * vectors[:, 1]
    return jnp.stack([first, second], axis=1)

def moved_along(partial_sum, axis_number, upward):
    length = partial_sum.shape[axis_number]
    widths = [(0, 0)] * partial_sum.ndim
    if upward:
        kept = lax.slice_in_dim(partial_sum, 0, length - 1, axis=axis_number)
        widths[axis_number] = (1, 0)
    else:
        kept = lax.slice_in_dim(partial_sum, 1, length, axis=axis_number)
        widths[axis_number] = (0, 1)
    return jnp.pad(kept, widths)

def transpose_apply(vectors, couplings, diagonal_blocks, well_vectors, well_ids):
    result = block_product(diagonal_blocks, vectors)
    moves = ((2, True), (2, False), (3, True), (3, False), (4, True), (4, False))
    for direction in range(6):
        axis_number, upward = moves[direction]
        result = result + moved_along(block_product(couplings[direction], vectors), axis_number, upward)
    flat_ids = well_ids.reshape(-1)
    weighted = (well_vectors[0] * vectors[:, 0] + well_vectors[1] * vectors[:, 1]).reshape(vectors.shape[0], -1)
    totals = jax.vmap(lambda row_values: jax.ops.segment_sum(row_values, flat_ids, num_segments=WELLS + 1))(weighted)
    totals = totals * (jnp.arange(WELLS + 1) < WELLS).astype(totals.dtype)
    spread = totals[:, flat_ids].reshape((vectors.shape[0],) + vectors.shape[2:])
    return result + jnp.stack([well_vectors[2] * spread, well_vectors[3] * spread], axis=1)

def inner(first, second):
    return lax.optimization_barrier(jnp.sum(first * second, axis=(1, 2, 3, 4)))

def widen(scalars):
    return scalars[:, None, None, None, None]

def small_solve(factor, target):
    return jax.scipy.linalg.cho_solve((factor, True), target)

def reference(couplings, diagonal_blocks, well_vectors, well_ids, right_side, initial_guess):
    batch_count = right_side.shape[0]
    residual = right_side - transpose_apply(initial_guess, couplings, diagonal_blocks, well_vectors, well_ids)
    start_norm = jnp.sqrt(inner(residual, residual))
    basis = [residual / widen(start_norm)]
    columns = []
    for step in range(ITERS):
        image = transpose_apply(basis[step], couplings, diagonal_blocks, well_vectors, well_ids)
        heights = jnp.stack([inner(vector, image) for vector in basis], axis=1)
        for position in range(len(basis)):
            image = image - widen(heights[:, position]) * basis[position]
        length = jnp.sqrt(inner(image, image))
        columns.append(jnp.concatenate([heights, length[:, None], jnp.zeros((batch_count, ITERS - 1 - step), jnp.float32)], axis=1))
        if step + 1 < ITERS:
            basis.append(image / widen(length))
    hessenberg = jnp.stack(columns, axis=2)
    gram = jnp.einsum('kij,kil->kjl', hessenberg, hessenberg, precision=lax.Precision.HIGHEST)
    target = start_norm[:, None] * hessenberg[:, 0, :]
    factor = jnp.linalg.cholesky(gram)
    weights = jax.vmap(small_solve)(factor, target)
    solution = initial_guess
    for position in range(ITERS):
        solution = solution + widen(weights[:, position]) * basis[position]
    return solution
```

```python
import jax
import jax.numpy as jnp
from jax import lax
from jax.sharding import PartitionSpec as P

WELLS = 40
ITERS = 3


def total_of(value):
    count = lax.axis_size("gx") * lax.axis_size("gy")
    copies = jnp.broadcast_to(value.reshape(1, -1), (count, value.size))
    parts = lax.all_to_all(copies, ("gx", "gy"), 0, 0, tiled=True)
    return jnp.sum(parts, axis=0).reshape(value.shape)


def from_behind(value, axis, steps):
    count = lax.axis_size(axis)
    leading, last = (max(0, -steps), min(count, count - steps))
    return lax.ppermute(value, axis, [(source, source + steps) for source in range(leading, last)])


def block_product(blocks, vectors):
    first = blocks[0] * vectors[:, 0] + blocks[2] * vectors[:, 1]
    second = blocks[1] * vectors[:, 0] + blocks[3] * vectors[:, 1]
    return jnp.stack([first, second], axis=1)


def moved_along(partial_sum, axis_number, upward):
    length = partial_sum.shape[axis_number]
    widths = [(0, 0)] * partial_sum.ndim
    if upward:
        kept = lax.slice_in_dim(partial_sum, 0, length - 1, axis=axis_number)
        widths[axis_number] = (1, 0)
    else:
        kept = lax.slice_in_dim(partial_sum, 1, length, axis=axis_number)
        widths[axis_number] = (0, 1)
    return jnp.pad(kept, widths)


def areal_terms(vectors, couplings):
    eastward = block_product(couplings[0], vectors)
    from_west = from_behind(eastward[:, :, -1:], "gx", 1)
    result = jnp.concatenate([from_west, eastward[:, :, :-1]], axis=2)
    westward = block_product(couplings[1], vectors)
    from_east = from_behind(westward[:, :, :1], "gx", -1)
    result = result + jnp.concatenate([westward[:, :, 1:], from_east], axis=2)
    northward = block_product(couplings[2], vectors)
    from_south = from_behind(northward[:, :, :, -1:], "gy", 1)
    result = result + jnp.concatenate([from_south, northward[:, :, :, :-1]], axis=3)
    southward = block_product(couplings[3], vectors)
    from_north = from_behind(southward[:, :, :, :1], "gy", -1)
    result = result + jnp.concatenate([southward[:, :, :, 1:], from_north], axis=3)
    return result


def well_partial(vectors, well_vectors, well_table):
    weighted = (well_vectors[0] * vectors[:, 0] + well_vectors[1] * vectors[:, 1]).reshape(
        vectors.shape[0], -1
    )
    return jnp.einsum("kc,wc->kw", weighted, well_table, precision=lax.Precision.HIGHEST)


def transpose_apply(vectors, totals, couplings, diagonal_blocks, well_vectors, well_table):
    result = block_product(diagonal_blocks, vectors)
    result = result + areal_terms(vectors, couplings)
    result = result + moved_along(block_product(couplings[4], vectors), 4, True)
    result = result + moved_along(block_product(couplings[5], vectors), 4, False)
    spread = jnp.dot(totals, well_table, precision=lax.Precision.HIGHEST).reshape(
        (vectors.shape[0],) + vectors.shape[2:]
    )
    return result + jnp.stack([well_vectors[2] * spread, well_vectors[3] * spread], axis=1)


def inner(first, second):
    return jnp.sum(first * second, axis=(1, 2, 3, 4))


def widen(scalars):
    return scalars[:, None, None, None, None]


def global_norm(vectors):
    return jnp.sqrt(total_of(inner(vectors, vectors)))


def small_solve(factor, target):
    return jax.scipy.linalg.cho_solve((factor, True), target)


def body(couplings, diagonal_blocks, well_vectors, well_ids, right_side, initial_guess):
    batch_count = right_side.shape[0]
    well_table = (well_ids.reshape(1, -1) == jnp.arange(WELLS, dtype=jnp.int32)[:, None]).astype(
        jnp.float32
    )

    def apply_with(vectors, totals):
        return transpose_apply(
            vectors, totals, couplings, diagonal_blocks, well_vectors, well_table
        )

    def apply_summed(vectors):
        totals = total_of(well_partial(vectors, well_vectors, well_table))
        return apply_with(vectors, totals)

    residual = right_side - apply_summed(initial_guess)
    columns = []
    start_norm = global_norm(residual)
    basis = [residual / widen(start_norm)]
    for step in range(ITERS):
        image = apply_summed(basis[step])
        heights = total_of(
            jnp.stack([inner(vector, image) for vector in basis], axis=1)
        )
        for position in range(len(basis)):
            image = image - widen(heights[:, position]) * basis[position]
        length = global_norm(image)
        columns.append(
            jnp.concatenate(
                [heights, length[:, None], jnp.zeros((batch_count, ITERS - 1 - step), jnp.float32)],
                axis=1,
            )
        )
        if step + 1 < ITERS:
            basis.append(image / widen(length))
    hessenberg = jnp.stack(columns, axis=2)
    gram = jnp.einsum("kij,kil->kjl", hessenberg, hessenberg, precision=lax.Precision.HIGHEST)
    target = start_norm[:, None] * hessenberg[:, 0, :]
    factor = jnp.linalg.cholesky(gram)
    weights = jax.vmap(small_solve)(factor, target)
    solution = initial_guess
    for position in range(ITERS):
        solution = solution + widen(weights[:, position]) * basis[position]
    return solution


def solution(mesh):
    in_specs = (
        P("member", None, "gx", "gy", None),
        P("member", "gx", "gy", None),
        P("member", "gx", "gy", None),
        P("gx", "gy", None),
        P("member", None, "gx", "gy", None),
        P("member", None, "gx", "gy", None),
    )
    out_specs = P("member", None, "gx", "gy", None)
    return jax.shard_map(body, mesh=mesh, in_specs=in_specs, out_specs=out_specs, check_vma=False)
```

```python
import functools

import jax
import jax.numpy as jnp
from jax import lax
from jax.experimental import pallas as pl
from jax.experimental.pallas import tpu as pltpu
from jax.sharding import PartitionSpec as P

WELLS = 40
RHS = 4
LANES = 128
LAT_UP, LAT_DOWN, RISE, FALL, DIAGONAL = 4, 8, 12, 16, 20
WELL_EQ, WELL_ID, GUESS, RIGHT = 24, 26, 27, 35
BACK_IN, BACK_EQ, BACK_ID, BACK_GUESS = 43, 47, 49, 50
FACE_PLANES = 58
CORNER_ROWS = 19
SIDE_IN, SIDE_EQ, SIDE_ID, SIDE_GUESS = 4, 8, 10, 11


def product(blocks, first, second):
    return [
        blocks(0) * first + blocks(2) * second,
        blocks(1) * first + blocks(3) * second,
    ]


def iota(shape, axis):
    return lax.broadcasted_iota(jnp.int32, shape, axis)


def roll_up(value, axis):
    return pltpu.roll(value, 1, axis)


def roll_down(value, axis):
    return pltpu.roll(value, value.shape[axis] - 1, axis)


def layer_moves(rising, falling):
    axis = rising.ndim - 1
    lane = iota(rising.shape, axis)
    up = jnp.where(lane == 0, 0.0, roll_up(rising, axis))
    down = jnp.where(lane == LANES - 1, 0.0, roll_down(falling, axis))
    return up + down


def block_stencil(couplings, diagonal, first, second, incoming):
    result = product(lambda e: diagonal[e], first, second)
    moved = [product(lambda e, d=d: couplings[d, e], first, second) for d in range(6)]
    row = iota(first.shape, 1)
    outgoing = [[], [], [], []]
    for b in range(2):
        east, west, north, south, rise, fall = (moved[d][b] for d in range(6))
        total = result[b] + jnp.concatenate([incoming[0][b][None], east[:-1]], axis=0)
        total = total + jnp.concatenate([west[1:], incoming[1][b][None]], axis=0)
        total = total + jnp.where(row == 0, incoming[2][b][:, None, :], roll_up(north, 1))
        total = total + jnp.where(
            row == row.shape[1] - 1, incoming[3][b][:, None, :], roll_down(south, 1)
        )
        result[b] = total + layer_moves(rise, fall)
        outgoing[0].append(west[0])
        outgoing[1].append(east[-1])
        outgoing[2].append(south[:, 0, :])
        outgoing[3].append(north[:, -1, :])
    return result, outgoing


def face_stencil(face, first, second, low_end, high_end, behind, entering):
    def planes(start):
        return lambda e: face[start + e]

    result = product(planes(DIAGONAL), first, second)
    up = product(planes(LAT_UP), first, second)
    down = product(planes(LAT_DOWN), first, second)
    rise = product(planes(RISE), first, second)
    fall = product(planes(FALL), first, second)
    row = iota(first.shape, 0)
    for b in range(2):
        total = result[b] + behind[b] + entering[b]
        total = total + jnp.where(row == 0, low_end[b], roll_up(up[b], 0))
        total = total + jnp.where(row == row.shape[0] - 1, high_end[b], roll_down(down[b], 0))
        result[b] = total + layer_moves(rise[b], fall[b])
    return result


def spread(totals, ids):
    table = jnp.broadcast_to(totals, (8, LANES))
    if ids.ndim == 2:
        return jnp.take_along_axis(table, ids, axis=1)
    return jnp.stack(
        [jnp.take_along_axis(table, ids[x], axis=1) for x in range(ids.shape[0])], axis=0
    )


def as_ids(plane):
    return plane.astype(jnp.int32)


class Corner:
    def __init__(self, pack, which, base):
        self.pack, self.start = pack, base * 8 + which

    def row(self, number):
        at = self.start + number
        return self.pack[at // 8, at % 8 : at % 8 + 1, :]


def corners_of(faces, base, rows):
    found = []
    for y_face in (2, 3):
        for x_end in range(2):
            found.append(Corner(faces[y_face], x_end * rows, base))
    return found


def corner_inputs(corners, values):
    ends = {}
    for c in range(4):
        x_end, y_end = c % 2, c // 2
        over_x = product(corners[c].row, *values[c])
        over_y = product(lambda e, c=c: corners[c].row(SIDE_IN + e), *values[c])
        ends[(2 + y_end, x_end)] = over_x
        ends[(x_end, y_end)] = over_y
    return ends


def put(row_number, lane_number, value, table):
    at = (iota(table.shape, 0) == row_number) & (iota(table.shape, 1) == lane_number)
    return jnp.where(at, value, table)


def full_sum(value):
    while value.ndim > 2:
        value = jnp.sum(value, axis=0)
    return jnp.sum(jnp.sum(value, axis=0, keepdims=True), axis=1, keepdims=True)


def segment_rows(ids, values, scratch):
    masks_at = [ids[x] for x in range(ids.shape[0])]
    fields = [[value[x] for x in range(ids.shape[0])] for value in values]
    scratch[:, WELLS:, :] = jnp.zeros_like(scratch[:, WELLS:, :])
    for w in range(WELLS):
        masks = [at == w for at in masks_at]
        for number, field in enumerate(fields):
            total = jnp.where(masks[0], field[0], 0.0)
            for x in range(1, len(masks)):
                total = total + jnp.where(masks[x], field[x], 0.0)
            scratch[number, w : w + 1, :] = jnp.sum(total, axis=0, keepdims=True)
    ones = jnp.ones((8, LANES), jnp.float32)
    rows = []
    for number in range(len(fields)):
        summed = lax.dot_general(
            ones,
            scratch[number],
            (((1,), (1,)), ((), ())),
            precision=lax.Precision.HIGHEST,
            preferred_element_type=jnp.float32,
        )
        rows.append(summed[0:1, :])
    return rows


def pack_rows(rows, table):
    for number, row in enumerate(rows):
        placed = row if number % 3 == 0 else pltpu.roll(row, WELLS * (number % 3), 1)
        table = table + jnp.where(
            iota(table.shape, 0) == number // 3, jnp.broadcast_to(placed, table.shape), 0.0
        )
    return table


def unpack_row(table, number):
    row = table[number // 3 : number // 3 + 1, :]
    if number % 3:
        row = pltpu.roll(row, LANES - WELLS * (number % 3), 1)
    return jnp.where(iota(row.shape, 1) < WELLS, row, 0.0)


def lane(table, row_number, lane_number):
    return table[row_number : row_number + 1, lane_number : lane_number + 1]


def lane_sum(row):
    return jnp.sum(row, axis=1, keepdims=True)


def pack_kernel(
    couplings, diagonal, wells, ids, right, guess, x_low, x_high, y_low, y_high
):
    last = guess.shape[2] - 1
    for axis, packs in ((0, (x_low, x_high)), (1, (y_low, y_high))):
        for end, pack in enumerate(packs):
            outer = 0 if end == 0 else last
            behind = 1 if end == 0 else last - 1
            inward = 2 * axis + (1 if end == 0 else 0)
            lateral = 2 * (1 - axis)

            def cut(ref, *index, at=outer):
                if axis == 0:
                    return ref[index + (at,)]
                return ref[index + (slice(None), at, slice(None))]

            for e in range(4):
                pack[e] = cut(couplings, inward, e)
                pack[LAT_UP + e] = cut(couplings, lateral, e)
                pack[LAT_DOWN + e] = cut(couplings, lateral + 1, e)
                pack[RISE + e] = cut(couplings, 4, e)
                pack[FALL + e] = cut(couplings, 5, e)
                pack[DIAGONAL + e] = cut(diagonal, e)
                pack[BACK_IN + e] = cut(couplings, inward, e, at=behind)
            for a in range(2):
                pack[WELL_EQ + a] = cut(wells, 2 + a)
                pack[BACK_EQ + a] = cut(wells, 2 + a, at=behind)
            pack[WELL_ID] = cut(ids).astype(jnp.float32)
            pack[BACK_ID] = cut(ids, at=behind).astype(jnp.float32)
            for k in range(RHS):
                for a in range(2):
                    pack[GUESS + 2 * k + a] = cut(guess, k, a)
                    pack[RIGHT + 2 * k + a] = cut(right, k, a)
                entering = product(
                    lambda e: cut(couplings, inward, e, at=behind),
                    cut(guess, k, 0, at=behind),
                    cut(guess, k, 1, at=behind),
                )
                pack[BACK_GUESS + 2 * k] = entering[0]
                pack[BACK_GUESS + 2 * k + 1] = entering[1]


def guess_kernel(wells, ids, guess, part, scratch):
    values = [wells[0] * guess[k, 0] + wells[1] * guess[k, 1] for k in range(RHS)]
    values.append(wells[0] * wells[2] + wells[1] * wells[3])
    values.append(wells[2] * wells[2] + wells[3] * wells[3])
    rows = segment_rows(ids, values, scratch)
    table = pack_rows(rows, jnp.zeros((8, LANES), jnp.float32))
    part[...] = jnp.broadcast_to(table[None, :2], part.shape)


def residual_kernel(
    couplings, diagonal, wells, ids, right, guess, fxl, fxh, fyl, fyh, parts,
    residual, image, residual_faces, x_low, x_high, y_low, y_high, part, small,
    scratch,
):
    faces = (fxl, fxh, fyl, fyh)
    totals = jnp.sum(parts[...], axis=0)
    corners = corners_of(faces, FACE_PLANES, CORNER_ROWS)
    all_ids = ids[...]
    face_ids = [as_ids(face[WELL_ID]) for face in faces]
    last = guess.shape[2] - 1
    table = jnp.zeros((8, LANES), jnp.float32)
    for k in range(RHS):
        s_row = unpack_row(totals, k)
        first, second = guess[k, 0], guess[k, 1]
        incoming = [
            product(
                lambda e, f=f: faces[f][e],
                faces[f][GUESS + 2 * k],
                faces[f][GUESS + 2 * k + 1],
            )
            for f in range(4)
        ]
        applied, outgoing = block_stencil(couplings, diagonal, first, second, incoming)
        at_wells = spread(s_row, all_ids)
        now = [
            right[k, a] - applied[a] - wells[2 + a] * at_wells for a in range(2)
        ]
        for a in range(2):
            residual[k, a] = now[a]
        ends = corner_inputs(
            corners,
            [[corners[c].row(SIDE_GUESS + 2 * k + a) for a in range(2)] for c in range(4)],
        )
        incoming = []
        for f in range(4):
            face = faces[f]
            there = face_stencil(
                face,
                face[GUESS + 2 * k],
                face[GUESS + 2 * k + 1],
                ends[(f, 0)],
                ends[(f, 1)],
                [face[BACK_GUESS + 2 * k + b] for b in range(2)],
                outgoing[f],
            )
            face_wells = spread(s_row, face_ids[f])
            outer = [
                face[RIGHT + 2 * k + a] - there[a] - face[WELL_EQ + a] * face_wells
                for a in range(2)
            ]
            for a in range(2):
                residual_faces[f, 2 * k + a] = outer[a]
            incoming.append(product(lambda e, f=f: faces[f][e], *outer))
        result, _ = block_stencil(couplings, diagonal, now[0], now[1], incoming)
        for a in range(2):
            image[k, a] = result[a]
            x_low[2 * k + a] = result[a][0]
            x_low[8 + 2 * k + a] = result[a][1]
            x_high[2 * k + a] = result[a][last]
            x_high[8 + 2 * k + a] = result[a][last - 1]
            y_low[2 * k + a] = result[a][:, 0, :]
            y_low[8 + 2 * k + a] = result[a][:, 1, :]
            y_high[2 * k + a] = result[a][:, last, :]
            y_high[8 + 2 * k + a] = result[a][:, last - 1, :]
        table = put(6, k, full_sum(now[0] * now[0] + now[1] * now[1]), table)
        table = put(6, 4 + k, full_sum(now[0] * result[0] + now[1] * result[1]), table)
        table = put(6, 8 + k, full_sum(result[0] * result[0] + result[1] * result[1]), table)
    values = []
    for side in (0, 2):
        for field in (residual, image):
            for k in range(RHS):
                values.append(wells[side] * field[k, 0] + wells[side + 1] * field[k, 1])
    rows = segment_rows(all_ids, values, scratch)
    table = pack_rows(rows, table)
    part[...] = jnp.broadcast_to(table[None], part.shape)
    small[...] = jnp.concatenate(
        [unpack_row(totals, 4), unpack_row(totals, 5), jnp.zeros((6, LANES), jnp.float32)], axis=0
    )


def first_step(totals, small, k):
    s_row, us_row = unpack_row(totals, k), unpack_row(totals, 4 + k)
    p_row, ps_row = unpack_row(totals, 8 + k), unpack_row(totals, 12 + k)
    within, equation = small[0:1, :], small[1:2, :]
    rr, rs, ss = (lane(totals, 6, 4 * i + k) for i in range(3))
    height = (rs + lane_sum(p_row * s_row)) / rr
    square = ss + lane_sum(2.0 * ps_row * s_row + equation * s_row * s_row)
    left = jnp.maximum(square - height * height * rr, 1e-7 * square)
    scale = lax.rsqrt(left)
    s_image = us_row + within * s_row
    s_second = (s_image - height * s_row) * scale
    p_second = (ps_row + equation * s_row - height * p_row) * scale
    shift = rs / rr + lane_sum(p_second * s_second)
    return dict(
        rr=rr, height=height, scale=scale, shift=shift, s_row=s_row, s_image=s_image,
        p_row=p_row, p_second=p_second,
    )


def krylov_kernel(
    couplings, diagonal, wells, ids, fxl, fxh, fyl, fyh, gxl, gxh, gyl, gyh,
    residual, image, residual_faces, parts, small_in,
    second_out, third_out, part, totals_out, scratch, values_scratch,
):
    faces, sent = (fxl, fxh, fyl, fyh), (gxl, gxh, gyl, gyh)
    totals = jnp.sum(parts[...], axis=0)
    totals_out[...] = totals
    small = small_in[...]
    corners = corners_of(faces, FACE_PLANES, CORNER_ROWS)
    sent_corners = corners_of(sent, 16, 8)
    all_ids = ids[...]
    face_ids = [as_ids(face[WELL_ID]) for face in faces]
    back_ids = [as_ids(face[BACK_ID]) for face in faces]
    corner_ids = [
        as_ids(jnp.broadcast_to(corner.row(SIDE_ID), (8, LANES))) for corner in corners
    ]
    table = jnp.zeros((8, LANES), jnp.float32)
    values = []
    for k in range(RHS):
        step = first_step(totals, small, k)
        height, scale, shift = step["height"], step["scale"], step["shift"]
        s_row, s_image = step["s_row"], step["s_image"]
        at_wells = spread(s_row, all_ids)
        now = [image[k, a] + wells[2 + a] * at_wells for a in range(2)]
        face_now, back_in = [], []
        for f in range(4):
            face, got = faces[f], sent[f]
            here = spread(s_row, face_ids[f])
            face_now.append([got[2 * k + a] + face[WELL_EQ + a] * here for a in range(2)])
            there = spread(s_row, back_ids[f])
            back = [got[8 + 2 * k + a] + face[BACK_EQ + a] * there for a in range(2)]
            back_in.append(product(lambda e, f=f: faces[f][BACK_IN + e], *back))
        corner_now = []
        for c in range(4):
            here = spread(s_row, corner_ids[c])[0:1, :]
            corner_now.append(
                [
                    sent_corners[c].row(2 * k + a) + corners[c].row(SIDE_EQ + a) * here
                    for a in range(2)
                ]
            )
        incoming = [product(lambda e, f=f: faces[f][e], *face_now[f]) for f in range(4)]
        applied, outgoing = block_stencil(couplings, diagonal, now[0], now[1], incoming)
        at_wells = spread(s_image, all_ids)
        second, third = [], []
        for a in range(2):
            twice = applied[a] + wells[2 + a] * at_wells
            base = (now[a] - height * residual[k, a]) * scale
            second.append(base)
            third.append((twice - height * now[a]) * scale - shift * base)
            second_out[k, a] = second[a]
            third_out[k, a] = third[a]
        ends = corner_inputs(corners, corner_now)
        incoming = []
        for f in range(4):
            face = faces[f]
            there = face_stencil(
                face, face_now[f][0], face_now[f][1], ends[(f, 0)], ends[(f, 1)], back_in[f],
                outgoing[f],
            )
            here = spread(s_image, face_ids[f])
            outer = []
            for a in range(2):
                twice = there[a] + face[WELL_EQ + a] * here
                base = (face_now[f][a] - height * residual_faces[f, 2 * k + a]) * scale
                outer.append((twice - height * face_now[f][a]) * scale - shift * base)
            incoming.append(product(lambda e, f=f: faces[f][e], *outer))
        result, _ = block_stencil(couplings, diagonal, third[0], third[1], incoming)
        fourth = [result[a] - shift * third[a] for a in range(2)]
        values_scratch[k] = wells[0] * third[0] + wells[1] * third[1]
        values_scratch[4 + k] = wells[2] * third[0] + wells[3] * third[1]
        values_scratch[8 + k] = wells[2] * fourth[0] + wells[3] * fourth[1]
        unit = lax.rsqrt(step["rr"])
        fields = [[residual[k, a] * unit for a in range(2)], second, third, fourth]
        number = 0
        for i in range(4):
            for j in range(i, 4):
                dot = full_sum(fields[i][0] * fields[j][0] + fields[i][1] * fields[j][1])
                table = put(4, 4 * number + k, dot, table)
                number += 1
    rows = segment_rows(all_ids, [values_scratch[n] for n in range(12)], scratch)
    table = pack_rows(rows, table)
    part[...] = jnp.broadcast_to(table[None], part.shape)


def solve_kernel(
    guess, residual, second, third, parts, first_totals, small_in, solution
):
    totals = jnp.sum(parts[...], axis=0)
    before, small = first_totals[...], small_in[...]
    equation = small[1:2, :]
    for k in range(RHS):
        step = first_step(before, small, k)
        unit = lax.rsqrt(step["rr"])
        beta = step["rr"] * unit
        s_third, p_third = unpack_row(totals, k), unpack_row(totals, 4 + k)
        p_fourth = unpack_row(totals, 8 + k)
        gram = {}
        number = 0
        for i in range(4):
            for j in range(i, 4):
                gram[(i, j)] = lane(totals, 4, 4 * number + k)
                number += 1
        gram[(0, 3)] += lane_sum(step["p_row"] * s_third) * unit
        gram[(1, 3)] += lane_sum(step["p_second"] * s_third)
        gram[(2, 3)] += lane_sum(p_third * s_third)
        gram[(3, 3)] += lane_sum(2.0 * p_fourth * s_third + equation * s_third * s_third)
        tiny = 1e-30
        inverse = [lax.rsqrt(jnp.maximum(gram[(i, i)], tiny)) for i in range(4)]
        length = [jnp.maximum(gram[(i, i)], tiny) * inverse[i] for i in range(4)]
        upper = {}
        for i in range(4):
            for j in range(i, 4):
                entry = gram[(i, j)] * inverse[i] * inverse[j]
                for m in range(i):
                    entry = entry - upper[(m, i)] * upper[(m, j)]
                if i == j:
                    pivot = lax.rsqrt(jnp.maximum(entry, 1e-6))
                    upper[(i, i)] = jnp.maximum(entry, 1e-6) * pivot
                    over = pivot
                else:
                    upper[(i, j)] = entry * over
        shift = step["shift"]
        following = lax.rsqrt(step["rr"]) / step["scale"]
        columns = [
            [(0, step["height"] * length[0]), (1, following * length[1])],
            [(1, shift * length[1]), (2, length[2])],
            [(2, shift * length[2]), (3, length[3])],
        ]
        zero = jnp.zeros_like(shift)
        hessenberg = [[zero] * 3 for _ in range(4)]
        for j in range(3):
            for i in range(j + 2):
                for m, factor in columns[j]:
                    if m >= i:
                        hessenberg[i][j] = hessenberg[i][j] + upper[(i, m)] * factor
        target = [beta * length[0] * upper[(0, 0)], zero, zero, zero]
        for j in range(3):
            top, bottom = hessenberg[j][j], hessenberg[j + 1][j]
            turn = lax.rsqrt(top * top + bottom * bottom)
            cosine, sine = top * turn, bottom * turn
            for m in range(j, 3):
                high, low = hessenberg[j][m], hessenberg[j + 1][m]
                hessenberg[j][m] = cosine * high + sine * low
                hessenberg[j + 1][m] = cosine * low - sine * high
            high, low = target[j], target[j + 1]
            target[j] = cosine * high + sine * low
            target[j + 1] = cosine * low - sine * high
        weights = [zero] * 3
        for i in (2, 1, 0):
            value = target[i]
            for j in range(i + 1, 3):
                value = value - hessenberg[i][j] * weights[j]
            weights[i] = value / hessenberg[i][i]
        for a in range(2):
            solution[k, a] = (
                guess[k, a]
                + (weights[0] * unit) * residual[k, a]
                + weights[1] * second[k, a]
                + weights[2] * third[k, a]
            )


def call(kernel, shapes, arguments, scratch=()):
    whole = pl.BlockSpec(memory_space=pltpu.VMEM)
    return pl.pallas_call(
        kernel,
        out_shape=[jax.ShapeDtypeStruct(shape, jnp.float32) for shape in shapes],
        in_specs=[whole] * len(arguments),
        out_specs=[whole] * len(shapes),
        scratch_shapes=[pltpu.VMEM(shape, jnp.float32) for shape in scratch],
        compiler_params=pltpu.CompilerParams(vmem_limit_bytes=24 << 20),
    )(*arguments)


def from_behind(value, axis, steps):
    count = lax.axis_size(axis)
    leading, last = (max(0, -steps), min(count, count - steps))
    return lax.ppermute(value, axis, [(source, source + steps) for source in range(leading, last)])


def exchanged(part):
    return lax.all_to_all(part, ("gx", "gy"), 0, 0, tiled=True)


def corner_planes(rows):
    stacked = jnp.concatenate(rows, axis=0)
    spare = -stacked.shape[0] % 8
    if spare:
        stacked = jnp.pad(stacked, ((0, spare), (0, 0)))
    return stacked.reshape(-1, 8, LANES)


def body(couplings, diagonal, wells, ids, right, guess):
    devices = lax.axis_size("gx") * lax.axis_size("gy")
    plane = (8, LANES)
    field = guess.shape
    last = guess.shape[2] - 1

    packs = call(
        pack_kernel,
        [(FACE_PLANES,) + plane] * 4,
        (couplings, diagonal, wells, ids, right, guess),
    )
    fxl = from_behind(packs[1], "gx", 1)
    fxh = from_behind(packs[0], "gx", -1)
    (part,) = call(guess_kernel, [(devices, 2, LANES)], (wells, ids, guess), [(6, LANES, LANES)])
    parts = exchanged(part)
    packed = []
    for pack, at, side in ((packs[2], 0, LAT_DOWN), (packs[3], last, LAT_UP)):
        rows = []
        for face in (fxl, fxh):
            rows += [face[0:4, at], face[side : side + 4, at], face[WELL_EQ : GUESS + 8, at]]
        packed.append(jnp.concatenate([pack, corner_planes(rows)], axis=0))
    fyl = from_behind(packed[1], "gy", 1)
    fyh = from_behind(packed[0], "gy", -1)

    residual, image, residual_faces, x_low, x_high, y_low, y_high, part, small = call(
        residual_kernel,
        [field, field, (4, 8) + plane]
        + [(16,) + plane] * 4
        + [(devices, 8, LANES), (8, LANES)],
        (couplings, diagonal, wells, ids, right, guess, fxl, fxh, fyl, fyh, parts),
        [(16, LANES, LANES)],
    )
    gxl = from_behind(x_high, "gx", 1)
    gxh = from_behind(x_low, "gx", -1)
    parts = exchanged(part)
    packed = []
    for pack, at in ((y_low, 0), (y_high, last)):
        rows = [face[0:8, at] for face in (gxl, gxh)]
        packed.append(jnp.concatenate([pack, corner_planes(rows)], axis=0))
    gyl = from_behind(packed[1], "gy", 1)
    gyh = from_behind(packed[0], "gy", -1)

    second, third, part, totals = call(
        krylov_kernel,
        [field, field, (devices, 8, LANES), (8, LANES)],
        (couplings, diagonal, wells, ids, fxl, fxh, fyl, fyh, gxl, gxh, gyl, gyh)
        + (residual, image, residual_faces, parts, small),
        [(12, LANES, LANES), (12,) + guess.shape[2:]],
    )
    parts = exchanged(part)
    (result,) = call(
        solve_kernel,
        [field],
        (guess, residual, second, third, parts, totals, small),
    )
    return result


def solution(mesh):
    in_specs = (
        P("member", None, "gx", "gy", None),
        P("member", "gx", "gy", None),
        P("member", "gx", "gy", None),
        P("gx", "gy", None),
        P("member", None, "gx", "gy", None),
        P("member", None, "gx", "gy", None),
    )
    out_specs = P("member", None, "gx", "gy", None)
    return jax.shard_map(body, mesh=mesh, in_specs=in_specs, out_specs=out_specs, check_vma=False)
```

```python
import jax
import jax.numpy as jnp
from jax import lax
from jax.experimental import pallas as pl
from jax.experimental.pallas import tpu as pltpu
from jax.sharding import PartitionSpec as P

WELLS = 40
RHS = 4
LANES = 128
LAT_UP, LAT_DOWN, RISE, FALL, DIAGONAL = 4, 8, 12, 16, 20
WELL_EQ, WELL_ID, GUESS, REST = 24, 26, 27, 35
BACK_IN, BACK_EQ, BACK_ID = 43, 47, 49
FACE_PLANES = 50
CORNER_PLANES = 5
CORNER_ROWS = 19
SIDE_IN, SIDE_EQ, SIDE_ID, SIDE_GUESS = 4, 8, 10, 11


def product(blocks, first, second):
    return [
        blocks(0) * first + blocks(2) * second,
        blocks(1) * first + blocks(3) * second,
    ]


def iota(shape, axis):
    return lax.broadcasted_iota(jnp.int32, shape, axis)


def roll_up(value, axis):
    return pltpu.roll(value, 1, axis)


def roll_down(value, axis):
    return pltpu.roll(value, value.shape[axis] - 1, axis)


def layer_moves(rising, falling):
    axis = rising.ndim - 1
    lane = iota(rising.shape, axis)
    up = jnp.where(lane == 0, 0.0, roll_up(rising, axis))
    down = jnp.where(lane == LANES - 1, 0.0, roll_down(falling, axis))
    return up + down


def block_stencil(couplings, diagonal, first, second, incoming):
    result = product(lambda e: diagonal[e], first, second)
    moved = [product(lambda e, d=d: couplings[d, e], first, second) for d in range(6)]
    row = iota(first.shape, 1)
    outgoing = [[], [], [], []]
    for b in range(2):
        east, west, north, south, rise, fall = (moved[d][b] for d in range(6))
        total = result[b] + jnp.concatenate([incoming[0][b][None], east[:-1]], axis=0)
        total = total + jnp.concatenate([west[1:], incoming[1][b][None]], axis=0)
        total = total + jnp.where(row == 0, incoming[2][b][:, None, :], roll_up(north, 1))
        total = total + jnp.where(
            row == row.shape[1] - 1, incoming[3][b][:, None, :], roll_down(south, 1)
        )
        result[b] = total + layer_moves(rise, fall)
        outgoing[0].append(west[0])
        outgoing[1].append(east[-1])
        outgoing[2].append(south[:, 0, :])
        outgoing[3].append(north[:, -1, :])
    return result, outgoing


def face_stencil(face, first, second, behind):
    def planes(start):
        return lambda e: face[start + e]

    result = product(planes(DIAGONAL), first, second)
    up = product(planes(LAT_UP), first, second)
    down = product(planes(LAT_DOWN), first, second)
    rise = product(planes(RISE), first, second)
    fall = product(planes(FALL), first, second)
    row = iota(first.shape, 0)
    for b in range(2):
        total = result[b] + behind[b] + layer_moves(rise[b], fall[b])
        total = total + jnp.where(row == 0, 0.0, roll_up(up[b], 0))
        result[b] = total + jnp.where(row == row.shape[0] - 1, 0.0, roll_down(down[b], 0))
    return result


def face_entries(low_end, high_end, entering):
    row = iota(entering[0].shape, 0)
    return [
        entering[b]
        + jnp.where(row == 0, low_end[b], 0.0)
        + jnp.where(row == row.shape[0] - 1, high_end[b], 0.0)
        for b in range(2)
    ]


def spread(totals, ids):
    table = jnp.broadcast_to(totals, (8, LANES))
    if ids.ndim == 2:
        return jnp.take_along_axis(table, ids, axis=1)
    return jnp.stack(
        [jnp.take_along_axis(table, ids[x], axis=1) for x in range(ids.shape[0])], axis=0
    )


def as_ids(plane):
    return plane.astype(jnp.int32)


class Corner:
    def __init__(self, pack, which, base):
        self.pack, self.start = pack, base * 8 + which

    def row(self, number):
        at = self.start + number
        return self.pack[at // 8, at % 8 : at % 8 + 1, :]


def corners_of(faces, base, rows):
    found = []
    for y_face in (2, 3):
        for x_end in range(2):
            found.append(Corner(faces[y_face], x_end * rows, base))
    return found


def corner_inputs(corners, values):
    ends = {}
    for c in range(4):
        x_end, y_end = c % 2, c // 2
        over_x = product(corners[c].row, *values[c])
        over_y = product(lambda e, c=c: corners[c].row(SIDE_IN + e), *values[c])
        ends[(2 + y_end, x_end)] = over_x
        ends[(x_end, y_end)] = over_y
    return ends


def put(row_number, lane_number, value, table):
    at = (iota(table.shape, 0) == row_number) & (iota(table.shape, 1) == lane_number)
    return jnp.where(at, value, table)


def full_sum(value):
    while value.ndim > 2:
        value = jnp.sum(value, axis=0)
    return jnp.sum(jnp.sum(value, axis=0, keepdims=True), axis=1, keepdims=True)


def segment_rows(ids, values, scratch):
    scratch[...] = jnp.zeros_like(scratch)
    count, depth = values.shape[0], ids.shape[0]

    def smallest(planes):
        least = planes[0]
        for plane in planes[1:]:
            least = jnp.minimum(least, plane)
        return jnp.min(least)

    def one_well(well):
        planes = [ids[x].astype(jnp.float32) for x in range(depth)]
        masks = [plane == well for plane in planes]
        at = well.astype(jnp.int32)
        for number in range(count):
            total = jnp.where(masks[0], values[number, 0], 0.0)
            for x in range(1, depth):
                total = total + jnp.where(masks[x], values[number, x], 0.0)
            scratch[number, pl.ds(at, 1), :] = jnp.sum(total, axis=0, keepdims=True)
        return smallest([jnp.where(plane > well, plane, float(WELLS)) for plane in planes])

    first = smallest([ids[x].astype(jnp.float32) for x in range(depth)])
    lax.while_loop(lambda well: well < WELLS, one_well, first)
    rows = []
    for number in range(count):
        summed = jnp.sum(scratch[number], axis=1, keepdims=True)
        shape = scratch.shape[1:]
        on_lanes = jnp.where(iota(shape, 0) == iota(shape, 1), summed, 0.0)
        rows.append(jnp.sum(on_lanes, axis=0, keepdims=True))
    return rows


def pack_rows(rows, table):
    for number, row in enumerate(rows):
        placed = row if number % 3 == 0 else pltpu.roll(row, WELLS * (number % 3), 1)
        table = table + jnp.where(
            iota(table.shape, 0) == number // 3, jnp.broadcast_to(placed, table.shape), 0.0
        )
    return table


def unpack_row(table, number):
    row = table[number // 3 : number // 3 + 1, :]
    if number % 3:
        row = pltpu.roll(row, LANES - WELLS * (number % 3), 1)
    return jnp.where(iota(row.shape, 1) < WELLS, row, 0.0)


def lane(table, row_number, lane_number):
    return table[row_number : row_number + 1, lane_number : lane_number + 1]


def lane_sum(row):
    return jnp.sum(row, axis=1, keepdims=True)


def pack_kernel(
    couplings_in, diagonal_in, wells_in, ids_in, right_in, guess_in,
    x_low, x_high, y_low, y_high,
    couplings, diagonal, wells, ids, right, guess, arrived,
):
    copies = [
        pltpu.make_async_copy(source, held, arrived.at[n])
        for n, (source, held) in enumerate(
            (
                (couplings_in, couplings),
                (diagonal_in, diagonal),
                (wells_in, wells),
                (ids_in, ids),
                (right_in, right),
                (guess_in, guess),
            )
        )
    ]
    for copy in copies:
        copy.start()
    for copy in copies:
        copy.wait()
    last = guess.shape[2] - 1
    for axis, packs in ((0, (x_low, x_high)), (1, (y_low, y_high))):
        for end, pack in enumerate(packs):
            outer = 0 if end == 0 else last
            behind = 1 if end == 0 else last - 1
            inward = 2 * axis + (1 if end == 0 else 0)
            lateral = 2 * (1 - axis)

            def cut(ref, *index, at=outer):
                if axis == 0:
                    return ref[index + (at,)]
                return ref[index + (slice(None), at, slice(None))]

            for e in range(4):
                pack[e] = cut(couplings, inward, e)
                pack[LAT_UP + e] = cut(couplings, lateral, e)
                pack[LAT_DOWN + e] = cut(couplings, lateral + 1, e)
                pack[RISE + e] = cut(couplings, 4, e)
                pack[FALL + e] = cut(couplings, 5, e)
                pack[DIAGONAL + e] = cut(diagonal, e)
                pack[BACK_IN + e] = cut(couplings, inward, e, at=behind)
            for a in range(2):
                pack[WELL_EQ + a] = cut(wells, 2 + a)
                pack[BACK_EQ + a] = cut(wells, 2 + a, at=behind)
            pack[WELL_ID] = cut(ids).astype(jnp.float32)
            pack[BACK_ID] = cut(ids, at=behind).astype(jnp.float32)
            for k in range(RHS):
                here = [cut(guess, k, a) for a in range(2)]
                entering = product(
                    lambda e: pack[BACK_IN + e],
                    cut(guess, k, 0, at=behind),
                    cut(guess, k, 1, at=behind),
                )
                local = face_stencil(pack, here[0], here[1], entering)
                for a in range(2):
                    pack[GUESS + 2 * k + a] = here[a]
                    pack[REST + 2 * k + a] = cut(right, k, a) - local[a]


def corner_kernel(y_low, y_high, fxl, fxh, low_out, high_out):
    last = fxl.shape[1] - 1
    for own, out, at, side in ((y_low, low_out, 0, LAT_DOWN), (y_high, high_out, last, LAT_UP)):
        for n in range(FACE_PLANES):
            out[n] = own[n]
        row = FACE_PLANES * 8
        out[FACE_PLANES + CORNER_PLANES - 1] = jnp.zeros(out.shape[1:], jnp.float32)
        for face in (fxl, fxh):
            for n in (*range(4), *range(side, side + 4), *range(WELL_EQ, REST)):
                out[row // 8, row % 8 : row % 8 + 1, :] = face[n, at : at + 1, :]
                row += 1


def image_corner_kernel(y_low, y_high, gxl, gxh, low_out, high_out):
    last = gxl.shape[1] - 1
    for own, out, at in ((y_low, low_out, 0), (y_high, high_out, last)):
        for n in range(16):
            out[n] = own[n]
        for x_end, face in enumerate((gxl, gxh)):
            for n in range(8):
                out[16 + x_end, n : n + 1, :] = face[n, at : at + 1, :]


def guess_kernel(wells, ids, guess, part, values, scratch):
    for k in range(RHS):
        values[k] = wells[0] * guess[k, 0] + wells[1] * guess[k, 1]
    values[4] = wells[0] * wells[2] + wells[1] * wells[3]
    values[5] = wells[2] * wells[2] + wells[3] * wells[3]
    rows = segment_rows(ids, values, scratch)
    table = pack_rows(rows, jnp.zeros((8, LANES), jnp.float32))
    part[...] = jnp.broadcast_to(table[None, :2], part.shape)


def residual_kernel(
    couplings, diagonal, wells, ids, right, guess, fxl, fxh, fyl, fyh, parts,
    residual, image, residual_faces, x_low, x_high, y_low, y_high, small,
):
    faces = (fxl, fxh, fyl, fyh)
    totals = jnp.sum(parts[...], axis=0)
    corners = corners_of(faces, FACE_PLANES, CORNER_ROWS)
    all_ids = ids[...]
    face_ids = [as_ids(face[WELL_ID]) for face in faces]
    last = guess.shape[2] - 1
    for k in range(RHS):
        s_row = unpack_row(totals, k)
        first, second = guess[k, 0], guess[k, 1]
        incoming = [
            product(
                lambda e, f=f: faces[f][e],
                faces[f][GUESS + 2 * k],
                faces[f][GUESS + 2 * k + 1],
            )
            for f in range(4)
        ]
        applied, outgoing = block_stencil(couplings, diagonal, first, second, incoming)
        at_wells = spread(s_row, all_ids)
        now = [
            right[k, a] - applied[a] - wells[2 + a] * at_wells for a in range(2)
        ]
        for a in range(2):
            residual[k, a] = now[a]
        ends = corner_inputs(
            corners,
            [[corners[c].row(SIDE_GUESS + 2 * k + a) for a in range(2)] for c in range(4)],
        )
        incoming = []
        for f in range(4):
            face = faces[f]
            there = face_entries(ends[(f, 0)], ends[(f, 1)], outgoing[f])
            face_wells = spread(s_row, face_ids[f])
            outer = [
                face[REST + 2 * k + a] - there[a] - face[WELL_EQ + a] * face_wells
                for a in range(2)
            ]
            for a in range(2):
                residual_faces[f, 2 * k + a] = outer[a]
            incoming.append(product(lambda e, f=f: faces[f][e], *outer))
        result, _ = block_stencil(couplings, diagonal, now[0], now[1], incoming)
        for a in range(2):
            image[k, a] = result[a]
            x_low[2 * k + a] = result[a][0]
            x_low[8 + 2 * k + a] = result[a][1]
            x_high[2 * k + a] = result[a][last]
            x_high[8 + 2 * k + a] = result[a][last - 1]
            y_low[2 * k + a] = result[a][:, 0, :]
            y_low[8 + 2 * k + a] = result[a][:, 1, :]
            y_high[2 * k + a] = result[a][:, last, :]
            y_high[8 + 2 * k + a] = result[a][:, last - 1, :]
    small[...] = jnp.concatenate(
        [unpack_row(totals, 4), unpack_row(totals, 5), jnp.zeros((6, LANES), jnp.float32)], axis=0
    )


def moments_kernel(wells, ids, residual, image, part, values, scratch):
    table = jnp.zeros((8, LANES), jnp.float32)
    for k in range(RHS):
        now = [residual[k, a] for a in range(2)]
        result = [image[k, a] for a in range(2)]
        for n, field in enumerate((now, result)):
            values[4 * n + k] = wells[0] * field[0] + wells[1] * field[1]
            values[8 + 4 * n + k] = wells[2] * field[0] + wells[3] * field[1]
        table = put(6, k, full_sum(now[0] * now[0] + now[1] * now[1]), table)
        table = put(6, 4 + k, full_sum(now[0] * result[0] + now[1] * result[1]), table)
        table = put(6, 8 + k, full_sum(result[0] * result[0] + result[1] * result[1]), table)
    rows = segment_rows(ids, values, scratch)
    table = pack_rows(rows, table)
    part[...] = jnp.broadcast_to(table[None], part.shape)


def first_step(totals, small, k):
    s_row, us_row = unpack_row(totals, k), unpack_row(totals, 4 + k)
    p_row, ps_row = unpack_row(totals, 8 + k), unpack_row(totals, 12 + k)
    within, equation = small[0:1, :], small[1:2, :]
    rr, rs, ss = (lane(totals, 6, 4 * i + k) for i in range(3))
    height = (rs + lane_sum(p_row * s_row)) / rr
    square = ss + lane_sum(2.0 * ps_row * s_row + equation * s_row * s_row)
    left = jnp.maximum(square - height * height * rr, 1e-7 * square)
    scale = lax.rsqrt(left)
    s_image = us_row + within * s_row
    s_second = (s_image - height * s_row) * scale
    p_second = (ps_row + equation * s_row - height * p_row) * scale
    shift = rs / rr + lane_sum(p_second * s_second)
    return dict(
        rr=rr, height=height, scale=scale, shift=shift, s_row=s_row, s_image=s_image,
        p_row=p_row, p_second=p_second,
    )


def krylov_kernel(
    couplings, diagonal, wells, ids, fxl, fxh, fyl, fyh, gxl, gxh, gyl, gyh,
    residual, image, residual_faces, parts, small_in,
    second_out, third_out, part, totals_out, scratch, values_scratch,
):
    faces, sent = (fxl, fxh, fyl, fyh), (gxl, gxh, gyl, gyh)
    totals = jnp.sum(parts[...], axis=0)
    totals_out[...] = totals
    small = small_in[...]
    corners = corners_of(faces, FACE_PLANES, CORNER_ROWS)
    sent_corners = corners_of(sent, 16, 8)
    all_ids = ids[...]
    face_ids = [as_ids(face[WELL_ID]) for face in faces]
    back_ids = [as_ids(face[BACK_ID]) for face in faces]
    corner_ids = [
        as_ids(jnp.broadcast_to(corner.row(SIDE_ID), (8, LANES))) for corner in corners
    ]
    table = jnp.zeros((8, LANES), jnp.float32)
    values = []
    for k in range(RHS):
        step = first_step(totals, small, k)
        height, scale, shift = step["height"], step["scale"], step["shift"]
        s_row, s_image = step["s_row"], step["s_image"]
        at_wells = spread(s_row, all_ids)
        now = [image[k, a] + wells[2 + a] * at_wells for a in range(2)]
        face_now, back_in = [], []
        for f in range(4):
            face, got = faces[f], sent[f]
            here = spread(s_row, face_ids[f])
            face_now.append([got[2 * k + a] + face[WELL_EQ + a] * here for a in range(2)])
            there = spread(s_row, back_ids[f])
            back = [got[8 + 2 * k + a] + face[BACK_EQ + a] * there for a in range(2)]
            back_in.append(product(lambda e, f=f: faces[f][BACK_IN + e], *back))
        corner_now = []
        for c in range(4):
            here = spread(s_row, corner_ids[c])[0:1, :]
            corner_now.append(
                [
                    sent_corners[c].row(2 * k + a) + corners[c].row(SIDE_EQ + a) * here
                    for a in range(2)
                ]
            )
        incoming = [product(lambda e, f=f: faces[f][e], *face_now[f]) for f in range(4)]
        applied, outgoing = block_stencil(couplings, diagonal, now[0], now[1], incoming)
        at_wells = spread(s_image, all_ids)
        second, third = [], []
        for a in range(2):
            twice = applied[a] + wells[2 + a] * at_wells
            base = (now[a] - height * residual[k, a]) * scale
            second.append(base)
            third.append((twice - height * now[a]) * scale - shift * base)
            second_out[k, a] = second[a]
            third_out[k, a] = third[a]
        ends = corner_inputs(corners, corner_now)
        incoming = []
        for f in range(4):
            face = faces[f]
            there = face_stencil(face, face_now[f][0], face_now[f][1], back_in[f])
            over = face_entries(ends[(f, 0)], ends[(f, 1)], outgoing[f])
            here = spread(s_image, face_ids[f])
            outer = []
            for a in range(2):
                twice = there[a] + over[a] + face[WELL_EQ + a] * here
                base = (face_now[f][a] - height * residual_faces[f, 2 * k + a]) * scale
                outer.append((twice - height * face_now[f][a]) * scale - shift * base)
            incoming.append(product(lambda e, f=f: faces[f][e], *outer))
        result, _ = block_stencil(couplings, diagonal, third[0], third[1], incoming)
        fourth = [result[a] - shift * third[a] for a in range(2)]
        values_scratch[k] = wells[0] * third[0] + wells[1] * third[1]
        values_scratch[4 + k] = wells[2] * third[0] + wells[3] * third[1]
        values_scratch[8 + k] = wells[2] * fourth[0] + wells[3] * fourth[1]
        unit = lax.rsqrt(step["rr"])
        fields = [[residual[k, a] * unit for a in range(2)], second, third, fourth]
        number = 0
        for i in range(4):
            for j in range(i, 4):
                dot = full_sum(fields[i][0] * fields[j][0] + fields[i][1] * fields[j][1])
                table = put(4, 4 * number + k, dot, table)
                number += 1
    rows = segment_rows(ids, values_scratch, scratch)
    table = pack_rows(rows, table)
    part[...] = jnp.broadcast_to(table[None], part.shape)


def solve_kernel(
    guess, residual, second, third, parts, first_totals, small_in, solution
):
    totals = jnp.sum(parts[...], axis=0)
    before, small = first_totals[...], small_in[...]
    equation = small[1:2, :]
    for k in range(RHS):
        step = first_step(before, small, k)
        unit = lax.rsqrt(step["rr"])
        beta = step["rr"] * unit
        s_third, p_third = unpack_row(totals, k), unpack_row(totals, 4 + k)
        p_fourth = unpack_row(totals, 8 + k)
        gram = {}
        number = 0
        for i in range(4):
            for j in range(i, 4):
                gram[(i, j)] = lane(totals, 4, 4 * number + k)
                number += 1
        gram[(0, 3)] += lane_sum(step["p_row"] * s_third) * unit
        gram[(1, 3)] += lane_sum(step["p_second"] * s_third)
        gram[(2, 3)] += lane_sum(p_third * s_third)
        gram[(3, 3)] += lane_sum(2.0 * p_fourth * s_third + equation * s_third * s_third)
        tiny = 1e-30
        inverse = [lax.rsqrt(jnp.maximum(gram[(i, i)], tiny)) for i in range(4)]
        length = [jnp.maximum(gram[(i, i)], tiny) * inverse[i] for i in range(4)]
        upper = {}
        for i in range(4):
            for j in range(i, 4):
                entry = gram[(i, j)] * inverse[i] * inverse[j]
                for m in range(i):
                    entry = entry - upper[(m, i)] * upper[(m, j)]
                if i == j:
                    pivot = lax.rsqrt(jnp.maximum(entry, 1e-6))
                    upper[(i, i)] = jnp.maximum(entry, 1e-6) * pivot
                    over = pivot
                else:
                    upper[(i, j)] = entry * over
        shift = step["shift"]
        following = lax.rsqrt(step["rr"]) / step["scale"]
        columns = [
            [(0, step["height"] * length[0]), (1, following * length[1])],
            [(1, shift * length[1]), (2, length[2])],
            [(2, shift * length[2]), (3, length[3])],
        ]
        zero = jnp.zeros_like(shift)
        hessenberg = [[zero] * 3 for _ in range(4)]
        for j in range(3):
            for i in range(j + 2):
                for m, factor in columns[j]:
                    if m >= i:
                        hessenberg[i][j] = hessenberg[i][j] + upper[(i, m)] * factor
        target = [beta * length[0] * upper[(0, 0)], zero, zero, zero]
        for j in range(3):
            top, bottom = hessenberg[j][j], hessenberg[j + 1][j]
            turn = lax.rsqrt(top * top + bottom * bottom)
            cosine, sine = top * turn, bottom * turn
            for m in range(j, 3):
                high, low = hessenberg[j][m], hessenberg[j + 1][m]
                hessenberg[j][m] = cosine * high + sine * low
                hessenberg[j + 1][m] = cosine * low - sine * high
            high, low = target[j], target[j + 1]
            target[j] = cosine * high + sine * low
            target[j + 1] = cosine * low - sine * high
        weights = [zero] * 3
        for i in (2, 1, 0):
            value = target[i]
            for j in range(i + 1, 3):
                value = value - hessenberg[i][j] * weights[j]
            weights[i] = value / hessenberg[i][i]
        for a in range(2):
            solution[k, a] = (
                guess[k, a]
                + (weights[0] * unit) * residual[k, a]
                + weights[1] * second[k, a]
                + weights[2] * third[k, a]
            )


def call(kernel, shapes, arguments, scratch=(), own_copies=False, cost=0):
    whole = pl.BlockSpec(memory_space=pltpu.VMEM)
    far = pl.BlockSpec(memory_space=pl.ANY)
    return pl.pallas_call(
        kernel,
        out_shape=[jax.ShapeDtypeStruct(shape, jnp.float32) for shape in shapes],
        in_specs=[far if own_copies else whole] * len(arguments),
        out_specs=[whole] * len(shapes),
        scratch_shapes=list(scratch),
        compiler_params=pltpu.CompilerParams(vmem_limit_bytes=24 << 20),
        cost_estimate=pl.CostEstimate(flops=cost, bytes_accessed=cost, transcendentals=0)
        if cost
        else None,
    )(*arguments)


def held(*shape):
    return pltpu.VMEM(shape, jnp.float32)


def from_behind(value, axis, steps):
    count = lax.axis_size(axis)
    leading, last = (max(0, -steps), min(count, count - steps))
    return lax.ppermute(value, axis, [(source, source + steps) for source in range(leading, last)])


def exchanged(part):
    return lax.all_to_all(part, ("gx", "gy"), 0, 0, tiled=True)


def body(couplings, diagonal, wells, ids, right, guess):
    devices = lax.axis_size("gx") * lax.axis_size("gy")
    plane = (8, LANES)
    field = guess.shape
    block = guess.shape[2:]
    arguments = (couplings, diagonal, wells, ids, right, guess)

    x_low, x_high, y_low, y_high = call(
        pack_kernel,
        [(FACE_PLANES,) + plane] * 4,
        arguments,
        [pltpu.VMEM(argument.shape, argument.dtype) for argument in arguments]
        + [pltpu.SemaphoreType.DMA((len(arguments),))],
        own_copies=True,
    )
    fxl = from_behind(x_high, "gx", 1)
    fxh = from_behind(x_low, "gx", -1)
    (part,) = call(
        guess_kernel,
        [(devices, 2, LANES)],
        (wells, ids, guess),
        [held(6, *block), held(6, WELLS, LANES)],
        cost=4 << 20,
    )
    parts = exchanged(part)
    y_low, y_high = call(
        corner_kernel,
        [(FACE_PLANES + CORNER_PLANES,) + plane] * 2,
        (y_low, y_high, fxl, fxh),
    )
    fyl = from_behind(y_high, "gy", 1)
    fyh = from_behind(y_low, "gy", -1)

    faces = (fxl, fxh, fyl, fyh)
    residual, image, residual_faces, x_low, x_high, y_low, y_high, small = call(
        residual_kernel,
        [field, field, (4, 8) + plane] + [(16,) + plane] * 4 + [(8, LANES)],
        arguments + faces + (parts,),
    )
    gxl = from_behind(x_high, "gx", 1)
    gxh = from_behind(x_low, "gx", -1)
    (part,) = call(
        moments_kernel,
        [(devices, 8, LANES)],
        (wells, ids, residual, image),
        [held(16, *block), held(16, WELLS, LANES)],
        cost=4 << 20,
    )
    parts = exchanged(part)
    y_low, y_high = call(
        image_corner_kernel, [(18,) + plane] * 2, (y_low, y_high, gxl, gxh)
    )
    gyl = from_behind(y_high, "gy", 1)
    gyh = from_behind(y_low, "gy", -1)

    second, third, part, totals = call(
        krylov_kernel,
        [field, field, (devices, 8, LANES), (8, LANES)],
        (couplings, diagonal, wells, ids) + faces + (gxl, gxh, gyl, gyh)
        + (residual, image, residual_faces, parts, small),
        [held(12, WELLS, LANES), held(12, *block)],
    )
    parts = exchanged(part)
    (result,) = call(
        solve_kernel,
        [field],
        (guess, residual, second, third, parts, totals, small),
    )
    return result


def solution(mesh):
    in_specs = (
        P("member", None, "gx", "gy", None),
        P("member", "gx", "gy", None),
        P("member", "gx", "gy", None),
        P("gx", "gy", None),
        P("member", None, "gx", "gy", None),
        P("member", None, "gx", "gy", None),
    )
    out_specs = P("member", None, "gx", "gy", None)
    return jax.shard_map(body, mesh=mesh, in_specs=in_specs, out_specs=out_specs, check_vma=False)
```

```python
import jax
import jax.numpy as jnp
from jax import lax
from jax.experimental import pallas as pl
from jax.experimental.pallas import tpu as pltpu
from jax.sharding import PartitionSpec as P

WELLS = 40
RHS = 4
LANES = 128
LAT_UP, LAT_DOWN, RISE, FALL, DIAGONAL = 4, 8, 12, 16, 20
WELL_EQ, WELL_ID, GUESS, REST = 24, 26, 27, 35
BACK_IN, BACK_EQ, BACK_ID = 43, 47, 49
FACE_PLANES = 50
CORNER_PLANES = 5
CORNER_ROWS = 19
SIDE_IN, SIDE_EQ, SIDE_ID, SIDE_GUESS = 4, 8, 10, 11


def product(blocks, first, second):
    return [
        blocks(0) * first + blocks(2) * second,
        blocks(1) * first + blocks(3) * second,
    ]


def iota(shape, axis):
    return lax.broadcasted_iota(jnp.int32, shape, axis)


def roll_up(value, axis):
    return pltpu.roll(value, 1, axis)


def roll_down(value, axis):
    return pltpu.roll(value, value.shape[axis] - 1, axis)


def layer_moves(rising, falling):
    axis = rising.ndim - 1
    lane = iota(rising.shape, axis)
    up = jnp.where(lane == 0, 0.0, roll_up(rising, axis))
    down = jnp.where(lane == LANES - 1, 0.0, roll_down(falling, axis))
    return up + down


def block_stencil(couplings, diagonal, first, second, incoming):
    result = product(lambda e: diagonal[e], first, second)
    moved = [product(lambda e, d=d: couplings[d, e], first, second) for d in range(6)]
    row = iota(first.shape, 1)
    outgoing = [[], [], [], []]
    for b in range(2):
        east, west, north, south, rise, fall = (moved[d][b] for d in range(6))
        total = result[b] + jnp.concatenate([incoming[0][b][None], east[:-1]], axis=0)
        total = total + jnp.concatenate([west[1:], incoming[1][b][None]], axis=0)
        total = total + jnp.where(row == 0, incoming[2][b][:, None, :], roll_up(north, 1))
        total = total + jnp.where(
            row == row.shape[1] - 1, incoming[3][b][:, None, :], roll_down(south, 1)
        )
        result[b] = total + layer_moves(rise, fall)
        outgoing[0].append(west[0])
        outgoing[1].append(east[-1])
        outgoing[2].append(south[:, 0, :])
        outgoing[3].append(north[:, -1, :])
    return result, outgoing


def face_stencil(face, first, second, behind):
    def planes(start):
        return lambda e: face[start + e]

    result = product(planes(DIAGONAL), first, second)
    up = product(planes(LAT_UP), first, second)
    down = product(planes(LAT_DOWN), first, second)
    rise = product(planes(RISE), first, second)
    fall = product(planes(FALL), first, second)
    row = iota(first.shape, 0)
    for b in range(2):
        total = result[b] + behind[b] + layer_moves(rise[b], fall[b])
        total = total + jnp.where(row == 0, 0.0, roll_up(up[b], 0))
        result[b] = total + jnp.where(row == row.shape[0] - 1, 0.0, roll_down(down[b], 0))
    return result


def face_entries(low_end, high_end, entering):
    row = iota(entering[0].shape, 0)
    return [
        entering[b]
        + jnp.where(row == 0, low_end[b], 0.0)
        + jnp.where(row == row.shape[0] - 1, high_end[b], 0.0)
        for b in range(2)
    ]


def spread(totals, ids):
    table = jnp.broadcast_to(totals, (8, LANES))
    if ids.ndim == 2:
        return jnp.take_along_axis(table, ids, axis=1)
    return jnp.stack(
        [jnp.take_along_axis(table, ids[x], axis=1) for x in range(ids.shape[0])], axis=0
    )


def as_ids(plane):
    return plane.astype(jnp.int32)


class Corner:
    def __init__(self, pack, which, base):
        self.pack, self.start = pack, base * 8 + which

    def row(self, number):
        at = self.start + number
        return self.pack[at // 8, at % 8 : at % 8 + 1, :]


def corners_of(faces, base, rows):
    found = []
    for y_face in (2, 3):
        for x_end in range(2):
            found.append(Corner(faces[y_face], x_end * rows, base))
    return found


def corner_inputs(corners, values):
    ends = {}
    for c in range(4):
        x_end, y_end = c % 2, c // 2
        over_x = product(corners[c].row, *values[c])
        over_y = product(lambda e, c=c: corners[c].row(SIDE_IN + e), *values[c])
        ends[(2 + y_end, x_end)] = over_x
        ends[(x_end, y_end)] = over_y
    return ends


def put(row_number, lane_number, value, table):
    at = (iota(table.shape, 0) == row_number) & (iota(table.shape, 1) == lane_number)
    return jnp.where(at, value, table)


def full_sum(value):
    while value.ndim > 2:
        value = jnp.sum(value, axis=0)
    return jnp.sum(jnp.sum(value, axis=0, keepdims=True), axis=1, keepdims=True)


def list_wells(ids, present):
    depth = ids.shape[0]

    def smallest(planes):
        least = planes[0]
        for plane in planes[1:]:
            least = jnp.minimum(least, plane)
        return jnp.min(least)

    planes = [ids[x].astype(jnp.float32) for x in range(depth)]

    def one_well(state):
        number, well = state
        present[number] = well.astype(jnp.int32)
        after = [jnp.where(plane > well, plane, float(WELLS)) for plane in planes]
        return number + 1, smallest(after)

    number, _ = lax.while_loop(
        lambda state: state[1] < WELLS, one_well, (jnp.int32(1), smallest(planes))
    )
    present[0] = number - 1


def segment_rows(ids, values, scratch, present):
    scratch[...] = jnp.zeros_like(scratch)
    count, depth = values.shape[0], ids.shape[0]

    def one_well(step, _):
        well = present[step + 1]
        masks = [ids[x] == well for x in range(depth)]
        for number in range(count):
            total = jnp.where(masks[0], values[number, 0], 0.0)
            for x in range(1, depth):
                total = total + jnp.where(masks[x], values[number, x], 0.0)
            scratch[number, pl.ds(well, 1), :] = jnp.sum(total, axis=0, keepdims=True)
        return 0

    lax.fori_loop(0, present[0], one_well, 0)
    rows = []
    for number in range(count):
        summed = jnp.sum(scratch[number], axis=1, keepdims=True)
        shape = scratch.shape[1:]
        on_lanes = jnp.where(iota(shape, 0) == iota(shape, 1), summed, 0.0)
        rows.append(jnp.sum(on_lanes, axis=0, keepdims=True))
    return rows


def pack_rows(rows, table):
    for number, row in enumerate(rows):
        placed = row if number % 3 == 0 else pltpu.roll(row, WELLS * (number % 3), 1)
        table = table + jnp.where(
            iota(table.shape, 0) == number // 3, jnp.broadcast_to(placed, table.shape), 0.0
        )
    return table


def unpack_row(table, number):
    row = table[number // 3 : number // 3 + 1, :]
    if number % 3:
        row = pltpu.roll(row, LANES - WELLS * (number % 3), 1)
    return jnp.where(iota(row.shape, 1) < WELLS, row, 0.0)


def lane(table, row_number, lane_number):
    return table[row_number : row_number + 1, lane_number : lane_number + 1]


def lane_sum(row):
    return jnp.sum(row, axis=1, keepdims=True)


def fill_pack(pack, inward, lateral, cut):
    couplings, diagonal, wells, ids, right, guess = range(6)
    for e in range(4):
        pack[e] = cut(couplings, (inward, e), 0)
        pack[LAT_UP + e] = cut(couplings, (lateral, e), 0)
        pack[LAT_DOWN + e] = cut(couplings, (lateral + 1, e), 0)
        pack[RISE + e] = cut(couplings, (4, e), 0)
        pack[FALL + e] = cut(couplings, (5, e), 0)
        pack[DIAGONAL + e] = cut(diagonal, (e,), 0)
        pack[BACK_IN + e] = cut(couplings, (inward, e), 1)
    for a in range(2):
        pack[WELL_EQ + a] = cut(wells, (2 + a,), 0)
        pack[BACK_EQ + a] = cut(wells, (2 + a,), 1)
    pack[WELL_ID] = cut(ids, (), 0).astype(jnp.float32)
    pack[BACK_ID] = cut(ids, (), 1).astype(jnp.float32)
    for k in range(RHS):
        here = [cut(guess, (k, a), 0) for a in range(2)]
        back = [cut(guess, (k, a), 1) for a in range(2)]
        entering = product(lambda e: pack[BACK_IN + e], *back)
        local = face_stencil(pack, here[0], here[1], entering)
        for a in range(2):
            pack[GUESS + 2 * k + a] = here[a]
            pack[REST + 2 * k + a] = cut(right, (k, a), 0) - local[a]


def x_pack_kernel(*refs):
    sources, packs, held_ends, arrived = refs[:6], refs[6:8], refs[8:20], refs[20]
    copies = []
    for n, source in enumerate(sources):
        lead = (slice(None),) * (len(source.shape) - 3)
        depth = source.shape[-3]
        for end, start in enumerate((0, depth - 2)):
            copies.append(
                pltpu.make_async_copy(
                    source.at[lead + (pl.ds(start, 2),)],
                    held_ends[2 * n + end],
                    arrived.at[2 * n + end],
                )
            )
    for copy in copies:
        copy.start()
    for copy in copies:
        copy.wait()
    for end, pack in enumerate(packs):
        fill_pack(
            pack,
            1 - end,
            2,
            lambda n, index, layer: held_ends[2 * n + end][
                index + (1 - layer if end else layer,)
            ],
        )


def y_pack(arguments, packs):
    last = arguments[-1].shape[-2] - 1
    for end, pack in enumerate(packs):
        fill_pack(
            pack,
            3 - end,
            0,
            lambda n, index, layer: arguments[n][
                index + (slice(None), last - layer if end else layer, slice(None))
            ],
        )


def corner_kernel(y_low, y_high, fxl, fxh, table, low_out, high_out, part):
    part[...] = jnp.broadcast_to(table[...][None, :2], part.shape)
    last = fxl.shape[1] - 1
    for own, out, at, side in ((y_low, low_out, 0, LAT_DOWN), (y_high, high_out, last, LAT_UP)):
        for n in range(FACE_PLANES):
            out[n] = own[n]
        row = FACE_PLANES * 8
        out[FACE_PLANES + CORNER_PLANES - 1] = jnp.zeros(out.shape[1:], jnp.float32)
        for face in (fxl, fxh):
            for n in (*range(4), *range(side, side + 4), *range(WELL_EQ, REST)):
                out[row // 8, row % 8 : row % 8 + 1, :] = face[n, at : at + 1, :]
                row += 1


def image_corner_kernel(y_low, y_high, gxl, gxh, table, low_out, high_out, part):
    part[...] = jnp.broadcast_to(table[...][None], part.shape)
    last = gxl.shape[1] - 1
    for own, out, at in ((y_low, low_out, 0), (y_high, high_out, last)):
        for n in range(16):
            out[n] = own[n]
        for x_end, face in enumerate((gxl, gxh)):
            for n in range(8):
                out[16 + x_end, n : n + 1, :] = face[n, at : at + 1, :]


def guess_kernel(
    couplings, diagonal, wells, ids, right, guess,
    table_out, present, y_low, y_high, values, scratch,
):
    y_pack((couplings, diagonal, wells, ids, right, guess), (y_low, y_high))
    list_wells(ids, present)
    for k in range(RHS):
        values[k] = wells[0] * guess[k, 0] + wells[1] * guess[k, 1]
    values[4] = wells[0] * wells[2] + wells[1] * wells[3]
    values[5] = wells[2] * wells[2] + wells[3] * wells[3]
    rows = segment_rows(ids, values, scratch, present)
    table_out[...] = pack_rows(rows, jnp.zeros((8, LANES), jnp.float32))


def residual_kernel(
    couplings, diagonal, wells, ids, right, guess, fxl, fxh, fyl, fyh, parts,
    residual, image, residual_faces, x_low, x_high, y_low, y_high, small,
):
    faces = (fxl, fxh, fyl, fyh)
    totals = jnp.sum(parts[...], axis=0)
    corners = corners_of(faces, FACE_PLANES, CORNER_ROWS)
    all_ids = ids[...]
    face_ids = [as_ids(face[WELL_ID]) for face in faces]
    last = guess.shape[2] - 1
    for k in range(RHS):
        s_row = unpack_row(totals, k)
        first, second = guess[k, 0], guess[k, 1]
        incoming = [
            product(
                lambda e, f=f: faces[f][e],
                faces[f][GUESS + 2 * k],
                faces[f][GUESS + 2 * k + 1],
            )
            for f in range(4)
        ]
        applied, outgoing = block_stencil(couplings, diagonal, first, second, incoming)
        at_wells = spread(s_row, all_ids)
        now = [
            right[k, a] - applied[a] - wells[2 + a] * at_wells for a in range(2)
        ]
        for a in range(2):
            residual[k, a] = now[a]
        ends = corner_inputs(
            corners,
            [[corners[c].row(SIDE_GUESS + 2 * k + a) for a in range(2)] for c in range(4)],
        )
        incoming = []
        for f in range(4):
            face = faces[f]
            there = face_entries(ends[(f, 0)], ends[(f, 1)], outgoing[f])
            face_wells = spread(s_row, face_ids[f])
            outer = [
                face[REST + 2 * k + a] - there[a] - face[WELL_EQ + a] * face_wells
                for a in range(2)
            ]
            for a in range(2):
                residual_faces[f, 2 * k + a] = outer[a]
            incoming.append(product(lambda e, f=f: faces[f][e], *outer))
        result, _ = block_stencil(couplings, diagonal, now[0], now[1], incoming)
        for a in range(2):
            image[k, a] = result[a]
            x_low[2 * k + a] = result[a][0]
            x_low[8 + 2 * k + a] = result[a][1]
            x_high[2 * k + a] = result[a][last]
            x_high[8 + 2 * k + a] = result[a][last - 1]
            y_low[2 * k + a] = result[a][:, 0, :]
            y_low[8 + 2 * k + a] = result[a][:, 1, :]
            y_high[2 * k + a] = result[a][:, last, :]
            y_high[8 + 2 * k + a] = result[a][:, last - 1, :]
    small[...] = jnp.concatenate(
        [unpack_row(totals, 4), unpack_row(totals, 5), jnp.zeros((6, LANES), jnp.float32)], axis=0
    )


def moments_kernel(wells, ids, residual, image, present, table_out, values, scratch):
    table = jnp.zeros((8, LANES), jnp.float32)
    for k in range(RHS):
        now = [residual[k, a] for a in range(2)]
        result = [image[k, a] for a in range(2)]
        for n, field in enumerate((now, result)):
            values[4 * n + k] = wells[0] * field[0] + wells[1] * field[1]
            values[8 + 4 * n + k] = wells[2] * field[0] + wells[3] * field[1]
        table = put(6, k, full_sum(now[0] * now[0] + now[1] * now[1]), table)
        table = put(6, 4 + k, full_sum(now[0] * result[0] + now[1] * result[1]), table)
        table = put(6, 8 + k, full_sum(result[0] * result[0] + result[1] * result[1]), table)
    rows = segment_rows(ids, values, scratch, present)
    table_out[...] = pack_rows(rows, table)


def first_step(totals, small, k):
    s_row, us_row = unpack_row(totals, k), unpack_row(totals, 4 + k)
    p_row, ps_row = unpack_row(totals, 8 + k), unpack_row(totals, 12 + k)
    within, equation = small[0:1, :], small[1:2, :]
    rr, rs, ss = (lane(totals, 6, 4 * i + k) for i in range(3))
    height = (rs + lane_sum(p_row * s_row)) / rr
    square = ss + lane_sum(2.0 * ps_row * s_row + equation * s_row * s_row)
    left = jnp.maximum(square - height * height * rr, 1e-7 * square)
    scale = lax.rsqrt(left)
    s_image = us_row + within * s_row
    s_second = (s_image - height * s_row) * scale
    p_second = (ps_row + equation * s_row - height * p_row) * scale
    shift = rs / rr + lane_sum(p_second * s_second)
    return dict(
        rr=rr, height=height, scale=scale, shift=shift, s_row=s_row, s_image=s_image,
        p_row=p_row, p_second=p_second,
    )


def krylov_kernel(
    couplings, diagonal, wells, ids, fxl, fxh, fyl, fyh, gxl, gxh, gyl, gyh,
    residual, image, residual_faces, parts, small_in, present,
    second_out, third_out, part, totals_out, scratch, values_scratch,
):
    faces, sent = (fxl, fxh, fyl, fyh), (gxl, gxh, gyl, gyh)
    totals = jnp.sum(parts[...], axis=0)
    totals_out[...] = totals
    small = small_in[...]
    corners = corners_of(faces, FACE_PLANES, CORNER_ROWS)
    sent_corners = corners_of(sent, 16, 8)
    all_ids = ids[...]
    face_ids = [as_ids(face[WELL_ID]) for face in faces]
    back_ids = [as_ids(face[BACK_ID]) for face in faces]
    corner_ids = [
        as_ids(jnp.broadcast_to(corner.row(SIDE_ID), (8, LANES))) for corner in corners
    ]
    table = jnp.zeros((8, LANES), jnp.float32)
    values = []
    for k in range(RHS):
        step = first_step(totals, small, k)
        height, scale, shift = step["height"], step["scale"], step["shift"]
        s_row, s_image = step["s_row"], step["s_image"]
        at_wells = spread(s_row, all_ids)
        now = [image[k, a] + wells[2 + a] * at_wells for a in range(2)]
        face_now, back_in = [], []
        for f in range(4):
            face, got = faces[f], sent[f]
            here = spread(s_row, face_ids[f])
            face_now.append([got[2 * k + a] + face[WELL_EQ + a] * here for a in range(2)])
            there = spread(s_row, back_ids[f])
            back = [got[8 + 2 * k + a] + face[BACK_EQ + a] * there for a in range(2)]
            back_in.append(product(lambda e, f=f: faces[f][BACK_IN + e], *back))
        corner_now = []
        for c in range(4):
            here = spread(s_row, corner_ids[c])[0:1, :]
            corner_now.append(
                [
                    sent_corners[c].row(2 * k + a) + corners[c].row(SIDE_EQ + a) * here
                    for a in range(2)
                ]
            )
        incoming = [product(lambda e, f=f: faces[f][e], *face_now[f]) for f in range(4)]
        applied, outgoing = block_stencil(couplings, diagonal, now[0], now[1], incoming)
        at_wells = spread(s_image, all_ids)
        second, third = [], []
        for a in range(2):
            twice = applied[a] + wells[2 + a] * at_wells
            base = (now[a] - height * residual[k, a]) * scale
            second.append(base)
            third.append((twice - height * now[a]) * scale - shift * base)
            second_out[k, a] = second[a]
            third_out[k, a] = third[a]
        ends = corner_inputs(corners, corner_now)
        incoming = []
        for f in range(4):
            face = faces[f]
            there = face_stencil(face, face_now[f][0], face_now[f][1], back_in[f])
            over = face_entries(ends[(f, 0)], ends[(f, 1)], outgoing[f])
            here = spread(s_image, face_ids[f])
            outer = []
            for a in range(2):
                twice = there[a] + over[a] + face[WELL_EQ + a] * here
                base = (face_now[f][a] - height * residual_faces[f, 2 * k + a]) * scale
                outer.append((twice - height * face_now[f][a]) * scale - shift * base)
            incoming.append(product(lambda e, f=f: faces[f][e], *outer))
        result, _ = block_stencil(couplings, diagonal, third[0], third[1], incoming)
        fourth = [result[a] - shift * third[a] for a in range(2)]
        values_scratch[k] = wells[0] * third[0] + wells[1] * third[1]
        values_scratch[4 + k] = wells[2] * third[0] + wells[3] * third[1]
        values_scratch[8 + k] = wells[2] * fourth[0] + wells[3] * fourth[1]
        unit = lax.rsqrt(step["rr"])
        fields = [[residual[k, a] * unit for a in range(2)], second, third, fourth]
        number = 0
        for i in range(4):
            for j in range(i, 4):
                dot = full_sum(fields[i][0] * fields[j][0] + fields[i][1] * fields[j][1])
                table = put(4, 4 * number + k, dot, table)
                number += 1
    rows = segment_rows(ids, values_scratch, scratch, present)
    table = pack_rows(rows, table)
    part[...] = jnp.broadcast_to(table[None], part.shape)


def solve_kernel(
    guess, residual, second, third, parts, first_totals, small_in, solution
):
    totals = jnp.sum(parts[...], axis=0)
    before, small = first_totals[...], small_in[...]
    equation = small[1:2, :]
    for k in range(RHS):
        step = first_step(before, small, k)
        unit = lax.rsqrt(step["rr"])
        beta = step["rr"] * unit
        s_third, p_third = unpack_row(totals, k), unpack_row(totals, 4 + k)
        p_fourth = unpack_row(totals, 8 + k)
        gram = {}
        number = 0
        for i in range(4):
            for j in range(i, 4):
                gram[(i, j)] = lane(totals, 4, 4 * number + k)
                number += 1
        gram[(0, 3)] += lane_sum(step["p_row"] * s_third) * unit
        gram[(1, 3)] += lane_sum(step["p_second"] * s_third)
        gram[(2, 3)] += lane_sum(p_third * s_third)
        gram[(3, 3)] += lane_sum(2.0 * p_fourth * s_third + equation * s_third * s_third)
        tiny = 1e-30
        inverse = [lax.rsqrt(jnp.maximum(gram[(i, i)], tiny)) for i in range(4)]
        length = [jnp.maximum(gram[(i, i)], tiny) * inverse[i] for i in range(4)]
        upper = {}
        for i in range(4):
            for j in range(i, 4):
                entry = gram[(i, j)] * inverse[i] * inverse[j]
                for m in range(i):
                    entry = entry - upper[(m, i)] * upper[(m, j)]
                if i == j:
                    pivot = lax.rsqrt(jnp.maximum(entry, 1e-6))
                    upper[(i, i)] = jnp.maximum(entry, 1e-6) * pivot
                    over = pivot
                else:
                    upper[(i, j)] = entry * over
        shift = step["shift"]
        following = lax.rsqrt(step["rr"]) / step["scale"]
        columns = [
            [(0, step["height"] * length[0]), (1, following * length[1])],
            [(1, shift * length[1]), (2, length[2])],
            [(2, shift * length[2]), (3, length[3])],
        ]
        zero = jnp.zeros_like(shift)
        hessenberg = [[zero] * 3 for _ in range(4)]
        for j in range(3):
            for i in range(j + 2):
                for m, factor in columns[j]:
                    if m >= i:
                        hessenberg[i][j] = hessenberg[i][j] + upper[(i, m)] * factor
        target = [beta * length[0] * upper[(0, 0)], zero, zero, zero]
        for j in range(3):
            top, bottom = hessenberg[j][j], hessenberg[j + 1][j]
            turn = lax.rsqrt(top * top + bottom * bottom)
            cosine, sine = top * turn, bottom * turn
            for m in range(j, 3):
                high, low = hessenberg[j][m], hessenberg[j + 1][m]
                hessenberg[j][m] = cosine * high + sine * low
                hessenberg[j + 1][m] = cosine * low - sine * high
            high, low = target[j], target[j + 1]
            target[j] = cosine * high + sine * low
            target[j + 1] = cosine * low - sine * high
        weights = [zero] * 3
        for i in (2, 1, 0):
            value = target[i]
            for j in range(i + 1, 3):
                value = value - hessenberg[i][j] * weights[j]
            weights[i] = value / hessenberg[i][i]
        for a in range(2):
            solution[k, a] = (
                guess[k, a]
                + (weights[0] * unit) * residual[k, a]
                + weights[1] * second[k, a]
                + weights[2] * third[k, a]
            )


def call(kernel, shapes, arguments, scratch=(), own_copies=False, cost=0, grant=24 << 20):
    whole = pl.BlockSpec(memory_space=pltpu.VMEM)
    far = pl.BlockSpec(memory_space=pltpu.HBM)
    scalars = pl.BlockSpec(memory_space=pltpu.SMEM)

    def place(array):
        if len(array.shape) == 1:
            return scalars
        return far if own_copies else whole

    outs = [
        jax.ShapeDtypeStruct(shape, jnp.float32 if len(shape) > 1 else jnp.int32)
        for shape in shapes
    ]
    return pl.pallas_call(
        kernel,
        out_shape=outs,
        in_specs=[place(argument) for argument in arguments],
        out_specs=[scalars if len(shape) == 1 else whole for shape in shapes],
        scratch_shapes=list(scratch),
        compiler_params=pltpu.CompilerParams(vmem_limit_bytes=grant),
        cost_estimate=pl.CostEstimate(flops=cost, bytes_accessed=cost, transcendentals=0)
        if cost
        else None,
    )(*arguments)


def held(*shape):
    return pltpu.VMEM(shape, jnp.float32)


def from_behind(value, axis, steps):
    count = lax.axis_size(axis)
    leading, last = (max(0, -steps), min(count, count - steps))
    return lax.ppermute(value, axis, [(source, source + steps) for source in range(leading, last)])


def exchanged(part):
    return lax.all_to_all(part, ("gx", "gy"), 0, 0, tiled=True)


def body(couplings, diagonal, wells, ids, right, guess):
    devices = lax.axis_size("gx") * lax.axis_size("gy")
    plane = (8, LANES)
    field = guess.shape
    block = guess.shape[2:]
    arguments = (couplings, diagonal, wells, ids, right, guess)

    ends = []
    for argument in arguments:
        shape = argument.shape[:-3] + (2,) + argument.shape[-2:]
        ends += [pltpu.VMEM(shape, argument.dtype)] * 2
    x_low, x_high = call(
        x_pack_kernel,
        [(FACE_PLANES,) + plane] * 2,
        arguments,
        ends + [pltpu.SemaphoreType.DMA((len(ends),))],
        own_copies=True,
        grant=60 << 20,
    )
    fxl = from_behind(x_high, "gx", 1)
    fxh = from_behind(x_low, "gx", -1)
    table, present, y_low, y_high = call(
        guess_kernel,
        [plane, (WELLS + 1,)] + [(FACE_PLANES,) + plane] * 2,
        arguments,
        [held(6, *block), held(6, WELLS, LANES)],
        cost=4 << 20,
    )
    y_low, y_high, part = call(
        corner_kernel,
        [(FACE_PLANES + CORNER_PLANES,) + plane] * 2 + [(devices, 2, LANES)],
        (y_low, y_high, fxl, fxh, table),
    )
    parts = exchanged(part)
    fyl = from_behind(y_high, "gy", 1)
    fyh = from_behind(y_low, "gy", -1)

    faces = (fxl, fxh, fyl, fyh)
    residual, image, residual_faces, x_low, x_high, y_low, y_high, small = call(
        residual_kernel,
        [field, field, (4, 8) + plane] + [(16,) + plane] * 4 + [(8, LANES)],
        arguments + faces + (parts,),
    )
    gxl = from_behind(x_high, "gx", 1)
    gxh = from_behind(x_low, "gx", -1)
    (table,) = call(
        moments_kernel,
        [plane],
        (wells, ids, residual, image, present),
        [held(16, *block), held(16, WELLS, LANES)],
        cost=4 << 20,
    )
    y_low, y_high, part = call(
        image_corner_kernel,
        [(18,) + plane] * 2 + [(devices, 8, LANES)],
        (y_low, y_high, gxl, gxh, table),
    )
    parts = exchanged(part)
    gyl = from_behind(y_high, "gy", 1)
    gyh = from_behind(y_low, "gy", -1)

    second, third, part, totals = call(
        krylov_kernel,
        [field, field, (devices, 8, LANES), (8, LANES)],
        (couplings, diagonal, wells, ids) + faces + (gxl, gxh, gyl, gyh)
        + (residual, image, residual_faces, parts, small, present),
        [held(12, WELLS, LANES), held(12, *block)],
    )
    parts = exchanged(part)
    (result,) = call(
        solve_kernel,
        [field],
        (guess, residual, second, third, parts, totals, small),
    )
    return result


def solution(mesh):
    in_specs = (
        P("member", None, "gx", "gy", None),
        P("member", "gx", "gy", None),
        P("member", "gx", "gy", None),
        P("gx", "gy", None),
        P("member", None, "gx", "gy", None),
        P("member", None, "gx", "gy", None),
    )
    out_specs = P("member", None, "gx", "gy", None)
    return jax.shard_map(body, mesh=mesh, in_specs=in_specs, out_specs=out_specs, check_vma=False)
```

```python
import jax
import jax.numpy as jnp
from jax import lax
from jax.experimental import pallas as pl
from jax.experimental.pallas import tpu as pltpu
from jax.sharding import PartitionSpec as P

WELLS = 40
RHS = 4
LANES = 128
LAT_UP, LAT_DOWN, RISE, FALL, DIAGONAL = 4, 8, 12, 16, 20
WELL_EQ, WELL_ID, GUESS, REST = 24, 26, 27, 35
BACK_IN, BACK_EQ, BACK_ID = 43, 47, 49
FACE_PLANES = 50
CORNER_PLANES = 5
CORNER_ROWS = 19
SIDE_IN, SIDE_EQ, SIDE_ID, SIDE_GUESS = 4, 8, 10, 11


def product(blocks, first, second):
    return [
        blocks(0) * first + blocks(2) * second,
        blocks(1) * first + blocks(3) * second,
    ]


def iota(shape, axis):
    return lax.broadcasted_iota(jnp.int32, shape, axis)


def roll_up(value, axis):
    return pltpu.roll(value, 1, axis)


def roll_down(value, axis):
    return pltpu.roll(value, value.shape[axis] - 1, axis)


def layer_moves(rising, falling):
    axis = rising.ndim - 1
    lane = iota(rising.shape, axis)
    up = jnp.where(lane == 0, 0.0, roll_up(rising, axis))
    down = jnp.where(lane == LANES - 1, 0.0, roll_down(falling, axis))
    return up + down


def block_stencil(couplings, diagonal, first, second, incoming):
    result = product(lambda e: diagonal[e], first, second)
    moved = [product(lambda e, d=d: couplings[d, e], first, second) for d in range(6)]
    row = iota(first.shape, 1)
    outgoing = [[], [], [], []]
    for b in range(2):
        east, west, north, south, rise, fall = (moved[d][b] for d in range(6))
        total = result[b] + jnp.concatenate([incoming[0][b][None], east[:-1]], axis=0)
        total = total + jnp.concatenate([west[1:], incoming[1][b][None]], axis=0)
        total = total + jnp.where(row == 0, incoming[2][b][:, None, :], roll_up(north, 1))
        total = total + jnp.where(
            row == row.shape[1] - 1, incoming[3][b][:, None, :], roll_down(south, 1)
        )
        result[b] = total + layer_moves(rise, fall)
        outgoing[0].append(west[0])
        outgoing[1].append(east[-1])
        outgoing[2].append(south[:, 0, :])
        outgoing[3].append(north[:, -1, :])
    return result, outgoing


def face_stencil(face, first, second, behind):
    def planes(start):
        return lambda e: face[start + e]

    result = product(planes(DIAGONAL), first, second)
    up = product(planes(LAT_UP), first, second)
    down = product(planes(LAT_DOWN), first, second)
    rise = product(planes(RISE), first, second)
    fall = product(planes(FALL), first, second)
    row = iota(first.shape, 0)
    for b in range(2):
        total = result[b] + behind[b] + layer_moves(rise[b], fall[b])
        total = total + jnp.where(row == 0, 0.0, roll_up(up[b], 0))
        result[b] = total + jnp.where(row == row.shape[0] - 1, 0.0, roll_down(down[b], 0))
    return result


def face_entries(low_end, high_end, entering):
    row = iota(entering[0].shape, 0)
    return [
        entering[b]
        + jnp.where(row == 0, low_end[b], 0.0)
        + jnp.where(row == row.shape[0] - 1, high_end[b], 0.0)
        for b in range(2)
    ]


def spread(totals, ids):
    table = jnp.broadcast_to(totals, (8, LANES))
    if ids.ndim == 2:
        return jnp.take_along_axis(table, ids, axis=1)
    return jnp.stack(
        [jnp.take_along_axis(table, ids[x], axis=1) for x in range(ids.shape[0])], axis=0
    )


def as_ids(plane):
    return plane.astype(jnp.int32)


class Corner:
    def __init__(self, pack, which, base):
        self.pack, self.start = pack, base * 8 + which

    def row(self, number):
        at = self.start + number
        return self.pack[at // 8, at % 8 : at % 8 + 1, :]


def corners_of(faces, base, rows):
    found = []
    for y_face in (2, 3):
        for x_end in range(2):
            found.append(Corner(faces[y_face], x_end * rows, base))
    return found


def corner_inputs(corners, values):
    ends = {}
    for c in range(4):
        x_end, y_end = c % 2, c // 2
        over_x = product(corners[c].row, *values[c])
        over_y = product(lambda e, c=c: corners[c].row(SIDE_IN + e), *values[c])
        ends[(2 + y_end, x_end)] = over_x
        ends[(x_end, y_end)] = over_y
    return ends


def put(row_number, lane_number, value, table):
    at = (iota(table.shape, 0) == row_number) & (iota(table.shape, 1) == lane_number)
    return jnp.where(at, value, table)


def full_sum(value):
    while value.ndim > 2:
        value = jnp.sum(value, axis=0)
    return jnp.sum(jnp.sum(value, axis=0, keepdims=True), axis=1, keepdims=True)


def list_wells(ids, present):
    depth = ids.shape[0]

    def smallest(planes):
        least = planes[0]
        for plane in planes[1:]:
            least = jnp.minimum(least, plane)
        return jnp.min(least)

    planes = [ids[x].astype(jnp.float32) for x in range(depth)]

    def one_well(state):
        number, well = state
        present[number] = well.astype(jnp.int32)
        after = [jnp.where(plane > well, plane, float(WELLS)) for plane in planes]
        return number + 1, smallest(after)

    number, _ = lax.while_loop(
        lambda state: state[1] < WELLS, one_well, (jnp.int32(1), smallest(planes))
    )
    present[0] = number - 1


def segment_rows(ids, values, scratch, present):
    scratch[...] = jnp.zeros_like(scratch)
    count, depth = values.shape[0], ids.shape[0]

    def one_well(step, _):
        well = present[step + 1]
        masks = [ids[x] == well for x in range(depth)]
        for number in range(count):
            total = jnp.where(masks[0], values[number, 0], 0.0)
            for x in range(1, depth):
                total = total + jnp.where(masks[x], values[number, x], 0.0)
            scratch[number, pl.ds(well, 1), :] = jnp.sum(total, axis=0, keepdims=True)
        return 0

    lax.fori_loop(0, present[0], one_well, 0)
    rows = []
    for number in range(count):
        summed = jnp.sum(scratch[number], axis=1, keepdims=True)
        shape = scratch.shape[1:]
        on_lanes = jnp.where(iota(shape, 0) == iota(shape, 1), summed, 0.0)
        rows.append(jnp.sum(on_lanes, axis=0, keepdims=True))
    return rows


def pack_rows(rows, table):
    for number, row in enumerate(rows):
        placed = row if number % 3 == 0 else pltpu.roll(row, WELLS * (number % 3), 1)
        table = table + jnp.where(
            iota(table.shape, 0) == number // 3, jnp.broadcast_to(placed, table.shape), 0.0
        )
    return table


def unpack_row(table, number):
    row = table[number // 3 : number // 3 + 1, :]
    if number % 3:
        row = pltpu.roll(row, LANES - WELLS * (number % 3), 1)
    return jnp.where(iota(row.shape, 1) < WELLS, row, 0.0)


def lane(table, row_number, lane_number):
    return table[row_number : row_number + 1, lane_number : lane_number + 1]


def lane_sum(row):
    return jnp.sum(row, axis=1, keepdims=True)


def fill_pack(pack, inward, lateral, cut):
    couplings, diagonal, wells, ids, right, guess = range(6)
    for e in range(4):
        pack[e] = cut(couplings, (inward, e), 0)
        pack[LAT_UP + e] = cut(couplings, (lateral, e), 0)
        pack[LAT_DOWN + e] = cut(couplings, (lateral + 1, e), 0)
        pack[RISE + e] = cut(couplings, (4, e), 0)
        pack[FALL + e] = cut(couplings, (5, e), 0)
        pack[DIAGONAL + e] = cut(diagonal, (e,), 0)
        pack[BACK_IN + e] = cut(couplings, (inward, e), 1)
    for a in range(2):
        pack[WELL_EQ + a] = cut(wells, (2 + a,), 0)
        pack[BACK_EQ + a] = cut(wells, (2 + a,), 1)
    pack[WELL_ID] = cut(ids, (), 0).astype(jnp.float32)
    pack[BACK_ID] = cut(ids, (), 1).astype(jnp.float32)
    for k in range(RHS):
        here = [cut(guess, (k, a), 0) for a in range(2)]
        back = [cut(guess, (k, a), 1) for a in range(2)]
        entering = product(lambda e: pack[BACK_IN + e], *back)
        local = face_stencil(pack, here[0], here[1], entering)
        for a in range(2):
            pack[GUESS + 2 * k + a] = here[a]
            pack[REST + 2 * k + a] = cut(right, (k, a), 0) - local[a]


def x_pack_kernel(*refs):
    sources, packs, held_ends, arrived = refs[:6], refs[6:8], refs[8:20], refs[20]
    copies = []
    for n, source in enumerate(sources):
        lead = (slice(None),) * (len(source.shape) - 3)
        depth = source.shape[-3]
        for end, start in enumerate((0, depth - 2)):
            copies.append(
                pltpu.make_async_copy(
                    source.at[lead + (pl.ds(start, 2),)],
                    held_ends[2 * n + end],
                    arrived.at[2 * n + end],
                )
            )
    for copy in copies:
        copy.start()
    for copy in copies:
        copy.wait()
    for end, pack in enumerate(packs):
        fill_pack(
            pack,
            1 - end,
            2,
            lambda n, index, layer: held_ends[2 * n + end][
                index + (1 - layer if end else layer,)
            ],
        )


def y_pack(arguments, packs):
    last = arguments[-1].shape[-2] - 1
    for end, pack in enumerate(packs):
        fill_pack(
            pack,
            3 - end,
            0,
            lambda n, index, layer: arguments[n][
                index + (slice(None), last - layer if end else layer, slice(None))
            ],
        )


def corner_kernel(y_low, y_high, fxl, fxh, low_out, high_out):
    last = fxl.shape[1] - 1
    for own, out, at, side in ((y_low, low_out, 0, LAT_DOWN), (y_high, high_out, last, LAT_UP)):
        for n in range(FACE_PLANES):
            out[n] = own[n]
        row = FACE_PLANES * 8
        out[FACE_PLANES + CORNER_PLANES - 1] = jnp.zeros(out.shape[1:], jnp.float32)
        for face in (fxl, fxh):
            for n in (*range(4), *range(side, side + 4), *range(WELL_EQ, REST)):
                out[row // 8, row % 8 : row % 8 + 1, :] = face[n, at : at + 1, :]
                row += 1


def image_corner_kernel(y_low, y_high, gxl, gxh, low_out, high_out):
    last = gxl.shape[1] - 1
    for own, out, at in ((y_low, low_out, 0), (y_high, high_out, last)):
        for n in range(16):
            out[n] = own[n]
        for x_end, face in enumerate((gxl, gxh)):
            for n in range(8):
                out[16 + x_end, n : n + 1, :] = face[n, at : at + 1, :]


def guess_kernel(
    couplings, diagonal, wells, ids, right, guess,
    table_out, present, y_low, y_high, values, scratch,
):
    y_pack((couplings, diagonal, wells, ids, right, guess), (y_low, y_high))
    list_wells(ids, present)
    for k in range(RHS):
        values[k] = wells[0] * guess[k, 0] + wells[1] * guess[k, 1]
    values[4] = wells[0] * wells[2] + wells[1] * wells[3]
    values[5] = wells[2] * wells[2] + wells[3] * wells[3]
    rows = segment_rows(ids, values, scratch, present)
    table_out[...] = pack_rows(rows, jnp.zeros((8, LANES), jnp.float32))


def residual_kernel(
    couplings, diagonal, wells, ids, right, guess, fxl, fxh, fyl, fyh, parts,
    residual, image, residual_faces, x_low, x_high, y_low, y_high, small,
):
    faces = (fxl, fxh, fyl, fyh)
    totals = jnp.sum(parts[...], axis=0)
    corners = corners_of(faces, FACE_PLANES, CORNER_ROWS)
    all_ids = ids[...]
    face_ids = [as_ids(face[WELL_ID]) for face in faces]
    last = guess.shape[2] - 1
    for k in range(RHS):
        s_row = unpack_row(totals, k)
        first, second = guess[k, 0], guess[k, 1]
        incoming = [
            product(
                lambda e, f=f: faces[f][e],
                faces[f][GUESS + 2 * k],
                faces[f][GUESS + 2 * k + 1],
            )
            for f in range(4)
        ]
        applied, outgoing = block_stencil(couplings, diagonal, first, second, incoming)
        at_wells = spread(s_row, all_ids)
        now = [
            right[k, a] - applied[a] - wells[2 + a] * at_wells for a in range(2)
        ]
        for a in range(2):
            residual[k, a] = now[a]
        ends = corner_inputs(
            corners,
            [[corners[c].row(SIDE_GUESS + 2 * k + a) for a in range(2)] for c in range(4)],
        )
        incoming = []
        for f in range(4):
            face = faces[f]
            there = face_entries(ends[(f, 0)], ends[(f, 1)], outgoing[f])
            face_wells = spread(s_row, face_ids[f])
            outer = [
                face[REST + 2 * k + a] - there[a] - face[WELL_EQ + a] * face_wells
                for a in range(2)
            ]
            for a in range(2):
                residual_faces[f, 2 * k + a] = outer[a]
            incoming.append(product(lambda e, f=f: faces[f][e], *outer))
        result, _ = block_stencil(couplings, diagonal, now[0], now[1], incoming)
        for a in range(2):
            image[k, a] = result[a]
            x_low[2 * k + a] = result[a][0]
            x_low[8 + 2 * k + a] = result[a][1]
            x_high[2 * k + a] = result[a][last]
            x_high[8 + 2 * k + a] = result[a][last - 1]
            y_low[2 * k + a] = result[a][:, 0, :]
            y_low[8 + 2 * k + a] = result[a][:, 1, :]
            y_high[2 * k + a] = result[a][:, last, :]
            y_high[8 + 2 * k + a] = result[a][:, last - 1, :]
    small[...] = jnp.concatenate(
        [unpack_row(totals, 4), unpack_row(totals, 5), jnp.zeros((6, LANES), jnp.float32)], axis=0
    )


def moments_kernel(wells, ids, residual, image, present, table_out, values, scratch):
    table = jnp.zeros((8, LANES), jnp.float32)
    for k in range(RHS):
        now = [residual[k, a] for a in range(2)]
        result = [image[k, a] for a in range(2)]
        for n, field in enumerate((now, result)):
            values[4 * n + k] = wells[0] * field[0] + wells[1] * field[1]
            values[8 + 4 * n + k] = wells[2] * field[0] + wells[3] * field[1]
        table = put(6, k, full_sum(now[0] * now[0] + now[1] * now[1]), table)
        table = put(6, 4 + k, full_sum(now[0] * result[0] + now[1] * result[1]), table)
        table = put(6, 8 + k, full_sum(result[0] * result[0] + result[1] * result[1]), table)
    rows = segment_rows(ids, values, scratch, present)
    table_out[...] = pack_rows(rows, table)


def first_step(totals, small, k):
    s_row, us_row = unpack_row(totals, k), unpack_row(totals, 4 + k)
    p_row, ps_row = unpack_row(totals, 8 + k), unpack_row(totals, 12 + k)
    within, equation = small[0:1, :], small[1:2, :]
    rr, rs, ss = (lane(totals, 6, 4 * i + k) for i in range(3))
    height = (rs + lane_sum(p_row * s_row)) / rr
    square = ss + lane_sum(2.0 * ps_row * s_row + equation * s_row * s_row)
    left = jnp.maximum(square - height * height * rr, 1e-7 * square)
    scale = lax.rsqrt(left)
    s_image = us_row + within * s_row
    s_second = (s_image - height * s_row) * scale
    p_second = (ps_row + equation * s_row - height * p_row) * scale
    shift = rs / rr + lane_sum(p_second * s_second)
    return dict(
        rr=rr, height=height, scale=scale, shift=shift, s_row=s_row, s_image=s_image,
        p_row=p_row, p_second=p_second,
    )


def krylov_kernel(
    couplings, diagonal, wells, ids, fxl, fxh, fyl, fyh, gxl, gxh, gyl, gyh,
    residual, image, residual_faces, parts, small_in, present,
    second_out, third_out, part, totals_out, scratch, values_scratch,
):
    faces, sent = (fxl, fxh, fyl, fyh), (gxl, gxh, gyl, gyh)
    totals = jnp.sum(parts[...], axis=0)
    totals_out[...] = totals
    small = small_in[...]
    corners = corners_of(faces, FACE_PLANES, CORNER_ROWS)
    sent_corners = corners_of(sent, 16, 8)
    all_ids = ids[...]
    face_ids = [as_ids(face[WELL_ID]) for face in faces]
    back_ids = [as_ids(face[BACK_ID]) for face in faces]
    corner_ids = [
        as_ids(jnp.broadcast_to(corner.row(SIDE_ID), (8, LANES))) for corner in corners
    ]
    table = jnp.zeros((8, LANES), jnp.float32)
    values = []
    for k in range(RHS):
        step = first_step(totals, small, k)
        height, scale, shift = step["height"], step["scale"], step["shift"]
        s_row, s_image = step["s_row"], step["s_image"]
        at_wells = spread(s_row, all_ids)
        now = [image[k, a] + wells[2 + a] * at_wells for a in range(2)]
        face_now, back_in = [], []
        for f in range(4):
            face, got = faces[f], sent[f]
            here = spread(s_row, face_ids[f])
            face_now.append([got[2 * k + a] + face[WELL_EQ + a] * here for a in range(2)])
            there = spread(s_row, back_ids[f])
            back = [got[8 + 2 * k + a] + face[BACK_EQ + a] * there for a in range(2)]
            back_in.append(product(lambda e, f=f: faces[f][BACK_IN + e], *back))
        corner_now = []
        for c in range(4):
            here = spread(s_row, corner_ids[c])[0:1, :]
            corner_now.append(
                [
                    sent_corners[c].row(2 * k + a) + corners[c].row(SIDE_EQ + a) * here
                    for a in range(2)
                ]
            )
        incoming = [product(lambda e, f=f: faces[f][e], *face_now[f]) for f in range(4)]
        applied, outgoing = block_stencil(couplings, diagonal, now[0], now[1], incoming)
        at_wells = spread(s_image, all_ids)
        second, third = [], []
        for a in range(2):
            twice = applied[a] + wells[2 + a] * at_wells
            base = (now[a] - height * residual[k, a]) * scale
            second.append(base)
            third.append((twice - height * now[a]) * scale - shift * base)
            second_out[k, a] = second[a]
            third_out[k, a] = third[a]
        ends = corner_inputs(corners, corner_now)
        incoming = []
        for f in range(4):
            face = faces[f]
            there = face_stencil(face, face_now[f][0], face_now[f][1], back_in[f])
            over = face_entries(ends[(f, 0)], ends[(f, 1)], outgoing[f])
            here = spread(s_image, face_ids[f])
            outer = []
            for a in range(2):
                twice = there[a] + over[a] + face[WELL_EQ + a] * here
                base = (face_now[f][a] - height * residual_faces[f, 2 * k + a]) * scale
                outer.append((twice - height * face_now[f][a]) * scale - shift * base)
            incoming.append(product(lambda e, f=f: faces[f][e], *outer))
        result, _ = block_stencil(couplings, diagonal, third[0], third[1], incoming)
        fourth = [result[a] - shift * third[a] for a in range(2)]
        values_scratch[k] = wells[0] * third[0] + wells[1] * third[1]
        values_scratch[4 + k] = wells[2] * third[0] + wells[3] * third[1]
        values_scratch[8 + k] = wells[2] * fourth[0] + wells[3] * fourth[1]
        unit = lax.rsqrt(step["rr"])
        fields = [[residual[k, a] * unit for a in range(2)], second, third, fourth]
        number = 0
        for i in range(4):
            for j in range(i, 4):
                dot = full_sum(fields[i][0] * fields[j][0] + fields[i][1] * fields[j][1])
                table = put(4, 4 * number + k, dot, table)
                number += 1
    rows = segment_rows(ids, values_scratch, scratch, present)
    table = pack_rows(rows, table)
    part[...] = jnp.broadcast_to(table[None], part.shape)


def solve_kernel(
    guess, residual, second, third, parts, first_totals, small_in, solution
):
    totals = jnp.sum(parts[...], axis=0)
    before, small = first_totals[...], small_in[...]
    equation = small[1:2, :]
    for k in range(RHS):
        step = first_step(before, small, k)
        unit = lax.rsqrt(step["rr"])
        beta = step["rr"] * unit
        s_third, p_third = unpack_row(totals, k), unpack_row(totals, 4 + k)
        p_fourth = unpack_row(totals, 8 + k)
        gram = {}
        number = 0
        for i in range(4):
            for j in range(i, 4):
                gram[(i, j)] = lane(totals, 4, 4 * number + k)
                number += 1
        gram[(0, 3)] += lane_sum(step["p_row"] * s_third) * unit
        gram[(1, 3)] += lane_sum(step["p_second"] * s_third)
        gram[(2, 3)] += lane_sum(p_third * s_third)
        gram[(3, 3)] += lane_sum(2.0 * p_fourth * s_third + equation * s_third * s_third)
        tiny = 1e-30
        inverse = [lax.rsqrt(jnp.maximum(gram[(i, i)], tiny)) for i in range(4)]
        length = [jnp.maximum(gram[(i, i)], tiny) * inverse[i] for i in range(4)]
        upper = {}
        for i in range(4):
            for j in range(i, 4):
                entry = gram[(i, j)] * inverse[i] * inverse[j]
                for m in range(i):
                    entry = entry - upper[(m, i)] * upper[(m, j)]
                if i == j:
                    pivot = lax.rsqrt(jnp.maximum(entry, 1e-6))
                    upper[(i, i)] = jnp.maximum(entry, 1e-6) * pivot
                    over = pivot
                else:
                    upper[(i, j)] = entry * over
        shift = step["shift"]
        following = lax.rsqrt(step["rr"]) / step["scale"]
        columns = [
            [(0, step["height"] * length[0]), (1, following * length[1])],
            [(1, shift * length[1]), (2, length[2])],
            [(2, shift * length[2]), (3, length[3])],
        ]
        zero = jnp.zeros_like(shift)
        hessenberg = [[zero] * 3 for _ in range(4)]
        for j in range(3):
            for i in range(j + 2):
                for m, factor in columns[j]:
                    if m >= i:
                        hessenberg[i][j] = hessenberg[i][j] + upper[(i, m)] * factor
        target = [beta * length[0] * upper[(0, 0)], zero, zero, zero]
        for j in range(3):
            top, bottom = hessenberg[j][j], hessenberg[j + 1][j]
            turn = lax.rsqrt(top * top + bottom * bottom)
            cosine, sine = top * turn, bottom * turn
            for m in range(j, 3):
                high, low = hessenberg[j][m], hessenberg[j + 1][m]
                hessenberg[j][m] = cosine * high + sine * low
                hessenberg[j + 1][m] = cosine * low - sine * high
            high, low = target[j], target[j + 1]
            target[j] = cosine * high + sine * low
            target[j + 1] = cosine * low - sine * high
        weights = [zero] * 3
        for i in (2, 1, 0):
            value = target[i]
            for j in range(i + 1, 3):
                value = value - hessenberg[i][j] * weights[j]
            weights[i] = value / hessenberg[i][i]
        for a in range(2):
            solution[k, a] = (
                guess[k, a]
                + (weights[0] * unit) * residual[k, a]
                + weights[1] * second[k, a]
                + weights[2] * third[k, a]
            )


def call(kernel, shapes, arguments, scratch=(), own_copies=False, cost=0, grant=24 << 20):
    whole = pl.BlockSpec(memory_space=pltpu.VMEM)
    far = pl.BlockSpec(memory_space=pltpu.HBM)
    scalars = pl.BlockSpec(memory_space=pltpu.SMEM)

    def place(array):
        if len(array.shape) == 1:
            return scalars
        return far if own_copies else whole

    outs = [
        jax.ShapeDtypeStruct(shape, jnp.float32 if len(shape) > 1 else jnp.int32)
        for shape in shapes
    ]
    return pl.pallas_call(
        kernel,
        out_shape=outs,
        in_specs=[place(argument) for argument in arguments],
        out_specs=[scalars if len(shape) == 1 else whole for shape in shapes],
        scratch_shapes=list(scratch),
        compiler_params=pltpu.CompilerParams(vmem_limit_bytes=grant),
        cost_estimate=pl.CostEstimate(flops=cost, bytes_accessed=cost, transcendentals=0)
        if cost
        else None,
    )(*arguments)


def held(*shape):
    return pltpu.VMEM(shape, jnp.float32)


def from_behind(value, axis, steps):
    count = lax.axis_size(axis)
    leading, last = (max(0, -steps), min(count, count - steps))
    return lax.ppermute(value, axis, [(source, source + steps) for source in range(leading, last)])


def exchanged(part):
    return lax.all_to_all(part, ("gx", "gy"), 0, 0, tiled=True)


def body(couplings, diagonal, wells, ids, right, guess):
    devices = lax.axis_size("gx") * lax.axis_size("gy")
    plane = (8, LANES)
    field = guess.shape
    block = guess.shape[2:]
    arguments = (couplings, diagonal, wells, ids, right, guess)

    ends = []
    for argument in arguments:
        shape = argument.shape[:-3] + (2,) + argument.shape[-2:]
        ends += [pltpu.VMEM(shape, argument.dtype)] * 2
    x_low, x_high = call(
        x_pack_kernel,
        [(FACE_PLANES,) + plane] * 2,
        arguments,
        ends + [pltpu.SemaphoreType.DMA((len(ends),))],
        own_copies=True,
        grant=60 << 20,
    )
    fxl = from_behind(x_high, "gx", 1)
    fxh = from_behind(x_low, "gx", -1)
    table, present, y_low, y_high = call(
        guess_kernel,
        [plane, (WELLS + 1,)] + [(FACE_PLANES,) + plane] * 2,
        arguments,
        [held(6, *block), held(6, WELLS, LANES)],
        cost=4 << 20,
    )
    y_low, y_high = call(
        corner_kernel,
        [(FACE_PLANES + CORNER_PLANES,) + plane] * 2,
        (y_low, y_high, fxl, fxh),
    )
    parts = lax.all_gather(table, ("gx", "gy"))
    fyl = from_behind(y_high, "gy", 1)
    fyh = from_behind(y_low, "gy", -1)

    faces = (fxl, fxh, fyl, fyh)
    residual, image, residual_faces, x_low, x_high, y_low, y_high, small = call(
        residual_kernel,
        [field, field, (4, 8) + plane] + [(16,) + plane] * 4 + [(8, LANES)],
        arguments + faces + (parts,),
    )
    gxl = from_behind(x_high, "gx", 1)
    gxh = from_behind(x_low, "gx", -1)
    (table,) = call(
        moments_kernel,
        [plane],
        (wells, ids, residual, image, present),
        [held(16, *block), held(16, WELLS, LANES)],
        cost=4 << 20,
    )
    y_low, y_high = call(
        image_corner_kernel, [(18,) + plane] * 2, (y_low, y_high, gxl, gxh)
    )
    parts = lax.all_gather(table, ("gx", "gy"))
    gyl = from_behind(y_high, "gy", 1)
    gyh = from_behind(y_low, "gy", -1)

    second, third, part, totals = call(
        krylov_kernel,
        [field, field, (devices, 8, LANES), (8, LANES)],
        (couplings, diagonal, wells, ids) + faces + (gxl, gxh, gyl, gyh)
        + (residual, image, residual_faces, parts, small, present),
        [held(12, WELLS, LANES), held(12, *block)],
    )
    parts = exchanged(part)
    (result,) = call(
        solve_kernel,
        [field],
        (guess, residual, second, third, parts, totals, small),
    )
    return result


def solution(mesh):
    in_specs = (
        P("member", None, "gx", "gy", None),
        P("member", "gx", "gy", None),
        P("member", "gx", "gy", None),
        P("gx", "gy", None),
        P("member", None, "gx", "gy", None),
        P("member", None, "gx", "gy", None),
    )
    out_specs = P("member", None, "gx", "gy", None)
    return jax.shard_map(body, mesh=mesh, in_specs=in_specs, out_specs=out_specs, check_vma=False)
```

```python
import jax
import jax.numpy as jnp
from jax import lax
from jax.experimental import pallas as pl
from jax.experimental.pallas import tpu as pltpu
from jax.sharding import PartitionSpec as P

WELLS = 40
RHS = 4
LANES = 128
LAT_UP, LAT_DOWN, RISE, FALL, DIAGONAL = 4, 8, 12, 16, 20
WELL_EQ, WELL_ID, GUESS, REST = 24, 26, 27, 35
BACK_IN, BACK_EQ, BACK_ID = 43, 47, 49
FACE_PLANES = 50
CORNER_PLANES = 5
CORNER_ROWS = 19
SIDE_IN, SIDE_EQ, SIDE_ID, SIDE_GUESS = 4, 8, 10, 11


def product(blocks, first, second):
    return [
        blocks(0) * first + blocks(2) * second,
        blocks(1) * first + blocks(3) * second,
    ]


def iota(shape, axis):
    return lax.broadcasted_iota(jnp.int32, shape, axis)


def roll_up(value, axis):
    return pltpu.roll(value, 1, axis)


def roll_down(value, axis):
    return pltpu.roll(value, value.shape[axis] - 1, axis)


def layer_moves(rising, falling):
    axis = rising.ndim - 1
    lane = iota(rising.shape, axis)
    up = jnp.where(lane == 0, 0.0, roll_up(rising, axis))
    down = jnp.where(lane == LANES - 1, 0.0, roll_down(falling, axis))
    return up + down


def block_stencil(couplings, diagonal, first, second, incoming):
    result = product(lambda e: diagonal[e], first, second)
    moved = [product(lambda e, d=d: couplings[d, e], first, second) for d in range(6)]
    row = iota(first.shape, 1)
    outgoing = [[], [], [], []]
    for b in range(2):
        east, west, north, south, rise, fall = (moved[d][b] for d in range(6))
        total = result[b] + jnp.concatenate([incoming[0][b][None], east[:-1]], axis=0)
        total = total + jnp.concatenate([west[1:], incoming[1][b][None]], axis=0)
        total = total + jnp.where(row == 0, incoming[2][b][:, None, :], roll_up(north, 1))
        total = total + jnp.where(
            row == row.shape[1] - 1, incoming[3][b][:, None, :], roll_down(south, 1)
        )
        result[b] = total + layer_moves(rise, fall)
        outgoing[0].append(west[0])
        outgoing[1].append(east[-1])
        outgoing[2].append(south[:, 0, :])
        outgoing[3].append(north[:, -1, :])
    return result, outgoing


def face_stencil(face, first, second, behind):
    def planes(start):
        return lambda e: face[start + e]

    result = product(planes(DIAGONAL), first, second)
    up = product(planes(LAT_UP), first, second)
    down = product(planes(LAT_DOWN), first, second)
    rise = product(planes(RISE), first, second)
    fall = product(planes(FALL), first, second)
    row = iota(first.shape, 0)
    for b in range(2):
        total = result[b] + behind[b] + layer_moves(rise[b], fall[b])
        total = total + jnp.where(row == 0, 0.0, roll_up(up[b], 0))
        result[b] = total + jnp.where(row == row.shape[0] - 1, 0.0, roll_down(down[b], 0))
    return result


def face_entries(low_end, high_end, entering):
    row = iota(entering[0].shape, 0)
    return [
        entering[b]
        + jnp.where(row == 0, low_end[b], 0.0)
        + jnp.where(row == row.shape[0] - 1, high_end[b], 0.0)
        for b in range(2)
    ]


def spread(totals, ids):
    table = jnp.broadcast_to(totals, (8, LANES))
    if ids.ndim == 2:
        return jnp.take_along_axis(table, ids, axis=1)
    return jnp.stack(
        [jnp.take_along_axis(table, ids[x], axis=1) for x in range(ids.shape[0])], axis=0
    )


def as_ids(plane):
    return plane.astype(jnp.int32)


class Corner:
    def __init__(self, pack, which, base):
        self.pack, self.start = pack, base * 8 + which

    def row(self, number):
        at = self.start + number
        return self.pack[at // 8, at % 8 : at % 8 + 1, :]


def corners_of(faces, base, rows):
    found = []
    for y_face in (2, 3):
        for x_end in range(2):
            found.append(Corner(faces[y_face], x_end * rows, base))
    return found


def corner_inputs(corners, values):
    ends = {}
    for c in range(4):
        x_end, y_end = c % 2, c // 2
        over_x = product(corners[c].row, *values[c])
        over_y = product(lambda e, c=c: corners[c].row(SIDE_IN + e), *values[c])
        ends[(2 + y_end, x_end)] = over_x
        ends[(x_end, y_end)] = over_y
    return ends


def tile_sum(first, second):
    value = first[0] * second[0] + first[1] * second[1]
    return jnp.sum(jnp.sum(value, axis=0), axis=0, keepdims=True)


def list_wells(ids, present):
    depth = ids.shape[0]

    def smallest(planes):
        least = planes[0]
        for plane in planes[1:]:
            least = jnp.minimum(least, plane)
        return jnp.min(least)

    planes = [ids[x].astype(jnp.float32) for x in range(depth)]

    def one_well(state):
        number, well = state
        present[number] = well.astype(jnp.int32)
        after = [jnp.where(plane > well, plane, float(WELLS)) for plane in planes]
        return number + 1, smallest(after)

    number, _ = lax.while_loop(
        lambda state: state[1] < WELLS, one_well, (jnp.int32(1), smallest(planes))
    )
    present[0] = number - 1


def segment_rows(ids, values, scratch, present):
    scratch[...] = jnp.zeros_like(scratch)
    count, depth = values.shape[0], ids.shape[0]

    def one_well(step, _):
        well = present[step + 1]
        masks = [ids[x] == well for x in range(depth)]
        for number in range(count):
            total = jnp.where(masks[0], values[number, 0], 0.0)
            for x in range(1, depth):
                total = total + jnp.where(masks[x], values[number, x], 0.0)
            scratch[number, pl.ds(well, 1), :] = jnp.sum(total, axis=0, keepdims=True)
        return 0

    lax.fori_loop(0, present[0], one_well, 0)
    rows = []
    for number in range(count):
        summed = jnp.sum(scratch[number], axis=1, keepdims=True)
        shape = scratch.shape[1:]
        on_lanes = jnp.where(iota(shape, 0) == iota(shape, 1), summed, 0.0)
        rows.append(jnp.sum(on_lanes, axis=0, keepdims=True))
    return rows


def pack_rows(rows, table):
    for number, row in enumerate(rows):
        placed = row if number % 3 == 0 else pltpu.roll(row, WELLS * (number % 3), 1)
        table = table + jnp.where(
            iota(table.shape, 0) == number // 3, jnp.broadcast_to(placed, table.shape), 0.0
        )
    return table


def unpack_row(table, number):
    row = table[number // 3 : number // 3 + 1, :]
    if number % 3:
        row = pltpu.roll(row, LANES - WELLS * (number % 3), 1)
    return jnp.where(iota(row.shape, 1) < WELLS, row, 0.0)


def place_rows(rows, table):
    for number, row in enumerate(rows):
        group, k = divmod(number, RHS)
        at = k + RHS * (group // 3)
        placed = pltpu.roll(row, WELLS * group, 1) if group in (1, 2) else row
        table = table + jnp.where(
            iota(table.shape, 0) == at, jnp.broadcast_to(placed, table.shape), 0.0
        )
    return table


def place_columns(dots, first_lane, table):
    for number in range(dots.shape[0]):
        column = jnp.sum(dots[number], axis=1, keepdims=True)
        table = table + jnp.where(iota(table.shape, 1) == first_lane + number, column, 0.0)
    return table


def take_group(table, group):
    if group in (1, 2):
        table = pltpu.roll(table, LANES - WELLS * group, 1)
    start = RHS * (group // 3)
    rows = table[start : start + RHS, :]
    return jnp.where(iota(rows.shape, 1) < WELLS, rows, 0.0)


def take_column(table, lane):
    return table[RHS : 2 * RHS, lane : lane + 1]


def lane_sum(row):
    return jnp.sum(row, axis=1, keepdims=True)


def fill_pack(pack, inward, lateral, cut):
    couplings, diagonal, wells, ids, right, guess = range(6)
    for e in range(4):
        pack[e] = cut(couplings, (inward, e), 0)
        pack[LAT_UP + e] = cut(couplings, (lateral, e), 0)
        pack[LAT_DOWN + e] = cut(couplings, (lateral + 1, e), 0)
        pack[RISE + e] = cut(couplings, (4, e), 0)
        pack[FALL + e] = cut(couplings, (5, e), 0)
        pack[DIAGONAL + e] = cut(diagonal, (e,), 0)
        pack[BACK_IN + e] = cut(couplings, (inward, e), 1)
    for a in range(2):
        pack[WELL_EQ + a] = cut(wells, (2 + a,), 0)
        pack[BACK_EQ + a] = cut(wells, (2 + a,), 1)
    pack[WELL_ID] = cut(ids, (), 0).astype(jnp.float32)
    pack[BACK_ID] = cut(ids, (), 1).astype(jnp.float32)
    for k in range(RHS):
        here = [cut(guess, (k, a), 0) for a in range(2)]
        back = [cut(guess, (k, a), 1) for a in range(2)]
        entering = product(lambda e: pack[BACK_IN + e], *back)
        local = face_stencil(pack, here[0], here[1], entering)
        for a in range(2):
            pack[GUESS + 2 * k + a] = here[a]
            pack[REST + 2 * k + a] = cut(right, (k, a), 0) - local[a]


def x_pack_kernel(*refs):
    sources, packs, held_ends, arrived = refs[:6], refs[6:8], refs[8:20], refs[20]
    copies = []
    for n, source in enumerate(sources):
        lead = (slice(None),) * (len(source.shape) - 3)
        depth = source.shape[-3]
        for end, start in enumerate((0, depth - 2)):
            copies.append(
                pltpu.make_async_copy(
                    source.at[lead + (pl.ds(start, 2),)],
                    held_ends[2 * n + end],
                    arrived.at[2 * n + end],
                )
            )
    for copy in copies:
        copy.start()
    for copy in copies:
        copy.wait()
    for end, pack in enumerate(packs):
        fill_pack(
            pack,
            1 - end,
            2,
            lambda n, index, layer: held_ends[2 * n + end][
                index + (1 - layer if end else layer,)
            ],
        )


def y_pack(arguments, packs):
    last = arguments[-1].shape[-2] - 1
    for end, pack in enumerate(packs):
        fill_pack(
            pack,
            3 - end,
            0,
            lambda n, index, layer: arguments[n][
                index + (slice(None), last - layer if end else layer, slice(None))
            ],
        )


def corner_kernel(y_low, y_high, fxl, fxh, low_out, high_out):
    last = fxl.shape[1] - 1
    for own, out, at, side in ((y_low, low_out, 0, LAT_DOWN), (y_high, high_out, last, LAT_UP)):
        for n in range(FACE_PLANES):
            out[n] = own[n]
        row = FACE_PLANES * 8
        out[FACE_PLANES + CORNER_PLANES - 1] = jnp.zeros(out.shape[1:], jnp.float32)
        for face in (fxl, fxh):
            for n in (*range(4), *range(side, side + 4), *range(WELL_EQ, REST)):
                out[row // 8, row % 8 : row % 8 + 1, :] = face[n, at : at + 1, :]
                row += 1


def image_corner_kernel(y_low, y_high, gxl, gxh, low_out, high_out):
    last = gxl.shape[1] - 1
    for own, out, at in ((y_low, low_out, 0), (y_high, high_out, last)):
        for n in range(16):
            out[n] = own[n]
        for x_end, face in enumerate((gxl, gxh)):
            for n in range(8):
                out[16 + x_end, n : n + 1, :] = face[n, at : at + 1, :]


def guess_kernel(
    couplings, diagonal, wells, ids, right, guess,
    part, present, y_low, y_high, values, scratch,
):
    y_pack((couplings, diagonal, wells, ids, right, guess), (y_low, y_high))
    list_wells(ids, present)
    for k in range(RHS):
        values[k] = wells[0] * guess[k, 0] + wells[1] * guess[k, 1]
    values[4] = wells[0] * wells[2] + wells[1] * wells[3]
    values[5] = wells[2] * wells[2] + wells[3] * wells[3]
    rows = segment_rows(ids, values, scratch, present)
    table = pack_rows(rows, jnp.zeros((8, LANES), jnp.float32))
    part[...] = jnp.broadcast_to(table[None, :2], part.shape)


def residual_kernel(
    couplings, diagonal, wells, ids, right, guess, fxl, fxh, fyl, fyh, parts,
    residual, image, residual_faces, x_low, x_high, y_low, y_high, small,
):
    faces = (fxl, fxh, fyl, fyh)
    totals = jnp.sum(parts[...], axis=0)
    corners = corners_of(faces, FACE_PLANES, CORNER_ROWS)
    all_ids = ids[...]
    face_ids = [as_ids(face[WELL_ID]) for face in faces]
    last = guess.shape[2] - 1
    for k in range(RHS):
        s_row = unpack_row(totals, k)
        first, second = guess[k, 0], guess[k, 1]
        incoming = [
            product(
                lambda e, f=f: faces[f][e],
                faces[f][GUESS + 2 * k],
                faces[f][GUESS + 2 * k + 1],
            )
            for f in range(4)
        ]
        applied, outgoing = block_stencil(couplings, diagonal, first, second, incoming)
        at_wells = spread(s_row, all_ids)
        now = [
            right[k, a] - applied[a] - wells[2 + a] * at_wells for a in range(2)
        ]
        for a in range(2):
            residual[k, a] = now[a]
        ends = corner_inputs(
            corners,
            [[corners[c].row(SIDE_GUESS + 2 * k + a) for a in range(2)] for c in range(4)],
        )
        incoming = []
        for f in range(4):
            face = faces[f]
            there = face_entries(ends[(f, 0)], ends[(f, 1)], outgoing[f])
            face_wells = spread(s_row, face_ids[f])
            outer = [
                face[REST + 2 * k + a] - there[a] - face[WELL_EQ + a] * face_wells
                for a in range(2)
            ]
            for a in range(2):
                residual_faces[f, 2 * k + a] = outer[a]
            incoming.append(product(lambda e, f=f: faces[f][e], *outer))
        result, _ = block_stencil(couplings, diagonal, now[0], now[1], incoming)
        for a in range(2):
            image[k, a] = result[a]
            x_low[2 * k + a] = result[a][0]
            x_low[8 + 2 * k + a] = result[a][1]
            x_high[2 * k + a] = result[a][last]
            x_high[8 + 2 * k + a] = result[a][last - 1]
            y_low[2 * k + a] = result[a][:, 0, :]
            y_low[8 + 2 * k + a] = result[a][:, 1, :]
            y_high[2 * k + a] = result[a][:, last, :]
            y_high[8 + 2 * k + a] = result[a][:, last - 1, :]
    small[...] = jnp.concatenate(
        [unpack_row(totals, 4), unpack_row(totals, 5), jnp.zeros((6, LANES), jnp.float32)], axis=0
    )


def moments_kernel(
    wells, ids, residual, image, present, part, values, scratch, dots
):
    dots[...] = jnp.zeros_like(dots)
    for k in range(RHS):
        now = [residual[k, a] for a in range(2)]
        result = [image[k, a] for a in range(2)]
        for n, field in enumerate((now, result)):
            values[4 * n + k] = wells[0] * field[0] + wells[1] * field[1]
            values[8 + 4 * n + k] = wells[2] * field[0] + wells[3] * field[1]
        row = slice(RHS + k, RHS + k + 1)
        dots[0, row, :] = tile_sum(now, now)
        dots[1, row, :] = tile_sum(now, result)
        dots[2, row, :] = tile_sum(result, result)
    rows = segment_rows(ids, values, scratch, present)
    table = place_rows(rows, jnp.zeros((8, LANES), jnp.float32))
    table = place_columns(dots, WELLS, table)
    part[...] = jnp.broadcast_to(table[None], part.shape)


def first_step(totals, small):
    s_row, us_row, p_row, ps_row = (take_group(totals, group) for group in range(4))
    within, equation = small[0:1, :], small[1:2, :]
    rr, rs, ss = (take_column(totals, WELLS + i) for i in range(3))
    height = (rs + lane_sum(p_row * s_row)) / rr
    square = ss + lane_sum(2.0 * ps_row * s_row + equation * s_row * s_row)
    left = jnp.maximum(square - height * height * rr, 1e-7 * square)
    scale = lax.rsqrt(left)
    s_image = us_row + within * s_row
    s_second = (s_image - height * s_row) * scale
    p_second = (ps_row + equation * s_row - height * p_row) * scale
    shift = rs / rr + lane_sum(p_second * s_second)
    unit = lax.rsqrt(rr)
    following = left * scale * unit
    return s_row, s_image, p_row, p_second, (unit, rr * unit, height, shift, following, scale)


def krylov_kernel(
    couplings, diagonal, wells, ids, fxl, fxh, fyl, fyh, gxl, gxh, gyl, gyh,
    residual, image, residual_faces, parts, small_in, present,
    second_out, third_out, part, known, scratch, values_scratch, dots,
):
    faces, sent = (fxl, fxh, fyl, fyh), (gxl, gxh, gyl, gyh)
    totals = jnp.sum(parts[...], axis=0)
    small = small_in[...]
    s_rows, s_images, p_rows, p_seconds, scalars = first_step(totals, small)
    known[0:RHS, :] = p_rows
    known[RHS : 2 * RHS, :] = p_seconds
    columns = jnp.zeros((RHS, LANES), jnp.float32)
    for n, column in enumerate(scalars):
        columns = columns + jnp.where(iota(columns.shape, 1) == n, column, 0.0)
    known[2 * RHS : 3 * RHS, :] = columns
    known[3 * RHS :, :] = jnp.broadcast_to(small[1:2, :], (RHS, LANES))
    dots[...] = jnp.zeros_like(dots)
    corners = corners_of(faces, FACE_PLANES, CORNER_ROWS)
    sent_corners = corners_of(sent, 16, 8)
    all_ids = ids[...]
    face_ids = [as_ids(face[WELL_ID]) for face in faces]
    back_ids = [as_ids(face[BACK_ID]) for face in faces]
    corner_ids = [
        as_ids(jnp.broadcast_to(corner.row(SIDE_ID), (8, LANES))) for corner in corners
    ]
    for k in range(RHS):
        unit, _, height, shift, _, scale = (column[k : k + 1, :] for column in scalars)
        s_row, s_image = s_rows[k : k + 1, :], s_images[k : k + 1, :]
        at_wells = spread(s_row, all_ids)
        now = [image[k, a] + wells[2 + a] * at_wells for a in range(2)]
        face_now, back_in = [], []
        for f in range(4):
            face, got = faces[f], sent[f]
            here = spread(s_row, face_ids[f])
            face_now.append([got[2 * k + a] + face[WELL_EQ + a] * here for a in range(2)])
            there = spread(s_row, back_ids[f])
            back = [got[8 + 2 * k + a] + face[BACK_EQ + a] * there for a in range(2)]
            back_in.append(product(lambda e, f=f: faces[f][BACK_IN + e], *back))
        corner_now = []
        for c in range(4):
            here = spread(s_row, corner_ids[c])[0:1, :]
            corner_now.append(
                [
                    sent_corners[c].row(2 * k + a) + corners[c].row(SIDE_EQ + a) * here
                    for a in range(2)
                ]
            )
        incoming = [product(lambda e, f=f: faces[f][e], *face_now[f]) for f in range(4)]
        applied, outgoing = block_stencil(couplings, diagonal, now[0], now[1], incoming)
        at_wells = spread(s_image, all_ids)
        second, third = [], []
        for a in range(2):
            twice = applied[a] + wells[2 + a] * at_wells
            base = (now[a] - height * residual[k, a]) * scale
            second.append(base)
            third.append((twice - height * now[a]) * scale - shift * base)
            second_out[k, a] = second[a]
            third_out[k, a] = third[a]
        ends = corner_inputs(corners, corner_now)
        incoming = []
        for f in range(4):
            face = faces[f]
            there = face_stencil(face, face_now[f][0], face_now[f][1], back_in[f])
            over = face_entries(ends[(f, 0)], ends[(f, 1)], outgoing[f])
            here = spread(s_image, face_ids[f])
            outer = []
            for a in range(2):
                twice = there[a] + over[a] + face[WELL_EQ + a] * here
                base = (face_now[f][a] - height * residual_faces[f, 2 * k + a]) * scale
                outer.append((twice - height * face_now[f][a]) * scale - shift * base)
            incoming.append(product(lambda e, f=f: faces[f][e], *outer))
        result, _ = block_stencil(couplings, diagonal, third[0], third[1], incoming)
        fourth = [result[a] - shift * third[a] for a in range(2)]
        values_scratch[k] = wells[0] * third[0] + wells[1] * third[1]
        values_scratch[4 + k] = wells[2] * third[0] + wells[3] * third[1]
        values_scratch[8 + k] = wells[2] * fourth[0] + wells[3] * fourth[1]
        fields = [[residual[k, a] * unit for a in range(2)], second, third, fourth]
        number = 0
        for i in range(4):
            for j in range(i, 4):
                dots[number, RHS + k : RHS + k + 1, :] = tile_sum(fields[i], fields[j])
                number += 1
    rows = segment_rows(ids, values_scratch, scratch, present)
    table = place_rows(rows, jnp.zeros((8, LANES), jnp.float32))
    table = place_columns(dots, 0, table)
    part[...] = jnp.broadcast_to(table[None], part.shape)


def solve_kernel(guess, residual, second, third, parts, known, solution):
    totals = jnp.sum(parts[...], axis=0)
    s_third, p_third, p_fourth = (take_group(totals, group) for group in range(3))
    p_first, p_second = known[0:RHS, :], known[RHS : 2 * RHS, :]
    unit, beta, height, shift, following = (
        known[2 * RHS : 3 * RHS, n : n + 1] for n in range(5)
    )
    equation = known[3 * RHS :, :]
    gram = {}
    number = 0
    for i in range(4):
        for j in range(i, 4):
            gram[(i, j)] = take_column(totals, number)
            number += 1
    gram[(0, 3)] += lane_sum(p_first * s_third) * unit
    gram[(1, 3)] += lane_sum(p_second * s_third)
    gram[(2, 3)] += lane_sum(p_third * s_third)
    gram[(3, 3)] += lane_sum(2.0 * p_fourth * s_third + equation * s_third * s_third)
    tiny = 1e-30
    inverse = [lax.rsqrt(jnp.maximum(gram[(i, i)], tiny)) for i in range(4)]
    length = [jnp.maximum(gram[(i, i)], tiny) * inverse[i] for i in range(4)]
    upper = {}
    for i in range(4):
        for j in range(i, 4):
            entry = gram[(i, j)] * inverse[i] * inverse[j]
            for m in range(i):
                entry = entry - upper[(m, i)] * upper[(m, j)]
            if i == j:
                pivot = lax.rsqrt(jnp.maximum(entry, 1e-6))
                upper[(i, i)] = jnp.maximum(entry, 1e-6) * pivot
                over = pivot
            else:
                upper[(i, j)] = entry * over
    columns = [
        [(0, height * length[0]), (1, following * length[1])],
        [(1, shift * length[1]), (2, length[2])],
        [(2, shift * length[2]), (3, length[3])],
    ]
    zero = jnp.zeros_like(shift)
    hessenberg = [[zero] * 3 for _ in range(4)]
    for j in range(3):
        for i in range(j + 2):
            for m, factor in columns[j]:
                if m >= i:
                    hessenberg[i][j] = hessenberg[i][j] + upper[(i, m)] * factor
    target = [beta * length[0] * upper[(0, 0)], zero, zero, zero]
    turns = []
    for j in range(3):
        top, bottom = hessenberg[j][j], hessenberg[j + 1][j]
        turn = lax.rsqrt(top * top + bottom * bottom)
        turns.append(turn)
        cosine, sine = top * turn, bottom * turn
        for m in range(j, 3):
            high, low = hessenberg[j][m], hessenberg[j + 1][m]
            hessenberg[j][m] = cosine * high + sine * low
            hessenberg[j + 1][m] = cosine * low - sine * high
        high, low = target[j], target[j + 1]
        target[j] = cosine * high + sine * low
        target[j + 1] = cosine * low - sine * high
    weights = [zero] * 3
    for i in (2, 1, 0):
        value = target[i]
        for j in range(i + 1, 3):
            value = value - hessenberg[i][j] * weights[j]
        weights[i] = value * turns[i]
    for k in range(RHS):
        on_first, on_second, on_third = (
            column[k : k + 1, :] for column in (weights[0] * unit, weights[1], weights[2])
        )
        for a in range(2):
            solution[k, a] = (
                guess[k, a]
                + on_first * residual[k, a]
                + on_second * second[k, a]
                + on_third * third[k, a]
            )


def call(kernel, shapes, arguments, scratch=(), own_copies=False, cost=0, grant=24 << 20):
    whole = pl.BlockSpec(memory_space=pltpu.VMEM)
    far = pl.BlockSpec(memory_space=pltpu.HBM)
    scalars = pl.BlockSpec(memory_space=pltpu.SMEM)

    def place(array):
        if len(array.shape) == 1:
            return scalars
        return far if own_copies else whole

    outs = [
        jax.ShapeDtypeStruct(shape, jnp.float32 if len(shape) > 1 else jnp.int32)
        for shape in shapes
    ]
    return pl.pallas_call(
        kernel,
        out_shape=outs,
        in_specs=[place(argument) for argument in arguments],
        out_specs=[scalars if len(shape) == 1 else whole for shape in shapes],
        scratch_shapes=list(scratch),
        compiler_params=pltpu.CompilerParams(vmem_limit_bytes=grant),
        cost_estimate=pl.CostEstimate(flops=cost, bytes_accessed=cost, transcendentals=0)
        if cost
        else None,
    )(*arguments)


def held(*shape):
    return pltpu.VMEM(shape, jnp.float32)


def from_behind(value, axis, steps):
    count = lax.axis_size(axis)
    leading, last = (max(0, -steps), min(count, count - steps))
    return lax.ppermute(value, axis, [(source, source + steps) for source in range(leading, last)])


def exchanged(part):
    return lax.all_to_all(part, ("gx", "gy"), 0, 0, tiled=True)


def body(couplings, diagonal, wells, ids, right, guess):
    devices = lax.axis_size("gx") * lax.axis_size("gy")
    plane = (8, LANES)
    field = guess.shape
    block = guess.shape[2:]
    arguments = (couplings, diagonal, wells, ids, right, guess)

    ends = []
    for argument in arguments:
        shape = argument.shape[:-3] + (2,) + argument.shape[-2:]
        ends += [pltpu.VMEM(shape, argument.dtype)] * 2
    x_low, x_high = call(
        x_pack_kernel,
        [(FACE_PLANES,) + plane] * 2,
        arguments,
        ends + [pltpu.SemaphoreType.DMA((len(ends),))],
        own_copies=True,
        grant=60 << 20,
    )
    fxl = from_behind(x_high, "gx", 1)
    fxh = from_behind(x_low, "gx", -1)
    part, present, y_low, y_high = call(
        guess_kernel,
        [(devices, 2, LANES), (WELLS + 1,)] + [(FACE_PLANES,) + plane] * 2,
        arguments,
        [held(6, *block), held(6, WELLS, LANES)],
        cost=4 << 20,
    )
    parts = exchanged(part)
    y_low, y_high = call(
        corner_kernel,
        [(FACE_PLANES + CORNER_PLANES,) + plane] * 2,
        (y_low, y_high, fxl, fxh),
        cost=256 << 20,
    )
    fyl = from_behind(y_high, "gy", 1)
    fyh = from_behind(y_low, "gy", -1)

    faces = (fxl, fxh, fyl, fyh)
    residual, image, residual_faces, x_low, x_high, y_low, y_high, small = call(
        residual_kernel,
        [field, field, (4, 8) + plane] + [(16,) + plane] * 4 + [(8, LANES)],
        arguments + faces + (parts,),
    )
    gxl = from_behind(x_high, "gx", 1)
    gxh = from_behind(x_low, "gx", -1)
    (part,) = call(
        moments_kernel,
        [(devices, 8, LANES)],
        (wells, ids, residual, image, present),
        [held(16, *block), held(16, WELLS, LANES), held(3, *plane)],
        cost=4 << 20,
    )
    parts = exchanged(part)
    y_low, y_high = call(
        image_corner_kernel,
        [(18,) + plane] * 2,
        (y_low, y_high, gxl, gxh),
        cost=256 << 20,
    )
    gyl = from_behind(y_high, "gy", 1)
    gyh = from_behind(y_low, "gy", -1)

    second, third, part, known = call(
        krylov_kernel,
        [field, field, (devices, 8, LANES), (4 * RHS, LANES)],
        (couplings, diagonal, wells, ids) + faces + (gxl, gxh, gyl, gyh)
        + (residual, image, residual_faces, parts, small, present),
        [held(12, WELLS, LANES), held(12, *block), held(10, *plane)],
    )
    parts = exchanged(part)
    (result,) = call(
        solve_kernel,
        [field],
        (guess, residual, second, third, parts, known),
    )
    return result


def solution(mesh):
    in_specs = (
        P("member", None, "gx", "gy", None),
        P("member", "gx", "gy", None),
        P("member", "gx", "gy", None),
        P("gx", "gy", None),
        P("member", None, "gx", "gy", None),
        P("member", None, "gx", "gy", None),
    )
    out_specs = P("member", None, "gx", "gy", None)
    return jax.shard_map(body, mesh=mesh, in_specs=in_specs, out_specs=out_specs, check_vma=False)
```

```python
import jax
import jax.numpy as jnp
from jax import lax
from jax.experimental import pallas as pl
from jax.experimental.pallas import tpu as pltpu
from jax.sharding import PartitionSpec as P

WELLS = 40
RHS = 4
LANES = 128
LAT_UP, LAT_DOWN, RISE, FALL, DIAGONAL = 4, 8, 12, 16, 20
WELL_EQ, WELL_ID, GUESS, REST = 24, 26, 27, 35
BACK_IN, BACK_EQ, BACK_ID = 43, 47, 49
FACE_PLANES = 50
CORNER_PLANES = 5
CORNER_ROWS = 19
SIDE_IN, SIDE_EQ, SIDE_ID, SIDE_GUESS = 4, 8, 10, 11


def product(blocks, first, second):
    return [
        blocks(0) * first + blocks(2) * second,
        blocks(1) * first + blocks(3) * second,
    ]


def iota(shape, axis):
    return lax.broadcasted_iota(jnp.int32, shape, axis)


def roll_up(value, axis):
    return pltpu.roll(value, 1, axis)


def roll_down(value, axis):
    return pltpu.roll(value, value.shape[axis] - 1, axis)


def layer_moves(rising, falling):
    axis = rising.ndim - 1
    lane = iota(rising.shape, axis)
    up = jnp.where(lane == 0, 0.0, roll_up(rising, axis))
    down = jnp.where(lane == LANES - 1, 0.0, roll_down(falling, axis))
    return up + down


def block_stencil(couplings, diagonal, first, second, incoming):
    result = product(lambda e: diagonal[e], first, second)
    moved = [product(lambda e, d=d: couplings[d, e], first, second) for d in range(6)]
    row = iota(first.shape, 1)
    outgoing = [[], [], [], []]
    for b in range(2):
        east, west, north, south, rise, fall = (moved[d][b] for d in range(6))
        total = result[b] + jnp.concatenate([incoming[0][b][None], east[:-1]], axis=0)
        total = total + jnp.concatenate([west[1:], incoming[1][b][None]], axis=0)
        total = total + jnp.where(row == 0, incoming[2][b][:, None, :], roll_up(north, 1))
        total = total + jnp.where(
            row == row.shape[1] - 1, incoming[3][b][:, None, :], roll_down(south, 1)
        )
        result[b] = total + layer_moves(rise, fall)
        outgoing[0].append(west[0])
        outgoing[1].append(east[-1])
        outgoing[2].append(south[:, 0, :])
        outgoing[3].append(north[:, -1, :])
    return result, outgoing


def face_stencil(face, first, second, behind):
    def planes(start):
        return lambda e: face[start + e]

    result = product(planes(DIAGONAL), first, second)
    up = product(planes(LAT_UP), first, second)
    down = product(planes(LAT_DOWN), first, second)
    rise = product(planes(RISE), first, second)
    fall = product(planes(FALL), first, second)
    row = iota(first.shape, 0)
    for b in range(2):
        total = result[b] + behind[b] + layer_moves(rise[b], fall[b])
        total = total + jnp.where(row == 0, 0.0, roll_up(up[b], 0))
        result[b] = total + jnp.where(row == row.shape[0] - 1, 0.0, roll_down(down[b], 0))
    return result


def face_entries(low_end, high_end, entering):
    row = iota(entering[0].shape, 0)
    return [
        entering[b]
        + jnp.where(row == 0, low_end[b], 0.0)
        + jnp.where(row == row.shape[0] - 1, high_end[b], 0.0)
        for b in range(2)
    ]


def spread(totals, ids):
    table = jnp.broadcast_to(totals, (8, LANES))
    if ids.ndim == 2:
        return jnp.take_along_axis(table, ids, axis=1)
    return jnp.stack(
        [jnp.take_along_axis(table, ids[x], axis=1) for x in range(ids.shape[0])], axis=0
    )


def as_ids(plane):
    return plane.astype(jnp.int32)


class Corner:
    def __init__(self, pack, which, base):
        self.pack, self.start = pack, base * 8 + which

    def row(self, number):
        at = self.start + number
        return self.pack[at // 8, at % 8 : at % 8 + 1, :]


def corners_of(faces, base, rows):
    found = []
    for y_face in (2, 3):
        for x_end in range(2):
            found.append(Corner(faces[y_face], x_end * rows, base))
    return found


def corner_inputs(corners, values):
    ends = {}
    for c in range(4):
        x_end, y_end = c % 2, c // 2
        over_x = product(corners[c].row, *values[c])
        over_y = product(lambda e, c=c: corners[c].row(SIDE_IN + e), *values[c])
        ends[(2 + y_end, x_end)] = over_x
        ends[(x_end, y_end)] = over_y
    return ends


def tile_sum(first, second):
    value = first[0] * second[0] + first[1] * second[1]
    return jnp.sum(jnp.sum(value, axis=0), axis=0, keepdims=True)


def list_wells(ids, present):
    depth = ids.shape[0]

    def smallest(planes):
        least = planes[0]
        for plane in planes[1:]:
            least = jnp.minimum(least, plane)
        return jnp.min(least)

    planes = [ids[x].astype(jnp.float32) for x in range(depth)]

    def one_well(state):
        number, well = state
        present[number] = well.astype(jnp.int32)
        after = [jnp.where(plane > well, plane, float(WELLS)) for plane in planes]
        return number + 1, smallest(after)

    number, _ = lax.while_loop(
        lambda state: state[1] < WELLS, one_well, (jnp.int32(1), smallest(planes))
    )
    present[0] = number - 1


def segment_rows(ids, values, scratch, present):
    scratch[...] = jnp.zeros_like(scratch)
    count, depth = values.shape[0], ids.shape[0]

    def one_well(step, _):
        well = present[step + 1]
        masks = [ids[x] == well for x in range(depth)]
        for number in range(count):
            total = jnp.where(masks[0], values[number, 0], 0.0)
            for x in range(1, depth):
                total = total + jnp.where(masks[x], values[number, x], 0.0)
            scratch[number, pl.ds(well, 1), :] = jnp.sum(total, axis=0, keepdims=True)
        return 0

    lax.fori_loop(0, present[0], one_well, 0)
    rows = []
    for number in range(count):
        summed = jnp.sum(scratch[number], axis=1, keepdims=True)
        shape = scratch.shape[1:]
        on_lanes = jnp.where(iota(shape, 0) == iota(shape, 1), summed, 0.0)
        rows.append(jnp.sum(on_lanes, axis=0, keepdims=True))
    return rows


def pack_rows(rows, table):
    for number, row in enumerate(rows):
        placed = row if number % 3 == 0 else pltpu.roll(row, WELLS * (number % 3), 1)
        table = table + jnp.where(
            iota(table.shape, 0) == number // 3, jnp.broadcast_to(placed, table.shape), 0.0
        )
    return table


def unpack_row(table, number):
    row = table[number // 3 : number // 3 + 1, :]
    if number % 3:
        row = pltpu.roll(row, LANES - WELLS * (number % 3), 1)
    return jnp.where(iota(row.shape, 1) < WELLS, row, 0.0)


def place_rows(rows, table):
    for number, row in enumerate(rows):
        group, k = divmod(number, RHS)
        at = k + RHS * (group // 3)
        placed = pltpu.roll(row, WELLS * group, 1) if group in (1, 2) else row
        table = table + jnp.where(
            iota(table.shape, 0) == at, jnp.broadcast_to(placed, table.shape), 0.0
        )
    return table


def place_columns(dots, first_lane, table):
    for number in range(dots.shape[0]):
        column = jnp.sum(dots[number], axis=1, keepdims=True)
        table = table + jnp.where(iota(table.shape, 1) == first_lane + number, column, 0.0)
    return table


def take_group(table, group):
    if group in (1, 2):
        table = pltpu.roll(table, LANES - WELLS * group, 1)
    start = RHS * (group // 3)
    rows = table[start : start + RHS, :]
    return jnp.where(iota(rows.shape, 1) < WELLS, rows, 0.0)


def take_column(table, lane):
    return table[RHS : 2 * RHS, lane : lane + 1]


def lane_sum(row):
    return jnp.sum(row, axis=1, keepdims=True)


def fill_pack(pack, inward, lateral, cut):
    couplings, diagonal, wells, ids, right, guess = range(6)
    for e in range(4):
        pack[e] = cut(couplings, (inward, e), 0)
        pack[LAT_UP + e] = cut(couplings, (lateral, e), 0)
        pack[LAT_DOWN + e] = cut(couplings, (lateral + 1, e), 0)
        pack[RISE + e] = cut(couplings, (4, e), 0)
        pack[FALL + e] = cut(couplings, (5, e), 0)
        pack[DIAGONAL + e] = cut(diagonal, (e,), 0)
        pack[BACK_IN + e] = cut(couplings, (inward, e), 1)
    for a in range(2):
        pack[WELL_EQ + a] = cut(wells, (2 + a,), 0)
        pack[BACK_EQ + a] = cut(wells, (2 + a,), 1)
    pack[WELL_ID] = cut(ids, (), 0).astype(jnp.float32)
    pack[BACK_ID] = cut(ids, (), 1).astype(jnp.float32)
    for k in range(RHS):
        here = [cut(guess, (k, a), 0) for a in range(2)]
        back = [cut(guess, (k, a), 1) for a in range(2)]
        entering = product(lambda e: pack[BACK_IN + e], *back)
        local = face_stencil(pack, here[0], here[1], entering)
        for a in range(2):
            pack[GUESS + 2 * k + a] = here[a]
            pack[REST + 2 * k + a] = cut(right, (k, a), 0) - local[a]


def x_pack_kernel(*refs):
    sources, packs, held_ends, arrived = refs[:6], refs[6:8], refs[8:20], refs[20]
    copies = []
    for n, source in enumerate(sources):
        lead = (slice(None),) * (len(source.shape) - 3)
        depth = source.shape[-3]
        for end, start in enumerate((0, depth - 2)):
            copies.append(
                pltpu.make_async_copy(
                    source.at[lead + (pl.ds(start, 2),)],
                    held_ends[2 * n + end],
                    arrived.at[2 * n + end],
                )
            )
    for copy in copies:
        copy.start()
    for copy in copies:
        copy.wait()
    for end, pack in enumerate(packs):
        fill_pack(
            pack,
            1 - end,
            2,
            lambda n, index, layer: held_ends[2 * n + end][
                index + (1 - layer if end else layer,)
            ],
        )


def y_pack(arguments, packs):
    last = arguments[-1].shape[-2] - 1
    for end, pack in enumerate(packs):
        fill_pack(
            pack,
            3 - end,
            0,
            lambda n, index, layer: arguments[n][
                index + (slice(None), last - layer if end else layer, slice(None))
            ],
        )


def corner_kernel(y_low, y_high, fxl, fxh, low_out, high_out):
    last = fxl.shape[1] - 1
    for own, out, at, side in ((y_low, low_out, 0, LAT_DOWN), (y_high, high_out, last, LAT_UP)):
        for n in range(FACE_PLANES):
            out[n] = own[n]
        row = FACE_PLANES * 8
        out[FACE_PLANES + CORNER_PLANES - 1] = jnp.zeros(out.shape[1:], jnp.float32)
        for face in (fxl, fxh):
            for n in (*range(4), *range(side, side + 4), *range(WELL_EQ, REST)):
                out[row // 8, row % 8 : row % 8 + 1, :] = face[n, at : at + 1, :]
                row += 1


def image_corner_kernel(y_low, y_high, gxl, gxh, low_out, high_out):
    last = gxl.shape[1] - 1
    for own, out, at in ((y_low, low_out, 0), (y_high, high_out, last)):
        for n in range(16):
            out[n] = own[n]
        for x_end, face in enumerate((gxl, gxh)):
            for n in range(8):
                out[16 + x_end, n : n + 1, :] = face[n, at : at + 1, :]


def guess_kernel(
    couplings, diagonal, wells, ids, right, guess,
    part, present, y_low, y_high, values, scratch,
):
    y_pack((couplings, diagonal, wells, ids, right, guess), (y_low, y_high))
    list_wells(ids, present)
    for k in range(RHS):
        values[k] = wells[0] * guess[k, 0] + wells[1] * guess[k, 1]
    values[4] = wells[0] * wells[2] + wells[1] * wells[3]
    values[5] = wells[2] * wells[2] + wells[3] * wells[3]
    rows = segment_rows(ids, values, scratch, present)
    table = pack_rows(rows, jnp.zeros((8, LANES), jnp.float32))
    part[...] = jnp.broadcast_to(table[None], part.shape)


def residual_kernel(
    couplings, diagonal, wells, ids, right, guess, fxl, fxh, fyl, fyh, parts,
    residual, image, residual_faces, x_low, x_high, y_low, y_high, small,
):
    faces = (fxl, fxh, fyl, fyh)
    totals = jnp.sum(parts[...], axis=0)
    corners = corners_of(faces, FACE_PLANES, CORNER_ROWS)
    all_ids = ids[...]
    face_ids = [as_ids(face[WELL_ID]) for face in faces]
    last = guess.shape[2] - 1
    for k in range(RHS):
        s_row = unpack_row(totals, k)
        first, second = guess[k, 0], guess[k, 1]
        incoming = [
            product(
                lambda e, f=f: faces[f][e],
                faces[f][GUESS + 2 * k],
                faces[f][GUESS + 2 * k + 1],
            )
            for f in range(4)
        ]
        applied, outgoing = block_stencil(couplings, diagonal, first, second, incoming)
        at_wells = spread(s_row, all_ids)
        now = [
            right[k, a] - applied[a] - wells[2 + a] * at_wells for a in range(2)
        ]
        for a in range(2):
            residual[k, a] = now[a]
        ends = corner_inputs(
            corners,
            [[corners[c].row(SIDE_GUESS + 2 * k + a) for a in range(2)] for c in range(4)],
        )
        incoming = []
        for f in range(4):
            face = faces[f]
            there = face_entries(ends[(f, 0)], ends[(f, 1)], outgoing[f])
            face_wells = spread(s_row, face_ids[f])
            outer = [
                face[REST + 2 * k + a] - there[a] - face[WELL_EQ + a] * face_wells
                for a in range(2)
            ]
            for a in range(2):
                residual_faces[f, 2 * k + a] = outer[a]
            incoming.append(product(lambda e, f=f: faces[f][e], *outer))
        result, _ = block_stencil(couplings, diagonal, now[0], now[1], incoming)
        for a in range(2):
            image[k, a] = result[a]
            x_low[2 * k + a] = result[a][0]
            x_low[8 + 2 * k + a] = result[a][1]
            x_high[2 * k + a] = result[a][last]
            x_high[8 + 2 * k + a] = result[a][last - 1]
            y_low[2 * k + a] = result[a][:, 0, :]
            y_low[8 + 2 * k + a] = result[a][:, 1, :]
            y_high[2 * k + a] = result[a][:, last, :]
            y_high[8 + 2 * k + a] = result[a][:, last - 1, :]
    small[...] = jnp.concatenate(
        [unpack_row(totals, 4), unpack_row(totals, 5), jnp.zeros((6, LANES), jnp.float32)], axis=0
    )


def moments_kernel(
    wells, ids, residual, image, present, part, values, scratch, dots
):
    dots[...] = jnp.zeros_like(dots)
    for k in range(RHS):
        now = [residual[k, a] for a in range(2)]
        result = [image[k, a] for a in range(2)]
        for n, field in enumerate((now, result)):
            values[4 * n + k] = wells[0] * field[0] + wells[1] * field[1]
            values[8 + 4 * n + k] = wells[2] * field[0] + wells[3] * field[1]
        row = slice(RHS + k, RHS + k + 1)
        dots[0, row, :] = tile_sum(now, now)
        dots[1, row, :] = tile_sum(now, result)
        dots[2, row, :] = tile_sum(result, result)
    rows = segment_rows(ids, values, scratch, present)
    table = place_rows(rows, jnp.zeros((8, LANES), jnp.float32))
    table = place_columns(dots, WELLS, table)
    part[...] = jnp.broadcast_to(table[None], part.shape)


def first_step(totals, small):
    s_row, us_row, p_row, ps_row = (take_group(totals, group) for group in range(4))
    within, equation = small[0:1, :], small[1:2, :]
    rr, rs, ss = (take_column(totals, WELLS + i) for i in range(3))
    height = (rs + lane_sum(p_row * s_row)) / rr
    square = ss + lane_sum(2.0 * ps_row * s_row + equation * s_row * s_row)
    left = jnp.maximum(square - height * height * rr, 1e-7 * square)
    scale = lax.rsqrt(left)
    s_image = us_row + within * s_row
    s_second = (s_image - height * s_row) * scale
    p_second = (ps_row + equation * s_row - height * p_row) * scale
    shift = rs / rr + lane_sum(p_second * s_second)
    unit = lax.rsqrt(rr)
    following = left * scale * unit
    return s_row, s_image, p_row, p_second, (unit, rr * unit, height, shift, following, scale)


def krylov_kernel(
    couplings, diagonal, wells, ids, fxl, fxh, fyl, fyh, gxl, gxh, gyl, gyh,
    residual, image, residual_faces, parts, small_in, present,
    second_out, third_out, part, known, scratch, values_scratch, dots,
):
    faces, sent = (fxl, fxh, fyl, fyh), (gxl, gxh, gyl, gyh)
    totals = jnp.sum(parts[...], axis=0)
    small = small_in[...]
    s_rows, s_images, p_rows, p_seconds, scalars = first_step(totals, small)
    known[0:RHS, :] = p_rows
    known[RHS : 2 * RHS, :] = p_seconds
    columns = jnp.zeros((RHS, LANES), jnp.float32)
    for n, column in enumerate(scalars):
        columns = columns + jnp.where(iota(columns.shape, 1) == n, column, 0.0)
    known[2 * RHS : 3 * RHS, :] = columns
    known[3 * RHS :, :] = jnp.broadcast_to(small[1:2, :], (RHS, LANES))
    dots[...] = jnp.zeros_like(dots)
    corners = corners_of(faces, FACE_PLANES, CORNER_ROWS)
    sent_corners = corners_of(sent, 16, 8)
    all_ids = ids[...]
    face_ids = [as_ids(face[WELL_ID]) for face in faces]
    back_ids = [as_ids(face[BACK_ID]) for face in faces]
    corner_ids = [
        as_ids(jnp.broadcast_to(corner.row(SIDE_ID), (8, LANES))) for corner in corners
    ]
    for k in range(RHS):
        unit, _, height, shift, _, scale = (column[k : k + 1, :] for column in scalars)
        s_row, s_image = s_rows[k : k + 1, :], s_images[k : k + 1, :]
        at_wells = spread(s_row, all_ids)
        now = [image[k, a] + wells[2 + a] * at_wells for a in range(2)]
        face_now, back_in = [], []
        for f in range(4):
            face, got = faces[f], sent[f]
            here = spread(s_row, face_ids[f])
            face_now.append([got[2 * k + a] + face[WELL_EQ + a] * here for a in range(2)])
            there = spread(s_row, back_ids[f])
            back = [got[8 + 2 * k + a] + face[BACK_EQ + a] * there for a in range(2)]
            back_in.append(product(lambda e, f=f: faces[f][BACK_IN + e], *back))
        corner_now = []
        for c in range(4):
            here = spread(s_row, corner_ids[c])[0:1, :]
            corner_now.append(
                [
                    sent_corners[c].row(2 * k + a) + corners[c].row(SIDE_EQ + a) * here
                    for a in range(2)
                ]
            )
        incoming = [product(lambda e, f=f: faces[f][e], *face_now[f]) for f in range(4)]
        applied, outgoing = block_stencil(couplings, diagonal, now[0], now[1], incoming)
        at_wells = spread(s_image, all_ids)
        second, third = [], []
        for a in range(2):
            twice = applied[a] + wells[2 + a] * at_wells
            base = (now[a] - height * residual[k, a]) * scale
            second.append(base)
            third.append((twice - height * now[a]) * scale - shift * base)
            second_out[k, a] = second[a]
            third_out[k, a] = third[a]
        ends = corner_inputs(corners, corner_now)
        incoming = []
        for f in range(4):
            face = faces[f]
            there = face_stencil(face, face_now[f][0], face_now[f][1], back_in[f])
            over = face_entries(ends[(f, 0)], ends[(f, 1)], outgoing[f])
            here = spread(s_image, face_ids[f])
            outer = []
            for a in range(2):
                twice = there[a] + over[a] + face[WELL_EQ + a] * here
                base = (face_now[f][a] - height * residual_faces[f, 2 * k + a]) * scale
                outer.append((twice - height * face_now[f][a]) * scale - shift * base)
            incoming.append(product(lambda e, f=f: faces[f][e], *outer))
        result, _ = block_stencil(couplings, diagonal, third[0], third[1], incoming)
        fourth = [result[a] - shift * third[a] for a in range(2)]
        values_scratch[k] = wells[0] * third[0] + wells[1] * third[1]
        values_scratch[4 + k] = wells[2] * third[0] + wells[3] * third[1]
        values_scratch[8 + k] = wells[2] * fourth[0] + wells[3] * fourth[1]
        fields = [[residual[k, a] * unit for a in range(2)], second, third, fourth]
        number = 0
        for i in range(4):
            for j in range(i, 4):
                dots[number, RHS + k : RHS + k + 1, :] = tile_sum(fields[i], fields[j])
                number += 1
    rows = segment_rows(ids, values_scratch, scratch, present)
    table = place_rows(rows, jnp.zeros((8, LANES), jnp.float32))
    table = place_columns(dots, 0, table)
    part[...] = jnp.broadcast_to(table[None], part.shape)


def solve_kernel(guess, residual, second, third, parts, known, solution):
    totals = jnp.sum(parts[...], axis=0)
    s_third, p_third, p_fourth = (take_group(totals, group) for group in range(3))
    p_first, p_second = known[0:RHS, :], known[RHS : 2 * RHS, :]
    unit, beta, height, shift, following = (
        known[2 * RHS : 3 * RHS, n : n + 1] for n in range(5)
    )
    equation = known[3 * RHS :, :]
    gram = {}
    number = 0
    for i in range(4):
        for j in range(i, 4):
            gram[(i, j)] = take_column(totals, number)
            number += 1
    gram[(0, 3)] += lane_sum(p_first * s_third) * unit
    gram[(1, 3)] += lane_sum(p_second * s_third)
    gram[(2, 3)] += lane_sum(p_third * s_third)
    gram[(3, 3)] += lane_sum(2.0 * p_fourth * s_third + equation * s_third * s_third)
    tiny = 1e-30
    inverse = [lax.rsqrt(jnp.maximum(gram[(i, i)], tiny)) for i in range(4)]
    length = [jnp.maximum(gram[(i, i)], tiny) * inverse[i] for i in range(4)]
    upper = {}
    for i in range(4):
        for j in range(i, 4):
            entry = gram[(i, j)] * inverse[i] * inverse[j]
            for m in range(i):
                entry = entry - upper[(m, i)] * upper[(m, j)]
            if i == j:
                pivot = lax.rsqrt(jnp.maximum(entry, 1e-6))
                upper[(i, i)] = jnp.maximum(entry, 1e-6) * pivot
                over = pivot
            else:
                upper[(i, j)] = entry * over
    columns = [
        [(0, height * length[0]), (1, following * length[1])],
        [(1, shift * length[1]), (2, length[2])],
        [(2, shift * length[2]), (3, length[3])],
    ]
    zero = jnp.zeros_like(shift)
    hessenberg = [[zero] * 3 for _ in range(4)]
    for j in range(3):
        for i in range(j + 2):
            for m, factor in columns[j]:
                if m >= i:
                    hessenberg[i][j] = hessenberg[i][j] + upper[(i, m)] * factor
    target = [beta * length[0] * upper[(0, 0)], zero, zero, zero]
    turns = []
    for j in range(3):
        top, bottom = hessenberg[j][j], hessenberg[j + 1][j]
        turn = lax.rsqrt(top * top + bottom * bottom)
        turns.append(turn)
        cosine, sine = top * turn, bottom * turn
        for m in range(j, 3):
            high, low = hessenberg[j][m], hessenberg[j + 1][m]
            hessenberg[j][m] = cosine * high + sine * low
            hessenberg[j + 1][m] = cosine * low - sine * high
        high, low = target[j], target[j + 1]
        target[j] = cosine * high + sine * low
        target[j + 1] = cosine * low - sine * high
    weights = [zero] * 3
    for i in (2, 1, 0):
        value = target[i]
        for j in range(i + 1, 3):
            value = value - hessenberg[i][j] * weights[j]
        weights[i] = value * turns[i]
    for k in range(RHS):
        on_first, on_second, on_third = (
            column[k : k + 1, :] for column in (weights[0] * unit, weights[1], weights[2])
        )
        for a in range(2):
            solution[k, a] = (
                guess[k, a]
                + on_first * residual[k, a]
                + on_second * second[k, a]
                + on_third * third[k, a]
            )


def call(kernel, shapes, arguments, scratch=(), own_copies=False, cost=0, grant=24 << 20):
    whole = pl.BlockSpec(memory_space=pltpu.VMEM)
    far = pl.BlockSpec(memory_space=pltpu.HBM)
    scalars = pl.BlockSpec(memory_space=pltpu.SMEM)

    def place(array):
        if len(array.shape) == 1:
            return scalars
        return far if own_copies else whole

    outs = [
        jax.ShapeDtypeStruct(shape, jnp.float32 if len(shape) > 1 else jnp.int32)
        for shape in shapes
    ]
    return pl.pallas_call(
        kernel,
        out_shape=outs,
        in_specs=[place(argument) for argument in arguments],
        out_specs=[scalars if len(shape) == 1 else whole for shape in shapes],
        scratch_shapes=list(scratch),
        compiler_params=pltpu.CompilerParams(vmem_limit_bytes=grant),
        cost_estimate=pl.CostEstimate(flops=cost, bytes_accessed=cost, transcendentals=0)
        if cost
        else None,
    )(*arguments)


def held(*shape):
    return pltpu.VMEM(shape, jnp.float32)


def nothing(value, other, same):
    pass


def after(value, other):
    anywhere = pl.BlockSpec(memory_space=pl.ANY)
    return pl.pallas_call(
        nothing,
        out_shape=jax.ShapeDtypeStruct(value.shape, value.dtype),
        in_specs=[anywhere] * 2,
        out_specs=anywhere,
        input_output_aliases={0: 0},
    )(value, other)


def from_behind(value, axis, steps):
    count = lax.axis_size(axis)
    leading, last = (max(0, -steps), min(count, count - steps))
    return lax.ppermute(value, axis, [(source, source + steps) for source in range(leading, last)])


def exchanged(part):
    return lax.all_to_all(part, ("gx", "gy"), 0, 0, tiled=True)


def body(couplings, diagonal, wells, ids, right, guess):
    devices = lax.axis_size("gx") * lax.axis_size("gy")
    plane = (8, LANES)
    field = guess.shape
    block = guess.shape[2:]
    arguments = (couplings, diagonal, wells, ids, right, guess)

    ends = []
    for argument in arguments:
        shape = argument.shape[:-3] + (2,) + argument.shape[-2:]
        ends += [pltpu.VMEM(shape, argument.dtype)] * 2
    x_low, x_high = call(
        x_pack_kernel,
        [(FACE_PLANES,) + plane] * 2,
        arguments,
        ends + [pltpu.SemaphoreType.DMA((len(ends),))],
        own_copies=True,
        grant=60 << 20,
    )
    fxl = from_behind(x_high, "gx", 1)
    fxh = from_behind(x_low, "gx", -1)
    part, present, y_low, y_high = call(
        guess_kernel,
        [(devices, 8, LANES), (WELLS + 1,)] + [(FACE_PLANES,) + plane] * 2,
        arguments,
        [held(6, *block), held(6, WELLS, LANES)],
        cost=4 << 20,
    )
    parts = exchanged(after(part, fxl))
    y_low, y_high = call(
        corner_kernel,
        [(FACE_PLANES + CORNER_PLANES,) + plane] * 2,
        (y_low, y_high, fxl, fxh),
    )
    fyl = from_behind(y_high, "gy", 1)
    fyh = from_behind(y_low, "gy", -1)

    faces = (fxl, fxh, fyl, fyh)
    residual, image, residual_faces, x_low, x_high, y_low, y_high, small = call(
        residual_kernel,
        [field, field, (4, 8) + plane] + [(16,) + plane] * 4 + [(8, LANES)],
        arguments + faces + (parts,),
    )
    gxl = from_behind(x_high, "gx", 1)
    gxh = from_behind(x_low, "gx", -1)
    (part,) = call(
        moments_kernel,
        [(devices, 8, LANES)],
        (wells, ids, residual, image, present),
        [held(16, *block), held(16, WELLS, LANES), held(3, *plane)],
        cost=4 << 20,
    )
    parts = exchanged(after(part, gxl))
    y_low, y_high = call(
        image_corner_kernel,
        [(18,) + plane] * 2,
        (y_low, y_high, gxl, gxh),
    )
    gyl = from_behind(y_high, "gy", 1)
    gyh = from_behind(y_low, "gy", -1)

    second, third, part, known = call(
        krylov_kernel,
        [field, field, (devices, 8, LANES), (4 * RHS, LANES)],
        (couplings, diagonal, wells, ids) + faces + (gxl, gxh, gyl, gyh)
        + (residual, image, residual_faces, parts, small, present),
        [held(12, WELLS, LANES), held(12, *block), held(10, *plane)],
    )
    parts = exchanged(part)
    (result,) = call(
        solve_kernel,
        [field],
        (guess, residual, second, third, parts, known),
    )
    return result


def solution(mesh):
    in_specs = (
        P("member", None, "gx", "gy", None),
        P("member", "gx", "gy", None),
        P("member", "gx", "gy", None),
        P("gx", "gy", None),
        P("member", None, "gx", "gy", None),
        P("member", None, "gx", "gy", None),
    )
    out_specs = P("member", None, "gx", "gy", None)
    return jax.shard_map(body, mesh=mesh, in_specs=in_specs, out_specs=out_specs, check_vma=False)
```

```python
import jax
import jax.numpy as jnp
from jax import lax
from jax.experimental import pallas as pl
from jax.experimental.pallas import tpu as pltpu
from jax.sharding import PartitionSpec as P

WELLS = 40
RHS = 4
LANES = 128
LAT_UP, LAT_DOWN, RISE, FALL, DIAGONAL = 4, 8, 12, 16, 20
WELL_EQ, WELL_ID, GUESS, REST = 24, 26, 27, 35
BACK_IN, BACK_EQ, BACK_ID = 43, 47, 49
FACE_PLANES = 50
CORNER_PLANES = 5
CORNER_ROWS = 19
SIDE_IN, SIDE_EQ, SIDE_ID, SIDE_GUESS = 4, 8, 10, 11


def product(blocks, first, second):
    return [
        blocks(0) * first + blocks(2) * second,
        blocks(1) * first + blocks(3) * second,
    ]


def iota(shape, axis):
    return lax.broadcasted_iota(jnp.int32, shape, axis)


def roll_up(value, axis):
    return pltpu.roll(value, 1, axis)


def roll_down(value, axis):
    return pltpu.roll(value, value.shape[axis] - 1, axis)


def layer_moves(rising, falling):
    axis = rising.ndim - 1
    lane = iota(rising.shape, axis)
    up = jnp.where(lane == 0, 0.0, roll_up(rising, axis))
    down = jnp.where(lane == LANES - 1, 0.0, roll_down(falling, axis))
    return up + down


def block_stencil(couplings, diagonal, first, second, incoming):
    result = product(lambda e: diagonal[e], first, second)
    moved = [product(lambda e, d=d: couplings[d, e], first, second) for d in range(6)]
    row = iota(first.shape, 1)
    outgoing = [[], [], [], []]
    for b in range(2):
        east, west, north, south, rise, fall = (moved[d][b] for d in range(6))
        total = result[b] + jnp.concatenate([incoming[0][b][None], east[:-1]], axis=0)
        total = total + jnp.concatenate([west[1:], incoming[1][b][None]], axis=0)
        total = total + jnp.where(row == 0, incoming[2][b][:, None, :], roll_up(north, 1))
        total = total + jnp.where(
            row == row.shape[1] - 1, incoming[3][b][:, None, :], roll_down(south, 1)
        )
        result[b] = total + layer_moves(rise, fall)
        outgoing[0].append(west[0])
        outgoing[1].append(east[-1])
        outgoing[2].append(south[:, 0, :])
        outgoing[3].append(north[:, -1, :])
    return result, outgoing


def face_stencil(face, first, second, behind):
    def planes(start):
        return lambda e: face[start + e]

    result = product(planes(DIAGONAL), first, second)
    up = product(planes(LAT_UP), first, second)
    down = product(planes(LAT_DOWN), first, second)
    rise = product(planes(RISE), first, second)
    fall = product(planes(FALL), first, second)
    row = iota(first.shape, 0)
    for b in range(2):
        total = result[b] + behind[b] + layer_moves(rise[b], fall[b])
        total = total + jnp.where(row == 0, 0.0, roll_up(up[b], 0))
        result[b] = total + jnp.where(row == row.shape[0] - 1, 0.0, roll_down(down[b], 0))
    return result


def face_entries(low_end, high_end, entering):
    row = iota(entering[0].shape, 0)
    return [
        entering[b]
        + jnp.where(row == 0, low_end[b], 0.0)
        + jnp.where(row == row.shape[0] - 1, high_end[b], 0.0)
        for b in range(2)
    ]


def spread(totals, ids):
    table = jnp.broadcast_to(totals, (8, LANES))
    if ids.ndim == 2:
        return jnp.take_along_axis(table, ids, axis=1)
    return jnp.stack(
        [jnp.take_along_axis(table, ids[x], axis=1) for x in range(ids.shape[0])], axis=0
    )


def as_ids(plane):
    return plane.astype(jnp.int32)


class Corner:
    def __init__(self, pack, which, base):
        self.pack, self.start = pack, base * 8 + which

    def row(self, number):
        at = self.start + number
        return self.pack[at // 8, at % 8 : at % 8 + 1, :]


def corners_of(faces, base, rows):
    found = []
    for y_face in (2, 3):
        for x_end in range(2):
            found.append(Corner(faces[y_face], x_end * rows, base))
    return found


def corner_inputs(corners, values):
    ends = {}
    for c in range(4):
        x_end, y_end = c % 2, c // 2
        over_x = product(corners[c].row, *values[c])
        over_y = product(lambda e, c=c: corners[c].row(SIDE_IN + e), *values[c])
        ends[(2 + y_end, x_end)] = over_x
        ends[(x_end, y_end)] = over_y
    return ends


def tile_sum(first, second):
    value = first[0] * second[0] + first[1] * second[1]
    return jnp.sum(jnp.sum(value, axis=0), axis=0, keepdims=True)


def list_wells(ids, present):
    depth = ids.shape[0]

    def smallest(planes):
        least = planes[0]
        for plane in planes[1:]:
            least = jnp.minimum(least, plane)
        return jnp.min(least)

    planes = [ids[x].astype(jnp.float32) for x in range(depth)]

    def one_well(state):
        number, well = state
        present[number] = well.astype(jnp.int32)
        after = [jnp.where(plane > well, plane, float(WELLS)) for plane in planes]
        return number + 1, smallest(after)

    number, _ = lax.while_loop(
        lambda state: state[1] < WELLS, one_well, (jnp.int32(1), smallest(planes))
    )
    present[0] = number - 1


def segment_rows(ids, values, scratch, present):
    scratch[...] = jnp.zeros_like(scratch)
    count, depth = values.shape[0], ids.shape[0]

    def one_well(step, _):
        well = present[step + 1]
        masks = [ids[x] == well for x in range(depth)]
        for number in range(count):
            total = jnp.where(masks[0], values[number, 0], 0.0)
            for x in range(1, depth):
                total = total + jnp.where(masks[x], values[number, x], 0.0)
            scratch[number, pl.ds(well, 1), :] = jnp.sum(total, axis=0, keepdims=True)
        return 0

    lax.fori_loop(0, present[0], one_well, 0)
    rows = []
    for number in range(count):
        summed = jnp.sum(scratch[number], axis=1, keepdims=True)
        shape = scratch.shape[1:]
        on_lanes = jnp.where(iota(shape, 0) == iota(shape, 1), summed, 0.0)
        rows.append(jnp.sum(on_lanes, axis=0, keepdims=True))
    return rows


def pack_rows(rows, table):
    for number, row in enumerate(rows):
        placed = row if number % 3 == 0 else pltpu.roll(row, WELLS * (number % 3), 1)
        table = table + jnp.where(
            iota(table.shape, 0) == number // 3, jnp.broadcast_to(placed, table.shape), 0.0
        )
    return table


def unpack_row(table, number):
    row = table[number // 3 : number // 3 + 1, :]
    if number % 3:
        row = pltpu.roll(row, LANES - WELLS * (number % 3), 1)
    return jnp.where(iota(row.shape, 1) < WELLS, row, 0.0)


def place_rows(rows, table):
    for number, row in enumerate(rows):
        group, k = divmod(number, RHS)
        at = k + RHS * (group // 3)
        placed = pltpu.roll(row, WELLS * group, 1) if group in (1, 2) else row
        table = table + jnp.where(
            iota(table.shape, 0) == at, jnp.broadcast_to(placed, table.shape), 0.0
        )
    return table


def place_columns(dots, first_lane, table):
    for number in range(dots.shape[0]):
        column = jnp.sum(dots[number], axis=1, keepdims=True)
        table = table + jnp.where(iota(table.shape, 1) == first_lane + number, column, 0.0)
    return table


def take_group(table, group):
    if group in (1, 2):
        table = pltpu.roll(table, LANES - WELLS * group, 1)
    start = RHS * (group // 3)
    rows = table[start : start + RHS, :]
    return jnp.where(iota(rows.shape, 1) < WELLS, rows, 0.0)


def take_column(table, lane):
    return table[RHS : 2 * RHS, lane : lane + 1]


def lane_sum(row):
    return jnp.sum(row, axis=1, keepdims=True)


def fill_pack(pack, inward, lateral, cut):
    couplings, diagonal, wells, ids, right, guess = range(6)
    for e in range(4):
        pack[e] = cut(couplings, (inward, e), 0)
        pack[LAT_UP + e] = cut(couplings, (lateral, e), 0)
        pack[LAT_DOWN + e] = cut(couplings, (lateral + 1, e), 0)
        pack[RISE + e] = cut(couplings, (4, e), 0)
        pack[FALL + e] = cut(couplings, (5, e), 0)
        pack[DIAGONAL + e] = cut(diagonal, (e,), 0)
        pack[BACK_IN + e] = cut(couplings, (inward, e), 1)
    for a in range(2):
        pack[WELL_EQ + a] = cut(wells, (2 + a,), 0)
        pack[BACK_EQ + a] = cut(wells, (2 + a,), 1)
    pack[WELL_ID] = cut(ids, (), 0).astype(jnp.float32)
    pack[BACK_ID] = cut(ids, (), 1).astype(jnp.float32)
    for k in range(RHS):
        here = [cut(guess, (k, a), 0) for a in range(2)]
        back = [cut(guess, (k, a), 1) for a in range(2)]
        entering = product(lambda e: pack[BACK_IN + e], *back)
        local = face_stencil(pack, here[0], here[1], entering)
        for a in range(2):
            pack[GUESS + 2 * k + a] = here[a]
            pack[REST + 2 * k + a] = cut(right, (k, a), 0) - local[a]


def x_pack_kernel(*refs):
    sources, packs, held_ends, arrived = refs[:6], refs[6:8], refs[8:20], refs[20]
    copies = []
    for n, source in enumerate(sources):
        lead = (slice(None),) * (len(source.shape) - 3)
        depth = source.shape[-3]
        for end, start in enumerate((0, depth - 2)):
            copies.append(
                pltpu.make_async_copy(
                    source.at[lead + (pl.ds(start, 2),)],
                    held_ends[2 * n + end],
                    arrived.at[2 * n + end],
                )
            )
    for copy in copies:
        copy.start()
    for copy in copies:
        copy.wait()
    for end, pack in enumerate(packs):
        fill_pack(
            pack,
            1 - end,
            2,
            lambda n, index, layer: held_ends[2 * n + end][
                index + (1 - layer if end else layer,)
            ],
        )


def y_pack(arguments, packs):
    last = arguments[-1].shape[-2] - 1
    for end, pack in enumerate(packs):
        fill_pack(
            pack,
            3 - end,
            0,
            lambda n, index, layer: arguments[n][
                index + (slice(None), last - layer if end else layer, slice(None))
            ],
        )


def fold(parts, part):
    part[...] = jnp.broadcast_to(jnp.sum(parts[...], axis=0)[None], part.shape)


def corner_kernel(y_low, y_high, fxl, fxh, parts, low_out, high_out, part):
    fold(parts, part)
    last = fxl.shape[1] - 1
    for own, out, at, side in ((y_low, low_out, 0, LAT_DOWN), (y_high, high_out, last, LAT_UP)):
        for n in range(FACE_PLANES):
            out[n] = own[n]
        row = FACE_PLANES * 8
        out[FACE_PLANES + CORNER_PLANES - 1] = jnp.zeros(out.shape[1:], jnp.float32)
        for face in (fxl, fxh):
            for n in (*range(4), *range(side, side + 4), *range(WELL_EQ, REST)):
                out[row // 8, row % 8 : row % 8 + 1, :] = face[n, at : at + 1, :]
                row += 1


def image_corner_kernel(y_low, y_high, gxl, gxh, parts, low_out, high_out, part):
    fold(parts, part)
    last = gxl.shape[1] - 1
    for own, out, at in ((y_low, low_out, 0), (y_high, high_out, last)):
        for n in range(16):
            out[n] = own[n]
        for x_end, face in enumerate((gxl, gxh)):
            for n in range(8):
                out[16 + x_end, n : n + 1, :] = face[n, at : at + 1, :]


def guess_kernel(
    couplings, diagonal, wells, ids, right, guess,
    part, present, y_low, y_high, values, scratch,
):
    y_pack((couplings, diagonal, wells, ids, right, guess), (y_low, y_high))
    list_wells(ids, present)
    for k in range(RHS):
        values[k] = wells[0] * guess[k, 0] + wells[1] * guess[k, 1]
    values[4] = wells[0] * wells[2] + wells[1] * wells[3]
    values[5] = wells[2] * wells[2] + wells[3] * wells[3]
    rows = segment_rows(ids, values, scratch, present)
    table = pack_rows(rows, jnp.zeros((8, LANES), jnp.float32))
    part[...] = jnp.broadcast_to(table[None, :2], part.shape)


def residual_kernel(
    couplings, diagonal, wells, ids, right, guess, fxl, fxh, fyl, fyh, parts,
    residual, image, residual_faces, x_low, x_high, y_low, y_high, small,
):
    faces = (fxl, fxh, fyl, fyh)
    totals = jnp.sum(parts[...], axis=0)
    corners = corners_of(faces, FACE_PLANES, CORNER_ROWS)
    all_ids = ids[...]
    face_ids = [as_ids(face[WELL_ID]) for face in faces]
    last = guess.shape[2] - 1
    for k in range(RHS):
        s_row = unpack_row(totals, k)
        first, second = guess[k, 0], guess[k, 1]
        incoming = [
            product(
                lambda e, f=f: faces[f][e],
                faces[f][GUESS + 2 * k],
                faces[f][GUESS + 2 * k + 1],
            )
            for f in range(4)
        ]
        applied, outgoing = block_stencil(couplings, diagonal, first, second, incoming)
        at_wells = spread(s_row, all_ids)
        now = [
            right[k, a] - applied[a] - wells[2 + a] * at_wells for a in range(2)
        ]
        for a in range(2):
            residual[k, a] = now[a]
        ends = corner_inputs(
            corners,
            [[corners[c].row(SIDE_GUESS + 2 * k + a) for a in range(2)] for c in range(4)],
        )
        incoming = []
        for f in range(4):
            face = faces[f]
            there = face_entries(ends[(f, 0)], ends[(f, 1)], outgoing[f])
            face_wells = spread(s_row, face_ids[f])
            outer = [
                face[REST + 2 * k + a] - there[a] - face[WELL_EQ + a] * face_wells
                for a in range(2)
            ]
            for a in range(2):
                residual_faces[f, 2 * k + a] = outer[a]
            incoming.append(product(lambda e, f=f: faces[f][e], *outer))
        result, _ = block_stencil(couplings, diagonal, now[0], now[1], incoming)
        for a in range(2):
            image[k, a] = result[a]
            x_low[2 * k + a] = result[a][0]
            x_low[8 + 2 * k + a] = result[a][1]
            x_high[2 * k + a] = result[a][last]
            x_high[8 + 2 * k + a] = result[a][last - 1]
            y_low[2 * k + a] = result[a][:, 0, :]
            y_low[8 + 2 * k + a] = result[a][:, 1, :]
            y_high[2 * k + a] = result[a][:, last, :]
            y_high[8 + 2 * k + a] = result[a][:, last - 1, :]
    small[...] = jnp.concatenate(
        [unpack_row(totals, 4), unpack_row(totals, 5), jnp.zeros((6, LANES), jnp.float32)], axis=0
    )


def moments_kernel(
    wells, ids, residual, image, present, part, values, scratch, dots
):
    dots[...] = jnp.zeros_like(dots)
    for k in range(RHS):
        now = [residual[k, a] for a in range(2)]
        result = [image[k, a] for a in range(2)]
        for n, field in enumerate((now, result)):
            values[4 * n + k] = wells[0] * field[0] + wells[1] * field[1]
            values[8 + 4 * n + k] = wells[2] * field[0] + wells[3] * field[1]
        row = slice(RHS + k, RHS + k + 1)
        dots[0, row, :] = tile_sum(now, now)
        dots[1, row, :] = tile_sum(now, result)
        dots[2, row, :] = tile_sum(result, result)
    rows = segment_rows(ids, values, scratch, present)
    table = place_rows(rows, jnp.zeros((8, LANES), jnp.float32))
    table = place_columns(dots, WELLS, table)
    part[...] = jnp.broadcast_to(table[None], part.shape)


def first_step(totals, small):
    s_row, us_row, p_row, ps_row = (take_group(totals, group) for group in range(4))
    within, equation = small[0:1, :], small[1:2, :]
    rr, rs, ss = (take_column(totals, WELLS + i) for i in range(3))
    height = (rs + lane_sum(p_row * s_row)) / rr
    square = ss + lane_sum(2.0 * ps_row * s_row + equation * s_row * s_row)
    left = jnp.maximum(square - height * height * rr, 1e-7 * square)
    scale = lax.rsqrt(left)
    s_image = us_row + within * s_row
    s_second = (s_image - height * s_row) * scale
    p_second = (ps_row + equation * s_row - height * p_row) * scale
    shift = rs / rr + lane_sum(p_second * s_second)
    unit = lax.rsqrt(rr)
    following = left * scale * unit
    return s_row, s_image, p_row, p_second, (unit, rr * unit, height, shift, following, scale)


def krylov_kernel(
    couplings, diagonal, wells, ids, fxl, fxh, fyl, fyh, gxl, gxh, gyl, gyh,
    residual, image, residual_faces, parts, small_in, present,
    second_out, third_out, part, known, scratch, values_scratch, dots,
):
    faces, sent = (fxl, fxh, fyl, fyh), (gxl, gxh, gyl, gyh)
    totals = jnp.sum(parts[...], axis=0)
    small = small_in[...]
    s_rows, s_images, p_rows, p_seconds, scalars = first_step(totals, small)
    known[0:RHS, :] = p_rows
    known[RHS : 2 * RHS, :] = p_seconds
    columns = jnp.zeros((RHS, LANES), jnp.float32)
    for n, column in enumerate(scalars):
        columns = columns + jnp.where(iota(columns.shape, 1) == n, column, 0.0)
    known[2 * RHS : 3 * RHS, :] = columns
    known[3 * RHS :, :] = jnp.broadcast_to(small[1:2, :], (RHS, LANES))
    dots[...] = jnp.zeros_like(dots)
    corners = corners_of(faces, FACE_PLANES, CORNER_ROWS)
    sent_corners = corners_of(sent, 16, 8)
    all_ids = ids[...]
    face_ids = [as_ids(face[WELL_ID]) for face in faces]
    back_ids = [as_ids(face[BACK_ID]) for face in faces]
    corner_ids = [
        as_ids(jnp.broadcast_to(corner.row(SIDE_ID), (8, LANES))) for corner in corners
    ]
    for k in range(RHS):
        unit, _, height, shift, _, scale = (column[k : k + 1, :] for column in scalars)
        s_row, s_image = s_rows[k : k + 1, :], s_images[k : k + 1, :]
        at_wells = spread(s_row, all_ids)
        now = [image[k, a] + wells[2 + a] * at_wells for a in range(2)]
        face_now, back_in = [], []
        for f in range(4):
            face, got = faces[f], sent[f]
            here = spread(s_row, face_ids[f])
            face_now.append([got[2 * k + a] + face[WELL_EQ + a] * here for a in range(2)])
            there = spread(s_row, back_ids[f])
            back = [got[8 + 2 * k + a] + face[BACK_EQ + a] * there for a in range(2)]
            back_in.append(product(lambda e, f=f: faces[f][BACK_IN + e], *back))
        corner_now = []
        for c in range(4):
            here = spread(s_row, corner_ids[c])[0:1, :]
            corner_now.append(
                [
                    sent_corners[c].row(2 * k + a) + corners[c].row(SIDE_EQ + a) * here
                    for a in range(2)
                ]
            )
        incoming = [product(lambda e, f=f: faces[f][e], *face_now[f]) for f in range(4)]
        applied, outgoing = block_stencil(couplings, diagonal, now[0], now[1], incoming)
        at_wells = spread(s_image, all_ids)
        second, third = [], []
        for a in range(2):
            twice = applied[a] + wells[2 + a] * at_wells
            base = (now[a] - height * residual[k, a]) * scale
            second.append(base)
            third.append((twice - height * now[a]) * scale - shift * base)
            second_out[k, a] = second[a]
            third_out[k, a] = third[a]
        ends = corner_inputs(corners, corner_now)
        incoming = []
        for f in range(4):
            face = faces[f]
            there = face_stencil(face, face_now[f][0], face_now[f][1], back_in[f])
            over = face_entries(ends[(f, 0)], ends[(f, 1)], outgoing[f])
            here = spread(s_image, face_ids[f])
            outer = []
            for a in range(2):
                twice = there[a] + over[a] + face[WELL_EQ + a] * here
                base = (face_now[f][a] - height * residual_faces[f, 2 * k + a]) * scale
                outer.append((twice - height * face_now[f][a]) * scale - shift * base)
            incoming.append(product(lambda e, f=f: faces[f][e], *outer))
        result, _ = block_stencil(couplings, diagonal, third[0], third[1], incoming)
        fourth = [result[a] - shift * third[a] for a in range(2)]
        values_scratch[k] = wells[0] * third[0] + wells[1] * third[1]
        values_scratch[4 + k] = wells[2] * third[0] + wells[3] * third[1]
        values_scratch[8 + k] = wells[2] * fourth[0] + wells[3] * fourth[1]
        fields = [[residual[k, a] * unit for a in range(2)], second, third, fourth]
        number = 0
        for i in range(4):
            for j in range(i, 4):
                dots[number, RHS + k : RHS + k + 1, :] = tile_sum(fields[i], fields[j])
                number += 1
    rows = segment_rows(ids, values_scratch, scratch, present)
    table = place_rows(rows, jnp.zeros((8, LANES), jnp.float32))
    table = place_columns(dots, 0, table)
    part[...] = jnp.broadcast_to(table[None], part.shape)


def solve_kernel(guess, residual, second, third, parts, known, solution):
    totals = jnp.sum(parts[...], axis=0)
    s_third, p_third, p_fourth = (take_group(totals, group) for group in range(3))
    p_first, p_second = known[0:RHS, :], known[RHS : 2 * RHS, :]
    unit, beta, height, shift, following = (
        known[2 * RHS : 3 * RHS, n : n + 1] for n in range(5)
    )
    equation = known[3 * RHS :, :]
    gram = {}
    number = 0
    for i in range(4):
        for j in range(i, 4):
            gram[(i, j)] = take_column(totals, number)
            number += 1
    gram[(0, 3)] += lane_sum(p_first * s_third) * unit
    gram[(1, 3)] += lane_sum(p_second * s_third)
    gram[(2, 3)] += lane_sum(p_third * s_third)
    gram[(3, 3)] += lane_sum(2.0 * p_fourth * s_third + equation * s_third * s_third)
    tiny = 1e-30
    inverse = [lax.rsqrt(jnp.maximum(gram[(i, i)], tiny)) for i in range(4)]
    length = [jnp.maximum(gram[(i, i)], tiny) * inverse[i] for i in range(4)]
    upper = {}
    for i in range(4):
        for j in range(i, 4):
            entry = gram[(i, j)] * inverse[i] * inverse[j]
            for m in range(i):
                entry = entry - upper[(m, i)] * upper[(m, j)]
            if i == j:
                pivot = lax.rsqrt(jnp.maximum(entry, 1e-6))
                upper[(i, i)] = jnp.maximum(entry, 1e-6) * pivot
                over = pivot
            else:
                upper[(i, j)] = entry * over
    columns = [
        [(0, height * length[0]), (1, following * length[1])],
        [(1, shift * length[1]), (2, length[2])],
        [(2, shift * length[2]), (3, length[3])],
    ]
    zero = jnp.zeros_like(shift)
    hessenberg = [[zero] * 3 for _ in range(4)]
    for j in range(3):
        for i in range(j + 2):
            for m, factor in columns[j]:
                if m >= i:
                    hessenberg[i][j] = hessenberg[i][j] + upper[(i, m)] * factor
    target = [beta * length[0] * upper[(0, 0)], zero, zero, zero]
    turns = []
    for j in range(3):
        top, bottom = hessenberg[j][j], hessenberg[j + 1][j]
        turn = lax.rsqrt(top * top + bottom * bottom)
        turns.append(turn)
        cosine, sine = top * turn, bottom * turn
        for m in range(j, 3):
            high, low = hessenberg[j][m], hessenberg[j + 1][m]
            hessenberg[j][m] = cosine * high + sine * low
            hessenberg[j + 1][m] = cosine * low - sine * high
        high, low = target[j], target[j + 1]
        target[j] = cosine * high + sine * low
        target[j + 1] = cosine * low - sine * high
    weights = [zero] * 3
    for i in (2, 1, 0):
        value = target[i]
        for j in range(i + 1, 3):
            value = value - hessenberg[i][j] * weights[j]
        weights[i] = value * turns[i]
    for k in range(RHS):
        on_first, on_second, on_third = (
            column[k : k + 1, :] for column in (weights[0] * unit, weights[1], weights[2])
        )
        for a in range(2):
            solution[k, a] = (
                guess[k, a]
                + on_first * residual[k, a]
                + on_second * second[k, a]
                + on_third * third[k, a]
            )


def call(kernel, shapes, arguments, scratch=(), own_copies=False, cost=0, grant=24 << 20):
    whole = pl.BlockSpec(memory_space=pltpu.VMEM)
    far = pl.BlockSpec(memory_space=pltpu.HBM)
    scalars = pl.BlockSpec(memory_space=pltpu.SMEM)

    def place(array):
        if len(array.shape) == 1:
            return scalars
        return far if own_copies else whole

    outs = [
        jax.ShapeDtypeStruct(shape, jnp.float32 if len(shape) > 1 else jnp.int32)
        for shape in shapes
    ]
    return pl.pallas_call(
        kernel,
        out_shape=outs,
        in_specs=[place(argument) for argument in arguments],
        out_specs=[scalars if len(shape) == 1 else whole for shape in shapes],
        scratch_shapes=list(scratch),
        compiler_params=pltpu.CompilerParams(vmem_limit_bytes=grant),
        cost_estimate=pl.CostEstimate(flops=cost, bytes_accessed=cost, transcendentals=0)
        if cost
        else None,
    )(*arguments)


def held(*shape):
    return pltpu.VMEM(shape, jnp.float32)


def from_behind(value, axis, steps):
    count = lax.axis_size(axis)
    leading, last = (max(0, -steps), min(count, count - steps))
    return lax.ppermute(value, axis, [(source, source + steps) for source in range(leading, last)])


def exchanged(part, axis):
    return lax.all_to_all(part, axis, 0, 0, tiled=True)


def body(couplings, diagonal, wells, ids, right, guess):
    across, along = lax.axis_size("gx"), lax.axis_size("gy")
    plane = (8, LANES)
    field = guess.shape
    block = guess.shape[2:]
    arguments = (couplings, diagonal, wells, ids, right, guess)

    ends = []
    for argument in arguments:
        shape = argument.shape[:-3] + (2,) + argument.shape[-2:]
        ends += [pltpu.VMEM(shape, argument.dtype)] * 2
    x_low, x_high = call(
        x_pack_kernel,
        [(FACE_PLANES,) + plane] * 2,
        arguments,
        ends + [pltpu.SemaphoreType.DMA((len(ends),))],
        own_copies=True,
        grant=60 << 20,
    )
    fxl = from_behind(x_high, "gx", 1)
    fxh = from_behind(x_low, "gx", -1)
    part, present, y_low, y_high = call(
        guess_kernel,
        [(across, 2, LANES), (WELLS + 1,)] + [(FACE_PLANES,) + plane] * 2,
        arguments,
        [held(6, *block), held(6, WELLS, LANES)],
        cost=4 << 20,
    )
    parts = exchanged(part, "gx")
    y_low, y_high, part = call(
        corner_kernel,
        [(FACE_PLANES + CORNER_PLANES,) + plane] * 2 + [(along, 2, LANES)],
        (y_low, y_high, fxl, fxh, parts),
    )
    parts = exchanged(part, "gy")
    fyl = from_behind(y_high, "gy", 1)
    fyh = from_behind(y_low, "gy", -1)

    faces = (fxl, fxh, fyl, fyh)
    residual, image, residual_faces, x_low, x_high, y_low, y_high, small = call(
        residual_kernel,
        [field, field, (4, 8) + plane] + [(16,) + plane] * 4 + [(8, LANES)],
        arguments + faces + (parts,),
    )
    gxl = from_behind(x_high, "gx", 1)
    gxh = from_behind(x_low, "gx", -1)
    (part,) = call(
        moments_kernel,
        [(across, 8, LANES)],
        (wells, ids, residual, image, present),
        [held(16, *block), held(16, WELLS, LANES), held(3, *plane)],
        cost=4 << 20,
    )
    parts = exchanged(part, "gx")
    y_low, y_high, part = call(
        image_corner_kernel,
        [(18,) + plane] * 2 + [(along, 8, LANES)],
        (y_low, y_high, gxl, gxh, parts),
    )
    parts = exchanged(part, "gy")
    gyl = from_behind(y_high, "gy", 1)
    gyh = from_behind(y_low, "gy", -1)

    second, third, part, known = call(
        krylov_kernel,
        [field, field, (across, 8, LANES), (4 * RHS, LANES)],
        (couplings, diagonal, wells, ids) + faces + (gxl, gxh, gyl, gyh)
        + (residual, image, residual_faces, parts, small, present),
        [held(12, WELLS, LANES), held(12, *block), held(10, *plane)],
    )
    parts = exchanged(part, "gx")
    (part,) = call(fold, [(along, 8, LANES)], (parts,))
    parts = exchanged(part, "gy")
    (result,) = call(
        solve_kernel,
        [field],
        (guess, residual, second, third, parts, known),
    )
    return result


def solution(mesh):
    in_specs = (
        P("member", None, "gx", "gy", None),
        P("member", "gx", "gy", None),
        P("member", "gx", "gy", None),
        P("gx", "gy", None),
        P("member", None, "gx", "gy", None),
        P("member", None, "gx", "gy", None),
    )
    out_specs = P("member", None, "gx", "gy", None)
    return jax.shard_map(body, mesh=mesh, in_specs=in_specs, out_specs=out_specs, check_vma=False)
```

```python
import jax
import jax.numpy as jnp
from jax import lax
from jax.experimental import pallas as pl
from jax.experimental.pallas import tpu as pltpu
from jax.sharding import PartitionSpec as P

WELLS = 40
RHS = 4
LANES = 128
WELL_EQ, WELL_ID, GUESS, REST, ENDS = 4, 6, 7, 15, 23
FACE_PLANES = 23
CORNER_PLANES = 5
LAT_UP, LAT_DOWN, RISE, FALL, DIAGONAL = 0, 4, 8, 12, 16
BACK_IN, BACK_EQ, BACK_ID = 20, 24, 26
LATE_PLANES = 27
IMAGE_PLANES = 16
SENT_PLANES = IMAGE_PLANES + LATE_PLANES
CORNER_ROWS = 19
SIDE_IN, SIDE_EQ, SIDE_ID, SIDE_GUESS = 4, 8, 10, 11


def product(blocks, first, second):
    return [
        blocks(0) * first + blocks(2) * second,
        blocks(1) * first + blocks(3) * second,
    ]


def iota(shape, axis):
    return lax.broadcasted_iota(jnp.int32, shape, axis)


def roll_up(value, axis):
    return pltpu.roll(value, 1, axis)


def roll_down(value, axis):
    return pltpu.roll(value, value.shape[axis] - 1, axis)


def layer_moves(rising, falling):
    axis = rising.ndim - 1
    lane = iota(rising.shape, axis)
    up = jnp.where(lane == 0, 0.0, roll_up(rising, axis))
    down = jnp.where(lane == LANES - 1, 0.0, roll_down(falling, axis))
    return up + down


def block_stencil(couplings, diagonal, first, second, incoming):
    result = product(lambda e: diagonal[e], first, second)
    moved = [product(lambda e, d=d: couplings[d, e], first, second) for d in range(6)]
    row = iota(first.shape, 1)
    outgoing = [[], [], [], []]
    for b in range(2):
        east, west, north, south, rise, fall = (moved[d][b] for d in range(6))
        total = result[b] + jnp.concatenate([incoming[0][b][None], east[:-1]], axis=0)
        total = total + jnp.concatenate([west[1:], incoming[1][b][None]], axis=0)
        total = total + jnp.where(row == 0, incoming[2][b][:, None, :], roll_up(north, 1))
        total = total + jnp.where(
            row == row.shape[1] - 1, incoming[3][b][:, None, :], roll_down(south, 1)
        )
        result[b] = total + layer_moves(rise, fall)
        outgoing[0].append(west[0])
        outgoing[1].append(east[-1])
        outgoing[2].append(south[:, 0, :])
        outgoing[3].append(north[:, -1, :])
    return result, outgoing


def face_stencil(late, first, second, behind):
    def planes(start):
        return lambda e: late(start + e)

    result = product(planes(DIAGONAL), first, second)
    up = product(planes(LAT_UP), first, second)
    down = product(planes(LAT_DOWN), first, second)
    rise = product(planes(RISE), first, second)
    fall = product(planes(FALL), first, second)
    row = iota(first.shape, 0)
    for b in range(2):
        total = result[b] + behind[b] + layer_moves(rise[b], fall[b])
        total = total + jnp.where(row == 0, 0.0, roll_up(up[b], 0))
        result[b] = total + jnp.where(row == row.shape[0] - 1, 0.0, roll_down(down[b], 0))
    return result


def face_entries(low_end, high_end, entering):
    row = iota(entering[0].shape, 0)
    return [
        entering[b]
        + jnp.where(row == 0, low_end[b], 0.0)
        + jnp.where(row == row.shape[0] - 1, high_end[b], 0.0)
        for b in range(2)
    ]


def spread(totals, ids):
    table = jnp.broadcast_to(totals, (8, LANES))
    if ids.ndim == 2:
        return jnp.take_along_axis(table, ids, axis=1)
    return jnp.stack(
        [jnp.take_along_axis(table, ids[x], axis=1) for x in range(ids.shape[0])], axis=0
    )


def as_ids(plane):
    return plane.astype(jnp.int32)


class Corner:
    def __init__(self, pack, which, base):
        self.pack, self.start = pack, base * 8 + which

    def row(self, number):
        at = self.start + number
        return self.pack[at // 8, at % 8 : at % 8 + 1, :]


def corners_of(faces, base, rows):
    found = []
    for y_face in (2, 3):
        for x_end in range(2):
            found.append(Corner(faces[y_face], x_end * rows, base))
    return found


def corner_inputs(corners, values):
    ends = {}
    for c in range(4):
        x_end, y_end = c % 2, c // 2
        over_x = product(corners[c].row, *values[c])
        over_y = product(lambda e, c=c: corners[c].row(SIDE_IN + e), *values[c])
        ends[(2 + y_end, x_end)] = over_x
        ends[(x_end, y_end)] = over_y
    return ends


def tile_sum(first, second):
    value = first[0] * second[0] + first[1] * second[1]
    return jnp.sum(jnp.sum(value, axis=0), axis=0, keepdims=True)


def list_wells(ids, present):
    depth = ids.shape[0]

    def smallest(planes):
        least = planes[0]
        for plane in planes[1:]:
            least = jnp.minimum(least, plane)
        return jnp.min(least)

    planes = [ids[x].astype(jnp.float32) for x in range(depth)]

    def one_well(state):
        number, well = state
        present[number] = well.astype(jnp.int32)
        after = [jnp.where(plane > well, plane, float(WELLS)) for plane in planes]
        return number + 1, smallest(after)

    number, _ = lax.while_loop(
        lambda state: state[1] < WELLS, one_well, (jnp.int32(1), smallest(planes))
    )
    present[0] = number - 1


def segment_rows(ids, values, scratch, present):
    scratch[...] = jnp.zeros_like(scratch)
    count, depth = values.shape[0], ids.shape[0]

    def one_well(step, _):
        well = present[step + 1]
        masks = [ids[x] == well for x in range(depth)]
        for number in range(count):
            total = jnp.where(masks[0], values[number, 0], 0.0)
            for x in range(1, depth):
                total = total + jnp.where(masks[x], values[number, x], 0.0)
            scratch[number, pl.ds(well, 1), :] = jnp.sum(total, axis=0, keepdims=True)
        return 0

    lax.fori_loop(0, present[0], one_well, 0)
    rows = []
    for number in range(count):
        summed = jnp.sum(scratch[number], axis=1, keepdims=True)
        shape = scratch.shape[1:]
        on_lanes = jnp.where(iota(shape, 0) == iota(shape, 1), summed, 0.0)
        rows.append(jnp.sum(on_lanes, axis=0, keepdims=True))
    return rows


def pack_rows(rows, table):
    for number, row in enumerate(rows):
        placed = row if number % 3 == 0 else pltpu.roll(row, WELLS * (number % 3), 1)
        table = table + jnp.where(
            iota(table.shape, 0) == number // 3, jnp.broadcast_to(placed, table.shape), 0.0
        )
    return table


def unpack_row(table, number):
    row = table[number // 3 : number // 3 + 1, :]
    if number % 3:
        row = pltpu.roll(row, LANES - WELLS * (number % 3), 1)
    return jnp.where(iota(row.shape, 1) < WELLS, row, 0.0)


def place_rows(rows, table):
    for number, row in enumerate(rows):
        group, k = divmod(number, RHS)
        at = k + RHS * (group // 3)
        placed = pltpu.roll(row, WELLS * group, 1) if group in (1, 2) else row
        table = table + jnp.where(
            iota(table.shape, 0) == at, jnp.broadcast_to(placed, table.shape), 0.0
        )
    return table


def place_columns(dots, first_lane, table):
    for number in range(dots.shape[0]):
        column = jnp.sum(dots[number], axis=1, keepdims=True)
        table = table + jnp.where(iota(table.shape, 1) == first_lane + number, column, 0.0)
    return table


def take_group(table, group):
    if group in (1, 2):
        table = pltpu.roll(table, LANES - WELLS * group, 1)
    start = RHS * (group // 3)
    rows = table[start : start + RHS, :]
    return jnp.where(iota(rows.shape, 1) < WELLS, rows, 0.0)


def take_column(table, lane):
    return table[RHS : 2 * RHS, lane : lane + 1]


def lane_sum(row):
    return jnp.sum(row, axis=1, keepdims=True)


COUPLINGS, DIAGONALS, WELL_FIELDS, IDS, RIGHT_SIDE, START = range(6)


def late_plane(cut, inward, lateral):
    def plane(n):
        if n < DIAGONAL:
            return cut(COUPLINGS, ((lateral, lateral + 1, 4, 5)[n // 4], n % 4), 0)
        if n < BACK_IN:
            return cut(DIAGONALS, (n - DIAGONAL,), 0)
        if n < BACK_EQ:
            return cut(COUPLINGS, (inward, n - BACK_IN), 1)
        if n < BACK_ID:
            return cut(WELL_FIELDS, (2 + n - BACK_EQ,), 1)
        return cut(IDS, (), 1).astype(jnp.float32)

    return plane


def fill_pack(pack, inward, lateral, cut):
    late = late_plane(cut, inward, lateral)
    for e in range(4):
        pack[e] = cut(COUPLINGS, (inward, e), 0)
    for a in range(2):
        pack[WELL_EQ + a] = cut(WELL_FIELDS, (2 + a,), 0)
    pack[WELL_ID] = cut(IDS, (), 0).astype(jnp.float32)
    for k in range(RHS):
        here = [cut(START, (k, a), 0) for a in range(2)]
        back = [cut(START, (k, a), 1) for a in range(2)]
        entering = product(lambda e: late(BACK_IN + e), *back)
        local = face_stencil(late, here[0], here[1], entering)
        for a in range(2):
            pack[GUESS + 2 * k + a] = here[a]
            pack[REST + 2 * k + a] = cut(RIGHT_SIDE, (k, a), 0) - local[a]
    if pack.shape[0] > ENDS:
        end = pack.shape[1] - 1
        for e in range(4):
            pack[ENDS, e : e + 1, :] = late(LAT_UP + e)[end : end + 1, :]
            pack[ENDS, 4 + e : 5 + e, :] = late(LAT_DOWN + e)[0:1, :]


def x_pack_kernel(*refs):
    sources, packs, held_ends, arrived = refs[:6], refs[6:8], refs[8:20], refs[20]
    copies = []
    for n, source in enumerate(sources):
        lead = (slice(None),) * (len(source.shape) - 3)
        depth = source.shape[-3]
        for end, start in enumerate((0, depth - 2)):
            copies.append(
                pltpu.make_async_copy(
                    source.at[lead + (pl.ds(start, 2),)],
                    held_ends[2 * n + end],
                    arrived.at[2 * n + end],
                )
            )
    for copy in copies:
        copy.start()
    for copy in copies:
        copy.wait()
    for end, pack in enumerate(packs):
        fill_pack(
            pack,
            1 - end,
            2,
            lambda n, index, layer: held_ends[2 * n + end][
                index + (1 - layer if end else layer,)
            ],
        )


def block_packs(arguments, y_packs, x_late, y_late):
    last = arguments[-1].shape[-2] - 1
    for end in range(2):

        def cut_x(n, index, layer):
            return arguments[n][index + (last - layer if end else layer,)]

        def cut_y(n, index, layer):
            return arguments[n][index + (slice(None), last - layer if end else layer, slice(None))]

        fill_pack(y_packs[end], 3 - end, 0, cut_y)
        x_plane, y_plane = late_plane(cut_x, 1 - end, 2), late_plane(cut_y, 3 - end, 0)
        for n in range(LATE_PLANES):
            x_late[end][n] = x_plane(n)
            y_late[end][n] = y_plane(n)


def spread_kernel(table, *rest):
    part = rest[-1]
    part[...] = jnp.broadcast_to(table[...][None], part.shape)


def corner_kernel(y_low, y_high, fxl, fxh, low_out, high_out):
    last = fxl.shape[1] - 1
    for own, out, at, side in ((y_low, low_out, 0, 4), (y_high, high_out, last, 0)):
        for n in range(FACE_PLANES):
            out[n] = own[n]
        row = FACE_PLANES * 8
        out[FACE_PLANES + CORNER_PLANES - 1] = jnp.zeros(out.shape[1:], jnp.float32)
        for face in (fxl, fxh):
            rows = [(n, at) for n in range(4)]
            rows += [(ENDS, side + e) for e in range(4)]
            rows += [(n, at) for n in range(WELL_EQ, REST)]
            for n, y in rows:
                out[row // 8, row % 8 : row % 8 + 1, :] = face[n, y : y + 1, :]
                row += 1


def image_corner_kernel(
    y_low, y_high, late_low, late_high, gxl, gxh, low_out, high_out
):
    last = gxl.shape[1] - 1
    for own, late, out, at in (
        (y_low, late_low, low_out, 0),
        (y_high, late_high, high_out, last),
    ):
        for n in range(IMAGE_PLANES):
            out[n] = own[n]
        for n in range(LATE_PLANES):
            out[IMAGE_PLANES + n] = late[n]
        for x_end, face in enumerate((gxl, gxh)):
            for n in range(8):
                out[SENT_PLANES + x_end, n : n + 1, :] = face[n, at : at + 1, :]


def guess_kernel(
    couplings, diagonal, wells, ids, right, guess,
    table_out, present, y_low, y_high, x_late_low, x_late_high, y_late_low, y_late_high,
    values, scratch,
):
    block_packs(
        (couplings, diagonal, wells, ids, right, guess),
        (y_low, y_high),
        (x_late_low, x_late_high),
        (y_late_low, y_late_high),
    )
    list_wells(ids, present)
    for k in range(RHS):
        values[k] = wells[0] * guess[k, 0] + wells[1] * guess[k, 1]
    values[4] = wells[0] * wells[2] + wells[1] * wells[3]
    values[5] = wells[2] * wells[2] + wells[3] * wells[3]
    rows = segment_rows(ids, values, scratch, present)
    table_out[...] = pack_rows(rows, jnp.zeros((8, LANES), jnp.float32))


def residual_kernel(
    couplings, diagonal, wells, ids, right, guess, fxl, fxh, fyl, fyh, parts,
    x_late_low, x_late_high,
    residual, image, residual_faces, x_low, x_high, y_low, y_high, small,
):
    faces = (fxl, fxh, fyl, fyh)
    totals = jnp.sum(parts[...], axis=0)
    corners = corners_of(faces, FACE_PLANES, CORNER_ROWS)
    all_ids = ids[...]
    face_ids = [as_ids(face[WELL_ID]) for face in faces]
    last = guess.shape[2] - 1
    for k in range(RHS):
        s_row = unpack_row(totals, k)
        first, second = guess[k, 0], guess[k, 1]
        incoming = [
            product(
                lambda e, f=f: faces[f][e],
                faces[f][GUESS + 2 * k],
                faces[f][GUESS + 2 * k + 1],
            )
            for f in range(4)
        ]
        applied, outgoing = block_stencil(couplings, diagonal, first, second, incoming)
        at_wells = spread(s_row, all_ids)
        now = [
            right[k, a] - applied[a] - wells[2 + a] * at_wells for a in range(2)
        ]
        for a in range(2):
            residual[k, a] = now[a]
        ends = corner_inputs(
            corners,
            [[corners[c].row(SIDE_GUESS + 2 * k + a) for a in range(2)] for c in range(4)],
        )
        incoming = []
        for f in range(4):
            face = faces[f]
            there = face_entries(ends[(f, 0)], ends[(f, 1)], outgoing[f])
            face_wells = spread(s_row, face_ids[f])
            outer = [
                face[REST + 2 * k + a] - there[a] - face[WELL_EQ + a] * face_wells
                for a in range(2)
            ]
            for a in range(2):
                residual_faces[f, 2 * k + a] = outer[a]
            incoming.append(product(lambda e, f=f: faces[f][e], *outer))
        result, _ = block_stencil(couplings, diagonal, now[0], now[1], incoming)
        for a in range(2):
            image[k, a] = result[a]
            x_low[2 * k + a] = result[a][0]
            x_low[8 + 2 * k + a] = result[a][1]
            x_high[2 * k + a] = result[a][last]
            x_high[8 + 2 * k + a] = result[a][last - 1]
            y_low[2 * k + a] = result[a][:, 0, :]
            y_low[8 + 2 * k + a] = result[a][:, 1, :]
            y_high[2 * k + a] = result[a][:, last, :]
            y_high[8 + 2 * k + a] = result[a][:, last - 1, :]
    for late, pack in ((x_late_low, x_low), (x_late_high, x_high)):
        for n in range(LATE_PLANES):
            pack[IMAGE_PLANES + n] = late[n]
    small[...] = jnp.concatenate(
        [unpack_row(totals, 4), unpack_row(totals, 5), jnp.zeros((6, LANES), jnp.float32)], axis=0
    )


def moments_kernel(
    wells, ids, residual, image, present, table_out, values, scratch, dots
):
    dots[...] = jnp.zeros_like(dots)
    for k in range(RHS):
        now = [residual[k, a] for a in range(2)]
        result = [image[k, a] for a in range(2)]
        for n, field in enumerate((now, result)):
            values[4 * n + k] = wells[0] * field[0] + wells[1] * field[1]
            values[8 + 4 * n + k] = wells[2] * field[0] + wells[3] * field[1]
        row = slice(RHS + k, RHS + k + 1)
        dots[0, row, :] = tile_sum(now, now)
        dots[1, row, :] = tile_sum(now, result)
        dots[2, row, :] = tile_sum(result, result)
    rows = segment_rows(ids, values, scratch, present)
    table = place_rows(rows, jnp.zeros((8, LANES), jnp.float32))
    table_out[...] = place_columns(dots, WELLS, table)


def first_step(totals, small):
    s_row, us_row, p_row, ps_row = (take_group(totals, group) for group in range(4))
    within, equation = small[0:1, :], small[1:2, :]
    rr, rs, ss = (take_column(totals, WELLS + i) for i in range(3))
    height = (rs + lane_sum(p_row * s_row)) / rr
    square = ss + lane_sum(2.0 * ps_row * s_row + equation * s_row * s_row)
    left = jnp.maximum(square - height * height * rr, 1e-7 * square)
    scale = lax.rsqrt(left)
    s_image = us_row + within * s_row
    s_second = (s_image - height * s_row) * scale
    p_second = (ps_row + equation * s_row - height * p_row) * scale
    shift = rs / rr + lane_sum(p_second * s_second)
    unit = lax.rsqrt(rr)
    following = left * scale * unit
    return s_row, s_image, p_row, p_second, (unit, rr * unit, height, shift, following, scale)


def krylov_kernel(
    couplings, diagonal, wells, ids, fxl, fxh, fyl, fyh, gxl, gxh, gyl, gyh,
    residual, image, residual_faces, parts, small_in, present,
    second_out, third_out, part, known, scratch, values_scratch, dots,
):
    faces, sent = (fxl, fxh, fyl, fyh), (gxl, gxh, gyl, gyh)
    totals = jnp.sum(parts[...], axis=0)
    small = small_in[...]
    s_rows, s_images, p_rows, p_seconds, scalars = first_step(totals, small)
    known[0:RHS, :] = p_rows
    known[RHS : 2 * RHS, :] = p_seconds
    columns = jnp.zeros((RHS, LANES), jnp.float32)
    for n, column in enumerate(scalars):
        columns = columns + jnp.where(iota(columns.shape, 1) == n, column, 0.0)
    known[2 * RHS : 3 * RHS, :] = columns
    known[3 * RHS :, :] = jnp.broadcast_to(small[1:2, :], (RHS, LANES))
    dots[...] = jnp.zeros_like(dots)
    corners = corners_of(faces, FACE_PLANES, CORNER_ROWS)
    sent_corners = corners_of(sent, SENT_PLANES, 8)
    all_ids = ids[...]
    face_ids = [as_ids(face[WELL_ID]) for face in faces]
    back_ids = [as_ids(got[IMAGE_PLANES + BACK_ID]) for got in sent]
    corner_ids = [
        as_ids(jnp.broadcast_to(corner.row(SIDE_ID), (8, LANES))) for corner in corners
    ]
    for k in range(RHS):
        unit, _, height, shift, _, scale = (column[k : k + 1, :] for column in scalars)
        s_row, s_image = s_rows[k : k + 1, :], s_images[k : k + 1, :]
        at_wells = spread(s_row, all_ids)
        now = [image[k, a] + wells[2 + a] * at_wells for a in range(2)]
        face_now, back_in = [], []
        for f in range(4):
            face, got = faces[f], sent[f]
            here = spread(s_row, face_ids[f])
            face_now.append([got[2 * k + a] + face[WELL_EQ + a] * here for a in range(2)])
            there = spread(s_row, back_ids[f])
            back = [
                got[8 + 2 * k + a] + got[IMAGE_PLANES + BACK_EQ + a] * there for a in range(2)
            ]
            back_in.append(product(lambda e, f=f: sent[f][IMAGE_PLANES + BACK_IN + e], *back))
        corner_now = []
        for c in range(4):
            here = spread(s_row, corner_ids[c])[0:1, :]
            corner_now.append(
                [
                    sent_corners[c].row(2 * k + a) + corners[c].row(SIDE_EQ + a) * here
                    for a in range(2)
                ]
            )
        incoming = [product(lambda e, f=f: faces[f][e], *face_now[f]) for f in range(4)]
        applied, outgoing = block_stencil(couplings, diagonal, now[0], now[1], incoming)
        at_wells = spread(s_image, all_ids)
        second, third = [], []
        for a in range(2):
            twice = applied[a] + wells[2 + a] * at_wells
            base = (now[a] - height * residual[k, a]) * scale
            second.append(base)
            third.append((twice - height * now[a]) * scale - shift * base)
            second_out[k, a] = second[a]
            third_out[k, a] = third[a]
        ends = corner_inputs(corners, corner_now)
        incoming = []
        for f in range(4):
            face = faces[f]
            there = face_stencil(
                lambda n, f=f: sent[f][IMAGE_PLANES + n], *face_now[f], back_in[f]
            )
            over = face_entries(ends[(f, 0)], ends[(f, 1)], outgoing[f])
            here = spread(s_image, face_ids[f])
            outer = []
            for a in range(2):
                twice = there[a] + over[a] + face[WELL_EQ + a] * here
                base = (face_now[f][a] - height * residual_faces[f, 2 * k + a]) * scale
                outer.append((twice - height * face_now[f][a]) * scale - shift * base)
            incoming.append(product(lambda e, f=f: faces[f][e], *outer))
        result, _ = block_stencil(couplings, diagonal, third[0], third[1], incoming)
        fourth = [result[a] - shift * third[a] for a in range(2)]
        values_scratch[k] = wells[0] * third[0] + wells[1] * third[1]
        values_scratch[4 + k] = wells[2] * third[0] + wells[3] * third[1]
        values_scratch[8 + k] = wells[2] * fourth[0] + wells[3] * fourth[1]
        fields = [[residual[k, a] * unit for a in range(2)], second, third, fourth]
        number = 0
        for i in range(4):
            for j in range(i, 4):
                dots[number, RHS + k : RHS + k + 1, :] = tile_sum(fields[i], fields[j])
                number += 1
    rows = segment_rows(ids, values_scratch, scratch, present)
    table = place_rows(rows, jnp.zeros((8, LANES), jnp.float32))
    table = place_columns(dots, 0, table)
    part[...] = jnp.broadcast_to(table[None], part.shape)


def solve_kernel(guess, residual, second, third, parts, known, solution):
    totals = jnp.sum(parts[...], axis=0)
    s_third, p_third, p_fourth = (take_group(totals, group) for group in range(3))
    p_first, p_second = known[0:RHS, :], known[RHS : 2 * RHS, :]
    unit, beta, height, shift, following = (
        known[2 * RHS : 3 * RHS, n : n + 1] for n in range(5)
    )
    equation = known[3 * RHS :, :]
    gram = {}
    number = 0
    for i in range(4):
        for j in range(i, 4):
            gram[(i, j)] = take_column(totals, number)
            number += 1
    gram[(0, 3)] += lane_sum(p_first * s_third) * unit
    gram[(1, 3)] += lane_sum(p_second * s_third)
    gram[(2, 3)] += lane_sum(p_third * s_third)
    gram[(3, 3)] += lane_sum(2.0 * p_fourth * s_third + equation * s_third * s_third)
    tiny = 1e-30
    inverse = [lax.rsqrt(jnp.maximum(gram[(i, i)], tiny)) for i in range(4)]
    length = [jnp.maximum(gram[(i, i)], tiny) * inverse[i] for i in range(4)]
    upper = {}
    for i in range(4):
        for j in range(i, 4):
            entry = gram[(i, j)] * inverse[i] * inverse[j]
            for m in range(i):
                entry = entry - upper[(m, i)] * upper[(m, j)]
            if i == j:
                pivot = lax.rsqrt(jnp.maximum(entry, 1e-6))
                upper[(i, i)] = jnp.maximum(entry, 1e-6) * pivot
                over = pivot
            else:
                upper[(i, j)] = entry * over
    columns = [
        [(0, height * length[0]), (1, following * length[1])],
        [(1, shift * length[1]), (2, length[2])],
        [(2, shift * length[2]), (3, length[3])],
    ]
    zero = jnp.zeros_like(shift)
    hessenberg = [[zero] * 3 for _ in range(4)]
    for j in range(3):
        for i in range(j + 2):
            for m, factor in columns[j]:
                if m >= i:
                    hessenberg[i][j] = hessenberg[i][j] + upper[(i, m)] * factor
    target = [beta * length[0] * upper[(0, 0)], zero, zero, zero]
    turns = []
    for j in range(3):
        top, bottom = hessenberg[j][j], hessenberg[j + 1][j]
        turn = lax.rsqrt(top * top + bottom * bottom)
        turns.append(turn)
        cosine, sine = top * turn, bottom * turn
        for m in range(j, 3):
            high, low = hessenberg[j][m], hessenberg[j + 1][m]
            hessenberg[j][m] = cosine * high + sine * low
            hessenberg[j + 1][m] = cosine * low - sine * high
        high, low = target[j], target[j + 1]
        target[j] = cosine * high + sine * low
        target[j + 1] = cosine * low - sine * high
    weights = [zero] * 3
    for i in (2, 1, 0):
        value = target[i]
        for j in range(i + 1, 3):
            value = value - hessenberg[i][j] * weights[j]
        weights[i] = value * turns[i]
    for k in range(RHS):
        on_first, on_second, on_third = (
            column[k : k + 1, :] for column in (weights[0] * unit, weights[1], weights[2])
        )
        for a in range(2):
            solution[k, a] = (
                guess[k, a]
                + on_first * residual[k, a]
                + on_second * second[k, a]
                + on_third * third[k, a]
            )


def call(kernel, shapes, arguments, scratch=(), own_copies=False, cost=0, grant=24 << 20):
    whole = pl.BlockSpec(memory_space=pltpu.VMEM)
    far = pl.BlockSpec(memory_space=pltpu.HBM)
    scalars = pl.BlockSpec(memory_space=pltpu.SMEM)

    def place(array):
        if len(array.shape) == 1:
            return scalars
        return far if own_copies else whole

    outs = [
        jax.ShapeDtypeStruct(shape, jnp.float32 if len(shape) > 1 else jnp.int32)
        for shape in shapes
    ]
    return pl.pallas_call(
        kernel,
        out_shape=outs,
        in_specs=[place(argument) for argument in arguments],
        out_specs=[scalars if len(shape) == 1 else whole for shape in shapes],
        scratch_shapes=list(scratch),
        compiler_params=pltpu.CompilerParams(vmem_limit_bytes=grant),
        cost_estimate=pl.CostEstimate(flops=cost, bytes_accessed=cost, transcendentals=0)
        if cost
        else None,
    )(*arguments)


def held(*shape):
    return pltpu.VMEM(shape, jnp.float32)


def from_behind(value, axis, steps):
    count = lax.axis_size(axis)
    leading, last = (max(0, -steps), min(count, count - steps))
    return lax.ppermute(value, axis, [(source, source + steps) for source in range(leading, last)])


def exchanged(part):
    return lax.all_to_all(part, ("gx", "gy"), 0, 0, tiled=True)


def body(couplings, diagonal, wells, ids, right, guess):
    devices = lax.axis_size("gx") * lax.axis_size("gy")
    plane = (8, LANES)
    field = guess.shape
    block = guess.shape[2:]
    arguments = (couplings, diagonal, wells, ids, right, guess)

    ends = []
    for argument in arguments:
        shape = argument.shape[:-3] + (2,) + argument.shape[-2:]
        ends += [pltpu.VMEM(shape, argument.dtype)] * 2
    x_low, x_high = call(
        x_pack_kernel,
        [(FACE_PLANES + 1,) + plane] * 2,
        arguments,
        ends + [pltpu.SemaphoreType.DMA((len(ends),))],
        own_copies=True,
        grant=60 << 20,
    )
    fxl = from_behind(x_high, "gx", 1)
    fxh = from_behind(x_low, "gx", -1)
    table, present, y_low, y_high, *late = call(
        guess_kernel,
        [plane, (WELLS + 1,)] + [(FACE_PLANES,) + plane] * 2 + [(LATE_PLANES,) + plane] * 4,
        arguments,
        [held(6, *block), held(6, WELLS, LANES)],
        cost=4 << 20,
    )
    (part,) = call(spread_kernel, [(devices, 8, LANES)], (table, fxl))
    parts = exchanged(part)
    y_low, y_high = call(
        corner_kernel,
        [(FACE_PLANES + CORNER_PLANES,) + plane] * 2,
        (y_low, y_high, fxl, fxh),
    )
    fyl = from_behind(y_high, "gy", 1)
    fyh = from_behind(y_low, "gy", -1)

    faces = (fxl, fxh, fyl, fyh)
    residual, image, residual_faces, x_low, x_high, y_low, y_high, small = call(
        residual_kernel,
        [field, field, (4, 8) + plane]
        + [(SENT_PLANES,) + plane] * 2
        + [(IMAGE_PLANES,) + plane] * 2
        + [(8, LANES)],
        arguments + faces + (parts, late[0], late[1]),
    )
    gxl = from_behind(x_high, "gx", 1)
    gxh = from_behind(x_low, "gx", -1)
    (table,) = call(
        moments_kernel,
        [plane],
        (wells, ids, residual, image, present),
        [held(16, *block), held(16, WELLS, LANES), held(3, *plane)],
        cost=4 << 20,
    )
    (part,) = call(spread_kernel, [(devices, 8, LANES)], (table, gxl, gxh))
    parts = exchanged(part)
    y_low, y_high = call(
        image_corner_kernel,
        [(SENT_PLANES + 2,) + plane] * 2,
        (y_low, y_high, late[2], late[3], gxl, gxh),
    )
    gyl = from_behind(y_high, "gy", 1)
    gyh = from_behind(y_low, "gy", -1)

    second, third, part, known = call(
        krylov_kernel,
        [field, field, (devices, 8, LANES), (4 * RHS, LANES)],
        (couplings, diagonal, wells, ids) + faces + (gxl, gxh, gyl, gyh)
        + (residual, image, residual_faces, parts, small, present),
        [held(12, WELLS, LANES), held(12, *block), held(10, *plane)],
    )
    parts = exchanged(part)
    (result,) = call(
        solve_kernel,
        [field],
        (guess, residual, second, third, parts, known),
    )
    return result


def solution(mesh):
    in_specs = (
        P("member", None, "gx", "gy", None),
        P("member", "gx", "gy", None),
        P("member", "gx", "gy", None),
        P("gx", "gy", None),
        P("member", None, "gx", "gy", None),
        P("member", None, "gx", "gy", None),
    )
    out_specs = P("member", None, "gx", "gy", None)
    return jax.shard_map(body, mesh=mesh, in_specs=in_specs, out_specs=out_specs, check_vma=False)
```

```python
import jax
import jax.numpy as jnp
from jax import lax
from jax.experimental import pallas as pl
from jax.experimental.pallas import tpu as pltpu
from jax.sharding import PartitionSpec as P

WELLS = 40
RHS = 4
LANES = 128
LAT_UP, LAT_DOWN, RISE, FALL, DIAGONAL = 4, 8, 12, 16, 20
WELL_EQ, WELL_ID, GUESS, REST = 24, 26, 27, 35
BACK_IN, BACK_EQ, BACK_ID = 43, 47, 49
FACE_PLANES = 50
CORNER_PLANES = 5
CORNER_ROWS = 19
SIDE_IN, SIDE_EQ, SIDE_ID, SIDE_GUESS = 4, 8, 10, 11


def product(blocks, first, second):
    return [
        blocks(0) * first + blocks(2) * second,
        blocks(1) * first + blocks(3) * second,
    ]


def iota(shape, axis):
    return lax.broadcasted_iota(jnp.int32, shape, axis)


def roll_up(value, axis):
    return pltpu.roll(value, 1, axis)


def roll_down(value, axis):
    return pltpu.roll(value, value.shape[axis] - 1, axis)


def layer_moves(rising, falling):
    axis = rising.ndim - 1
    lane = iota(rising.shape, axis)
    up = jnp.where(lane == 0, 0.0, roll_up(rising, axis))
    down = jnp.where(lane == LANES - 1, 0.0, roll_down(falling, axis))
    return up + down


def block_stencil(couplings, diagonal, first, second, incoming):
    result = product(lambda e: diagonal[e], first, second)
    moved = [product(lambda e, d=d: couplings[d, e], first, second) for d in range(6)]
    row = iota(first.shape, 1)
    outgoing = [[], [], [], []]
    for b in range(2):
        east, west, north, south, rise, fall = (moved[d][b] for d in range(6))
        total = result[b] + jnp.concatenate([incoming[0][b][None], east[:-1]], axis=0)
        total = total + jnp.concatenate([west[1:], incoming[1][b][None]], axis=0)
        total = total + jnp.where(row == 0, incoming[2][b][:, None, :], roll_up(north, 1))
        total = total + jnp.where(
            row == row.shape[1] - 1, incoming[3][b][:, None, :], roll_down(south, 1)
        )
        result[b] = total + layer_moves(rise, fall)
        outgoing[0].append(west[0])
        outgoing[1].append(east[-1])
        outgoing[2].append(south[:, 0, :])
        outgoing[3].append(north[:, -1, :])
    return result, outgoing


def face_stencil(face, first, second, behind):
    def planes(start):
        return lambda e: face[start + e]

    result = product(planes(DIAGONAL), first, second)
    up = product(planes(LAT_UP), first, second)
    down = product(planes(LAT_DOWN), first, second)
    rise = product(planes(RISE), first, second)
    fall = product(planes(FALL), first, second)
    row = iota(first.shape, 0)
    for b in range(2):
        total = result[b] + behind[b] + layer_moves(rise[b], fall[b])
        total = total + jnp.where(row == 0, 0.0, roll_up(up[b], 0))
        result[b] = total + jnp.where(row == row.shape[0] - 1, 0.0, roll_down(down[b], 0))
    return result


def face_entries(low_end, high_end, entering):
    row = iota(entering[0].shape, 0)
    return [
        entering[b]
        + jnp.where(row == 0, low_end[b], 0.0)
        + jnp.where(row == row.shape[0] - 1, high_end[b], 0.0)
        for b in range(2)
    ]


def spread(totals, ids):
    table = jnp.broadcast_to(totals, (8, LANES))
    if ids.ndim == 2:
        return jnp.take_along_axis(table, ids, axis=1)
    return jnp.stack(
        [jnp.take_along_axis(table, ids[x], axis=1) for x in range(ids.shape[0])], axis=0
    )


def as_ids(plane):
    return plane.astype(jnp.int32)


class Corner:
    def __init__(self, pack, which, base):
        self.pack, self.start = pack, base * 8 + which

    def row(self, number):
        at = self.start + number
        return self.pack[at // 8, at % 8 : at % 8 + 1, :]


def corners_of(faces, base, rows):
    found = []
    for y_face in (2, 3):
        for x_end in range(2):
            found.append(Corner(faces[y_face], x_end * rows, base))
    return found


def corner_inputs(corners, values):
    ends = {}
    for c in range(4):
        x_end, y_end = c % 2, c // 2
        over_x = product(corners[c].row, *values[c])
        over_y = product(lambda e, c=c: corners[c].row(SIDE_IN + e), *values[c])
        ends[(2 + y_end, x_end)] = over_x
        ends[(x_end, y_end)] = over_y
    return ends


def tile_sum(first, second):
    value = first[0] * second[0] + first[1] * second[1]
    return jnp.sum(jnp.sum(value, axis=0), axis=0, keepdims=True)


def list_wells(ids, present):
    depth = ids.shape[0]

    def smallest(planes):
        least = planes[0]
        for plane in planes[1:]:
            least = jnp.minimum(least, plane)
        return jnp.min(least)

    planes = [ids[x].astype(jnp.float32) for x in range(depth)]

    def one_well(state):
        number, well = state
        present[number] = well.astype(jnp.int32)
        after = [jnp.where(plane > well, plane, float(WELLS)) for plane in planes]
        return number + 1, smallest(after)

    number, _ = lax.while_loop(
        lambda state: state[1] < WELLS, one_well, (jnp.int32(1), smallest(planes))
    )
    present[0] = number - 1


def segment_rows(ids, values, scratch, present):
    scratch[...] = jnp.zeros_like(scratch)
    count, depth = values.shape[0], ids.shape[0]

    def one_well(step, _):
        well = present[step + 1]
        masks = [ids[x] == well for x in range(depth)]
        for number in range(count):
            total = jnp.where(masks[0], values[number, 0], 0.0)
            for x in range(1, depth):
                total = total + jnp.where(masks[x], values[number, x], 0.0)
            scratch[number, pl.ds(well, 1), :] = jnp.sum(total, axis=0, keepdims=True)
        return 0

    lax.fori_loop(0, present[0], one_well, 0)
    rows = []
    for number in range(count):
        summed = jnp.sum(scratch[number], axis=1, keepdims=True)
        shape = scratch.shape[1:]
        on_lanes = jnp.where(iota(shape, 0) == iota(shape, 1), summed, 0.0)
        rows.append(jnp.sum(on_lanes, axis=0, keepdims=True))
    return rows


def pack_rows(rows, table):
    for number, row in enumerate(rows):
        placed = row if number % 3 == 0 else pltpu.roll(row, WELLS * (number % 3), 1)
        table = table + jnp.where(
            iota(table.shape, 0) == number // 3, jnp.broadcast_to(placed, table.shape), 0.0
        )
    return table


def unpack_row(table, number):
    row = table[number // 3 : number // 3 + 1, :]
    if number % 3:
        row = pltpu.roll(row, LANES - WELLS * (number % 3), 1)
    return jnp.where(iota(row.shape, 1) < WELLS, row, 0.0)


def place_rows(rows, table):
    for number, row in enumerate(rows):
        group, k = divmod(number, RHS)
        at = k + RHS * (group // 3)
        placed = pltpu.roll(row, WELLS * group, 1) if group in (1, 2) else row
        table = table + jnp.where(
            iota(table.shape, 0) == at, jnp.broadcast_to(placed, table.shape), 0.0
        )
    return table


def place_columns(dots, first_lane, table):
    for number in range(dots.shape[0]):
        column = jnp.sum(dots[number], axis=1, keepdims=True)
        table = table + jnp.where(iota(table.shape, 1) == first_lane + number, column, 0.0)
    return table


def take_group(table, group):
    if group in (1, 2):
        table = pltpu.roll(table, LANES - WELLS * group, 1)
    start = RHS * (group // 3)
    rows = table[start : start + RHS, :]
    return jnp.where(iota(rows.shape, 1) < WELLS, rows, 0.0)


def take_column(table, lane):
    return table[RHS : 2 * RHS, lane : lane + 1]


def lane_sum(row):
    return jnp.sum(row, axis=1, keepdims=True)


def fill_pack(pack, inward, lateral, cut):
    couplings, diagonal, wells, ids, right, guess = range(6)
    for e in range(4):
        pack[e] = cut(couplings, (inward, e), 0)
        pack[LAT_UP + e] = cut(couplings, (lateral, e), 0)
        pack[LAT_DOWN + e] = cut(couplings, (lateral + 1, e), 0)
        pack[RISE + e] = cut(couplings, (4, e), 0)
        pack[FALL + e] = cut(couplings, (5, e), 0)
        pack[DIAGONAL + e] = cut(diagonal, (e,), 0)
        pack[BACK_IN + e] = cut(couplings, (inward, e), 1)
    for a in range(2):
        pack[WELL_EQ + a] = cut(wells, (2 + a,), 0)
        pack[BACK_EQ + a] = cut(wells, (2 + a,), 1)
    pack[WELL_ID] = cut(ids, (), 0).astype(jnp.float32)
    pack[BACK_ID] = cut(ids, (), 1).astype(jnp.float32)
    for k in range(RHS):
        here = [cut(guess, (k, a), 0) for a in range(2)]
        back = [cut(guess, (k, a), 1) for a in range(2)]
        entering = product(lambda e: pack[BACK_IN + e], *back)
        local = face_stencil(pack, here[0], here[1], entering)
        for a in range(2):
            pack[GUESS + 2 * k + a] = here[a]
            pack[REST + 2 * k + a] = cut(right, (k, a), 0) - local[a]


def x_pack_kernel(*refs):
    sources, packs, held_ends, arrived = refs[:6], refs[6:8], refs[8:20], refs[20]
    copies = []
    for n, source in enumerate(sources):
        lead = (slice(None),) * (len(source.shape) - 3)
        depth = source.shape[-3]
        for end, start in enumerate((0, depth - 2)):
            copies.append(
                pltpu.make_async_copy(
                    source.at[lead + (pl.ds(start, 2),)],
                    held_ends[2 * n + end],
                    arrived.at[2 * n + end],
                )
            )
    for copy in copies:
        copy.start()
    for copy in copies:
        copy.wait()
    for end, pack in enumerate(packs):
        fill_pack(
            pack,
            1 - end,
            2,
            lambda n, index, layer: held_ends[2 * n + end][
                index + (1 - layer if end else layer,)
            ],
        )


def y_pack(arguments, packs):
    last = arguments[-1].shape[-2] - 1
    for end, pack in enumerate(packs):
        fill_pack(
            pack,
            3 - end,
            0,
            lambda n, index, layer: arguments[n][
                index + (slice(None), last - layer if end else layer, slice(None))
            ],
        )


def corner_kernel(y_low, y_high, fxl, fxh, table, low_out, high_out, part):
    part[...] = jnp.broadcast_to(table[...][None, :2], part.shape)
    last = fxl.shape[1] - 1
    for own, out, at, side in ((y_low, low_out, 0, LAT_DOWN), (y_high, high_out, last, LAT_UP)):
        for n in range(FACE_PLANES):
            out[n] = own[n]
        row = FACE_PLANES * 8
        out[FACE_PLANES + CORNER_PLANES - 1] = jnp.zeros(out.shape[1:], jnp.float32)
        for face in (fxl, fxh):
            for n in (*range(4), *range(side, side + 4), *range(WELL_EQ, REST)):
                out[row // 8, row % 8 : row % 8 + 1, :] = face[n, at : at + 1, :]
                row += 1


def image_corner_kernel(y_low, y_high, gxl, gxh, table, low_out, high_out, part):
    part[...] = jnp.broadcast_to(table[...][None], part.shape)
    last = gxl.shape[1] - 1
    for own, out, at in ((y_low, low_out, 0), (y_high, high_out, last)):
        for n in range(16):
            out[n] = own[n]
        for x_end, face in enumerate((gxl, gxh)):
            for n in range(8):
                out[16 + x_end, n : n + 1, :] = face[n, at : at + 1, :]


def guess_kernel(
    couplings, diagonal, wells, ids, right, guess,
    table_out, present, y_low, y_high, values, scratch,
):
    y_pack((couplings, diagonal, wells, ids, right, guess), (y_low, y_high))
    list_wells(ids, present)
    for k in range(RHS):
        values[k] = wells[0] * guess[k, 0] + wells[1] * guess[k, 1]
    values[4] = wells[0] * wells[2] + wells[1] * wells[3]
    values[5] = wells[2] * wells[2] + wells[3] * wells[3]
    rows = segment_rows(ids, values, scratch, present)
    table_out[...] = pack_rows(rows, jnp.zeros((8, LANES), jnp.float32))


def residual_kernel(
    couplings, diagonal, wells, ids, right, guess, fxl, fxh, fyl, fyh, parts,
    residual, image, residual_faces, x_low, x_high, y_low, y_high, small,
):
    faces = (fxl, fxh, fyl, fyh)
    totals = jnp.sum(parts[...], axis=0)
    corners = corners_of(faces, FACE_PLANES, CORNER_ROWS)
    all_ids = ids[...]
    face_ids = [as_ids(face[WELL_ID]) for face in faces]
    last = guess.shape[2] - 1
    for k in range(RHS):
        s_row = unpack_row(totals, k)
        first, second = guess[k, 0], guess[k, 1]
        incoming = [
            product(
                lambda e, f=f: faces[f][e],
                faces[f][GUESS + 2 * k],
                faces[f][GUESS + 2 * k + 1],
            )
            for f in range(4)
        ]
        applied, outgoing = block_stencil(couplings, diagonal, first, second, incoming)
        at_wells = spread(s_row, all_ids)
        now = [
            right[k, a] - applied[a] - wells[2 + a] * at_wells for a in range(2)
        ]
        for a in range(2):
            residual[k, a] = now[a]
        ends = corner_inputs(
            corners,
            [[corners[c].row(SIDE_GUESS + 2 * k + a) for a in range(2)] for c in range(4)],
        )
        incoming = []
        for f in range(4):
            face = faces[f]
            there = face_entries(ends[(f, 0)], ends[(f, 1)], outgoing[f])
            face_wells = spread(s_row, face_ids[f])
            outer = [
                face[REST + 2 * k + a] - there[a] - face[WELL_EQ + a] * face_wells
                for a in range(2)
            ]
            for a in range(2):
                residual_faces[f, 2 * k + a] = outer[a]
            incoming.append(product(lambda e, f=f: faces[f][e], *outer))
        result, _ = block_stencil(couplings, diagonal, now[0], now[1], incoming)
        for a in range(2):
            image[k, a] = result[a]
            x_low[2 * k + a] = result[a][0]
            x_low[8 + 2 * k + a] = result[a][1]
            x_high[2 * k + a] = result[a][last]
            x_high[8 + 2 * k + a] = result[a][last - 1]
            y_low[2 * k + a] = result[a][:, 0, :]
            y_low[8 + 2 * k + a] = result[a][:, 1, :]
            y_high[2 * k + a] = result[a][:, last, :]
            y_high[8 + 2 * k + a] = result[a][:, last - 1, :]
    small[...] = jnp.concatenate(
        [unpack_row(totals, 4), unpack_row(totals, 5), jnp.zeros((6, LANES), jnp.float32)], axis=0
    )


def moments_kernel(
    wells, ids, residual, image, present, table_out, values, scratch, dots
):
    dots[...] = jnp.zeros_like(dots)
    for k in range(RHS):
        now = [residual[k, a] for a in range(2)]
        result = [image[k, a] for a in range(2)]
        for n, field in enumerate((now, result)):
            values[4 * n + k] = wells[0] * field[0] + wells[1] * field[1]
            values[8 + 4 * n + k] = wells[2] * field[0] + wells[3] * field[1]
        row = slice(RHS + k, RHS + k + 1)
        dots[0, row, :] = tile_sum(now, now)
        dots[1, row, :] = tile_sum(now, result)
        dots[2, row, :] = tile_sum(result, result)
    rows = segment_rows(ids, values, scratch, present)
    table = place_rows(rows, jnp.zeros((8, LANES), jnp.float32))
    table_out[...] = place_columns(dots, WELLS, table)


def first_step(totals, small):
    s_row, us_row, p_row, ps_row = (take_group(totals, group) for group in range(4))
    within, equation = small[0:1, :], small[1:2, :]
    rr, rs, ss = (take_column(totals, WELLS + i) for i in range(3))
    height = (rs + lane_sum(p_row * s_row)) / rr
    square = ss + lane_sum(2.0 * ps_row * s_row + equation * s_row * s_row)
    left = jnp.maximum(square - height * height * rr, 1e-7 * square)
    scale = lax.rsqrt(left)
    s_image = us_row + within * s_row
    s_second = (s_image - height * s_row) * scale
    p_second = (ps_row + equation * s_row - height * p_row) * scale
    shift = rs / rr + lane_sum(p_second * s_second)
    unit = lax.rsqrt(rr)
    following = left * scale * unit
    return s_row, s_image, p_row, p_second, (unit, rr * unit, height, shift, following, scale)


def krylov_kernel(
    couplings, diagonal, wells, ids, fxl, fxh, fyl, fyh, gxl, gxh, gyl, gyh,
    residual, image, residual_faces, parts, small_in, present,
    second_out, third_out, part, known, scratch, values_scratch, dots,
):
    faces, sent = (fxl, fxh, fyl, fyh), (gxl, gxh, gyl, gyh)
    totals = jnp.sum(parts[...], axis=0)
    small = small_in[...]
    s_rows, s_images, p_rows, p_seconds, scalars = first_step(totals, small)
    known[0:RHS, :] = p_rows
    known[RHS : 2 * RHS, :] = p_seconds
    columns = jnp.zeros((RHS, LANES), jnp.float32)
    for n, column in enumerate(scalars):
        columns = columns + jnp.where(iota(columns.shape, 1) == n, column, 0.0)
    known[2 * RHS : 3 * RHS, :] = columns
    known[3 * RHS :, :] = jnp.broadcast_to(small[1:2, :], (RHS, LANES))
    dots[...] = jnp.zeros_like(dots)
    corners = corners_of(faces, FACE_PLANES, CORNER_ROWS)
    sent_corners = corners_of(sent, 16, 8)
    all_ids = ids[...]
    face_ids = [as_ids(face[WELL_ID]) for face in faces]
    back_ids = [as_ids(face[BACK_ID]) for face in faces]
    corner_ids = [
        as_ids(jnp.broadcast_to(corner.row(SIDE_ID), (8, LANES))) for corner in corners
    ]
    for k in range(RHS):
        unit, _, height, shift, _, scale = (column[k : k + 1, :] for column in scalars)
        s_row, s_image = s_rows[k : k + 1, :], s_images[k : k + 1, :]
        at_wells = spread(s_row, all_ids)
        now = [image[k, a] + wells[2 + a] * at_wells for a in range(2)]
        face_now, back_in = [], []
        for f in range(4):
            face, got = faces[f], sent[f]
            here = spread(s_row, face_ids[f])
            face_now.append([got[2 * k + a] + face[WELL_EQ + a] * here for a in range(2)])
            there = spread(s_row, back_ids[f])
            back = [got[8 + 2 * k + a] + face[BACK_EQ + a] * there for a in range(2)]
            back_in.append(product(lambda e, f=f: faces[f][BACK_IN + e], *back))
        corner_now = []
        for c in range(4):
            here = spread(s_row, corner_ids[c])[0:1, :]
            corner_now.append(
                [
                    sent_corners[c].row(2 * k + a) + corners[c].row(SIDE_EQ + a) * here
                    for a in range(2)
                ]
            )
        incoming = [product(lambda e, f=f: faces[f][e], *face_now[f]) for f in range(4)]
        applied, outgoing = block_stencil(couplings, diagonal, now[0], now[1], incoming)
        at_wells = spread(s_image, all_ids)
        second, third = [], []
        for a in range(2):
            twice = applied[a] + wells[2 + a] * at_wells
            base = (now[a] - height * residual[k, a]) * scale
            second.append(base)
            third.append((twice - height * now[a]) * scale - shift * base)
            second_out[k, a] = second[a]
            third_out[k, a] = third[a]
        ends = corner_inputs(corners, corner_now)
        incoming = []
        for f in range(4):
            face = faces[f]
            there = face_stencil(face, face_now[f][0], face_now[f][1], back_in[f])
            over = face_entries(ends[(f, 0)], ends[(f, 1)], outgoing[f])
            here = spread(s_image, face_ids[f])
            outer = []
            for a in range(2):
                twice = there[a] + over[a] + face[WELL_EQ + a] * here
                base = (face_now[f][a] - height * residual_faces[f, 2 * k + a]) * scale
                outer.append((twice - height * face_now[f][a]) * scale - shift * base)
            incoming.append(product(lambda e, f=f: faces[f][e], *outer))
        result, _ = block_stencil(couplings, diagonal, third[0], third[1], incoming)
        fourth = [result[a] - shift * third[a] for a in range(2)]
        values_scratch[k] = wells[0] * third[0] + wells[1] * third[1]
        values_scratch[4 + k] = wells[2] * third[0] + wells[3] * third[1]
        values_scratch[8 + k] = wells[2] * fourth[0] + wells[3] * fourth[1]
        fields = [[residual[k, a] * unit for a in range(2)], second, third, fourth]
        number = 0
        for i in range(4):
            for j in range(i, 4):
                dots[number, RHS + k : RHS + k + 1, :] = tile_sum(fields[i], fields[j])
                number += 1
    rows = segment_rows(ids, values_scratch, scratch, present)
    table = place_rows(rows, jnp.zeros((8, LANES), jnp.float32))
    table = place_columns(dots, 0, table)
    part[...] = jnp.broadcast_to(table[None], part.shape)


def solve_kernel(guess, residual, second, third, parts, known, solution):
    totals = jnp.sum(parts[...], axis=0)
    s_third, p_third, p_fourth = (take_group(totals, group) for group in range(3))
    p_first, p_second = known[0:RHS, :], known[RHS : 2 * RHS, :]
    unit, beta, height, shift, following = (
        known[2 * RHS : 3 * RHS, n : n + 1] for n in range(5)
    )
    equation = known[3 * RHS :, :]
    gram = {}
    number = 0
    for i in range(4):
        for j in range(i, 4):
            gram[(i, j)] = take_column(totals, number)
            number += 1
    gram[(0, 3)] += lane_sum(p_first * s_third) * unit
    gram[(1, 3)] += lane_sum(p_second * s_third)
    gram[(2, 3)] += lane_sum(p_third * s_third)
    gram[(3, 3)] += lane_sum(2.0 * p_fourth * s_third + equation * s_third * s_third)
    tiny = 1e-30
    inverse = [lax.rsqrt(jnp.maximum(gram[(i, i)], tiny)) for i in range(4)]
    length = [jnp.maximum(gram[(i, i)], tiny) * inverse[i] for i in range(4)]
    upper = {}
    for i in range(4):
        for j in range(i, 4):
            entry = gram[(i, j)] * inverse[i] * inverse[j]
            for m in range(i):
                entry = entry - upper[(m, i)] * upper[(m, j)]
            if i == j:
                pivot = lax.rsqrt(jnp.maximum(entry, 1e-6))
                upper[(i, i)] = jnp.maximum(entry, 1e-6) * pivot
                over = pivot
            else:
                upper[(i, j)] = entry * over
    columns = [
        [(0, height * length[0]), (1, following * length[1])],
        [(1, shift * length[1]), (2, length[2])],
        [(2, shift * length[2]), (3, length[3])],
    ]
    zero = jnp.zeros_like(shift)
    hessenberg = [[zero] * 3 for _ in range(4)]
    for j in range(3):
        for i in range(j + 2):
            for m, factor in columns[j]:
                if m >= i:
                    hessenberg[i][j] = hessenberg[i][j] + upper[(i, m)] * factor
    target = [beta * length[0] * upper[(0, 0)], zero, zero, zero]
    turns = []
    for j in range(3):
        top, bottom = hessenberg[j][j], hessenberg[j + 1][j]
        turn = lax.rsqrt(top * top + bottom * bottom)
        turns.append(turn)
        cosine, sine = top * turn, bottom * turn
        for m in range(j, 3):
            high, low = hessenberg[j][m], hessenberg[j + 1][m]
            hessenberg[j][m] = cosine * high + sine * low
            hessenberg[j + 1][m] = cosine * low - sine * high
        high, low = target[j], target[j + 1]
        target[j] = cosine * high + sine * low
        target[j + 1] = cosine * low - sine * high
    weights = [zero] * 3
    for i in (2, 1, 0):
        value = target[i]
        for j in range(i + 1, 3):
            value = value - hessenberg[i][j] * weights[j]
        weights[i] = value * turns[i]
    for k in range(RHS):
        on_first, on_second, on_third = (
            column[k : k + 1, :] for column in (weights[0] * unit, weights[1], weights[2])
        )
        for a in range(2):
            solution[k, a] = (
                guess[k, a]
                + on_first * residual[k, a]
                + on_second * second[k, a]
                + on_third * third[k, a]
            )


def call(kernel, shapes, arguments, scratch=(), own_copies=False, cost=0, grant=24 << 20):
    whole = pl.BlockSpec(memory_space=pltpu.VMEM)
    far = pl.BlockSpec(memory_space=pltpu.HBM)
    scalars = pl.BlockSpec(memory_space=pltpu.SMEM)

    def place(array):
        if len(array.shape) == 1:
            return scalars
        return far if own_copies else whole

    outs = [
        jax.ShapeDtypeStruct(shape, jnp.float32 if len(shape) > 1 else jnp.int32)
        for shape in shapes
    ]
    return pl.pallas_call(
        kernel,
        out_shape=outs,
        in_specs=[place(argument) for argument in arguments],
        out_specs=[scalars if len(shape) == 1 else whole for shape in shapes],
        scratch_shapes=list(scratch),
        compiler_params=pltpu.CompilerParams(vmem_limit_bytes=grant),
        cost_estimate=pl.CostEstimate(flops=cost, bytes_accessed=cost, transcendentals=0)
        if cost
        else None,
    )(*arguments)


def held(*shape):
    return pltpu.VMEM(shape, jnp.float32)


def from_behind(value, axis, steps):
    count = lax.axis_size(axis)
    leading, last = (max(0, -steps), min(count, count - steps))
    return lax.ppermute(value, axis, [(source, source + steps) for source in range(leading, last)])


def exchanged(part):
    return lax.all_to_all(part, ("gx", "gy"), 0, 0, tiled=True)


def body(couplings, diagonal, wells, ids, right, guess):
    devices = lax.axis_size("gx") * lax.axis_size("gy")
    plane = (8, LANES)
    field = guess.shape
    block = guess.shape[2:]
    arguments = (couplings, diagonal, wells, ids, right, guess)

    ends = []
    for argument in arguments:
        shape = argument.shape[:-3] + (2,) + argument.shape[-2:]
        ends += [pltpu.VMEM(shape, argument.dtype)] * 2
    x_low, x_high = call(
        x_pack_kernel,
        [(FACE_PLANES,) + plane] * 2,
        [pltpu.with_memory_space_constraint(argument, pltpu.HBM) for argument in arguments],
        ends + [pltpu.SemaphoreType.DMA((len(ends),))],
        own_copies=True,
    )
    fxl = from_behind(x_high, "gx", 1)
    fxh = from_behind(x_low, "gx", -1)
    table, present, y_low, y_high = call(
        guess_kernel,
        [plane, (WELLS + 1,)] + [(FACE_PLANES,) + plane] * 2,
        arguments,
        [held(6, *block), held(6, WELLS, LANES)],
        cost=4 << 20,
    )
    y_low, y_high, part = call(
        corner_kernel,
        [(FACE_PLANES + CORNER_PLANES,) + plane] * 2 + [(devices, 2, LANES)],
        (y_low, y_high, fxl, fxh, table),
    )
    parts = exchanged(part)
    fyl = from_behind(y_high, "gy", 1)
    fyh = from_behind(y_low, "gy", -1)

    faces = (fxl, fxh, fyl, fyh)
    residual, image, residual_faces, x_low, x_high, y_low, y_high, small = call(
        residual_kernel,
        [field, field, (4, 8) + plane] + [(16,) + plane] * 4 + [(8, LANES)],
        arguments + faces + (parts,),
    )
    gxl = from_behind(x_high, "gx", 1)
    gxh = from_behind(x_low, "gx", -1)
    (table,) = call(
        moments_kernel,
        [plane],
        (wells, ids, residual, image, present),
        [held(16, *block), held(16, WELLS, LANES), held(3, *plane)],
        cost=4 << 20,
    )
    y_low, y_high, part = call(
        image_corner_kernel,
        [(18,) + plane] * 2 + [(devices, 8, LANES)],
        (y_low, y_high, gxl, gxh, table),
    )
    parts = exchanged(part)
    gyl = from_behind(y_high, "gy", 1)
    gyh = from_behind(y_low, "gy", -1)

    second, third, part, known = call(
        krylov_kernel,
        [field, field, (devices, 8, LANES), (4 * RHS, LANES)],
        (couplings, diagonal, wells, ids) + faces + (gxl, gxh, gyl, gyh)
        + (residual, image, residual_faces, parts, small, present),
        [held(12, WELLS, LANES), held(12, *block), held(10, *plane)],
    )
    parts = exchanged(part)
    (result,) = call(
        solve_kernel,
        [field],
        (guess, residual, second, third, parts, known),
    )
    return result


def solution(mesh):
    in_specs = (
        P("member", None, "gx", "gy", None),
        P("member", "gx", "gy", None),
        P("member", "gx", "gy", None),
        P("gx", "gy", None),
        P("member", None, "gx", "gy", None),
        P("member", None, "gx", "gy", None),
    )
    out_specs = P("member", None, "gx", "gy", None)
    return jax.shard_map(body, mesh=mesh, in_specs=in_specs, out_specs=out_specs, check_vma=False)
```

```python
import jax
import jax.numpy as jnp
from jax import lax
from jax.experimental import pallas as pl
from jax.experimental.pallas import tpu as pltpu
from jax.sharding import PartitionSpec as P

WELLS = 40
RHS = 4
LANES = 128
WELL_EQ, WELL_ID, GUESS, REST = 4, 6, 7, 15
UP_WELL, DOWN_WELL, RISE_WELL, FALL_WELL, DIAGONAL_WELL = 23, 25, 27, 29, 31
BACK_WELL, BACK_ID = 33, 35
FACE_PLANES = 36
ENDS = 36
CORNER_PLANES = 5
LAT_UP, LAT_DOWN, RISE, FALL, DIAGONAL, BACK_IN = 0, 4, 8, 12, 16, 20
LAYER_BLOCKS = 24
IMAGE_PLANES = 16
TABLE_ROWS = 6
CORNER_ROWS = 19
SIDE_IN, SIDE_EQ, SIDE_ID, SIDE_GUESS = 4, 8, 10, 11


def product(blocks, first, second):
    return [
        blocks(0) * first + blocks(2) * second,
        blocks(1) * first + blocks(3) * second,
    ]


def iota(shape, axis):
    return lax.broadcasted_iota(jnp.int32, shape, axis)


def roll_up(value, axis):
    return pltpu.roll(value, 1, axis)


def roll_down(value, axis):
    return pltpu.roll(value, value.shape[axis] - 1, axis)


def layer_moves(rising, falling):
    axis = rising.ndim - 1
    lane = iota(rising.shape, axis)
    up = jnp.where(lane == 0, 0.0, roll_up(rising, axis))
    down = jnp.where(lane == LANES - 1, 0.0, roll_down(falling, axis))
    return up + down


def block_stencil(couplings, diagonal, first, second, incoming):
    result = product(lambda e: diagonal[e], first, second)
    moved = [product(lambda e, d=d: couplings[d, e], first, second) for d in range(6)]
    row = iota(first.shape, 1)
    outgoing = [[], [], [], []]
    for b in range(2):
        east, west, north, south, rise, fall = (moved[d][b] for d in range(6))
        total = result[b] + jnp.concatenate([incoming[0][b][None], east[:-1]], axis=0)
        total = total + jnp.concatenate([west[1:], incoming[1][b][None]], axis=0)
        total = total + jnp.where(row == 0, incoming[2][b][:, None, :], roll_up(north, 1))
        total = total + jnp.where(
            row == row.shape[1] - 1, incoming[3][b][:, None, :], roll_down(south, 1)
        )
        result[b] = total + layer_moves(rise, fall)
        outgoing[0].append(west[0])
        outgoing[1].append(east[-1])
        outgoing[2].append(south[:, 0, :])
        outgoing[3].append(north[:, -1, :])
    return result, outgoing


def face_stencil(blocks, first, second, behind):
    def times(start):
        return product(lambda e: blocks(start + e), first, second)

    moves = [times(start) for start in (DIAGONAL, LAT_UP, LAT_DOWN, RISE, FALL)]
    return face_moves(*moves, behind)


def face_moves(kept, up, down, rise, fall, behind):
    result = list(kept)
    row = iota(kept[0].shape, 0)
    for b in range(2):
        total = result[b] + behind[b] + layer_moves(rise[b], fall[b])
        total = total + jnp.where(row == 0, 0.0, roll_up(up[b], 0))
        result[b] = total + jnp.where(row == row.shape[0] - 1, 0.0, roll_down(down[b], 0))
    return result


def face_entries(low_end, high_end, entering):
    row = iota(entering[0].shape, 0)
    return [
        entering[b]
        + jnp.where(row == 0, low_end[b], 0.0)
        + jnp.where(row == row.shape[0] - 1, high_end[b], 0.0)
        for b in range(2)
    ]


def spread(totals, ids):
    table = jnp.broadcast_to(totals, (8, LANES))
    if ids.ndim == 2:
        return jnp.take_along_axis(table, ids, axis=1)
    return jnp.stack(
        [jnp.take_along_axis(table, ids[x], axis=1) for x in range(ids.shape[0])], axis=0
    )


def as_ids(plane):
    return plane.astype(jnp.int32)


class Corner:
    def __init__(self, pack, which, base):
        self.pack, self.start = pack, base * 8 + which

    def row(self, number):
        at = self.start + number
        return self.pack[at // 8, at % 8 : at % 8 + 1, :]


def corners_of(faces, base, rows):
    found = []
    for y_face in (2, 3):
        for x_end in range(2):
            found.append(Corner(faces[y_face], x_end * rows, base))
    return found


def corner_inputs(corners, values):
    ends = {}
    for c in range(4):
        x_end, y_end = c % 2, c // 2
        over_x = product(corners[c].row, *values[c])
        over_y = product(lambda e, c=c: corners[c].row(SIDE_IN + e), *values[c])
        ends[(2 + y_end, x_end)] = over_x
        ends[(x_end, y_end)] = over_y
    return ends


def tile_sum(first, second):
    value = first[0] * second[0] + first[1] * second[1]
    return jnp.sum(jnp.sum(value, axis=0), axis=0, keepdims=True)


def list_wells(ids, present):
    depth = ids.shape[0]

    def smallest(planes):
        least = planes[0]
        for plane in planes[1:]:
            least = jnp.minimum(least, plane)
        return jnp.min(least)

    planes = [ids[x].astype(jnp.float32) for x in range(depth)]

    def one_well(state):
        number, well = state
        present[number] = well.astype(jnp.int32)
        after = [jnp.where(plane > well, plane, float(WELLS)) for plane in planes]
        return number + 1, smallest(after)

    number, _ = lax.while_loop(
        lambda state: state[1] < WELLS, one_well, (jnp.int32(1), smallest(planes))
    )
    present[0] = number - 1


def segment_rows(ids, values, scratch, present):
    scratch[...] = jnp.zeros_like(scratch)
    count, depth = values.shape[0], ids.shape[0]

    def one_well(step, _):
        well = present[step + 1]
        masks = [ids[x] == well for x in range(depth)]
        for number in range(count):
            total = jnp.where(masks[0], values[number, 0], 0.0)
            for x in range(1, depth):
                total = total + jnp.where(masks[x], values[number, x], 0.0)
            scratch[number, pl.ds(well, 1), :] = jnp.sum(total, axis=0, keepdims=True)
        return 0

    lax.fori_loop(0, present[0], one_well, 0)
    rows = []
    for number in range(count):
        summed = jnp.sum(scratch[number], axis=1, keepdims=True)
        shape = scratch.shape[1:]
        on_lanes = jnp.where(iota(shape, 0) == iota(shape, 1), summed, 0.0)
        rows.append(jnp.sum(on_lanes, axis=0, keepdims=True))
    return rows


def pack_rows(rows, table):
    for number, row in enumerate(rows):
        placed = row if number % 3 == 0 else pltpu.roll(row, WELLS * (number % 3), 1)
        table = table + jnp.where(
            iota(table.shape, 0) == number // 3, jnp.broadcast_to(placed, table.shape), 0.0
        )
    return table


def unpack_row(table, number):
    row = table[number // 3 : number // 3 + 1, :]
    if number % 3:
        row = pltpu.roll(row, LANES - WELLS * (number % 3), 1)
    return jnp.where(iota(row.shape, 1) < WELLS, row, 0.0)


def place_rows(rows, table):
    for number, row in enumerate(rows):
        group, k = divmod(number, RHS)
        at = k + RHS * (group // 3)
        placed = pltpu.roll(row, WELLS * group, 1) if group in (1, 2) else row
        table = table + jnp.where(
            iota(table.shape, 0) == at, jnp.broadcast_to(placed, table.shape), 0.0
        )
    return table


def place_columns(dots, first_lane, table):
    for number in range(dots.shape[0]):
        column = jnp.sum(dots[number], axis=1, keepdims=True)
        table = table + jnp.where(iota(table.shape, 1) == first_lane + number, column, 0.0)
    return table


def take_group(table, group):
    if group in (1, 2):
        table = pltpu.roll(table, LANES - WELLS * group, 1)
    start = RHS * (group // 3)
    rows = table[start : start + RHS, :]
    return jnp.where(iota(rows.shape, 1) < WELLS, rows, 0.0)


def take_column(table, lane):
    return table[RHS : 2 * RHS, lane : lane + 1]


def lane_sum(row):
    return jnp.sum(row, axis=1, keepdims=True)


COUPLINGS, DIAGONALS, WELL_FIELDS, IDS, RIGHT_SIDE, START = range(6)


def layer_blocks(cut, inward, lateral):
    def plane(n):
        if n < DIAGONAL:
            return cut(COUPLINGS, ((lateral, lateral + 1, 4, 5)[n // 4], n % 4), 0)
        if n < BACK_IN:
            return cut(DIAGONALS, (n - DIAGONAL,), 0)
        return cut(COUPLINGS, (inward, n - BACK_IN), 1)

    return plane


def fill_pack(pack, inward, lateral, cut):
    blocks = layer_blocks(cut, inward, lateral)
    for e in range(4):
        pack[e] = cut(COUPLINGS, (inward, e), 0)
    wells = [cut(WELL_FIELDS, (2 + a,), 0) for a in range(2)]
    for a in range(2):
        pack[WELL_EQ + a] = wells[a]
    pack[WELL_ID] = cut(IDS, (), 0).astype(jnp.float32)
    pack[BACK_ID] = cut(IDS, (), 1).astype(jnp.float32)
    for start, at in (
        (LAT_UP, UP_WELL),
        (LAT_DOWN, DOWN_WELL),
        (RISE, RISE_WELL),
        (FALL, FALL_WELL),
        (DIAGONAL, DIAGONAL_WELL),
        (BACK_IN, BACK_WELL),
    ):
        if start == BACK_IN:
            wells = [cut(WELL_FIELDS, (2 + a,), 1) for a in range(2)]
        for b, value in enumerate(product(lambda e: blocks(start + e), *wells)):
            pack[at + b] = value
    for k in range(RHS):
        here = [cut(START, (k, a), 0) for a in range(2)]
        back = [cut(START, (k, a), 1) for a in range(2)]
        entering = product(lambda e: blocks(BACK_IN + e), *back)
        local = face_stencil(blocks, here[0], here[1], entering)
        for a in range(2):
            pack[GUESS + 2 * k + a] = here[a]
            pack[REST + 2 * k + a] = cut(RIGHT_SIDE, (k, a), 0) - local[a]
    if pack.shape[0] > ENDS:
        end = pack.shape[1] - 1
        for e in range(4):
            pack[ENDS, e : e + 1, :] = blocks(LAT_UP + e)[end : end + 1, :]
            pack[ENDS, 4 + e : 5 + e, :] = blocks(LAT_DOWN + e)[0:1, :]


def x_pack_kernel(*refs):
    sources, packs, held_ends, arrived = refs[:6], refs[6:8], refs[8:20], refs[20]
    copies = []
    for n, source in enumerate(sources):
        lead = (slice(None),) * (len(source.shape) - 3)
        depth = source.shape[-3]
        for end, start in enumerate((0, depth - 2)):
            copies.append(
                pltpu.make_async_copy(
                    source.at[lead + (pl.ds(start, 2),)],
                    held_ends[2 * n + end],
                    arrived.at[2 * n + end],
                )
            )
    for copy in copies:
        copy.start()
    for copy in copies:
        copy.wait()
    for end, pack in enumerate(packs):
        fill_pack(
            pack,
            1 - end,
            2,
            lambda n, index, layer: held_ends[2 * n + end][
                index + (1 - layer if end else layer,)
            ],
        )


def y_packs(arguments, packs, all_blocks):
    last = arguments[-1].shape[-2] - 1
    for end in range(2):

        def cut(n, index, layer):
            return arguments[n][index + (slice(None), last - layer if end else layer, slice(None))]

        fill_pack(packs[end], 3 - end, 0, cut)
        blocks = layer_blocks(cut, 3 - end, 0)
        for n in range(LAYER_BLOCKS):
            all_blocks[end][n] = blocks(n)


def spread_kernel(table, face, part):
    part[...] = jnp.broadcast_to(table[...][None, : part.shape[1]], part.shape)


def corner_kernel(y_low, y_high, fxl, fxh, low_out, high_out):
    last = fxl.shape[1] - 1
    for own, out, at, side in ((y_low, low_out, 0, 4), (y_high, high_out, last, 0)):
        for n in range(FACE_PLANES):
            out[n] = own[n]
        row = FACE_PLANES * 8
        out[FACE_PLANES + CORNER_PLANES - 1] = jnp.zeros(out.shape[1:], jnp.float32)
        for face in (fxl, fxh):
            rows = [(n, at) for n in range(4)]
            rows += [(ENDS, side + e) for e in range(4)]
            rows += [(n, at) for n in range(WELL_EQ, REST)]
            for n, y in rows:
                out[row // 8, row % 8 : row % 8 + 1, :] = face[n, y : y + 1, :]
                row += 1


def image_corner_kernel(y_low, y_high, gxl, gxh, table, low_out, high_out, part):
    part[...] = jnp.broadcast_to(table[...][None], part.shape)
    last = gxl.shape[1] - 1
    for own, out, at in ((y_low, low_out, 0), (y_high, high_out, last)):
        for n in range(IMAGE_PLANES):
            out[n] = own[n]
        for x_end, face in enumerate((gxl, gxh)):
            for n in range(8):
                out[IMAGE_PLANES + x_end, n : n + 1, :] = face[n, at : at + 1, :]


def guess_kernel(
    couplings, diagonal, wells, ids, right, guess,
    table_out, present, y_low, y_high, low_blocks, high_blocks, values, scratch,
):
    y_packs(
        (couplings, diagonal, wells, ids, right, guess), (y_low, y_high), (low_blocks, high_blocks)
    )
    list_wells(ids, present)
    for k in range(RHS):
        values[k] = wells[0] * guess[k, 0] + wells[1] * guess[k, 1]
    values[4] = wells[0] * wells[2] + wells[1] * wells[3]
    values[5] = wells[2] * wells[2] + wells[3] * wells[3]
    rows = segment_rows(ids, values, scratch, present)
    table_out[...] = pack_rows(rows, jnp.zeros((8, LANES), jnp.float32))


def residual_kernel(
    couplings, diagonal, wells, ids, right, guess, fxl, fxh, fyl, fyh, parts,
    low_blocks, high_blocks,
    residual, image, residual_faces, x_low, x_high, y_low, y_high, small,
):
    faces = (fxl, fxh, fyl, fyh)
    totals = jnp.sum(parts[...], axis=0)
    corners = corners_of(faces, FACE_PLANES, CORNER_ROWS)
    all_ids = ids[...]
    face_ids = [as_ids(face[WELL_ID]) for face in faces]
    last = guess.shape[2] - 1
    for k in range(RHS):
        s_row = unpack_row(totals, k)
        first, second = guess[k, 0], guess[k, 1]
        incoming = [
            product(
                lambda e, f=f: faces[f][e],
                faces[f][GUESS + 2 * k],
                faces[f][GUESS + 2 * k + 1],
            )
            for f in range(4)
        ]
        applied, outgoing = block_stencil(couplings, diagonal, first, second, incoming)
        at_wells = spread(s_row, all_ids)
        now = [
            right[k, a] - applied[a] - wells[2 + a] * at_wells for a in range(2)
        ]
        for a in range(2):
            residual[k, a] = now[a]
        ends = corner_inputs(
            corners,
            [[corners[c].row(SIDE_GUESS + 2 * k + a) for a in range(2)] for c in range(4)],
        )
        incoming = []
        for f in range(4):
            face = faces[f]
            there = face_entries(ends[(f, 0)], ends[(f, 1)], outgoing[f])
            face_wells = spread(s_row, face_ids[f])
            outer = [
                face[REST + 2 * k + a] - there[a] - face[WELL_EQ + a] * face_wells
                for a in range(2)
            ]
            for a in range(2):
                residual_faces[f, 2 * k + a] = outer[a]
            incoming.append(product(lambda e, f=f: faces[f][e], *outer))
        result, _ = block_stencil(couplings, diagonal, now[0], now[1], incoming)
        for a in range(2):
            image[k, a] = result[a]
        for pack, here, back, blocks in (
            (
                x_low,
                [value[0] for value in result],
                [value[1] for value in result],
                layer_blocks(lambda n, i, layer: (couplings, diagonal)[n][i + (layer,)], 1, 2),
            ),
            (
                x_high,
                [value[last] for value in result],
                [value[last - 1] for value in result],
                layer_blocks(
                    lambda n, i, layer: (couplings, diagonal)[n][i + (last - layer,)], 0, 2
                ),
            ),
            (
                y_low,
                [value[:, 0, :] for value in result],
                [value[:, 1, :] for value in result],
                lambda n: low_blocks[n],
            ),
            (
                y_high,
                [value[:, last, :] for value in result],
                [value[:, last - 1, :] for value in result],
                lambda n: high_blocks[n],
            ),
        ):
            entering = product(lambda e: blocks(BACK_IN + e), *back)
            local = face_stencil(blocks, here[0], here[1], entering)
            for a in range(2):
                pack[2 * k + a] = here[a]
                pack[8 + 2 * k + a] = local[a]
    small[...] = jnp.concatenate(
        [unpack_row(totals, 4), unpack_row(totals, 5), jnp.zeros((6, LANES), jnp.float32)], axis=0
    )


def moments_kernel(
    wells, ids, residual, image, present, table_out, values, scratch, dots
):
    dots[...] = jnp.zeros_like(dots)
    for k in range(RHS):
        now = [residual[k, a] for a in range(2)]
        result = [image[k, a] for a in range(2)]
        for n, field in enumerate((now, result)):
            values[4 * n + k] = wells[0] * field[0] + wells[1] * field[1]
            values[8 + 4 * n + k] = wells[2] * field[0] + wells[3] * field[1]
        row = slice(RHS + k, RHS + k + 1)
        dots[0, row, :] = tile_sum(now, now)
        dots[1, row, :] = tile_sum(now, result)
        dots[2, row, :] = tile_sum(result, result)
    rows = segment_rows(ids, values, scratch, present)
    table = place_rows(rows, jnp.zeros((8, LANES), jnp.float32))
    table_out[...] = place_columns(dots, WELLS, table)


def first_step(totals, small):
    s_row, us_row, p_row, ps_row = (take_group(totals, group) for group in range(4))
    within, equation = small[0:1, :], small[1:2, :]
    rr, rs, ss = (take_column(totals, WELLS + i) for i in range(3))
    height = (rs + lane_sum(p_row * s_row)) / rr
    square = ss + lane_sum(2.0 * ps_row * s_row + equation * s_row * s_row)
    left = jnp.maximum(square - height * height * rr, 1e-7 * square)
    scale = lax.rsqrt(left)
    s_image = us_row + within * s_row
    s_second = (s_image - height * s_row) * scale
    p_second = (ps_row + equation * s_row - height * p_row) * scale
    shift = rs / rr + lane_sum(p_second * s_second)
    unit = lax.rsqrt(rr)
    following = left * scale * unit
    return s_row, s_image, p_row, p_second, (unit, rr * unit, height, shift, following, scale)


def krylov_kernel(
    couplings, diagonal, wells, ids, fxl, fxh, fyl, fyh, gxl, gxh, gyl, gyh,
    residual, image, residual_faces, parts, small_in, present,
    second_out, third_out, part, known, scratch, values_scratch, dots,
):
    faces, sent = (fxl, fxh, fyl, fyh), (gxl, gxh, gyl, gyh)
    totals = jnp.sum(parts[...], axis=0)
    small = small_in[...]
    s_rows, s_images, p_rows, p_seconds, scalars = first_step(totals, small)
    known[0:RHS, :] = p_rows
    known[RHS : 2 * RHS, :] = p_seconds
    columns = jnp.zeros((RHS, LANES), jnp.float32)
    for n, column in enumerate(scalars):
        columns = columns + jnp.where(iota(columns.shape, 1) == n, column, 0.0)
    known[2 * RHS : 3 * RHS, :] = columns
    known[3 * RHS :, :] = jnp.broadcast_to(small[1:2, :], (RHS, LANES))
    dots[...] = jnp.zeros_like(dots)
    corners = corners_of(faces, FACE_PLANES, CORNER_ROWS)
    sent_corners = corners_of(sent, IMAGE_PLANES, 8)
    all_ids = ids[...]
    face_ids = [as_ids(face[WELL_ID]) for face in faces]
    back_ids = [as_ids(face[BACK_ID]) for face in faces]
    corner_ids = [
        as_ids(jnp.broadcast_to(corner.row(SIDE_ID), (8, LANES))) for corner in corners
    ]
    for k in range(RHS):
        unit, _, height, shift, _, scale = (column[k : k + 1, :] for column in scalars)
        s_row, s_image = s_rows[k : k + 1, :], s_images[k : k + 1, :]
        at_wells = spread(s_row, all_ids)
        now = [image[k, a] + wells[2 + a] * at_wells for a in range(2)]
        face_now, local = [], []
        for f in range(4):
            face, got = faces[f], sent[f]
            here = spread(s_row, face_ids[f])
            behind = spread(s_row, back_ids[f])
            face_now.append([got[2 * k + a] + face[WELL_EQ + a] * here for a in range(2)])
            moves = [
                [face[at + b] * here for b in range(2)]
                for at in (DIAGONAL_WELL, UP_WELL, DOWN_WELL, RISE_WELL, FALL_WELL)
            ]
            entering = [face[BACK_WELL + b] * behind for b in range(2)]
            there = face_moves(*moves, entering)
            local.append([got[8 + 2 * k + b] + there[b] for b in range(2)])
        corner_now = []
        for c in range(4):
            here = spread(s_row, corner_ids[c])[0:1, :]
            corner_now.append(
                [
                    sent_corners[c].row(2 * k + a) + corners[c].row(SIDE_EQ + a) * here
                    for a in range(2)
                ]
            )
        incoming = [product(lambda e, f=f: faces[f][e], *face_now[f]) for f in range(4)]
        applied, outgoing = block_stencil(couplings, diagonal, now[0], now[1], incoming)
        at_wells = spread(s_image, all_ids)
        second, third = [], []
        for a in range(2):
            twice = applied[a] + wells[2 + a] * at_wells
            base = (now[a] - height * residual[k, a]) * scale
            second.append(base)
            third.append((twice - height * now[a]) * scale - shift * base)
            second_out[k, a] = second[a]
            third_out[k, a] = third[a]
        ends = corner_inputs(corners, corner_now)
        incoming = []
        for f in range(4):
            face = faces[f]
            over = face_entries(ends[(f, 0)], ends[(f, 1)], outgoing[f])
            here = spread(s_image, face_ids[f])
            outer = []
            for a in range(2):
                twice = local[f][a] + over[a] + face[WELL_EQ + a] * here
                base = (face_now[f][a] - height * residual_faces[f, 2 * k + a]) * scale
                outer.append((twice - height * face_now[f][a]) * scale - shift * base)
            incoming.append(product(lambda e, f=f: faces[f][e], *outer))
        result, _ = block_stencil(couplings, diagonal, third[0], third[1], incoming)
        fourth = [result[a] - shift * third[a] for a in range(2)]
        values_scratch[k] = wells[0] * third[0] + wells[1] * third[1]
        values_scratch[4 + k] = wells[2] * third[0] + wells[3] * third[1]
        values_scratch[8 + k] = wells[2] * fourth[0] + wells[3] * fourth[1]
        fields = [[residual[k, a] * unit for a in range(2)], second, third, fourth]
        number = 0
        for i in range(4):
            for j in range(i, 4):
                dots[number, RHS + k : RHS + k + 1, :] = tile_sum(fields[i], fields[j])
                number += 1
    rows = segment_rows(ids, values_scratch, scratch, present)
    table = place_rows(rows, jnp.zeros((8, LANES), jnp.float32))
    table = place_columns(dots, 0, table)
    part[...] = jnp.broadcast_to(table[None], part.shape)


def solve_kernel(guess, residual, second, third, parts, known, solution):
    totals = jnp.sum(parts[...], axis=0)
    s_third, p_third, p_fourth = (take_group(totals, group) for group in range(3))
    p_first, p_second = known[0:RHS, :], known[RHS : 2 * RHS, :]
    unit, beta, height, shift, following = (
        known[2 * RHS : 3 * RHS, n : n + 1] for n in range(5)
    )
    equation = known[3 * RHS :, :]
    gram = {}
    number = 0
    for i in range(4):
        for j in range(i, 4):
            gram[(i, j)] = take_column(totals, number)
            number += 1
    gram[(0, 3)] += lane_sum(p_first * s_third) * unit
    gram[(1, 3)] += lane_sum(p_second * s_third)
    gram[(2, 3)] += lane_sum(p_third * s_third)
    gram[(3, 3)] += lane_sum(2.0 * p_fourth * s_third + equation * s_third * s_third)
    tiny = 1e-30
    inverse = [lax.rsqrt(jnp.maximum(gram[(i, i)], tiny)) for i in range(4)]
    length = [jnp.maximum(gram[(i, i)], tiny) * inverse[i] for i in range(4)]
    upper = {}
    for i in range(4):
        for j in range(i, 4):
            entry = gram[(i, j)] * inverse[i] * inverse[j]
            for m in range(i):
                entry = entry - upper[(m, i)] * upper[(m, j)]
            if i == j:
                pivot = lax.rsqrt(jnp.maximum(entry, 1e-6))
                upper[(i, i)] = jnp.maximum(entry, 1e-6) * pivot
                over = pivot
            else:
                upper[(i, j)] = entry * over
    columns = [
        [(0, height * length[0]), (1, following * length[1])],
        [(1, shift * length[1]), (2, length[2])],
        [(2, shift * length[2]), (3, length[3])],
    ]
    zero = jnp.zeros_like(shift)
    hessenberg = [[zero] * 3 for _ in range(4)]
    for j in range(3):
        for i in range(j + 2):
            for m, factor in columns[j]:
                if m >= i:
                    hessenberg[i][j] = hessenberg[i][j] + upper[(i, m)] * factor
    target = [beta * length[0] * upper[(0, 0)], zero, zero, zero]
    turns = []
    for j in range(3):
        top, bottom = hessenberg[j][j], hessenberg[j + 1][j]
        turn = lax.rsqrt(top * top + bottom * bottom)
        turns.append(turn)
        cosine, sine = top * turn, bottom * turn
        for m in range(j, 3):
            high, low = hessenberg[j][m], hessenberg[j + 1][m]
            hessenberg[j][m] = cosine * high + sine * low
            hessenberg[j + 1][m] = cosine * low - sine * high
        high, low = target[j], target[j + 1]
        target[j] = cosine * high + sine * low
        target[j + 1] = cosine * low - sine * high
    weights = [zero] * 3
    for i in (2, 1, 0):
        value = target[i]
        for j in range(i + 1, 3):
            value = value - hessenberg[i][j] * weights[j]
        weights[i] = value * turns[i]
    for k in range(RHS):
        on_first, on_second, on_third = (
            column[k : k + 1, :] for column in (weights[0] * unit, weights[1], weights[2])
        )
        for a in range(2):
            solution[k, a] = (
                guess[k, a]
                + on_first * residual[k, a]
                + on_second * second[k, a]
                + on_third * third[k, a]
            )


def call(kernel, shapes, arguments, scratch=(), own_copies=False, cost=0, grant=24 << 20):
    whole = pl.BlockSpec(memory_space=pltpu.VMEM)
    far = pl.BlockSpec(memory_space=pltpu.HBM)
    scalars = pl.BlockSpec(memory_space=pltpu.SMEM)

    def place(array):
        if len(array.shape) == 1:
            return scalars
        return far if own_copies else whole

    outs = [
        jax.ShapeDtypeStruct(shape, jnp.float32 if len(shape) > 1 else jnp.int32)
        for shape in shapes
    ]
    return pl.pallas_call(
        kernel,
        out_shape=outs,
        in_specs=[place(argument) for argument in arguments],
        out_specs=[scalars if len(shape) == 1 else whole for shape in shapes],
        scratch_shapes=list(scratch),
        compiler_params=pltpu.CompilerParams(vmem_limit_bytes=grant),
        cost_estimate=pl.CostEstimate(flops=cost, bytes_accessed=cost, transcendentals=0)
        if cost
        else None,
    )(*arguments)


def held(*shape):
    return pltpu.VMEM(shape, jnp.float32)


def from_behind(value, axis, steps):
    count = lax.axis_size(axis)
    leading, last = (max(0, -steps), min(count, count - steps))
    return lax.ppermute(value, axis, [(source, source + steps) for source in range(leading, last)])


def exchanged(part):
    return lax.all_to_all(part, ("gx", "gy"), 0, 0, tiled=True)


def body(couplings, diagonal, wells, ids, right, guess):
    devices = lax.axis_size("gx") * lax.axis_size("gy")
    plane = (8, LANES)
    field = guess.shape
    block = guess.shape[2:]
    arguments = (couplings, diagonal, wells, ids, right, guess)

    ends = []
    for argument in arguments:
        shape = argument.shape[:-3] + (2,) + argument.shape[-2:]
        ends += [pltpu.VMEM(shape, argument.dtype)] * 2
    x_low, x_high = call(
        x_pack_kernel,
        [(FACE_PLANES + 1,) + plane] * 2,
        [pltpu.with_memory_space_constraint(argument, pltpu.HBM) for argument in arguments],
        ends + [pltpu.SemaphoreType.DMA((len(ends),))],
        own_copies=True,
    )
    fxl = from_behind(x_high, "gx", 1)
    fxh = from_behind(x_low, "gx", -1)
    table, present, y_low, y_high, *y_blocks = call(
        guess_kernel,
        [plane, (WELLS + 1,)] + [(FACE_PLANES,) + plane] * 2 + [(LAYER_BLOCKS,) + plane] * 2,
        arguments,
        [held(6, *block), held(6, WELLS, LANES)],
        cost=4 << 20,
    )
    (part,) = call(spread_kernel, [(devices, TABLE_ROWS, LANES)], (table, fxl))
    parts = exchanged(part)
    y_low, y_high = call(
        corner_kernel,
        [(FACE_PLANES + CORNER_PLANES,) + plane] * 2,
        (y_low, y_high, fxl, fxh),
    )
    fyl = from_behind(y_high, "gy", 1)
    fyh = from_behind(y_low, "gy", -1)

    faces = (fxl, fxh, fyl, fyh)
    residual, image, residual_faces, x_low, x_high, y_low, y_high, small = call(
        residual_kernel,
        [field, field, (4, 8) + plane] + [(IMAGE_PLANES,) + plane] * 4 + [(8, LANES)],
        arguments + faces + (parts, *y_blocks),
    )
    gxl = from_behind(x_high, "gx", 1)
    gxh = from_behind(x_low, "gx", -1)
    (table,) = call(
        moments_kernel,
        [plane],
        (wells, ids, residual, image, present),
        [held(16, *block), held(16, WELLS, LANES), held(3, *plane)],
        cost=4 << 20,
    )
    y_low, y_high, part = call(
        image_corner_kernel,
        [(IMAGE_PLANES + 2,) + plane] * 2 + [(devices, 8, LANES)],
        (y_low, y_high, gxl, gxh, table),
    )
    parts = exchanged(part)
    gyl = from_behind(y_high, "gy", 1)
    gyh = from_behind(y_low, "gy", -1)

    second, third, part, known = call(
        krylov_kernel,
        [field, field, (devices, 8, LANES), (4 * RHS, LANES)],
        (couplings, diagonal, wells, ids) + faces + (gxl, gxh, gyl, gyh)
        + (residual, image, residual_faces, parts, small, present),
        [held(12, WELLS, LANES), held(12, *block), held(10, *plane)],
    )
    parts = exchanged(part)
    (result,) = call(
        solve_kernel,
        [field],
        (guess, residual, second, third, parts, known),
    )
    return result


def solution(mesh):
    in_specs = (
        P("member", None, "gx", "gy", None),
        P("member", "gx", "gy", None),
        P("member", "gx", "gy", None),
        P("gx", "gy", None),
        P("member", None, "gx", "gy", None),
        P("member", None, "gx", "gy", None),
    )
    out_specs = P("member", None, "gx", "gy", None)
    return jax.shard_map(body, mesh=mesh, in_specs=in_specs, out_specs=out_specs, check_vma=False)
```

```python
import jax
import jax.numpy as jnp
from jax import lax
from jax.experimental import pallas as pl
from jax.experimental.pallas import tpu as pltpu
from jax.sharding import PartitionSpec as P

WELLS = 40
RHS = 4
LANES = 128
WELL_EQ, WELL_ID, GUESS, REST = 4, 6, 7, 15
UP_WELL, DOWN_WELL, RISE_WELL, FALL_WELL, DIAGONAL_WELL = 23, 25, 27, 29, 31
BACK_WELL, BACK_ID = 33, 35
FACE_PLANES = 36
ENDS = 36
CORNER_PLANES = 5
LAT_UP, LAT_DOWN, RISE, FALL, DIAGONAL, BACK_IN = 0, 4, 8, 12, 16, 20
LAYER_BLOCKS = 24
IMAGE_PLANES = 16
TABLE_ROWS = 6
GRAM_ENTRIES = 10
CORNER_ROWS = 19
SIDE_IN, SIDE_EQ, SIDE_ID, SIDE_GUESS = 4, 8, 10, 11


def product(blocks, first, second):
    return [
        blocks(0) * first + blocks(2) * second,
        blocks(1) * first + blocks(3) * second,
    ]


def iota(shape, axis):
    return lax.broadcasted_iota(jnp.int32, shape, axis)


def roll_up(value, axis):
    return pltpu.roll(value, 1, axis)


def roll_down(value, axis):
    return pltpu.roll(value, value.shape[axis] - 1, axis)


def layer_moves(rising, falling):
    axis = rising.ndim - 1
    lane = iota(rising.shape, axis)
    up = jnp.where(lane == 0, 0.0, roll_up(rising, axis))
    down = jnp.where(lane == LANES - 1, 0.0, roll_down(falling, axis))
    return up + down


def block_stencil(couplings, diagonal, first, second, incoming):
    result = product(lambda e: diagonal[e], first, second)
    moved = [product(lambda e, d=d: couplings[d, e], first, second) for d in range(6)]
    row = iota(first.shape, 1)
    outgoing = [[], [], [], []]
    for b in range(2):
        east, west, north, south, rise, fall = (moved[d][b] for d in range(6))
        total = result[b] + jnp.concatenate([incoming[0][b][None], east[:-1]], axis=0)
        total = total + jnp.concatenate([west[1:], incoming[1][b][None]], axis=0)
        total = total + jnp.where(row == 0, incoming[2][b][:, None, :], roll_up(north, 1))
        total = total + jnp.where(
            row == row.shape[1] - 1, incoming[3][b][:, None, :], roll_down(south, 1)
        )
        result[b] = total + layer_moves(rise, fall)
        outgoing[0].append(west[0])
        outgoing[1].append(east[-1])
        outgoing[2].append(south[:, 0, :])
        outgoing[3].append(north[:, -1, :])
    return result, outgoing


def face_stencil(blocks, first, second, behind):
    def times(start):
        return product(lambda e: blocks(start + e), first, second)

    moves = [times(start) for start in (DIAGONAL, LAT_UP, LAT_DOWN, RISE, FALL)]
    return face_moves(*moves, behind)


def face_moves(kept, up, down, rise, fall, behind):
    result = list(kept)
    row = iota(kept[0].shape, 0)
    for b in range(2):
        total = result[b] + behind[b] + layer_moves(rise[b], fall[b])
        total = total + jnp.where(row == 0, 0.0, roll_up(up[b], 0))
        result[b] = total + jnp.where(row == row.shape[0] - 1, 0.0, roll_down(down[b], 0))
    return result


def face_entries(low_end, high_end, entering):
    row = iota(entering[0].shape, 0)
    return [
        entering[b]
        + jnp.where(row == 0, low_end[b], 0.0)
        + jnp.where(row == row.shape[0] - 1, high_end[b], 0.0)
        for b in range(2)
    ]


def spread(totals, ids):
    table = jnp.broadcast_to(totals, (8, LANES))
    if ids.ndim == 2:
        return jnp.take_along_axis(table, ids, axis=1)
    return jnp.stack(
        [jnp.take_along_axis(table, ids[x], axis=1) for x in range(ids.shape[0])], axis=0
    )


def as_ids(plane):
    return plane.astype(jnp.int32)


class Corner:
    def __init__(self, pack, which, base):
        self.pack, self.start = pack, base * 8 + which

    def row(self, number):
        at = self.start + number
        return self.pack[at // 8, at % 8 : at % 8 + 1, :]


def corners_of(faces, base, rows):
    found = []
    for y_face in (2, 3):
        for x_end in range(2):
            found.append(Corner(faces[y_face], x_end * rows, base))
    return found


def corner_inputs(corners, values):
    ends = {}
    for c in range(4):
        x_end, y_end = c % 2, c // 2
        over_x = product(corners[c].row, *values[c])
        over_y = product(lambda e, c=c: corners[c].row(SIDE_IN + e), *values[c])
        ends[(2 + y_end, x_end)] = over_x
        ends[(x_end, y_end)] = over_y
    return ends


def tile_sum(first, second):
    value = first[0] * second[0] + first[1] * second[1]
    return jnp.sum(jnp.sum(value, axis=0), axis=0, keepdims=True)


def list_wells(ids, present):
    depth = ids.shape[0]

    def smallest(planes):
        least = planes[0]
        for plane in planes[1:]:
            least = jnp.minimum(least, plane)
        return jnp.min(least)

    planes = [ids[x].astype(jnp.float32) for x in range(depth)]

    def one_well(state):
        number, well = state
        present[number] = well.astype(jnp.int32)
        after = [jnp.where(plane > well, plane, float(WELLS)) for plane in planes]
        return number + 1, smallest(after)

    number, _ = lax.while_loop(
        lambda state: state[1] < WELLS, one_well, (jnp.int32(1), smallest(planes))
    )
    present[0] = number - 1


def segment_rows(ids, values, scratch, present):
    scratch[...] = jnp.zeros_like(scratch)
    count, depth = values.shape[0], ids.shape[0]

    def one_well(step, _):
        well = present[step + 1]
        masks = [ids[x] == well for x in range(depth)]
        for number in range(count):
            total = jnp.where(masks[0], values[number, 0], 0.0)
            for x in range(1, depth):
                total = total + jnp.where(masks[x], values[number, x], 0.0)
            scratch[number, pl.ds(well, 1), :] = jnp.sum(total, axis=0, keepdims=True)
        return 0

    lax.fori_loop(0, present[0], one_well, 0)
    rows = []
    for number in range(count):
        summed = jnp.sum(scratch[number], axis=1, keepdims=True)
        shape = scratch.shape[1:]
        on_lanes = jnp.where(iota(shape, 0) == iota(shape, 1), summed, 0.0)
        rows.append(jnp.sum(on_lanes, axis=0, keepdims=True))
    return rows


def pack_rows(rows, table):
    for number, row in enumerate(rows):
        placed = row if number % 3 == 0 else pltpu.roll(row, WELLS * (number % 3), 1)
        table = table + jnp.where(
            iota(table.shape, 0) == number // 3, jnp.broadcast_to(placed, table.shape), 0.0
        )
    return table


def unpack_row(table, number):
    row = table[number // 3 : number // 3 + 1, :]
    if number % 3:
        row = pltpu.roll(row, LANES - WELLS * (number % 3), 1)
    return jnp.where(iota(row.shape, 1) < WELLS, row, 0.0)


def place_rows(rows, table):
    for number, row in enumerate(rows):
        group, k = divmod(number, RHS)
        at = k + RHS * (group // 3)
        placed = pltpu.roll(row, WELLS * group, 1) if group in (1, 2) else row
        table = table + jnp.where(
            iota(table.shape, 0) == at, jnp.broadcast_to(placed, table.shape), 0.0
        )
    return table


def place_columns(dots, first_lane, table):
    for number in range(dots.shape[0]):
        column = jnp.sum(dots[number], axis=1, keepdims=True)
        table = table + jnp.where(iota(table.shape, 1) == first_lane + number, column, 0.0)
    return table


def take_group(table, group):
    if group in (1, 2):
        table = pltpu.roll(table, LANES - WELLS * group, 1)
    start = RHS * (group // 3)
    rows = table[start : start + RHS, :]
    return jnp.where(iota(rows.shape, 1) < WELLS, rows, 0.0)


def take_column(table, lane):
    return table[RHS : 2 * RHS, lane : lane + 1]


def lane_sum(row):
    return jnp.sum(row, axis=1, keepdims=True)


COUPLINGS, DIAGONALS, WELL_FIELDS, IDS, RIGHT_SIDE, START = range(6)


def layer_blocks(cut, inward, lateral):
    def plane(n):
        if n < DIAGONAL:
            return cut(COUPLINGS, ((lateral, lateral + 1, 4, 5)[n // 4], n % 4), 0)
        if n < BACK_IN:
            return cut(DIAGONALS, (n - DIAGONAL,), 0)
        return cut(COUPLINGS, (inward, n - BACK_IN), 1)

    return plane


def fill_pack(pack, inward, lateral, cut):
    blocks = layer_blocks(cut, inward, lateral)
    for e in range(4):
        pack[e] = cut(COUPLINGS, (inward, e), 0)
    wells = [cut(WELL_FIELDS, (2 + a,), 0) for a in range(2)]
    for a in range(2):
        pack[WELL_EQ + a] = wells[a]
    pack[WELL_ID] = cut(IDS, (), 0).astype(jnp.float32)
    pack[BACK_ID] = cut(IDS, (), 1).astype(jnp.float32)
    for start, at in (
        (LAT_UP, UP_WELL),
        (LAT_DOWN, DOWN_WELL),
        (RISE, RISE_WELL),
        (FALL, FALL_WELL),
        (DIAGONAL, DIAGONAL_WELL),
        (BACK_IN, BACK_WELL),
    ):
        if start == BACK_IN:
            wells = [cut(WELL_FIELDS, (2 + a,), 1) for a in range(2)]
        for b, value in enumerate(product(lambda e: blocks(start + e), *wells)):
            pack[at + b] = value
    for k in range(RHS):
        here = [cut(START, (k, a), 0) for a in range(2)]
        back = [cut(START, (k, a), 1) for a in range(2)]
        entering = product(lambda e: blocks(BACK_IN + e), *back)
        local = face_stencil(blocks, here[0], here[1], entering)
        for a in range(2):
            pack[GUESS + 2 * k + a] = here[a]
            pack[REST + 2 * k + a] = cut(RIGHT_SIDE, (k, a), 0) - local[a]
    if pack.shape[0] > ENDS:
        end = pack.shape[1] - 1
        for e in range(4):
            pack[ENDS, e : e + 1, :] = blocks(LAT_UP + e)[end : end + 1, :]
            pack[ENDS, 4 + e : 5 + e, :] = blocks(LAT_DOWN + e)[0:1, :]


def x_pack_kernel(*refs):
    sources, packs, held_ends, arrived = refs[:6], refs[6:8], refs[8:20], refs[20]
    copies = []
    for n, source in enumerate(sources):
        lead = (slice(None),) * (len(source.shape) - 3)
        depth = source.shape[-3]
        for end, start in enumerate((0, depth - 2)):
            copies.append(
                pltpu.make_async_copy(
                    source.at[lead + (pl.ds(start, 2),)],
                    held_ends[2 * n + end],
                    arrived.at[2 * n + end],
                )
            )
    for copy in copies:
        copy.start()
    for copy in copies:
        copy.wait()
    for end, pack in enumerate(packs):
        fill_pack(
            pack,
            1 - end,
            2,
            lambda n, index, layer: held_ends[2 * n + end][
                index + (1 - layer if end else layer,)
            ],
        )


def y_packs(arguments, packs, all_blocks):
    last = arguments[-1].shape[-2] - 1
    for end in range(2):

        def cut(n, index, layer):
            return arguments[n][index + (slice(None), last - layer if end else layer, slice(None))]

        fill_pack(packs[end], 3 - end, 0, cut)
        blocks = layer_blocks(cut, 3 - end, 0)
        for n in range(LAYER_BLOCKS):
            all_blocks[end][n] = blocks(n)


def send_out(table, chunks, part, sent):
    chunks[...] = jnp.broadcast_to(table[None, : chunks.shape[1]], chunks.shape)
    copy = pltpu.make_async_copy(chunks, part, sent.at[0])
    copy.start()
    return copy


def corner_kernel(y_low, y_high, fxl, fxh, low_out, high_out):
    last = fxl.shape[1] - 1
    for own, out, at, side in ((y_low, low_out, 0, 4), (y_high, high_out, last, 0)):
        for n in range(FACE_PLANES):
            out[n] = own[n]
        row = FACE_PLANES * 8
        out[FACE_PLANES + CORNER_PLANES - 1] = jnp.zeros(out.shape[1:], jnp.float32)
        for face in (fxl, fxh):
            rows = [(n, at) for n in range(4)]
            rows += [(ENDS, side + e) for e in range(4)]
            rows += [(n, at) for n in range(WELL_EQ, REST)]
            for n, y in rows:
                out[row // 8, row % 8 : row % 8 + 1, :] = face[n, y : y + 1, :]
                row += 1


def image_corner_kernel(y_low, y_high, gxl, gxh, low_out, high_out):
    last = gxl.shape[1] - 1
    for own, out, at in ((y_low, low_out, 0), (y_high, high_out, last)):
        for n in range(IMAGE_PLANES):
            out[n] = own[n]
        for x_end, face in enumerate((gxl, gxh)):
            for n in range(8):
                out[IMAGE_PLANES + x_end, n : n + 1, :] = face[n, at : at + 1, :]


def guess_kernel(
    couplings, diagonal, wells, ids, right, guess,
    part, present, y_low, y_high, low_blocks, high_blocks,
    values, scratch, chunks, sent,
):
    list_wells(ids, present)
    for k in range(RHS):
        values[k] = wells[0] * guess[k, 0] + wells[1] * guess[k, 1]
    values[4] = wells[0] * wells[2] + wells[1] * wells[3]
    values[5] = wells[2] * wells[2] + wells[3] * wells[3]
    rows = segment_rows(ids, values, scratch, present)
    table = pack_rows(rows, jnp.zeros((8, LANES), jnp.float32))
    copy = send_out(table, chunks, part, sent)
    y_packs(
        (couplings, diagonal, wells, ids, right, guess), (y_low, y_high), (low_blocks, high_blocks)
    )
    copy.wait()


def residual_kernel(
    couplings, diagonal, wells, ids, right, guess, fxl, fxh, fyl, fyh, parts,
    low_blocks, high_blocks,
    residual, image, residual_faces, x_low, x_high, y_low, y_high, small,
):
    faces = (fxl, fxh, fyl, fyh)
    totals = jnp.sum(parts[...], axis=0)
    corners = corners_of(faces, FACE_PLANES, CORNER_ROWS)
    all_ids = ids[...]
    face_ids = [as_ids(face[WELL_ID]) for face in faces]
    last = guess.shape[2] - 1
    for k in range(RHS):
        s_row = unpack_row(totals, k)
        first, second = guess[k, 0], guess[k, 1]
        incoming = [
            product(
                lambda e, f=f: faces[f][e],
                faces[f][GUESS + 2 * k],
                faces[f][GUESS + 2 * k + 1],
            )
            for f in range(4)
        ]
        applied, outgoing = block_stencil(couplings, diagonal, first, second, incoming)
        at_wells = spread(s_row, all_ids)
        now = [
            right[k, a] - applied[a] - wells[2 + a] * at_wells for a in range(2)
        ]
        for a in range(2):
            residual[k, a] = now[a]
        ends = corner_inputs(
            corners,
            [[corners[c].row(SIDE_GUESS + 2 * k + a) for a in range(2)] for c in range(4)],
        )
        incoming = []
        for f in range(4):
            face = faces[f]
            there = face_entries(ends[(f, 0)], ends[(f, 1)], outgoing[f])
            face_wells = spread(s_row, face_ids[f])
            outer = [
                face[REST + 2 * k + a] - there[a] - face[WELL_EQ + a] * face_wells
                for a in range(2)
            ]
            for a in range(2):
                residual_faces[f, 2 * k + a] = outer[a]
            incoming.append(product(lambda e, f=f: faces[f][e], *outer))
        result, _ = block_stencil(couplings, diagonal, now[0], now[1], incoming)
        for a in range(2):
            image[k, a] = result[a]
        for pack, here, back, blocks in (
            (
                x_low,
                [value[0] for value in result],
                [value[1] for value in result],
                layer_blocks(lambda n, i, layer: (couplings, diagonal)[n][i + (layer,)], 1, 2),
            ),
            (
                x_high,
                [value[last] for value in result],
                [value[last - 1] for value in result],
                layer_blocks(
                    lambda n, i, layer: (couplings, diagonal)[n][i + (last - layer,)], 0, 2
                ),
            ),
            (
                y_low,
                [value[:, 0, :] for value in result],
                [value[:, 1, :] for value in result],
                lambda n: low_blocks[n],
            ),
            (
                y_high,
                [value[:, last, :] for value in result],
                [value[:, last - 1, :] for value in result],
                lambda n: high_blocks[n],
            ),
        ):
            entering = product(lambda e: blocks(BACK_IN + e), *back)
            local = face_stencil(blocks, here[0], here[1], entering)
            for a in range(2):
                pack[2 * k + a] = here[a]
                pack[8 + 2 * k + a] = local[a]
    small[...] = jnp.concatenate(
        [unpack_row(totals, 4), unpack_row(totals, 5), jnp.zeros((6, LANES), jnp.float32)], axis=0
    )


def moments_kernel(
    wells, ids, residual, image, present, part, values, scratch, dots, chunks, sent
):
    dots[...] = jnp.zeros_like(dots)
    for k in range(RHS):
        now = [residual[k, a] for a in range(2)]
        result = [image[k, a] for a in range(2)]
        for n, field in enumerate((now, result)):
            values[4 * n + k] = wells[0] * field[0] + wells[1] * field[1]
            values[8 + 4 * n + k] = wells[2] * field[0] + wells[3] * field[1]
        row = slice(RHS + k, RHS + k + 1)
        dots[0, row, :] = tile_sum(now, now)
        dots[1, row, :] = tile_sum(now, result)
        dots[2, row, :] = tile_sum(result, result)
    rows = segment_rows(ids, values, scratch, present)
    table = place_rows(rows, jnp.zeros((8, LANES), jnp.float32))
    send_out(place_columns(dots, WELLS, table), chunks, part, sent).wait()


def first_step(totals, small):
    s_row, us_row, p_row, ps_row = (take_group(totals, group) for group in range(4))
    within, equation = small[0:1, :], small[1:2, :]
    rr, rs, ss = (take_column(totals, WELLS + i) for i in range(3))
    height = (rs + lane_sum(p_row * s_row)) / rr
    square = ss + lane_sum(2.0 * ps_row * s_row + equation * s_row * s_row)
    left = jnp.maximum(square - height * height * rr, 1e-7 * square)
    scale = lax.rsqrt(left)
    s_image = us_row + within * s_row
    s_second = (s_image - height * s_row) * scale
    p_second = (ps_row + equation * s_row - height * p_row) * scale
    shift = rs / rr + lane_sum(p_second * s_second)
    unit = lax.rsqrt(rr)
    following = left * scale * unit
    return s_row, s_image, p_row, p_second, (unit, rr * unit, height, shift, following, scale)


def krylov_kernel(
    couplings, diagonal, wells, ids, fxl, fxh, fyl, fyh, gxl, gxh, gyl, gyh,
    residual, image, residual_faces, parts, small_in, present,
    second_out, third_out, part, known, scratch, values_scratch, dots,
):
    faces, sent = (fxl, fxh, fyl, fyh), (gxl, gxh, gyl, gyh)
    totals = jnp.sum(parts[...], axis=0)
    small = small_in[...]
    s_rows, s_images, p_rows, p_seconds, scalars = first_step(totals, small)
    known[0:RHS, :] = p_rows
    known[RHS : 2 * RHS, :] = p_seconds
    columns = jnp.zeros((RHS, LANES), jnp.float32)
    for n, column in enumerate(scalars):
        columns = columns + jnp.where(iota(columns.shape, 1) == n, column, 0.0)
    known[2 * RHS : 3 * RHS, :] = columns
    known[3 * RHS :, :] = jnp.broadcast_to(small[1:2, :], (RHS, LANES))
    dots[...] = jnp.zeros_like(dots)
    corners = corners_of(faces, FACE_PLANES, CORNER_ROWS)
    sent_corners = corners_of(sent, IMAGE_PLANES, 8)
    all_ids = ids[...]
    face_ids = [as_ids(face[WELL_ID]) for face in faces]
    back_ids = [as_ids(face[BACK_ID]) for face in faces]
    corner_ids = [
        as_ids(jnp.broadcast_to(corner.row(SIDE_ID), (8, LANES))) for corner in corners
    ]
    for k in range(RHS):
        unit, _, height, shift, _, scale = (column[k : k + 1, :] for column in scalars)
        s_row, s_image = s_rows[k : k + 1, :], s_images[k : k + 1, :]
        at_wells = spread(s_row, all_ids)
        now = [image[k, a] + wells[2 + a] * at_wells for a in range(2)]
        face_now, spread_now = [], []
        for f in range(4):
            here = spread(s_row, face_ids[f])
            spread_now.append((here, spread(s_row, back_ids[f])))
            face_now.append(
                [sent[f][2 * k + a] + faces[f][WELL_EQ + a] * here for a in range(2)]
            )
        corner_now = []
        for c in range(4):
            here = spread(s_row, corner_ids[c])[0:1, :]
            corner_now.append(
                [
                    sent_corners[c].row(2 * k + a) + corners[c].row(SIDE_EQ + a) * here
                    for a in range(2)
                ]
            )
        incoming = [product(lambda e, f=f: faces[f][e], *face_now[f]) for f in range(4)]
        applied, outgoing = block_stencil(couplings, diagonal, now[0], now[1], incoming)
        at_wells = spread(s_image, all_ids)
        second, third = [], []
        for a in range(2):
            twice = applied[a] + wells[2 + a] * at_wells
            base = (now[a] - height * residual[k, a]) * scale
            second.append(base)
            third.append((twice - height * now[a]) * scale - shift * base)
            second_out[k, a] = second[a]
            third_out[k, a] = third[a]
        ends = corner_inputs(corners, corner_now)
        incoming = []
        for f in range(4):
            face = faces[f]
            here, behind = spread_now[f]
            moves = [
                [face[at + b] * here for b in range(2)]
                for at in (DIAGONAL_WELL, UP_WELL, DOWN_WELL, RISE_WELL, FALL_WELL)
            ]
            there = face_moves(*moves, [face[BACK_WELL + b] * behind for b in range(2)])
            local = [sent[f][8 + 2 * k + b] + there[b] for b in range(2)]
            over = face_entries(ends[(f, 0)], ends[(f, 1)], outgoing[f])
            here = spread(s_image, face_ids[f])
            outer = []
            for a in range(2):
                twice = local[a] + over[a] + face[WELL_EQ + a] * here
                base = (face_now[f][a] - height * residual_faces[f, 2 * k + a]) * scale
                outer.append((twice - height * face_now[f][a]) * scale - shift * base)
            incoming.append(product(lambda e, f=f: faces[f][e], *outer))
        result, _ = block_stencil(couplings, diagonal, third[0], third[1], incoming)
        fourth = [result[a] - shift * third[a] for a in range(2)]
        values_scratch[k] = wells[0] * third[0] + wells[1] * third[1]
        values_scratch[4 + k] = wells[2] * third[0] + wells[3] * third[1]
        values_scratch[8 + k] = wells[2] * fourth[0] + wells[3] * fourth[1]
        fields = [[residual[k, a] * unit for a in range(2)], second, third, fourth]
        number = 0
        for i in range(4):
            for j in range(i, 4):
                dots[number, RHS + k : RHS + k + 1, :] = tile_sum(fields[i], fields[j])
                number += 1
    rows = segment_rows(ids, values_scratch, scratch, present)
    table = place_rows(rows, jnp.zeros((8, LANES), jnp.float32))
    table = place_columns(dots, 0, table)
    gram = table[RHS : RHS + 1, :]
    for k in range(1, RHS):
        gram = gram + pltpu.roll(table[RHS + k : RHS + k + 1, :], GRAM_ENTRIES * k, 1)
    flat = jnp.concatenate([table[k : k + 1, :] for k in range(RHS)] + [gram], axis=1)
    part[...] = jnp.broadcast_to(flat[None], part.shape)


def solve_kernel(guess, residual, second, third, parts, known, solution):
    flat = jnp.sum(parts[...], axis=0)
    rows = [flat[:, LANES * n : LANES * (n + 1)] for n in range(RHS + 1)]
    for k in range(1, RHS):
        rows.append(pltpu.roll(rows[RHS], LANES - GRAM_ENTRIES * k, 1))
    totals = jnp.concatenate(rows, axis=0)
    s_third, p_third, p_fourth = (take_group(totals, group) for group in range(3))
    p_first, p_second = known[0:RHS, :], known[RHS : 2 * RHS, :]
    unit, beta, height, shift, following = (
        known[2 * RHS : 3 * RHS, n : n + 1] for n in range(5)
    )
    equation = known[3 * RHS :, :]
    gram = {}
    number = 0
    for i in range(4):
        for j in range(i, 4):
            gram[(i, j)] = take_column(totals, number)
            number += 1
    gram[(0, 3)] += lane_sum(p_first * s_third) * unit
    gram[(1, 3)] += lane_sum(p_second * s_third)
    gram[(2, 3)] += lane_sum(p_third * s_third)
    gram[(3, 3)] += lane_sum(2.0 * p_fourth * s_third + equation * s_third * s_third)
    tiny = 1e-30
    inverse = [lax.rsqrt(jnp.maximum(gram[(i, i)], tiny)) for i in range(4)]
    length = [jnp.maximum(gram[(i, i)], tiny) * inverse[i] for i in range(4)]
    upper = {}
    for i in range(4):
        for j in range(i, 4):
            entry = gram[(i, j)] * inverse[i] * inverse[j]
            for m in range(i):
                entry = entry - upper[(m, i)] * upper[(m, j)]
            if i == j:
                pivot = lax.rsqrt(jnp.maximum(entry, 1e-6))
                upper[(i, i)] = jnp.maximum(entry, 1e-6) * pivot
                over = pivot
            else:
                upper[(i, j)] = entry * over
    columns = [
        [(0, height * length[0]), (1, following * length[1])],
        [(1, shift * length[1]), (2, length[2])],
        [(2, shift * length[2]), (3, length[3])],
    ]
    zero = jnp.zeros_like(shift)
    hessenberg = [[zero] * 3 for _ in range(4)]
    for j in range(3):
        for i in range(j + 2):
            for m, factor in columns[j]:
                if m >= i:
                    hessenberg[i][j] = hessenberg[i][j] + upper[(i, m)] * factor
    target = [beta * length[0] * upper[(0, 0)], zero, zero, zero]
    turns = []
    for j in range(3):
        top, bottom = hessenberg[j][j], hessenberg[j + 1][j]
        turn = lax.rsqrt(top * top + bottom * bottom)
        turns.append(turn)
        cosine, sine = top * turn, bottom * turn
        for m in range(j, 3):
            high, low = hessenberg[j][m], hessenberg[j + 1][m]
            hessenberg[j][m] = cosine * high + sine * low
            hessenberg[j + 1][m] = cosine * low - sine * high
        high, low = target[j], target[j + 1]
        target[j] = cosine * high + sine * low
        target[j + 1] = cosine * low - sine * high
    weights = [zero] * 3
    for i in (2, 1, 0):
        value = target[i]
        for j in range(i + 1, 3):
            value = value - hessenberg[i][j] * weights[j]
        weights[i] = value * turns[i]
    for k in range(RHS):
        on_first, on_second, on_third = (
            column[k : k + 1, :] for column in (weights[0] * unit, weights[1], weights[2])
        )
        for a in range(2):
            solution[k, a] = (
                guess[k, a]
                + on_first * residual[k, a]
                + on_second * second[k, a]
                + on_third * third[k, a]
            )


def call(kernel, shapes, arguments, scratch=(), own_copies=False, cost=0, grant=24 << 20, out=0):
    whole = pl.BlockSpec(memory_space=pltpu.VMEM)
    far = pl.BlockSpec(memory_space=pltpu.HBM)
    scalars = pl.BlockSpec(memory_space=pltpu.SMEM)

    def place(array):
        if len(array.shape) == 1:
            return scalars
        return far if own_copies else whole

    outs = [
        jax.ShapeDtypeStruct(shape, jnp.float32 if len(shape) > 1 else jnp.int32)
        for shape in shapes
    ]
    outs[:out] = [pltpu.HBM(shape, jnp.float32) for shape in shapes[:out]]
    return pl.pallas_call(
        kernel,
        out_shape=outs,
        in_specs=[place(argument) for argument in arguments],
        out_specs=[far] * out + [scalars if len(shape) == 1 else whole for shape in shapes[out:]],
        scratch_shapes=list(scratch),
        compiler_params=pltpu.CompilerParams(vmem_limit_bytes=grant),
        cost_estimate=pl.CostEstimate(flops=cost, bytes_accessed=cost, transcendentals=0)
        if cost
        else None,
    )(*arguments)


def nothing(value, *rest):
    pass


def after(value, *others):
    far = pl.BlockSpec(memory_space=pltpu.HBM)
    anywhere = pl.BlockSpec(memory_space=pl.ANY)
    return pl.pallas_call(
        nothing,
        out_shape=pltpu.HBM(value.shape, value.dtype),
        in_specs=[far] + [anywhere] * len(others),
        out_specs=far,
        input_output_aliases={0: 0},
    )(pltpu.with_memory_space_constraint(value, pltpu.HBM), *others)


def held(*shape):
    return pltpu.VMEM(shape, jnp.float32)


def from_behind(value, axis, steps):
    count = lax.axis_size(axis)
    leading, last = (max(0, -steps), min(count, count - steps))
    return lax.ppermute(value, axis, [(source, source + steps) for source in range(leading, last)])


def exchanged(part):
    return lax.all_to_all(part, ("gx", "gy"), 0, 0, tiled=True)


def body(couplings, diagonal, wells, ids, right, guess):
    devices = lax.axis_size("gx") * lax.axis_size("gy")
    plane = (8, LANES)
    field = guess.shape
    block = guess.shape[2:]
    arguments = (couplings, diagonal, wells, ids, right, guess)

    ends = []
    for argument in arguments:
        shape = argument.shape[:-3] + (2,) + argument.shape[-2:]
        ends += [pltpu.VMEM(shape, argument.dtype)] * 2
    x_low, x_high = call(
        x_pack_kernel,
        [(FACE_PLANES + 1,) + plane] * 2,
        [pltpu.with_memory_space_constraint(argument, pltpu.HBM) for argument in arguments],
        ends + [pltpu.SemaphoreType.DMA((len(ends),))],
        own_copies=True,
    )
    fxl = from_behind(x_high, "gx", 1)
    fxh = from_behind(x_low, "gx", -1)
    first_chunks, chunks = (devices, TABLE_ROWS, LANES), (devices, 8, LANES)
    sent = pltpu.SemaphoreType.DMA((1,))
    part, present, y_low, y_high, *y_blocks = call(
        guess_kernel,
        [first_chunks, (WELLS + 1,)]
        + [(FACE_PLANES,) + plane] * 2
        + [(LAYER_BLOCKS,) + plane] * 2,
        arguments,
        [held(6, *block), held(6, WELLS, LANES), held(*first_chunks), sent],
        cost=4 << 20,
        out=1,
    )
    parts = exchanged(after(part, fxl))
    y_low, y_high = call(
        corner_kernel,
        [(FACE_PLANES + CORNER_PLANES,) + plane] * 2,
        (y_low, y_high, fxl, fxh),
    )
    fyl = from_behind(y_high, "gy", 1)
    fyh = from_behind(y_low, "gy", -1)

    faces = (fxl, fxh, fyl, fyh)
    residual, image, residual_faces, x_low, x_high, y_low, y_high, small = call(
        residual_kernel,
        [field, field, (4, 8) + plane] + [(IMAGE_PLANES,) + plane] * 4 + [(8, LANES)],
        arguments + faces + (parts, *y_blocks),
    )
    gxl = from_behind(x_high, "gx", 1)
    gxh = from_behind(x_low, "gx", -1)
    (part,) = call(
        moments_kernel,
        [chunks],
        (wells, ids, residual, image, present),
        [held(16, *block), held(16, WELLS, LANES), held(3, *plane), held(*chunks), sent],
        cost=4 << 20,
        out=1,
    )
    parts = exchanged(after(part, gxl, gxh))
    y_low, y_high = call(
        image_corner_kernel,
        [(IMAGE_PLANES + 2,) + plane] * 2,
        (y_low, y_high, gxl, gxh),
    )
    gyl = from_behind(y_high, "gy", 1)
    gyh = from_behind(y_low, "gy", -1)

    second, third, part, known = call(
        krylov_kernel,
        [field, field, (devices, 1, (RHS + 1) * LANES), (4 * RHS, LANES)],
        (couplings, diagonal, wells, ids) + faces + (gxl, gxh, gyl, gyh)
        + (residual, image, residual_faces, parts, small, present),
        [held(12, WELLS, LANES), held(12, *block), held(10, *plane)],
    )
    parts = exchanged(part)
    (result,) = call(
        solve_kernel,
        [field],
        (guess, residual, second, third, parts, known),
    )
    return result


def solution(mesh):
    in_specs = (
        P("member", None, "gx", "gy", None),
        P("member", "gx", "gy", None),
        P("member", "gx", "gy", None),
        P("gx", "gy", None),
        P("member", None, "gx", "gy", None),
        P("member", None, "gx", "gy", None),
    )
    out_specs = P("member", None, "gx", "gy", None)
    return jax.shard_map(body, mesh=mesh, in_specs=in_specs, out_specs=out_specs, check_vma=False)
```

```python
import jax
import jax.numpy as jnp
from jax import lax
from jax.experimental import pallas as pl
from jax.experimental.pallas import tpu as pltpu
from jax.sharding import PartitionSpec as P

WELLS = 40
RHS = 4
LANES = 128
WELL_EQ, WELL_ID, GUESS, REST = 4, 6, 7, 15
UP_WELL, DOWN_WELL, RISE_WELL, FALL_WELL, DIAGONAL_WELL = 23, 25, 27, 29, 31
BACK_WELL, BACK_ID = 33, 35
FACE_PLANES = 36
ENDS = 36
CORNER_PLANES = 5
LAT_UP, LAT_DOWN, RISE, FALL, DIAGONAL, BACK_IN = 0, 4, 8, 12, 16, 20
LAYER_BLOCKS = 24
IMAGE_PLANES = 16
TABLE_ROWS = 6
GRAM_ENTRIES = 10
CORNER_ROWS = 19
SIDE_IN, SIDE_EQ, SIDE_ID, SIDE_GUESS = 4, 8, 10, 11


def product(blocks, first, second):
    return [
        blocks(0) * first + blocks(2) * second,
        blocks(1) * first + blocks(3) * second,
    ]


def iota(shape, axis):
    return lax.broadcasted_iota(jnp.int32, shape, axis)


def roll_up(value, axis):
    return pltpu.roll(value, 1, axis)


def roll_down(value, axis):
    return pltpu.roll(value, value.shape[axis] - 1, axis)


def layer_moves(rising, falling):
    axis = rising.ndim - 1
    lane = iota(rising.shape, axis)
    up = jnp.where(lane == 0, 0.0, roll_up(rising, axis))
    down = jnp.where(lane == LANES - 1, 0.0, roll_down(falling, axis))
    return up + down


def block_stencil(couplings, diagonal, first, second, incoming):
    result = product(lambda e: diagonal[e], first, second)
    moved = [product(lambda e, d=d: couplings[d, e], first, second) for d in range(6)]
    row = iota(first.shape, 1)
    outgoing = [[], [], [], []]
    for b in range(2):
        east, west, north, south, rise, fall = (moved[d][b] for d in range(6))
        total = result[b] + jnp.concatenate([incoming[0][b][None], east[:-1]], axis=0)
        total = total + jnp.concatenate([west[1:], incoming[1][b][None]], axis=0)
        total = total + jnp.where(row == 0, incoming[2][b][:, None, :], roll_up(north, 1))
        total = total + jnp.where(
            row == row.shape[1] - 1, incoming[3][b][:, None, :], roll_down(south, 1)
        )
        result[b] = total + layer_moves(rise, fall)
        outgoing[0].append(west[0])
        outgoing[1].append(east[-1])
        outgoing[2].append(south[:, 0, :])
        outgoing[3].append(north[:, -1, :])
    return result, outgoing


def face_stencil(blocks, first, second, behind):
    def times(start):
        return product(lambda e: blocks(start + e), first, second)

    moves = [times(start) for start in (DIAGONAL, LAT_UP, LAT_DOWN, RISE, FALL)]
    return face_moves(*moves, behind)


def face_moves(kept, up, down, rise, fall, behind):
    result = list(kept)
    row = iota(kept[0].shape, 0)
    for b in range(2):
        total = result[b] + behind[b] + layer_moves(rise[b], fall[b])
        total = total + jnp.where(row == 0, 0.0, roll_up(up[b], 0))
        result[b] = total + jnp.where(row == row.shape[0] - 1, 0.0, roll_down(down[b], 0))
    return result


def face_entries(low_end, high_end, entering):
    row = iota(entering[0].shape, 0)
    return [
        entering[b]
        + jnp.where(row == 0, low_end[b], 0.0)
        + jnp.where(row == row.shape[0] - 1, high_end[b], 0.0)
        for b in range(2)
    ]


def spread(totals, ids):
    table = jnp.broadcast_to(totals, (8, LANES))
    if ids.ndim == 2:
        return jnp.take_along_axis(table, ids, axis=1)
    return jnp.stack(
        [jnp.take_along_axis(table, ids[x], axis=1) for x in range(ids.shape[0])], axis=0
    )


def as_ids(plane):
    return plane.astype(jnp.int32)


class Corner:
    def __init__(self, pack, which, base):
        self.pack, self.start = pack, base * 8 + which

    def row(self, number):
        at = self.start + number
        return self.pack[at // 8, at % 8 : at % 8 + 1, :]


def corners_of(faces, base, rows):
    found = []
    for y_face in (2, 3):
        for x_end in range(2):
            found.append(Corner(faces[y_face], x_end * rows, base))
    return found


def corner_inputs(corners, values):
    ends = {}
    for c in range(4):
        x_end, y_end = c % 2, c // 2
        over_x = product(corners[c].row, *values[c])
        over_y = product(lambda e, c=c: corners[c].row(SIDE_IN + e), *values[c])
        ends[(2 + y_end, x_end)] = over_x
        ends[(x_end, y_end)] = over_y
    return ends


def tile_sum(first, second):
    value = first[0] * second[0] + first[1] * second[1]
    return jnp.sum(jnp.sum(value, axis=0), axis=0, keepdims=True)


def list_wells(ids, present):
    depth = ids.shape[0]

    def smallest(planes):
        least = planes[0]
        for plane in planes[1:]:
            least = jnp.minimum(least, plane)
        return jnp.min(least)

    planes = [ids[x].astype(jnp.float32) for x in range(depth)]

    def one_well(state):
        number, well = state
        present[number] = well.astype(jnp.int32)
        after = [jnp.where(plane > well, plane, float(WELLS)) for plane in planes]
        return number + 1, smallest(after)

    number, _ = lax.while_loop(
        lambda state: state[1] < WELLS, one_well, (jnp.int32(1), smallest(planes))
    )
    present[0] = number - 1


def segment_rows(ids, values, scratch, present):
    scratch[...] = jnp.zeros_like(scratch)
    count, depth = values.shape[0], ids.shape[0]

    def one_well(step, _):
        well = present[step + 1]
        masks = [ids[x] == well for x in range(depth)]
        for number in range(count):
            total = jnp.where(masks[0], values[number, 0], 0.0)
            for x in range(1, depth):
                total = total + jnp.where(masks[x], values[number, x], 0.0)
            scratch[number, pl.ds(well, 1), :] = jnp.sum(total, axis=0, keepdims=True)
        return 0

    lax.fori_loop(0, present[0], one_well, 0)
    rows = []
    for number in range(count):
        summed = jnp.sum(scratch[number], axis=1, keepdims=True)
        shape = scratch.shape[1:]
        on_lanes = jnp.where(iota(shape, 0) == iota(shape, 1), summed, 0.0)
        rows.append(jnp.sum(on_lanes, axis=0, keepdims=True))
    return rows


def pack_rows(rows, table):
    for number, row in enumerate(rows):
        placed = row if number % 3 == 0 else pltpu.roll(row, WELLS * (number % 3), 1)
        table = table + jnp.where(
            iota(table.shape, 0) == number // 3, jnp.broadcast_to(placed, table.shape), 0.0
        )
    return table


def unpack_row(table, number):
    row = table[number // 3 : number // 3 + 1, :]
    if number % 3:
        row = pltpu.roll(row, LANES - WELLS * (number % 3), 1)
    return jnp.where(iota(row.shape, 1) < WELLS, row, 0.0)


def place_rows(rows, table):
    for number, row in enumerate(rows):
        group, k = divmod(number, RHS)
        at = k + RHS * (group // 3)
        placed = pltpu.roll(row, WELLS * group, 1) if group in (1, 2) else row
        table = table + jnp.where(
            iota(table.shape, 0) == at, jnp.broadcast_to(placed, table.shape), 0.0
        )
    return table


def place_columns(dots, first_lane, table):
    for number in range(dots.shape[0]):
        column = jnp.sum(dots[number], axis=1, keepdims=True)
        table = table + jnp.where(iota(table.shape, 1) == first_lane + number, column, 0.0)
    return table


def take_group(table, group):
    if group in (1, 2):
        table = pltpu.roll(table, LANES - WELLS * group, 1)
    start = RHS * (group // 3)
    rows = table[start : start + RHS, :]
    return jnp.where(iota(rows.shape, 1) < WELLS, rows, 0.0)


def take_column(table, lane):
    return table[RHS : 2 * RHS, lane : lane + 1]


def lane_sum(row):
    return jnp.sum(row, axis=1, keepdims=True)


COUPLINGS, DIAGONALS, WELL_FIELDS, IDS, RIGHT_SIDE, START = range(6)


def layer_blocks(cut, inward, lateral):
    def plane(n):
        if n < DIAGONAL:
            return cut(COUPLINGS, ((lateral, lateral + 1, 4, 5)[n // 4], n % 4), 0)
        if n < BACK_IN:
            return cut(DIAGONALS, (n - DIAGONAL,), 0)
        return cut(COUPLINGS, (inward, n - BACK_IN), 1)

    return plane


def fill_pack(pack, inward, lateral, cut):
    blocks = layer_blocks(cut, inward, lateral)
    for e in range(4):
        pack[e] = cut(COUPLINGS, (inward, e), 0)
    wells = [cut(WELL_FIELDS, (2 + a,), 0) for a in range(2)]
    for a in range(2):
        pack[WELL_EQ + a] = wells[a]
    pack[WELL_ID] = cut(IDS, (), 0).astype(jnp.float32)
    pack[BACK_ID] = cut(IDS, (), 1).astype(jnp.float32)
    for start, at in (
        (LAT_UP, UP_WELL),
        (LAT_DOWN, DOWN_WELL),
        (RISE, RISE_WELL),
        (FALL, FALL_WELL),
        (DIAGONAL, DIAGONAL_WELL),
        (BACK_IN, BACK_WELL),
    ):
        if start == BACK_IN:
            wells = [cut(WELL_FIELDS, (2 + a,), 1) for a in range(2)]
        for b, value in enumerate(product(lambda e: blocks(start + e), *wells)):
            pack[at + b] = value
    for k in range(RHS):
        here = [cut(START, (k, a), 0) for a in range(2)]
        back = [cut(START, (k, a), 1) for a in range(2)]
        entering = product(lambda e: blocks(BACK_IN + e), *back)
        local = face_stencil(blocks, here[0], here[1], entering)
        for a in range(2):
            pack[GUESS + 2 * k + a] = here[a]
            pack[REST + 2 * k + a] = cut(RIGHT_SIDE, (k, a), 0) - local[a]
    if pack.shape[0] > ENDS:
        end = pack.shape[1] - 1
        for e in range(4):
            pack[ENDS, e : e + 1, :] = blocks(LAT_UP + e)[end : end + 1, :]
            pack[ENDS, 4 + e : 5 + e, :] = blocks(LAT_DOWN + e)[0:1, :]


def x_pack_kernel(*refs):
    sources, packs, held_ends, arrived = refs[:6], refs[6:8], refs[8:20], refs[20]
    copies = []
    for n, source in enumerate(sources):
        lead = (slice(None),) * (len(source.shape) - 3)
        depth = source.shape[-3]
        for end, start in enumerate((0, depth - 2)):
            copies.append(
                pltpu.make_async_copy(
                    source.at[lead + (pl.ds(start, 2),)],
                    held_ends[2 * n + end],
                    arrived.at[2 * n + end],
                )
            )
    for copy in copies:
        copy.start()
    for copy in copies:
        copy.wait()
    for end, pack in enumerate(packs):
        fill_pack(
            pack,
            1 - end,
            2,
            lambda n, index, layer: held_ends[2 * n + end][
                index + (1 - layer if end else layer,)
            ],
        )


def y_packs(arguments, packs, all_blocks):
    last = arguments[-1].shape[-2] - 1
    for end in range(2):

        def cut(n, index, layer):
            return arguments[n][index + (slice(None), last - layer if end else layer, slice(None))]

        fill_pack(packs[end], 3 - end, 0, cut)
        blocks = layer_blocks(cut, 3 - end, 0)
        for n in range(LAYER_BLOCKS):
            all_blocks[end][n] = blocks(n)


def send_out(table, chunks, part, sent):
    rows = min(chunks.shape[1], table.shape[0])
    chunks[:, :rows, :] = jnp.broadcast_to(table[None, :rows], (chunks.shape[0], rows, LANES))
    copy = pltpu.make_async_copy(chunks, part, sent.at[0])
    copy.start()
    return copy


def corner_kernel(y_low, y_high, fxl, fxh, low_out, high_out):
    last = fxl.shape[1] - 1
    for own, out, at, side in ((y_low, low_out, 0, 4), (y_high, high_out, last, 0)):
        for n in range(FACE_PLANES):
            out[n] = own[n]
        row = FACE_PLANES * 8
        out[FACE_PLANES + CORNER_PLANES - 1] = jnp.zeros(out.shape[1:], jnp.float32)
        for face in (fxl, fxh):
            rows = [(n, at) for n in range(4)]
            rows += [(ENDS, side + e) for e in range(4)]
            rows += [(n, at) for n in range(WELL_EQ, REST)]
            for n, y in rows:
                out[row // 8, row % 8 : row % 8 + 1, :] = face[n, y : y + 1, :]
                row += 1


def diagonal_device(x_end, y_end):
    across, along = lax.axis_index("gx"), lax.axis_index("gy")
    there_x, there_y = across + 2 * x_end - 1, along + 2 * y_end - 1
    count_x, count_y = lax.axis_size("gx"), lax.axis_size("gy")
    exists = (there_x >= 0) & (there_x < count_x) & (there_y >= 0) & (there_y < count_y)
    return exists, jnp.where(exists, there_x * count_y + there_y, 0)


def guess_kernel(
    couplings, diagonal, wells, ids, right, guess,
    part, present, y_low, y_high, low_blocks, high_blocks,
    values, scratch, chunks, sent,
):
    list_wells(ids, present)
    for k in range(RHS):
        values[k] = wells[0] * guess[k, 0] + wells[1] * guess[k, 1]
    values[4] = wells[0] * wells[2] + wells[1] * wells[3]
    values[5] = wells[2] * wells[2] + wells[3] * wells[3]
    rows = segment_rows(ids, values, scratch, present)
    table = pack_rows(rows, jnp.zeros((8, LANES), jnp.float32))
    copy = send_out(table, chunks, part, sent)
    y_packs(
        (couplings, diagonal, wells, ids, right, guess), (y_low, y_high), (low_blocks, high_blocks)
    )
    copy.wait()


def residual_kernel(
    couplings, diagonal, wells, ids, right, guess, fxl, fxh, fyl, fyh, parts,
    low_blocks, high_blocks,
    residual, image, residual_faces, x_low, x_high, y_low, y_high, small,
):
    faces = (fxl, fxh, fyl, fyh)
    totals = jnp.sum(parts[...], axis=0)
    corners = corners_of(faces, FACE_PLANES, CORNER_ROWS)
    all_ids = ids[...]
    face_ids = [as_ids(face[WELL_ID]) for face in faces]
    last = guess.shape[2] - 1
    for k in range(RHS):
        s_row = unpack_row(totals, k)
        first, second = guess[k, 0], guess[k, 1]
        incoming = [
            product(
                lambda e, f=f: faces[f][e],
                faces[f][GUESS + 2 * k],
                faces[f][GUESS + 2 * k + 1],
            )
            for f in range(4)
        ]
        applied, outgoing = block_stencil(couplings, diagonal, first, second, incoming)
        at_wells = spread(s_row, all_ids)
        now = [
            right[k, a] - applied[a] - wells[2 + a] * at_wells for a in range(2)
        ]
        for a in range(2):
            residual[k, a] = now[a]
        ends = corner_inputs(
            corners,
            [[corners[c].row(SIDE_GUESS + 2 * k + a) for a in range(2)] for c in range(4)],
        )
        incoming = []
        for f in range(4):
            face = faces[f]
            there = face_entries(ends[(f, 0)], ends[(f, 1)], outgoing[f])
            face_wells = spread(s_row, face_ids[f])
            outer = [
                face[REST + 2 * k + a] - there[a] - face[WELL_EQ + a] * face_wells
                for a in range(2)
            ]
            for a in range(2):
                residual_faces[f, 2 * k + a] = outer[a]
            incoming.append(product(lambda e, f=f: faces[f][e], *outer))
        result, _ = block_stencil(couplings, diagonal, now[0], now[1], incoming)
        for a in range(2):
            image[k, a] = result[a]
        for pack, here, back, blocks in (
            (
                x_low,
                [value[0] for value in result],
                [value[1] for value in result],
                layer_blocks(lambda n, i, layer: (couplings, diagonal)[n][i + (layer,)], 1, 2),
            ),
            (
                x_high,
                [value[last] for value in result],
                [value[last - 1] for value in result],
                layer_blocks(
                    lambda n, i, layer: (couplings, diagonal)[n][i + (last - layer,)], 0, 2
                ),
            ),
            (
                y_low,
                [value[:, 0, :] for value in result],
                [value[:, 1, :] for value in result],
                lambda n: low_blocks[n],
            ),
            (
                y_high,
                [value[:, last, :] for value in result],
                [value[:, last - 1, :] for value in result],
                lambda n: high_blocks[n],
            ),
        ):
            entering = product(lambda e: blocks(BACK_IN + e), *back)
            local = face_stencil(blocks, here[0], here[1], entering)
            for a in range(2):
                pack[2 * k + a] = here[a]
                pack[8 + 2 * k + a] = local[a]
    small[...] = jnp.concatenate(
        [unpack_row(totals, 4), unpack_row(totals, 5), jnp.zeros((6, LANES), jnp.float32)], axis=0
    )


def moments_kernel(
    wells, ids, residual, image, present, part, values, scratch, dots, chunks, sent
):
    dots[...] = jnp.zeros_like(dots)
    for k in range(RHS):
        now = [residual[k, a] for a in range(2)]
        result = [image[k, a] for a in range(2)]
        for n, field in enumerate((now, result)):
            values[4 * n + k] = wells[0] * field[0] + wells[1] * field[1]
            values[8 + 4 * n + k] = wells[2] * field[0] + wells[3] * field[1]
        row = slice(RHS + k, RHS + k + 1)
        dots[0, row, :] = tile_sum(now, now)
        dots[1, row, :] = tile_sum(now, result)
        dots[2, row, :] = tile_sum(result, result)
    rows = segment_rows(ids, values, scratch, present)
    table = place_rows(rows, jnp.zeros((8, LANES), jnp.float32))
    chunks[:, 8:, :] = jnp.zeros_like(chunks[:, 8:, :])
    last = image.shape[2] - 1
    for x_end in range(2):
        for y_end in range(2):
            exists, place = diagonal_device(x_end, y_end)

            @pl.when(exists)
            def _():
                for k in range(RHS):
                    for a in range(2):
                        row, y = 8 + 2 * k + a, last * y_end
                        chunks[pl.ds(place, 1), row : row + 1, :] = image[
                            k, a, last * x_end, y : y + 1, :
                        ][None]

    send_out(place_columns(dots, WELLS, table), chunks, part, sent).wait()


def first_step(totals, small):
    s_row, us_row, p_row, ps_row = (take_group(totals, group) for group in range(4))
    within, equation = small[0:1, :], small[1:2, :]
    rr, rs, ss = (take_column(totals, WELLS + i) for i in range(3))
    height = (rs + lane_sum(p_row * s_row)) / rr
    square = ss + lane_sum(2.0 * ps_row * s_row + equation * s_row * s_row)
    left = jnp.maximum(square - height * height * rr, 1e-7 * square)
    scale = lax.rsqrt(left)
    s_image = us_row + within * s_row
    s_second = (s_image - height * s_row) * scale
    p_second = (ps_row + equation * s_row - height * p_row) * scale
    shift = rs / rr + lane_sum(p_second * s_second)
    unit = lax.rsqrt(rr)
    following = left * scale * unit
    return s_row, s_image, p_row, p_second, (unit, rr * unit, height, shift, following, scale)


def krylov_kernel(
    couplings, diagonal, wells, ids, fxl, fxh, fyl, fyh, gxl, gxh, gyl, gyh,
    residual, image, residual_faces, parts, small_in, present,
    second_out, third_out, part, known, scratch, values_scratch, dots,
):
    faces, sent = (fxl, fxh, fyl, fyh), (gxl, gxh, gyl, gyh)
    totals = jnp.sum(parts[:, 0:8, :], axis=0)
    small = small_in[...]
    s_rows, s_images, p_rows, p_seconds, scalars = first_step(totals, small)
    known[0:RHS, :] = p_rows
    known[RHS : 2 * RHS, :] = p_seconds
    columns = jnp.zeros((RHS, LANES), jnp.float32)
    for n, column in enumerate(scalars):
        columns = columns + jnp.where(iota(columns.shape, 1) == n, column, 0.0)
    known[2 * RHS : 3 * RHS, :] = columns
    known[3 * RHS :, :] = jnp.broadcast_to(small[1:2, :], (RHS, LANES))
    dots[...] = jnp.zeros_like(dots)
    corners = corners_of(faces, FACE_PLANES, CORNER_ROWS)
    places = [diagonal_device(c % 2, c // 2)[1] for c in range(4)]
    all_ids = ids[...]
    face_ids = [as_ids(face[WELL_ID]) for face in faces]
    back_ids = [as_ids(face[BACK_ID]) for face in faces]
    corner_ids = [
        as_ids(jnp.broadcast_to(corner.row(SIDE_ID), (8, LANES))) for corner in corners
    ]
    for k in range(RHS):
        unit, _, height, shift, _, scale = (column[k : k + 1, :] for column in scalars)
        s_row, s_image = s_rows[k : k + 1, :], s_images[k : k + 1, :]
        at_wells = spread(s_row, all_ids)
        now = [image[k, a] + wells[2 + a] * at_wells for a in range(2)]
        face_now, spread_now = [], []
        for f in range(4):
            here = spread(s_row, face_ids[f])
            spread_now.append((here, spread(s_row, back_ids[f])))
            face_now.append(
                [sent[f][2 * k + a] + faces[f][WELL_EQ + a] * here for a in range(2)]
            )
        corner_now = []
        for c in range(4):
            here = spread(s_row, corner_ids[c])[0:1, :]
            corner_now.append(
                [
                    parts[pl.ds(places[c], 1), 8 + 2 * k + a, :] + corners[c].row(SIDE_EQ + a) * here
                    for a in range(2)
                ]
            )
        incoming = [product(lambda e, f=f: faces[f][e], *face_now[f]) for f in range(4)]
        applied, outgoing = block_stencil(couplings, diagonal, now[0], now[1], incoming)
        at_wells = spread(s_image, all_ids)
        second, third = [], []
        for a in range(2):
            twice = applied[a] + wells[2 + a] * at_wells
            base = (now[a] - height * residual[k, a]) * scale
            second.append(base)
            third.append((twice - height * now[a]) * scale - shift * base)
            second_out[k, a] = second[a]
            third_out[k, a] = third[a]
        ends = corner_inputs(corners, corner_now)
        incoming = []
        for f in range(4):
            face = faces[f]
            here, behind = spread_now[f]
            moves = [
                [face[at + b] * here for b in range(2)]
                for at in (DIAGONAL_WELL, UP_WELL, DOWN_WELL, RISE_WELL, FALL_WELL)
            ]
            there = face_moves(*moves, [face[BACK_WELL + b] * behind for b in range(2)])
            local = [sent[f][8 + 2 * k + b] + there[b] for b in range(2)]
            over = face_entries(ends[(f, 0)], ends[(f, 1)], outgoing[f])
            here = spread(s_image, face_ids[f])
            outer = []
            for a in range(2):
                twice = local[a] + over[a] + face[WELL_EQ + a] * here
                base = (face_now[f][a] - height * residual_faces[f, 2 * k + a]) * scale
                outer.append((twice - height * face_now[f][a]) * scale - shift * base)
            incoming.append(product(lambda e, f=f: faces[f][e], *outer))
        result, _ = block_stencil(couplings, diagonal, third[0], third[1], incoming)
        fourth = [result[a] - shift * third[a] for a in range(2)]
        values_scratch[k] = wells[0] * third[0] + wells[1] * third[1]
        values_scratch[4 + k] = wells[2] * third[0] + wells[3] * third[1]
        values_scratch[8 + k] = wells[2] * fourth[0] + wells[3] * fourth[1]
        fields = [[residual[k, a] * unit for a in range(2)], second, third, fourth]
        number = 0
        for i in range(4):
            for j in range(i, 4):
                dots[number, RHS + k : RHS + k + 1, :] = tile_sum(fields[i], fields[j])
                number += 1
    rows = segment_rows(ids, values_scratch, scratch, present)
    table = place_rows(rows, jnp.zeros((8, LANES), jnp.float32))
    table = place_columns(dots, 0, table)
    gram = table[RHS : RHS + 1, :]
    for k in range(1, RHS):
        gram = gram + pltpu.roll(table[RHS + k : RHS + k + 1, :], GRAM_ENTRIES * k, 1)
    flat = jnp.concatenate([table[k : k + 1, :] for k in range(RHS)] + [gram], axis=1)
    part[...] = jnp.broadcast_to(flat[None], part.shape)


def solve_kernel(guess, residual, second, third, parts, known, solution):
    flat = jnp.sum(parts[...], axis=0)
    rows = [flat[:, LANES * n : LANES * (n + 1)] for n in range(RHS + 1)]
    for k in range(1, RHS):
        rows.append(pltpu.roll(rows[RHS], LANES - GRAM_ENTRIES * k, 1))
    totals = jnp.concatenate(rows, axis=0)
    s_third, p_third, p_fourth = (take_group(totals, group) for group in range(3))
    p_first, p_second = known[0:RHS, :], known[RHS : 2 * RHS, :]
    unit, beta, height, shift, following = (
        known[2 * RHS : 3 * RHS, n : n + 1] for n in range(5)
    )
    equation = known[3 * RHS :, :]
    gram = {}
    number = 0
    for i in range(4):
        for j in range(i, 4):
            gram[(i, j)] = take_column(totals, number)
            number += 1
    gram[(0, 3)] += lane_sum(p_first * s_third) * unit
    gram[(1, 3)] += lane_sum(p_second * s_third)
    gram[(2, 3)] += lane_sum(p_third * s_third)
    gram[(3, 3)] += lane_sum(2.0 * p_fourth * s_third + equation * s_third * s_third)
    tiny = 1e-30
    inverse = [lax.rsqrt(jnp.maximum(gram[(i, i)], tiny)) for i in range(4)]
    length = [jnp.maximum(gram[(i, i)], tiny) * inverse[i] for i in range(4)]
    upper = {}
    for i in range(4):
        for j in range(i, 4):
            entry = gram[(i, j)] * inverse[i] * inverse[j]
            for m in range(i):
                entry = entry - upper[(m, i)] * upper[(m, j)]
            if i == j:
                pivot = lax.rsqrt(jnp.maximum(entry, 1e-6))
                upper[(i, i)] = jnp.maximum(entry, 1e-6) * pivot
                over = pivot
            else:
                upper[(i, j)] = entry * over
    columns = [
        [(0, height * length[0]), (1, following * length[1])],
        [(1, shift * length[1]), (2, length[2])],
        [(2, shift * length[2]), (3, length[3])],
    ]
    zero = jnp.zeros_like(shift)
    hessenberg = [[zero] * 3 for _ in range(4)]
    for j in range(3):
        for i in range(j + 2):
            for m, factor in columns[j]:
                if m >= i:
                    hessenberg[i][j] = hessenberg[i][j] + upper[(i, m)] * factor
    target = [beta * length[0] * upper[(0, 0)], zero, zero, zero]
    turns = []
    for j in range(3):
        top, bottom = hessenberg[j][j], hessenberg[j + 1][j]
        turn = lax.rsqrt(top * top + bottom * bottom)
        turns.append(turn)
        cosine, sine = top * turn, bottom * turn
        for m in range(j, 3):
            high, low = hessenberg[j][m], hessenberg[j + 1][m]
            hessenberg[j][m] = cosine * high + sine * low
            hessenberg[j + 1][m] = cosine * low - sine * high
        high, low = target[j], target[j + 1]
        target[j] = cosine * high + sine * low
        target[j + 1] = cosine * low - sine * high
    weights = [zero] * 3
    for i in (2, 1, 0):
        value = target[i]
        for j in range(i + 1, 3):
            value = value - hessenberg[i][j] * weights[j]
        weights[i] = value * turns[i]
    for k in range(RHS):
        on_first, on_second, on_third = (
            column[k : k + 1, :] for column in (weights[0] * unit, weights[1], weights[2])
        )
        for a in range(2):
            solution[k, a] = (
                guess[k, a]
                + on_first * residual[k, a]
                + on_second * second[k, a]
                + on_third * third[k, a]
            )


def call(kernel, shapes, arguments, scratch=(), own_copies=False, cost=0, grant=24 << 20, out=0):
    whole = pl.BlockSpec(memory_space=pltpu.VMEM)
    far = pl.BlockSpec(memory_space=pltpu.HBM)
    scalars = pl.BlockSpec(memory_space=pltpu.SMEM)

    def place(array):
        if len(array.shape) == 1:
            return scalars
        return far if own_copies else whole

    outs = [
        jax.ShapeDtypeStruct(shape, jnp.float32 if len(shape) > 1 else jnp.int32)
        for shape in shapes
    ]
    outs[:out] = [pltpu.HBM(shape, jnp.float32) for shape in shapes[:out]]
    return pl.pallas_call(
        kernel,
        out_shape=outs,
        in_specs=[place(argument) for argument in arguments],
        out_specs=[far] * out + [scalars if len(shape) == 1 else whole for shape in shapes[out:]],
        scratch_shapes=list(scratch),
        compiler_params=pltpu.CompilerParams(vmem_limit_bytes=grant),
        cost_estimate=pl.CostEstimate(flops=cost, bytes_accessed=cost, transcendentals=0)
        if cost
        else None,
    )(*arguments)


def nothing(value, *rest):
    pass


def after(value, *others):
    far = pl.BlockSpec(memory_space=pltpu.HBM)
    near = pl.BlockSpec(memory_space=pltpu.VMEM)
    return pl.pallas_call(
        nothing,
        out_shape=pltpu.HBM(value.shape, value.dtype),
        in_specs=[far] + [near] * len(others),
        out_specs=far,
        input_output_aliases={0: 0},
    )(pltpu.with_memory_space_constraint(value, pltpu.HBM), *others)


def held(*shape):
    return pltpu.VMEM(shape, jnp.float32)


def from_behind(value, axis, steps):
    count = lax.axis_size(axis)
    leading, last = (max(0, -steps), min(count, count - steps))
    return lax.ppermute(value, axis, [(source, source + steps) for source in range(leading, last)])


def exchanged(part):
    return lax.all_to_all(part, ("gx", "gy"), 0, 0, tiled=True)


def body(couplings, diagonal, wells, ids, right, guess):
    devices = lax.axis_size("gx") * lax.axis_size("gy")
    plane = (8, LANES)
    field = guess.shape
    block = guess.shape[2:]
    arguments = (couplings, diagonal, wells, ids, right, guess)

    ends = []
    for argument in arguments:
        shape = argument.shape[:-3] + (2,) + argument.shape[-2:]
        ends += [pltpu.VMEM(shape, argument.dtype)] * 2
    x_low, x_high = call(
        x_pack_kernel,
        [(FACE_PLANES + 1,) + plane] * 2,
        [pltpu.with_memory_space_constraint(argument, pltpu.HBM) for argument in arguments],
        ends + [pltpu.SemaphoreType.DMA((len(ends),))],
        own_copies=True,
    )
    fxl = from_behind(x_high, "gx", 1)
    fxh = from_behind(x_low, "gx", -1)
    first_chunks, chunks = (devices, TABLE_ROWS, LANES), (devices, 16, LANES)
    sent = pltpu.SemaphoreType.DMA((1,))
    part, present, y_low, y_high, *y_blocks = call(
        guess_kernel,
        [first_chunks, (WELLS + 1,)]
        + [(FACE_PLANES,) + plane] * 2
        + [(LAYER_BLOCKS,) + plane] * 2,
        arguments,
        [held(6, *block), held(6, WELLS, LANES), held(*first_chunks), sent],
        cost=4 << 20,
        out=1,
    )
    parts = exchanged(after(part, fxl))
    y_low, y_high = call(
        corner_kernel,
        [(FACE_PLANES + CORNER_PLANES,) + plane] * 2,
        (y_low, y_high, fxl, fxh),
    )
    fyl = from_behind(y_high, "gy", 1)
    fyh = from_behind(y_low, "gy", -1)

    faces = (fxl, fxh, fyl, fyh)
    residual, image, residual_faces, x_low, x_high, y_low, y_high, small = call(
        residual_kernel,
        [field, field, (4, 8) + plane] + [(IMAGE_PLANES,) + plane] * 4 + [(8, LANES)],
        arguments + faces + (parts, *y_blocks),
    )
    gxl = from_behind(x_high, "gx", 1)
    gxh = from_behind(x_low, "gx", -1)
    (part,) = call(
        moments_kernel,
        [chunks],
        (wells, ids, residual, image, present),
        [held(16, *block), held(16, WELLS, LANES), held(3, *plane), held(*chunks), sent],
        cost=4 << 20,
        out=1,
    )
    parts = exchanged(part)
    gyl = from_behind(y_high, "gy", 1)
    gyh = from_behind(y_low, "gy", -1)

    second, third, part, known = call(
        krylov_kernel,
        [field, field, (devices, 1, (RHS + 1) * LANES), (4 * RHS, LANES)],
        (couplings, diagonal, wells, ids) + faces + (gxl, gxh, gyl, gyh)
        + (residual, image, residual_faces, parts, small, present),
        [held(12, WELLS, LANES), held(12, *block), held(10, *plane)],
    )
    parts = exchanged(part)
    (result,) = call(
        solve_kernel,
        [field],
        (guess, residual, second, third, parts, known),
    )
    return result


def solution(mesh):
    in_specs = (
        P("member", None, "gx", "gy", None),
        P("member", "gx", "gy", None),
        P("member", "gx", "gy", None),
        P("gx", "gy", None),
        P("member", None, "gx", "gy", None),
        P("member", None, "gx", "gy", None),
    )
    out_specs = P("member", None, "gx", "gy", None)
    return jax.shard_map(body, mesh=mesh, in_specs=in_specs, out_specs=out_specs, check_vma=False)
```

```python
import jax
import jax.numpy as jnp
from jax import lax
from jax.experimental import pallas as pl
from jax.experimental.pallas import tpu as pltpu
from jax.sharding import PartitionSpec as P

WELLS = 40
RHS = 4
LANES = 128
WELL_EQ, WELL_ID, GUESS, REST = 4, 6, 7, 15
UP_WELL, DOWN_WELL, RISE_WELL, FALL_WELL, DIAGONAL_WELL = 23, 25, 27, 29, 31
BACK_WELL, BACK_ID = 33, 35
FACE_PLANES = 36
ENDS = 36
CORNER_PLANES = 5
LAT_UP, LAT_DOWN, RISE, FALL, DIAGONAL, BACK_IN = 0, 4, 8, 12, 16, 20
LAYER_BLOCKS = 24
IMAGE_PLANES = 16
TABLE_ROWS = 6
GRAM_ENTRIES = 10
CORNER_ROWS = 19
SIDE_IN, SIDE_EQ, SIDE_ID, SIDE_GUESS = 4, 8, 10, 11


def product(blocks, first, second):
    return [
        blocks(0) * first + blocks(2) * second,
        blocks(1) * first + blocks(3) * second,
    ]


def iota(shape, axis):
    return lax.broadcasted_iota(jnp.int32, shape, axis)


def roll_up(value, axis):
    return pltpu.roll(value, 1, axis)


def roll_down(value, axis):
    return pltpu.roll(value, value.shape[axis] - 1, axis)


def layer_moves(rising, falling):
    axis = rising.ndim - 1
    lane = iota(rising.shape, axis)
    up = jnp.where(lane == 0, 0.0, roll_up(rising, axis))
    down = jnp.where(lane == LANES - 1, 0.0, roll_down(falling, axis))
    return up + down


def block_stencil(couplings, diagonal, first, second, incoming):
    result = product(lambda e: diagonal[e], first, second)
    moved = [product(lambda e, d=d: couplings[d, e], first, second) for d in range(6)]
    row = iota(first.shape, 1)
    outgoing = [[], [], [], []]
    for b in range(2):
        east, west, north, south, rise, fall = (moved[d][b] for d in range(6))
        total = result[b] + jnp.concatenate([incoming[0][b][None], east[:-1]], axis=0)
        total = total + jnp.concatenate([west[1:], incoming[1][b][None]], axis=0)
        total = total + jnp.where(row == 0, incoming[2][b][:, None, :], roll_up(north, 1))
        total = total + jnp.where(
            row == row.shape[1] - 1, incoming[3][b][:, None, :], roll_down(south, 1)
        )
        result[b] = total + layer_moves(rise, fall)
        outgoing[0].append(west[0])
        outgoing[1].append(east[-1])
        outgoing[2].append(south[:, 0, :])
        outgoing[3].append(north[:, -1, :])
    return result, outgoing


def face_stencil(blocks, first, second, behind):
    def times(start):
        return product(lambda e: blocks(start + e), first, second)

    moves = [times(start) for start in (DIAGONAL, LAT_UP, LAT_DOWN, RISE, FALL)]
    return face_moves(*moves, behind)


def face_moves(kept, up, down, rise, fall, behind):
    result = list(kept)
    row = iota(kept[0].shape, 0)
    for b in range(2):
        total = result[b] + behind[b] + layer_moves(rise[b], fall[b])
        total = total + jnp.where(row == 0, 0.0, roll_up(up[b], 0))
        result[b] = total + jnp.where(row == row.shape[0] - 1, 0.0, roll_down(down[b], 0))
    return result


def face_entries(low_end, high_end, entering):
    row = iota(entering[0].shape, 0)
    return [
        entering[b]
        + jnp.where(row == 0, low_end[b], 0.0)
        + jnp.where(row == row.shape[0] - 1, high_end[b], 0.0)
        for b in range(2)
    ]


def spread(totals, ids):
    table = jnp.broadcast_to(totals, (8, LANES))
    if ids.ndim == 2:
        return jnp.take_along_axis(table, ids, axis=1)
    return jnp.stack(
        [jnp.take_along_axis(table, ids[x], axis=1) for x in range(ids.shape[0])], axis=0
    )


def as_ids(plane):
    return plane.astype(jnp.int32)


class Corner:
    def __init__(self, pack, which, base):
        self.pack, self.start = pack, base * 8 + which

    def row(self, number):
        at = self.start + number
        return self.pack[at // 8, at % 8 : at % 8 + 1, :]


def corners_of(faces, base, rows):
    found = []
    for y_face in (2, 3):
        for x_end in range(2):
            found.append(Corner(faces[y_face], x_end * rows, base))
    return found


def corner_inputs(corners, values):
    ends = {}
    for c in range(4):
        x_end, y_end = c % 2, c // 2
        over_x = product(corners[c].row, *values[c])
        over_y = product(lambda e, c=c: corners[c].row(SIDE_IN + e), *values[c])
        ends[(2 + y_end, x_end)] = over_x
        ends[(x_end, y_end)] = over_y
    return ends


def tile_sum(first, second):
    value = first[0] * second[0] + first[1] * second[1]
    return jnp.sum(jnp.sum(value, axis=0), axis=0, keepdims=True)


def list_wells(ids, present):
    depth = ids.shape[0]

    def smallest(planes):
        least = planes[0]
        for plane in planes[1:]:
            least = jnp.minimum(least, plane)
        return jnp.min(least)

    planes = [ids[x].astype(jnp.float32) for x in range(depth)]

    def one_well(state):
        number, well = state
        present[number] = well.astype(jnp.int32)
        after = [jnp.where(plane > well, plane, float(WELLS)) for plane in planes]
        return number + 1, smallest(after)

    number, _ = lax.while_loop(
        lambda state: state[1] < WELLS, one_well, (jnp.int32(1), smallest(planes))
    )
    present[0] = number - 1


def segment_rows(ids, values, scratch, present):
    scratch[...] = jnp.zeros_like(scratch)
    count, depth = values.shape[0], ids.shape[0]

    def one_well(step, _):
        well = present[step + 1]
        masks = [ids[x] == well for x in range(depth)]
        for number in range(count):
            total = jnp.where(masks[0], values[number, 0], 0.0)
            for x in range(1, depth):
                total = total + jnp.where(masks[x], values[number, x], 0.0)
            scratch[number, pl.ds(well, 1), :] = jnp.sum(total, axis=0, keepdims=True)
        return 0

    lax.fori_loop(0, present[0], one_well, 0)
    rows = []
    for number in range(count):
        summed = jnp.sum(scratch[number], axis=1, keepdims=True)
        shape = scratch.shape[1:]
        on_lanes = jnp.where(iota(shape, 0) == iota(shape, 1), summed, 0.0)
        rows.append(jnp.sum(on_lanes, axis=0, keepdims=True))
    return rows


def pack_rows(rows, table):
    for number, row in enumerate(rows):
        placed = row if number % 3 == 0 else pltpu.roll(row, WELLS * (number % 3), 1)
        table = table + jnp.where(
            iota(table.shape, 0) == number // 3, jnp.broadcast_to(placed, table.shape), 0.0
        )
    return table


def unpack_row(table, number):
    row = table[number // 3 : number // 3 + 1, :]
    if number % 3:
        row = pltpu.roll(row, LANES - WELLS * (number % 3), 1)
    return jnp.where(iota(row.shape, 1) < WELLS, row, 0.0)


def place_rows(rows, table):
    for number, row in enumerate(rows):
        group, k = divmod(number, RHS)
        at = k + RHS * (group // 3)
        placed = pltpu.roll(row, WELLS * group, 1) if group in (1, 2) else row
        table = table + jnp.where(
            iota(table.shape, 0) == at, jnp.broadcast_to(placed, table.shape), 0.0
        )
    return table


def place_columns(dots, first_lane, table):
    for number in range(dots.shape[0]):
        column = jnp.sum(dots[number], axis=1, keepdims=True)
        table = table + jnp.where(iota(table.shape, 1) == first_lane + number, column, 0.0)
    return table


def take_group(table, group):
    if group in (1, 2):
        table = pltpu.roll(table, LANES - WELLS * group, 1)
    start = RHS * (group // 3)
    rows = table[start : start + RHS, :]
    return jnp.where(iota(rows.shape, 1) < WELLS, rows, 0.0)


def take_column(table, lane):
    return table[RHS : 2 * RHS, lane : lane + 1]


def lane_sum(row):
    return jnp.sum(row, axis=1, keepdims=True)


COUPLINGS, DIAGONALS, WELL_FIELDS, IDS, RIGHT_SIDE, START = range(6)


def layer_blocks(cut, inward, lateral):
    def plane(n):
        if n < DIAGONAL:
            return cut(COUPLINGS, ((lateral, lateral + 1, 4, 5)[n // 4], n % 4), 0)
        if n < BACK_IN:
            return cut(DIAGONALS, (n - DIAGONAL,), 0)
        return cut(COUPLINGS, (inward, n - BACK_IN), 1)

    return plane


def fill_pack(pack, inward, lateral, cut):
    blocks = layer_blocks(cut, inward, lateral)
    for e in range(4):
        pack[e] = cut(COUPLINGS, (inward, e), 0)
    wells = [cut(WELL_FIELDS, (2 + a,), 0) for a in range(2)]
    for a in range(2):
        pack[WELL_EQ + a] = wells[a]
    pack[WELL_ID] = cut(IDS, (), 0).astype(jnp.float32)
    pack[BACK_ID] = cut(IDS, (), 1).astype(jnp.float32)
    for start, at in (
        (LAT_UP, UP_WELL),
        (LAT_DOWN, DOWN_WELL),
        (RISE, RISE_WELL),
        (FALL, FALL_WELL),
        (DIAGONAL, DIAGONAL_WELL),
        (BACK_IN, BACK_WELL),
    ):
        if start == BACK_IN:
            wells = [cut(WELL_FIELDS, (2 + a,), 1) for a in range(2)]
        for b, value in enumerate(product(lambda e: blocks(start + e), *wells)):
            pack[at + b] = value
    for k in range(RHS):
        here = [cut(START, (k, a), 0) for a in range(2)]
        back = [cut(START, (k, a), 1) for a in range(2)]
        entering = product(lambda e: blocks(BACK_IN + e), *back)
        local = face_stencil(blocks, here[0], here[1], entering)
        for a in range(2):
            pack[GUESS + 2 * k + a] = here[a]
            pack[REST + 2 * k + a] = cut(RIGHT_SIDE, (k, a), 0) - local[a]
    if pack.shape[0] > ENDS:
        end = pack.shape[1] - 1
        for e in range(4):
            pack[ENDS, e : e + 1, :] = blocks(LAT_UP + e)[end : end + 1, :]
            pack[ENDS, 4 + e : 5 + e, :] = blocks(LAT_DOWN + e)[0:1, :]


def x_pack_kernel(*refs):
    sources, packs, held_ends, arrived = refs[:6], refs[6:8], refs[8:20], refs[20]
    copies = []
    for n, source in enumerate(sources):
        lead = (slice(None),) * (len(source.shape) - 3)
        depth = source.shape[-3]
        for end, start in enumerate((0, depth - 2)):
            copies.append(
                pltpu.make_async_copy(
                    source.at[lead + (pl.ds(start, 2),)],
                    held_ends[2 * n + end],
                    arrived.at[2 * n + end],
                )
            )
    for copy in copies:
        copy.start()
    for copy in copies:
        copy.wait()
    for end, pack in enumerate(packs):
        fill_pack(
            pack,
            1 - end,
            2,
            lambda n, index, layer: held_ends[2 * n + end][
                index + (1 - layer if end else layer,)
            ],
        )


def y_cut(arguments, end):
    last = arguments[0].shape[-2] - 1

    def cut(n, index, layer):
        return arguments[n][index + (slice(None), last - layer if end else layer, slice(None))]

    return cut


def send_out(table, chunks, part, sent):
    chunks[...] = jnp.broadcast_to(table[None, : chunks.shape[1]], chunks.shape)
    copy = pltpu.make_async_copy(chunks, part, sent.at[0])
    copy.start()
    return copy


def corner_kernel(y_low, y_high, fxl, fxh, low_out, high_out):
    last = fxl.shape[1] - 1
    for own, out, at, side in ((y_low, low_out, 0, 4), (y_high, high_out, last, 0)):
        for n in range(FACE_PLANES):
            out[n] = own[n]
        row = FACE_PLANES * 8
        out[FACE_PLANES + CORNER_PLANES - 1] = jnp.zeros(out.shape[1:], jnp.float32)
        for face in (fxl, fxh):
            rows = [(n, at) for n in range(4)]
            rows += [(ENDS, side + e) for e in range(4)]
            rows += [(n, at) for n in range(WELL_EQ, REST)]
            for n, y in rows:
                out[row // 8, row % 8 : row % 8 + 1, :] = face[n, y : y + 1, :]
                row += 1


def image_corner_kernel(y_low, y_high, gxl, gxh, low_out, high_out):
    last = gxl.shape[1] - 1
    for own, out, at in ((y_low, low_out, 0), (y_high, high_out, last)):
        for n in range(IMAGE_PLANES):
            out[n] = own[n]
        for x_end, face in enumerate((gxl, gxh)):
            for n in range(8):
                out[IMAGE_PLANES + x_end, n : n + 1, :] = face[n, at : at + 1, :]


def guess_kernel(
    couplings, diagonal, wells, ids, right, guess,
    part, present, y_low, y_high, values, scratch, chunks, sent,
):
    list_wells(ids, present)
    for k in range(RHS):
        values[k] = wells[0] * guess[k, 0] + wells[1] * guess[k, 1]
    values[4] = wells[0] * wells[2] + wells[1] * wells[3]
    values[5] = wells[2] * wells[2] + wells[3] * wells[3]
    rows = segment_rows(ids, values, scratch, present)
    table = pack_rows(rows, jnp.zeros((8, LANES), jnp.float32))
    copy = send_out(table, chunks, part, sent)
    arguments = (couplings, diagonal, wells, ids, right, guess)
    for end, pack in enumerate((y_low, y_high)):
        fill_pack(pack, 3 - end, 0, y_cut(arguments, end))
    copy.wait()


def block_kernel(
    couplings, diagonal, right, guess, sent_face, rest, leaving, low_blocks, high_blocks
):
    nothing_enters = [[jnp.zeros(guess.shape[3:], jnp.float32)] * 2] * 4
    for k in range(RHS):
        inside, outgoing = block_stencil(
            couplings, diagonal, guess[k, 0], guess[k, 1], nothing_enters
        )
        for a in range(2):
            rest[k, a] = right[k, a] - inside[a]
            for f in range(4):
                leaving[f, 2 * k + a] = outgoing[f][a]
    for end, kept in enumerate((low_blocks, high_blocks)):
        blocks = layer_blocks(y_cut((couplings, diagonal), end), 3 - end, 0)
        for n in range(LAYER_BLOCKS):
            kept[n] = blocks(n)


def residual_kernel(
    couplings, diagonal, wells, ids, fxl, fxh, fyl, fyh, parts,
    rest, leaving, low_blocks, high_blocks,
    residual, image, residual_faces, x_low, x_high, y_low, y_high, small,
):
    faces = (fxl, fxh, fyl, fyh)
    totals = jnp.sum(parts[...], axis=0)
    corners = corners_of(faces, FACE_PLANES, CORNER_ROWS)
    all_ids = ids[...]
    face_ids = [as_ids(face[WELL_ID]) for face in faces]
    last = rest.shape[2] - 1
    row = iota(rest.shape[2:], 1)
    for k in range(RHS):
        s_row = unpack_row(totals, k)
        entering = [
            product(
                lambda e, f=f: faces[f][e],
                faces[f][GUESS + 2 * k],
                faces[f][GUESS + 2 * k + 1],
            )
            for f in range(4)
        ]
        outgoing = [[leaving[f, 2 * k + b] for b in range(2)] for f in range(4)]
        at_wells = spread(s_row, all_ids)
        now = []
        for a in range(2):
            value = rest[k, a] - wells[2 + a] * at_wells
            over_x = [
                (value[0] - entering[0][a])[None],
                value[1:last],
                (value[last] - entering[1][a])[None],
            ]
            value = jnp.concatenate(over_x, axis=0)
            value = value - jnp.where(row == 0, entering[2][a][:, None, :], 0.0)
            now.append(value - jnp.where(row == last, entering[3][a][:, None, :], 0.0))
        for a in range(2):
            residual[k, a] = now[a]
        ends = corner_inputs(
            corners,
            [[corners[c].row(SIDE_GUESS + 2 * k + a) for a in range(2)] for c in range(4)],
        )
        incoming = []
        for f in range(4):
            face = faces[f]
            there = face_entries(ends[(f, 0)], ends[(f, 1)], outgoing[f])
            face_wells = spread(s_row, face_ids[f])
            outer = [
                face[REST + 2 * k + a] - there[a] - face[WELL_EQ + a] * face_wells
                for a in range(2)
            ]
            for a in range(2):
                residual_faces[f, 2 * k + a] = outer[a]
            incoming.append(product(lambda e, f=f: faces[f][e], *outer))
        result, _ = block_stencil(couplings, diagonal, now[0], now[1], incoming)
        for a in range(2):
            image[k, a] = result[a]
        for pack, here, back, blocks in (
            (
                x_low,
                [value[0] for value in result],
                [value[1] for value in result],
                layer_blocks(lambda n, i, layer: (couplings, diagonal)[n][i + (layer,)], 1, 2),
            ),
            (
                x_high,
                [value[last] for value in result],
                [value[last - 1] for value in result],
                layer_blocks(
                    lambda n, i, layer: (couplings, diagonal)[n][i + (last - layer,)], 0, 2
                ),
            ),
            (
                y_low,
                [value[:, 0, :] for value in result],
                [value[:, 1, :] for value in result],
                lambda n: low_blocks[n],
            ),
            (
                y_high,
                [value[:, last, :] for value in result],
                [value[:, last - 1, :] for value in result],
                lambda n: high_blocks[n],
            ),
        ):
            entering = product(lambda e: blocks(BACK_IN + e), *back)
            local = face_stencil(blocks, here[0], here[1], entering)
            for a in range(2):
                pack[2 * k + a] = here[a]
                pack[8 + 2 * k + a] = local[a]
    small[...] = jnp.concatenate(
        [unpack_row(totals, 4), unpack_row(totals, 5), jnp.zeros((6, LANES), jnp.float32)], axis=0
    )


def moments_kernel(
    wells, ids, residual, image, present, part, values, scratch, dots, chunks, sent
):
    dots[...] = jnp.zeros_like(dots)
    for k in range(RHS):
        now = [residual[k, a] for a in range(2)]
        result = [image[k, a] for a in range(2)]
        for n, field in enumerate((now, result)):
            values[4 * n + k] = wells[0] * field[0] + wells[1] * field[1]
            values[8 + 4 * n + k] = wells[2] * field[0] + wells[3] * field[1]
        row = slice(RHS + k, RHS + k + 1)
        dots[0, row, :] = tile_sum(now, now)
        dots[1, row, :] = tile_sum(now, result)
        dots[2, row, :] = tile_sum(result, result)
    rows = segment_rows(ids, values, scratch, present)
    table = place_rows(rows, jnp.zeros((8, LANES), jnp.float32))
    send_out(place_columns(dots, WELLS, table), chunks, part, sent).wait()


def first_step(totals, small):
    s_row, us_row, p_row, ps_row = (take_group(totals, group) for group in range(4))
    within, equation = small[0:1, :], small[1:2, :]
    rr, rs, ss = (take_column(totals, WELLS + i) for i in range(3))
    height = (rs + lane_sum(p_row * s_row)) / rr
    square = ss + lane_sum(2.0 * ps_row * s_row + equation * s_row * s_row)
    left = jnp.maximum(square - height * height * rr, 1e-7 * square)
    scale = lax.rsqrt(left)
    s_image = us_row + within * s_row
    s_second = (s_image - height * s_row) * scale
    p_second = (ps_row + equation * s_row - height * p_row) * scale
    shift = rs / rr + lane_sum(p_second * s_second)
    unit = lax.rsqrt(rr)
    following = left * scale * unit
    return s_row, s_image, p_row, p_second, (unit, rr * unit, height, shift, following, scale)


def krylov_kernel(
    couplings, diagonal, wells, ids, fxl, fxh, fyl, fyh, gxl, gxh, gyl, gyh,
    residual, image, residual_faces, parts, small_in, present,
    second_out, third_out, part, known, scratch, values_scratch, dots,
):
    faces, sent = (fxl, fxh, fyl, fyh), (gxl, gxh, gyl, gyh)
    totals = jnp.sum(parts[...], axis=0)
    small = small_in[...]
    s_rows, s_images, p_rows, p_seconds, scalars = first_step(totals, small)
    known[0:RHS, :] = p_rows
    known[RHS : 2 * RHS, :] = p_seconds
    columns = jnp.zeros((RHS, LANES), jnp.float32)
    for n, column in enumerate(scalars):
        columns = columns + jnp.where(iota(columns.shape, 1) == n, column, 0.0)
    known[2 * RHS : 3 * RHS, :] = columns
    known[3 * RHS :, :] = jnp.broadcast_to(small[1:2, :], (RHS, LANES))
    dots[...] = jnp.zeros_like(dots)
    corners = corners_of(faces, FACE_PLANES, CORNER_ROWS)
    sent_corners = corners_of(sent, IMAGE_PLANES, 8)
    all_ids = ids[...]
    face_ids = [as_ids(face[WELL_ID]) for face in faces]
    back_ids = [as_ids(face[BACK_ID]) for face in faces]
    corner_ids = [
        as_ids(jnp.broadcast_to(corner.row(SIDE_ID), (8, LANES))) for corner in corners
    ]
    for k in range(RHS):
        unit, _, height, shift, _, scale = (column[k : k + 1, :] for column in scalars)
        s_row, s_image = s_rows[k : k + 1, :], s_images[k : k + 1, :]
        at_wells = spread(s_row, all_ids)
        now = [image[k, a] + wells[2 + a] * at_wells for a in range(2)]
        face_now, spread_now = [], []
        for f in range(4):
            here = spread(s_row, face_ids[f])
            spread_now.append((here, spread(s_row, back_ids[f])))
            face_now.append(
                [sent[f][2 * k + a] + faces[f][WELL_EQ + a] * here for a in range(2)]
            )
        corner_now = []
        for c in range(4):
            here = spread(s_row, corner_ids[c])[0:1, :]
            corner_now.append(
                [
                    sent_corners[c].row(2 * k + a) + corners[c].row(SIDE_EQ + a) * here
                    for a in range(2)
                ]
            )
        incoming = [product(lambda e, f=f: faces[f][e], *face_now[f]) for f in range(4)]
        applied, outgoing = block_stencil(couplings, diagonal, now[0], now[1], incoming)
        at_wells = spread(s_image, all_ids)
        second, third = [], []
        for a in range(2):
            twice = applied[a] + wells[2 + a] * at_wells
            base = (now[a] - height * residual[k, a]) * scale
            second.append(base)
            third.append((twice - height * now[a]) * scale - shift * base)
            second_out[k, a] = second[a]
            third_out[k, a] = third[a]
        ends = corner_inputs(corners, corner_now)
        incoming = []
        for f in range(4):
            face = faces[f]
            here, behind = spread_now[f]
            moves = [
                [face[at + b] * here for b in range(2)]
                for at in (DIAGONAL_WELL, UP_WELL, DOWN_WELL, RISE_WELL, FALL_WELL)
            ]
            there = face_moves(*moves, [face[BACK_WELL + b] * behind for b in range(2)])
            local = [sent[f][8 + 2 * k + b] + there[b] for b in range(2)]
            over = face_entries(ends[(f, 0)], ends[(f, 1)], outgoing[f])
            here = spread(s_image, face_ids[f])
            outer = []
            for a in range(2):
                twice = local[a] + over[a] + face[WELL_EQ + a] * here
                base = (face_now[f][a] - height * residual_faces[f, 2 * k + a]) * scale
                outer.append((twice - height * face_now[f][a]) * scale - shift * base)
            incoming.append(product(lambda e, f=f: faces[f][e], *outer))
        result, _ = block_stencil(couplings, diagonal, third[0], third[1], incoming)
        fourth = [result[a] - shift * third[a] for a in range(2)]
        values_scratch[k] = wells[0] * third[0] + wells[1] * third[1]
        values_scratch[4 + k] = wells[2] * third[0] + wells[3] * third[1]
        values_scratch[8 + k] = wells[2] * fourth[0] + wells[3] * fourth[1]
        fields = [[residual[k, a] * unit for a in range(2)], second, third, fourth]
        number = 0
        for i in range(4):
            for j in range(i, 4):
                dots[number, RHS + k : RHS + k + 1, :] = tile_sum(fields[i], fields[j])
                number += 1
    rows = segment_rows(ids, values_scratch, scratch, present)
    table = place_rows(rows, jnp.zeros((8, LANES), jnp.float32))
    table = place_columns(dots, 0, table)
    gram = table[RHS : RHS + 1, :]
    for k in range(1, RHS):
        gram = gram + pltpu.roll(table[RHS + k : RHS + k + 1, :], GRAM_ENTRIES * k, 1)
    flat = jnp.concatenate([table[k : k + 1, :] for k in range(RHS)] + [gram], axis=1)
    part[...] = jnp.broadcast_to(flat[None], part.shape)


def solve_kernel(guess, residual, second, third, parts, known, solution):
    flat = jnp.sum(parts[...], axis=0)
    rows = [flat[:, LANES * n : LANES * (n + 1)] for n in range(RHS + 1)]
    for k in range(1, RHS):
        rows.append(pltpu.roll(rows[RHS], LANES - GRAM_ENTRIES * k, 1))
    totals = jnp.concatenate(rows, axis=0)
    s_third, p_third, p_fourth = (take_group(totals, group) for group in range(3))
    p_first, p_second = known[0:RHS, :], known[RHS : 2 * RHS, :]
    unit, beta, height, shift, following = (
        known[2 * RHS : 3 * RHS, n : n + 1] for n in range(5)
    )
    equation = known[3 * RHS :, :]
    gram = {}
    number = 0
    for i in range(4):
        for j in range(i, 4):
            gram[(i, j)] = take_column(totals, number)
            number += 1
    gram[(0, 3)] += lane_sum(p_first * s_third) * unit
    gram[(1, 3)] += lane_sum(p_second * s_third)
    gram[(2, 3)] += lane_sum(p_third * s_third)
    gram[(3, 3)] += lane_sum(2.0 * p_fourth * s_third + equation * s_third * s_third)
    tiny = 1e-30
    inverse = [lax.rsqrt(jnp.maximum(gram[(i, i)], tiny)) for i in range(4)]
    length = [jnp.maximum(gram[(i, i)], tiny) * inverse[i] for i in range(4)]
    upper = {}
    for i in range(4):
        for j in range(i, 4):
            entry = gram[(i, j)] * inverse[i] * inverse[j]
            for m in range(i):
                entry = entry - upper[(m, i)] * upper[(m, j)]
            if i == j:
                pivot = lax.rsqrt(jnp.maximum(entry, 1e-6))
                upper[(i, i)] = jnp.maximum(entry, 1e-6) * pivot
                over = pivot
            else:
                upper[(i, j)] = entry * over
    columns = [
        [(0, height * length[0]), (1, following * length[1])],
        [(1, shift * length[1]), (2, length[2])],
        [(2, shift * length[2]), (3, length[3])],
    ]
    zero = jnp.zeros_like(shift)
    hessenberg = [[zero] * 3 for _ in range(4)]
    for j in range(3):
        for i in range(j + 2):
            for m, factor in columns[j]:
                if m >= i:
                    hessenberg[i][j] = hessenberg[i][j] + upper[(i, m)] * factor
    target = [beta * length[0] * upper[(0, 0)], zero, zero, zero]
    turns = []
    for j in range(3):
        top, bottom = hessenberg[j][j], hessenberg[j + 1][j]
        turn = lax.rsqrt(top * top + bottom * bottom)
        turns.append(turn)
        cosine, sine = top * turn, bottom * turn
        for m in range(j, 3):
            high, low = hessenberg[j][m], hessenberg[j + 1][m]
            hessenberg[j][m] = cosine * high + sine * low
            hessenberg[j + 1][m] = cosine * low - sine * high
        high, low = target[j], target[j + 1]
        target[j] = cosine * high + sine * low
        target[j + 1] = cosine * low - sine * high
    weights = [zero] * 3
    for i in (2, 1, 0):
        value = target[i]
        for j in range(i + 1, 3):
            value = value - hessenberg[i][j] * weights[j]
        weights[i] = value * turns[i]
    for k in range(RHS):
        on_first, on_second, on_third = (
            column[k : k + 1, :] for column in (weights[0] * unit, weights[1], weights[2])
        )
        for a in range(2):
            solution[k, a] = (
                guess[k, a]
                + on_first * residual[k, a]
                + on_second * second[k, a]
                + on_third * third[k, a]
            )


def call(kernel, shapes, arguments, scratch=(), own_copies=False, cost=0, grant=24 << 20, out=0):
    whole = pl.BlockSpec(memory_space=pltpu.VMEM)
    far = pl.BlockSpec(memory_space=pltpu.HBM)
    scalars = pl.BlockSpec(memory_space=pltpu.SMEM)

    def place(array):
        if len(array.shape) == 1:
            return scalars
        return far if own_copies else whole

    outs = [
        jax.ShapeDtypeStruct(shape, jnp.float32 if len(shape) > 1 else jnp.int32)
        for shape in shapes
    ]
    outs[:out] = [pltpu.HBM(shape, jnp.float32) for shape in shapes[:out]]
    return pl.pallas_call(
        kernel,
        out_shape=outs,
        in_specs=[place(argument) for argument in arguments],
        out_specs=[far] * out + [scalars if len(shape) == 1 else whole for shape in shapes[out:]],
        scratch_shapes=list(scratch),
        compiler_params=pltpu.CompilerParams(vmem_limit_bytes=grant),
        cost_estimate=pl.CostEstimate(flops=cost, bytes_accessed=cost, transcendentals=0)
        if cost
        else None,
    )(*arguments)


def nothing(value, *rest):
    pass


def after(value, *others):
    far = pl.BlockSpec(memory_space=pltpu.HBM)
    near = pl.BlockSpec(memory_space=pltpu.VMEM)
    return pl.pallas_call(
        nothing,
        out_shape=pltpu.HBM(value.shape, value.dtype),
        in_specs=[far] + [near] * len(others),
        out_specs=far,
        input_output_aliases={0: 0},
        compiler_params=pltpu.CompilerParams(vmem_limit_bytes=1 << 20),
    )(pltpu.with_memory_space_constraint(value, pltpu.HBM), *others)


def held(*shape):
    return pltpu.VMEM(shape, jnp.float32)


def from_behind(value, axis, steps):
    count = lax.axis_size(axis)
    leading, last = (max(0, -steps), min(count, count - steps))
    return lax.ppermute(value, axis, [(source, source + steps) for source in range(leading, last)])


def exchanged(part):
    return lax.all_to_all(part, ("gx", "gy"), 0, 0, tiled=True)


def body(couplings, diagonal, wells, ids, right, guess):
    devices = lax.axis_size("gx") * lax.axis_size("gy")
    plane = (8, LANES)
    field = guess.shape
    block = guess.shape[2:]
    arguments = (couplings, diagonal, wells, ids, right, guess)

    ends = []
    for argument in arguments:
        shape = argument.shape[:-3] + (2,) + argument.shape[-2:]
        ends += [pltpu.VMEM(shape, argument.dtype)] * 2
    x_low, x_high = call(
        x_pack_kernel,
        [(FACE_PLANES + 1,) + plane] * 2,
        [pltpu.with_memory_space_constraint(argument, pltpu.HBM) for argument in arguments],
        ends + [pltpu.SemaphoreType.DMA((len(ends),))],
        own_copies=True,
    )
    fxl = from_behind(x_high, "gx", 1)
    fxh = from_behind(x_low, "gx", -1)
    first_chunks, chunks = (devices, TABLE_ROWS, LANES), (devices, 8, LANES)
    sent = pltpu.SemaphoreType.DMA((1,))
    part, present, y_low, y_high = call(
        guess_kernel,
        [first_chunks, (WELLS + 1,)] + [(FACE_PLANES,) + plane] * 2,
        arguments,
        [held(6, *block), held(6, WELLS, LANES), held(*first_chunks), sent],
        cost=4 << 20,
        out=1,
    )
    parts = exchanged(after(part, fxl))
    y_low, y_high = call(
        corner_kernel,
        [(FACE_PLANES + CORNER_PLANES,) + plane] * 2,
        (y_low, y_high, fxl, fxh),
    )
    fyl = from_behind(y_high, "gy", 1)
    fyh = from_behind(y_low, "gy", -1)

    ahead = call(
        block_kernel,
        [field, (4, 8) + plane] + [(LAYER_BLOCKS,) + plane] * 2,
        (couplings, diagonal, right, guess, y_low),
        cost=4 << 20,
    )

    faces = (fxl, fxh, fyl, fyh)
    residual, image, residual_faces, x_low, x_high, y_low, y_high, small = call(
        residual_kernel,
        [field, field, (4, 8) + plane] + [(IMAGE_PLANES,) + plane] * 4 + [(8, LANES)],
        (couplings, diagonal, wells, ids) + faces + (parts, *ahead),
    )
    gxl = from_behind(x_high, "gx", 1)
    gxh = from_behind(x_low, "gx", -1)
    (part,) = call(
        moments_kernel,
        [chunks],
        (wells, ids, residual, image, present),
        [held(16, *block), held(16, WELLS, LANES), held(3, *plane), held(*chunks), sent],
        cost=4 << 20,
        out=1,
    )
    parts = exchanged(after(part, gxl, gxh))
    y_low, y_high = call(
        image_corner_kernel,
        [(IMAGE_PLANES + 2,) + plane] * 2,
        (y_low, y_high, gxl, gxh),
    )
    gyl = from_behind(y_high, "gy", 1)
    gyh = from_behind(y_low, "gy", -1)

    second, third, part, known = call(
        krylov_kernel,
        [field, field, (devices, 1, (RHS + 1) * LANES), (4 * RHS, LANES)],
        (couplings, diagonal, wells, ids) + faces + (gxl, gxh, gyl, gyh)
        + (residual, image, residual_faces, parts, small, present),
        [held(12, WELLS, LANES), held(12, *block), held(10, *plane)],
    )
    parts = exchanged(part)
    (result,) = call(
        solve_kernel,
        [field],
        (guess, residual, second, third, parts, known),
    )
    return result


def solution(mesh):
    in_specs = (
        P("member", None, "gx", "gy", None),
        P("member", "gx", "gy", None),
        P("member", "gx", "gy", None),
        P("gx", "gy", None),
        P("member", None, "gx", "gy", None),
        P("member", None, "gx", "gy", None),
    )
    out_specs = P("member", None, "gx", "gy", None)
    return jax.shard_map(body, mesh=mesh, in_specs=in_specs, out_specs=out_specs, check_vma=False)
```

```python
import jax
import jax.numpy as jnp
from jax import lax
from jax.experimental import pallas as pl
from jax.experimental.pallas import tpu as pltpu
from jax.sharding import PartitionSpec as P

WELLS = 40
RHS = 4
LANES = 128
WELL_EQ, WELL_ID, GUESS, REST = 4, 6, 7, 15
UP_WELL, DOWN_WELL, RISE_WELL, FALL_WELL, DIAGONAL_WELL = 23, 25, 27, 29, 31
BACK_WELL, BACK_ID = 33, 35
FACE_PLANES = 36
ENDS = 36
CORNER_PLANES = 5
LAT_UP, LAT_DOWN, RISE, FALL, DIAGONAL, BACK_IN = 0, 4, 8, 12, 16, 20
LAYER_BLOCKS = 24
IMAGE_PLANES = 16
TABLE_ROWS = 6
GRAM_ENTRIES = 10
CORNER_ROWS = 19
SIDE_IN, SIDE_EQ, SIDE_ID, SIDE_GUESS = 4, 8, 10, 11


def product(blocks, first, second):
    return [
        blocks(0) * first + blocks(2) * second,
        blocks(1) * first + blocks(3) * second,
    ]


def iota(shape, axis):
    return lax.broadcasted_iota(jnp.int32, shape, axis)


def roll_up(value, axis):
    return pltpu.roll(value, 1, axis)


def roll_down(value, axis):
    return pltpu.roll(value, value.shape[axis] - 1, axis)


def layer_moves(rising, falling):
    axis = rising.ndim - 1
    lane = iota(rising.shape, axis)
    up = jnp.where(lane == 0, 0.0, roll_up(rising, axis))
    down = jnp.where(lane == LANES - 1, 0.0, roll_down(falling, axis))
    return up + down


def block_stencil(couplings, diagonal, first, second, incoming):
    result = product(lambda e: diagonal[e], first, second)
    moved = [product(lambda e, d=d: couplings[d, e], first, second) for d in range(6)]
    row = iota(first.shape, 1)
    outgoing = [[], [], [], []]
    for b in range(2):
        east, west, north, south, rise, fall = (moved[d][b] for d in range(6))
        total = result[b] + jnp.concatenate([incoming[0][b][None], east[:-1]], axis=0)
        total = total + jnp.concatenate([west[1:], incoming[1][b][None]], axis=0)
        total = total + jnp.where(row == 0, incoming[2][b][:, None, :], roll_up(north, 1))
        total = total + jnp.where(
            row == row.shape[1] - 1, incoming[3][b][:, None, :], roll_down(south, 1)
        )
        result[b] = total + layer_moves(rise, fall)
        outgoing[0].append(west[0])
        outgoing[1].append(east[-1])
        outgoing[2].append(south[:, 0, :])
        outgoing[3].append(north[:, -1, :])
    return result, outgoing


def face_stencil(blocks, first, second, behind):
    def times(start):
        return product(lambda e: blocks(start + e), first, second)

    moves = [times(start) for start in (DIAGONAL, LAT_UP, LAT_DOWN, RISE, FALL)]
    return face_moves(*moves, behind)


def face_moves(kept, up, down, rise, fall, behind):
    result = list(kept)
    row = iota(kept[0].shape, 0)
    for b in range(2):
        total = result[b] + behind[b] + layer_moves(rise[b], fall[b])
        total = total + jnp.where(row == 0, 0.0, roll_up(up[b], 0))
        result[b] = total + jnp.where(row == row.shape[0] - 1, 0.0, roll_down(down[b], 0))
    return result


def face_entries(low_end, high_end, entering):
    row = iota(entering[0].shape, 0)
    return [
        entering[b]
        + jnp.where(row == 0, low_end[b], 0.0)
        + jnp.where(row == row.shape[0] - 1, high_end[b], 0.0)
        for b in range(2)
    ]


def spread(totals, ids):
    table = jnp.broadcast_to(totals, (8, LANES))
    if ids.ndim == 2:
        return jnp.take_along_axis(table, ids, axis=1)
    return jnp.stack(
        [jnp.take_along_axis(table, ids[x], axis=1) for x in range(ids.shape[0])], axis=0
    )


def as_ids(plane):
    return plane.astype(jnp.int32)


class Corner:
    def __init__(self, pack, which, base):
        self.pack, self.start = pack, base * 8 + which

    def row(self, number):
        at = self.start + number
        return self.pack[at // 8, at % 8 : at % 8 + 1, :]


def corners_of(faces, base, rows):
    found = []
    for y_face in (2, 3):
        for x_end in range(2):
            found.append(Corner(faces[y_face], x_end * rows, base))
    return found


def corner_inputs(corners, values):
    ends = {}
    for c in range(4):
        x_end, y_end = c % 2, c // 2
        over_x = product(corners[c].row, *values[c])
        over_y = product(lambda e, c=c: corners[c].row(SIDE_IN + e), *values[c])
        ends[(2 + y_end, x_end)] = over_x
        ends[(x_end, y_end)] = over_y
    return ends


def tile_sum(first, second):
    value = first[0] * second[0] + first[1] * second[1]
    return jnp.sum(jnp.sum(value, axis=0), axis=0, keepdims=True)


def list_wells(ids, present):
    planes = [ids[x].astype(jnp.float32) for x in range(ids.shape[0])]
    middle = WELLS // 2
    halves = ((0.0, float(middle)), (float(middle), float(WELLS)))

    def least(above, top):
        found = [jnp.where((p > above) & (p < top), p, top) for p in planes]
        value = found[0]
        for other in found[1:]:
            value = jnp.minimum(value, other)
        return jnp.min(value)

    def greatest(base, below):
        found = [jnp.where((p >= base) & (p < below), p, base - 1.0) for p in planes]
        value = found[0]
        for other in found[1:]:
            value = jnp.maximum(value, other)
        return jnp.max(value)

    def some_left(state):
        return (state[1] <= state[2]) | (state[3] <= state[4])

    def step(state):
        number, ends = state[0], state[1:]
        after = []
        for half, (base, top) in enumerate(halves):
            low, high = ends[2 * half], ends[2 * half + 1]
            present[number] = low.astype(jnp.int32)
            number = number + jnp.where(low <= high, 1, 0)
            present[number] = high.astype(jnp.int32)
            number = number + jnp.where(low < high, 1, 0)
            after += [least(low, top), greatest(base, high)]
        return (number, *after)

    ends = []
    for base, top in halves:
        ends += [least(base - 1.0, top), greatest(base, top)]
    state = lax.while_loop(some_left, step, (jnp.int32(1), *ends))
    present[0] = state[0] - 1


def segment_rows(ids, values, scratch, present):
    scratch[...] = jnp.zeros_like(scratch)
    count, depth = values.shape[0], ids.shape[0]

    def one_well(step, _):
        well = present[step + 1]
        masks = [ids[x] == well for x in range(depth)]
        for number in range(count):
            total = jnp.where(masks[0], values[number, 0], 0.0)
            for x in range(1, depth):
                total = total + jnp.where(masks[x], values[number, x], 0.0)
            scratch[number, pl.ds(well, 1), :] = jnp.sum(total, axis=0, keepdims=True)
        return 0

    lax.fori_loop(0, present[0], one_well, 0)
    rows = []
    for number in range(count):
        summed = jnp.sum(scratch[number], axis=1, keepdims=True)
        shape = scratch.shape[1:]
        on_lanes = jnp.where(iota(shape, 0) == iota(shape, 1), summed, 0.0)
        rows.append(jnp.sum(on_lanes, axis=0, keepdims=True))
    return rows


def pack_rows(rows, table):
    for number, row in enumerate(rows):
        placed = row if number % 3 == 0 else pltpu.roll(row, WELLS * (number % 3), 1)
        table = table + jnp.where(
            iota(table.shape, 0) == number // 3, jnp.broadcast_to(placed, table.shape), 0.0
        )
    return table


def unpack_row(table, number):
    row = table[number // 3 : number // 3 + 1, :]
    if number % 3:
        row = pltpu.roll(row, LANES - WELLS * (number % 3), 1)
    return jnp.where(iota(row.shape, 1) < WELLS, row, 0.0)


def place_rows(rows, table):
    for number, row in enumerate(rows):
        group, k = divmod(number, RHS)
        at = k + RHS * (group // 3)
        placed = pltpu.roll(row, WELLS * group, 1) if group in (1, 2) else row
        table = table + jnp.where(
            iota(table.shape, 0) == at, jnp.broadcast_to(placed, table.shape), 0.0
        )
    return table


def place_columns(dots, first_lane, table):
    for number in range(dots.shape[0]):
        column = jnp.sum(dots[number], axis=1, keepdims=True)
        table = table + jnp.where(iota(table.shape, 1) == first_lane + number, column, 0.0)
    return table


def take_group(table, group):
    if group in (1, 2):
        table = pltpu.roll(table, LANES - WELLS * group, 1)
    start = RHS * (group // 3)
    rows = table[start : start + RHS, :]
    return jnp.where(iota(rows.shape, 1) < WELLS, rows, 0.0)


def take_column(table, lane):
    return table[RHS : 2 * RHS, lane : lane + 1]


def lane_sum(row):
    return jnp.sum(row, axis=1, keepdims=True)


def on_even(axis):
    return lax.rem(lax.axis_index(axis), 2) == 0


def by_pair(axis, low, high, first, second):
    @pl.when(on_even(axis))
    def _():
        first[...] = high[...]
        second[...] = low[...]

    @pl.when(jnp.logical_not(on_even(axis)))
    def _():
        first[...] = low[...]
        second[...] = high[...]


def by_side(axis, first, second, low, high):
    by_pair(axis, second, first, high, low)


COUPLINGS, DIAGONALS, WELL_FIELDS, IDS, RIGHT_SIDE, START = range(6)


def layer_blocks(cut, inward, lateral):
    def plane(n):
        if n < DIAGONAL:
            return cut(COUPLINGS, ((lateral, lateral + 1, 4, 5)[n // 4], n % 4), 0)
        if n < BACK_IN:
            return cut(DIAGONALS, (n - DIAGONAL,), 0)
        return cut(COUPLINGS, (inward, n - BACK_IN), 1)

    return plane


def fill_pack(pack, inward, lateral, cut):
    blocks = layer_blocks(cut, inward, lateral)
    for e in range(4):
        pack[e] = cut(COUPLINGS, (inward, e), 0)
    wells = [cut(WELL_FIELDS, (2 + a,), 0) for a in range(2)]
    for a in range(2):
        pack[WELL_EQ + a] = wells[a]
    pack[WELL_ID] = cut(IDS, (), 0).astype(jnp.float32)
    pack[BACK_ID] = cut(IDS, (), 1).astype(jnp.float32)
    for start, at in (
        (LAT_UP, UP_WELL),
        (LAT_DOWN, DOWN_WELL),
        (RISE, RISE_WELL),
        (FALL, FALL_WELL),
        (DIAGONAL, DIAGONAL_WELL),
        (BACK_IN, BACK_WELL),
    ):
        if start == BACK_IN:
            wells = [cut(WELL_FIELDS, (2 + a,), 1) for a in range(2)]
        for b, value in enumerate(product(lambda e: blocks(start + e), *wells)):
            pack[at + b] = value
    for k in range(RHS):
        here = [cut(START, (k, a), 0) for a in range(2)]
        back = [cut(START, (k, a), 1) for a in range(2)]
        entering = product(lambda e: blocks(BACK_IN + e), *back)
        local = face_stencil(blocks, here[0], here[1], entering)
        for a in range(2):
            pack[GUESS + 2 * k + a] = here[a]
            pack[REST + 2 * k + a] = cut(RIGHT_SIDE, (k, a), 0) - local[a]
    if pack.shape[0] > ENDS:
        end = pack.shape[1] - 1
        for e in range(4):
            pack[ENDS, e : e + 1, :] = blocks(LAT_UP + e)[end : end + 1, :]
            pack[ENDS, 4 + e : 5 + e, :] = blocks(LAT_DOWN + e)[0:1, :]


def x_pack_kernel(*refs):
    sources, first, second, held_ends, arrived = refs[:6], refs[6], refs[7], refs[8:20], refs[20]
    packs = refs[21:23]
    copies = []
    for n, source in enumerate(sources):
        lead = (slice(None),) * (len(source.shape) - 3)
        depth = source.shape[-3]
        for end, start in enumerate((0, depth - 2)):
            copies.append(
                pltpu.make_async_copy(
                    source.at[lead + (pl.ds(start, 2),)],
                    held_ends[2 * n + end],
                    arrived.at[2 * n + end],
                )
            )
    for copy in copies:
        copy.start()
    for copy in copies:
        copy.wait()
    for end, pack in enumerate(packs):
        fill_pack(
            pack,
            1 - end,
            2,
            lambda n, index, layer: held_ends[2 * n + end][
                index + (1 - layer if end else layer,)
            ],
        )
    by_pair("gx", *packs, first, second)


def y_cut(arguments, end):
    last = arguments[0].shape[-2] - 1

    def cut(n, index, layer):
        return arguments[n][index + (slice(None), last - layer if end else layer, slice(None))]

    return cut


def send_out(table, chunks, part, sent):
    chunks[...] = jnp.broadcast_to(table[None, : chunks.shape[1]], chunks.shape)
    copy = pltpu.make_async_copy(chunks, part, sent.at[0])
    copy.start()
    return copy


def corner_kernel(y_low, y_high, came_first, came_second, first, second, fxl, fxh, *outs):
    by_side("gx", came_first, came_second, fxl, fxh)
    last = fxl.shape[1] - 1
    for own, out, at, side in ((y_low, outs[0], 0, 4), (y_high, outs[1], last, 0)):
        for n in range(FACE_PLANES):
            out[n] = own[n]
        row = FACE_PLANES * 8
        out[FACE_PLANES + CORNER_PLANES - 1] = jnp.zeros(out.shape[1:], jnp.float32)
        for face in (fxl, fxh):
            rows = [(n, at) for n in range(4)]
            rows += [(ENDS, side + e) for e in range(4)]
            rows += [(n, at) for n in range(WELL_EQ, REST)]
            for n, y in rows:
                out[row // 8, row % 8 : row % 8 + 1, :] = face[n, y : y + 1, :]
                row += 1
    by_pair("gy", *outs, first, second)


def image_corner_kernel(y_low, y_high, came_first, came_second, first, second, gxl, gxh, *outs):
    by_side("gx", came_first, came_second, gxl, gxh)
    last = gxl.shape[1] - 1
    for own, out, at in ((y_low, outs[0], 0), (y_high, outs[1], last)):
        for n in range(IMAGE_PLANES):
            out[n] = own[n]
        for x_end, face in enumerate((gxl, gxh)):
            for n in range(8):
                out[IMAGE_PLANES + x_end, n : n + 1, :] = face[n, at : at + 1, :]
    by_pair("gy", *outs, first, second)


def guess_kernel(
    couplings, diagonal, wells, ids, right, guess,
    part, present, y_low, y_high, values, scratch, chunks, sent,
):
    list_wells(ids, present)
    for k in range(RHS):
        values[k] = wells[0] * guess[k, 0] + wells[1] * guess[k, 1]
    values[4] = wells[0] * wells[2] + wells[1] * wells[3]
    values[5] = wells[2] * wells[2] + wells[3] * wells[3]
    rows = segment_rows(ids, values, scratch, present)
    table = pack_rows(rows, jnp.zeros((8, LANES), jnp.float32))
    copy = send_out(table, chunks, part, sent)
    arguments = (couplings, diagonal, wells, ids, right, guess)
    for end, pack in enumerate((y_low, y_high)):
        fill_pack(pack, 3 - end, 0, y_cut(arguments, end))
    copy.wait()


def block_kernel(
    couplings, diagonal, right, guess, sent_face, rest, leaving, low_blocks, high_blocks
):
    nothing_enters = [[jnp.zeros(guess.shape[3:], jnp.float32)] * 2] * 4
    for k in range(RHS):
        inside, outgoing = block_stencil(
            couplings, diagonal, guess[k, 0], guess[k, 1], nothing_enters
        )
        for a in range(2):
            rest[k, a] = right[k, a] - inside[a]
            for f in range(4):
                leaving[f, 2 * k + a] = outgoing[f][a]
    for end, kept in enumerate((low_blocks, high_blocks)):
        blocks = layer_blocks(y_cut((couplings, diagonal), end), 3 - end, 0)
        for n in range(LAYER_BLOCKS):
            kept[n] = blocks(n)


def residual_kernel(
    couplings, diagonal, wells, ids, fxl, fxh, came_first, came_second, parts,
    rest, leaving, low_blocks, high_blocks,
    residual, image, residual_faces, x_first, x_second, y_low, y_high, small, fyl, fyh,
    x_low, x_high,
):
    by_side("gy", came_first, came_second, fyl, fyh)
    faces = (fxl, fxh, fyl, fyh)
    totals = jnp.sum(parts[...], axis=0)
    corners = corners_of(faces, FACE_PLANES, CORNER_ROWS)
    all_ids = ids[...]
    face_ids = [as_ids(face[WELL_ID]) for face in faces]
    last = rest.shape[2] - 1
    row = iota(rest.shape[2:], 1)
    for k in range(RHS):
        s_row = unpack_row(totals, k)
        entering = [
            product(
                lambda e, f=f: faces[f][e],
                faces[f][GUESS + 2 * k],
                faces[f][GUESS + 2 * k + 1],
            )
            for f in range(4)
        ]
        outgoing = [[leaving[f, 2 * k + b] for b in range(2)] for f in range(4)]
        at_wells = spread(s_row, all_ids)
        now = []
        for a in range(2):
            value = rest[k, a] - wells[2 + a] * at_wells
            over_x = [
                (value[0] - entering[0][a])[None],
                value[1:last],
                (value[last] - entering[1][a])[None],
            ]
            value = jnp.concatenate(over_x, axis=0)
            value = value - jnp.where(row == 0, entering[2][a][:, None, :], 0.0)
            now.append(value - jnp.where(row == last, entering[3][a][:, None, :], 0.0))
        for a in range(2):
            residual[k, a] = now[a]
        ends = corner_inputs(
            corners,
            [[corners[c].row(SIDE_GUESS + 2 * k + a) for a in range(2)] for c in range(4)],
        )
        incoming = []
        for f in range(4):
            face = faces[f]
            there = face_entries(ends[(f, 0)], ends[(f, 1)], outgoing[f])
            face_wells = spread(s_row, face_ids[f])
            outer = [
                face[REST + 2 * k + a] - there[a] - face[WELL_EQ + a] * face_wells
                for a in range(2)
            ]
            for a in range(2):
                residual_faces[f, 2 * k + a] = outer[a]
            incoming.append(product(lambda e, f=f: faces[f][e], *outer))
        result, _ = block_stencil(couplings, diagonal, now[0], now[1], incoming)
        for a in range(2):
            image[k, a] = result[a]
        for pack, here, back, blocks in (
            (
                x_low,
                [value[0] for value in result],
                [value[1] for value in result],
                layer_blocks(lambda n, i, layer: (couplings, diagonal)[n][i + (layer,)], 1, 2),
            ),
            (
                x_high,
                [value[last] for value in result],
                [value[last - 1] for value in result],
                layer_blocks(
                    lambda n, i, layer: (couplings, diagonal)[n][i + (last - layer,)], 0, 2
                ),
            ),
            (
                y_low,
                [value[:, 0, :] for value in result],
                [value[:, 1, :] for value in result],
                lambda n: low_blocks[n],
            ),
            (
                y_high,
                [value[:, last, :] for value in result],
                [value[:, last - 1, :] for value in result],
                lambda n: high_blocks[n],
            ),
        ):
            entering = product(lambda e: blocks(BACK_IN + e), *back)
            local = face_stencil(blocks, here[0], here[1], entering)
            for a in range(2):
                pack[2 * k + a] = here[a]
                pack[8 + 2 * k + a] = local[a]
    by_pair("gx", x_low, x_high, x_first, x_second)
    small[...] = jnp.concatenate(
        [unpack_row(totals, 4), unpack_row(totals, 5), jnp.zeros((6, LANES), jnp.float32)], axis=0
    )


def moments_kernel(
    wells, ids, residual, image, present, part, values, scratch, dots, chunks, sent
):
    dots[...] = jnp.zeros_like(dots)
    for k in range(RHS):
        now = [residual[k, a] for a in range(2)]
        result = [image[k, a] for a in range(2)]
        for n, field in enumerate((now, result)):
            values[4 * n + k] = wells[0] * field[0] + wells[1] * field[1]
            values[8 + 4 * n + k] = wells[2] * field[0] + wells[3] * field[1]
        row = slice(RHS + k, RHS + k + 1)
        dots[0, row, :] = tile_sum(now, now)
        dots[1, row, :] = tile_sum(now, result)
        dots[2, row, :] = tile_sum(result, result)
    rows = segment_rows(ids, values, scratch, present)
    table = place_rows(rows, jnp.zeros((8, LANES), jnp.float32))
    send_out(place_columns(dots, WELLS, table), chunks, part, sent).wait()


def first_step(totals, small):
    s_row, us_row, p_row, ps_row = (take_group(totals, group) for group in range(4))
    within, equation = small[0:1, :], small[1:2, :]
    rr, rs, ss = (take_column(totals, WELLS + i) for i in range(3))
    height = (rs + lane_sum(p_row * s_row)) / rr
    square = ss + lane_sum(2.0 * ps_row * s_row + equation * s_row * s_row)
    left = jnp.maximum(square - height * height * rr, 1e-7 * square)
    scale = lax.rsqrt(left)
    s_image = us_row + within * s_row
    s_second = (s_image - height * s_row) * scale
    p_second = (ps_row + equation * s_row - height * p_row) * scale
    shift = rs / rr + lane_sum(p_second * s_second)
    unit = lax.rsqrt(rr)
    following = left * scale * unit
    return s_row, s_image, p_row, p_second, (unit, rr * unit, height, shift, following, scale)


def krylov_kernel(
    couplings, diagonal, wells, ids, fxl, fxh, fyl, fyh, gxl, gxh, came_first, came_second,
    residual, image, residual_faces, parts, small_in, present,
    second_out, third_out, part, known, scratch, values_scratch, dots, gyl, gyh,
):
    by_side("gy", came_first, came_second, gyl, gyh)
    faces, sent = (fxl, fxh, fyl, fyh), (gxl, gxh, gyl, gyh)
    totals = jnp.sum(parts[...], axis=0)
    small = small_in[...]
    s_rows, s_images, p_rows, p_seconds, scalars = first_step(totals, small)
    known[0:RHS, :] = p_rows
    known[RHS : 2 * RHS, :] = p_seconds
    columns = jnp.zeros((RHS, LANES), jnp.float32)
    for n, column in enumerate(scalars):
        columns = columns + jnp.where(iota(columns.shape, 1) == n, column, 0.0)
    known[2 * RHS : 3 * RHS, :] = columns
    known[3 * RHS :, :] = jnp.broadcast_to(small[1:2, :], (RHS, LANES))
    dots[...] = jnp.zeros_like(dots)
    corners = corners_of(faces, FACE_PLANES, CORNER_ROWS)
    sent_corners = corners_of(sent, IMAGE_PLANES, 8)
    all_ids = ids[...]
    face_ids = [as_ids(face[WELL_ID]) for face in faces]
    back_ids = [as_ids(face[BACK_ID]) for face in faces]
    corner_ids = [
        as_ids(jnp.broadcast_to(corner.row(SIDE_ID), (8, LANES))) for corner in corners
    ]
    for k in range(RHS):
        unit, _, height, shift, _, scale = (column[k : k + 1, :] for column in scalars)
        s_row, s_image = s_rows[k : k + 1, :], s_images[k : k + 1, :]
        at_wells = spread(s_row, all_ids)
        now = [image[k, a] + wells[2 + a] * at_wells for a in range(2)]
        face_now, spread_now = [], []
        for f in range(4):
            here = spread(s_row, face_ids[f])
            spread_now.append((here, spread(s_row, back_ids[f])))
            face_now.append(
                [sent[f][2 * k + a] + faces[f][WELL_EQ + a] * here for a in range(2)]
            )
        corner_now = []
        for c in range(4):
            here = spread(s_row, corner_ids[c])[0:1, :]
            corner_now.append(
                [
                    sent_corners[c].row(2 * k + a) + corners[c].row(SIDE_EQ + a) * here
                    for a in range(2)
                ]
            )
        incoming = [product(lambda e, f=f: faces[f][e], *face_now[f]) for f in range(4)]
        applied, outgoing = block_stencil(couplings, diagonal, now[0], now[1], incoming)
        at_wells = spread(s_image, all_ids)
        second, third = [], []
        for a in range(2):
            twice = applied[a] + wells[2 + a] * at_wells
            base = (now[a] - height * residual[k, a]) * scale
            second.append(base)
            third.append((twice - height * now[a]) * scale - shift * base)
            second_out[k, a] = second[a]
            third_out[k, a] = third[a]
        ends = corner_inputs(corners, corner_now)
        incoming = []
        for f in range(4):
            face = faces[f]
            here, behind = spread_now[f]
            moves = [
                [face[at + b] * here for b in range(2)]
                for at in (DIAGONAL_WELL, UP_WELL, DOWN_WELL, RISE_WELL, FALL_WELL)
            ]
            there = face_moves(*moves, [face[BACK_WELL + b] * behind for b in range(2)])
            local = [sent[f][8 + 2 * k + b] + there[b] for b in range(2)]
            over = face_entries(ends[(f, 0)], ends[(f, 1)], outgoing[f])
            here = spread(s_image, face_ids[f])
            outer = []
            for a in range(2):
                twice = local[a] + over[a] + face[WELL_EQ + a] * here
                base = (face_now[f][a] - height * residual_faces[f, 2 * k + a]) * scale
                outer.append((twice - height * face_now[f][a]) * scale - shift * base)
            incoming.append(product(lambda e, f=f: faces[f][e], *outer))
        result, _ = block_stencil(couplings, diagonal, third[0], third[1], incoming)
        fourth = [result[a] - shift * third[a] for a in range(2)]
        values_scratch[k] = wells[0] * third[0] + wells[1] * third[1]
        values_scratch[4 + k] = wells[2] * third[0] + wells[3] * third[1]
        values_scratch[8 + k] = wells[2] * fourth[0] + wells[3] * fourth[1]
        fields = [[residual[k, a] * unit for a in range(2)], second, third, fourth]
        number = 0
        for i in range(4):
            for j in range(i, 4):
                dots[number, RHS + k : RHS + k + 1, :] = tile_sum(fields[i], fields[j])
                number += 1
    rows = segment_rows(ids, values_scratch, scratch, present)
    table = place_rows(rows, jnp.zeros((8, LANES), jnp.float32))
    table = place_columns(dots, 0, table)
    gram = table[RHS : RHS + 1, :]
    for k in range(1, RHS):
        gram = gram + pltpu.roll(table[RHS + k : RHS + k + 1, :], GRAM_ENTRIES * k, 1)
    flat = jnp.concatenate([table[k : k + 1, :] for k in range(RHS)] + [gram], axis=1)
    part[...] = jnp.broadcast_to(flat[None], part.shape)


def solve_kernel(guess, residual, second, third, parts, known, solution):
    flat = jnp.sum(parts[...], axis=0)
    rows = [flat[:, LANES * n : LANES * (n + 1)] for n in range(RHS + 1)]
    for k in range(1, RHS):
        rows.append(pltpu.roll(rows[RHS], LANES - GRAM_ENTRIES * k, 1))
    totals = jnp.concatenate(rows, axis=0)
    s_third, p_third, p_fourth = (take_group(totals, group) for group in range(3))
    p_first, p_second = known[0:RHS, :], known[RHS : 2 * RHS, :]
    unit, beta, height, shift, following = (
        known[2 * RHS : 3 * RHS, n : n + 1] for n in range(5)
    )
    equation = known[3 * RHS :, :]
    gram = {}
    number = 0
    for i in range(4):
        for j in range(i, 4):
            gram[(i, j)] = take_column(totals, number)
            number += 1
    gram[(0, 3)] += lane_sum(p_first * s_third) * unit
    gram[(1, 3)] += lane_sum(p_second * s_third)
    gram[(2, 3)] += lane_sum(p_third * s_third)
    gram[(3, 3)] += lane_sum(2.0 * p_fourth * s_third + equation * s_third * s_third)
    tiny = 1e-30
    inverse = [lax.rsqrt(jnp.maximum(gram[(i, i)], tiny)) for i in range(4)]
    length = [jnp.maximum(gram[(i, i)], tiny) * inverse[i] for i in range(4)]
    upper = {}
    for i in range(4):
        for j in range(i, 4):
            entry = gram[(i, j)] * inverse[i] * inverse[j]
            for m in range(i):
                entry = entry - upper[(m, i)] * upper[(m, j)]
            if i == j:
                pivot = lax.rsqrt(jnp.maximum(entry, 1e-6))
                upper[(i, i)] = jnp.maximum(entry, 1e-6) * pivot
                over = pivot
            else:
                upper[(i, j)] = entry * over
    columns = [
        [(0, height * length[0]), (1, following * length[1])],
        [(1, shift * length[1]), (2, length[2])],
        [(2, shift * length[2]), (3, length[3])],
    ]
    zero = jnp.zeros_like(shift)
    hessenberg = [[zero] * 3 for _ in range(4)]
    for j in range(3):
        for i in range(j + 2):
            for m, factor in columns[j]:
                if m >= i:
                    hessenberg[i][j] = hessenberg[i][j] + upper[(i, m)] * factor
    target = [beta * length[0] * upper[(0, 0)], zero, zero, zero]
    turns = []
    for j in range(3):
        top, bottom = hessenberg[j][j], hessenberg[j + 1][j]
        turn = lax.rsqrt(top * top + bottom * bottom)
        turns.append(turn)
        cosine, sine = top * turn, bottom * turn
        for m in range(j, 3):
            high, low = hessenberg[j][m], hessenberg[j + 1][m]
            hessenberg[j][m] = cosine * high + sine * low
            hessenberg[j + 1][m] = cosine * low - sine * high
        high, low = target[j], target[j + 1]
        target[j] = cosine * high + sine * low
        target[j + 1] = cosine * low - sine * high
    weights = [zero] * 3
    for i in (2, 1, 0):
        value = target[i]
        for j in range(i + 1, 3):
            value = value - hessenberg[i][j] * weights[j]
        weights[i] = value * turns[i]
    for k in range(RHS):
        on_first, on_second, on_third = (
            column[k : k + 1, :] for column in (weights[0] * unit, weights[1], weights[2])
        )
        for a in range(2):
            solution[k, a] = (
                guess[k, a]
                + on_first * residual[k, a]
                + on_second * second[k, a]
                + on_third * third[k, a]
            )


def call(kernel, shapes, arguments, scratch=(), own_copies=False, cost=0, grant=24 << 20, out=0):
    whole = pl.BlockSpec(memory_space=pltpu.VMEM)
    far = pl.BlockSpec(memory_space=pltpu.HBM)
    scalars = pl.BlockSpec(memory_space=pltpu.SMEM)

    def place(array):
        if len(array.shape) == 1:
            return scalars
        return far if own_copies else whole

    outs = [
        jax.ShapeDtypeStruct(shape, jnp.float32 if len(shape) > 1 else jnp.int32)
        for shape in shapes
    ]
    outs[:out] = [pltpu.HBM(shape, jnp.float32) for shape in shapes[:out]]
    return pl.pallas_call(
        kernel,
        out_shape=outs,
        in_specs=[place(argument) for argument in arguments],
        out_specs=[far] * out + [scalars if len(shape) == 1 else whole for shape in shapes[out:]],
        scratch_shapes=list(scratch),
        compiler_params=pltpu.CompilerParams(vmem_limit_bytes=grant),
        cost_estimate=pl.CostEstimate(flops=cost, bytes_accessed=cost, transcendentals=0)
        if cost
        else None,
    )(*arguments)


def nothing(value, *rest):
    pass


def after(value, *others):
    far = pl.BlockSpec(memory_space=pltpu.HBM)
    near = pl.BlockSpec(memory_space=pltpu.VMEM)
    return pl.pallas_call(
        nothing,
        out_shape=pltpu.HBM(value.shape, value.dtype),
        in_specs=[far] + [near] * len(others),
        out_specs=far,
        input_output_aliases={0: 0},
        compiler_params=pltpu.CompilerParams(vmem_limit_bytes=1 << 20),
    )(pltpu.with_memory_space_constraint(value, pltpu.HBM), *others)


def held(*shape):
    return pltpu.VMEM(shape, jnp.float32)


def swapped(first, second, axis):
    results = []
    for start, value in enumerate((first, second)):
        pairs = []
        for low in range(start, lax.axis_size(axis) - 1, 2):
            pairs += [(low, low + 1), (low + 1, low)]
        results.append(lax.ppermute(value, axis, pairs) if pairs else jnp.zeros_like(value))
    return results


def exchanged(part):
    return lax.all_to_all(part, ("gx", "gy"), 0, 0, tiled=True)


def body(couplings, diagonal, wells, ids, right, guess):
    devices = lax.axis_size("gx") * lax.axis_size("gy")
    plane = (8, LANES)
    field = guess.shape
    block = guess.shape[2:]
    arguments = (couplings, diagonal, wells, ids, right, guess)

    ends = []
    for argument in arguments:
        shape = argument.shape[:-3] + (2,) + argument.shape[-2:]
        ends += [pltpu.VMEM(shape, argument.dtype)] * 2
    x_first, x_second = call(
        x_pack_kernel,
        [(FACE_PLANES + 1,) + plane] * 2,
        [pltpu.with_memory_space_constraint(argument, pltpu.HBM) for argument in arguments],
        ends
        + [pltpu.SemaphoreType.DMA((len(ends),))]
        + [held(FACE_PLANES + 1, *plane)] * 2,
        own_copies=True,
    )
    came_x = swapped(x_first, x_second, "gx")
    first_chunks, chunks = (devices, TABLE_ROWS, LANES), (devices, 8, LANES)
    sent = pltpu.SemaphoreType.DMA((1,))
    part, present, y_low, y_high = call(
        guess_kernel,
        [first_chunks, (WELLS + 8,)] + [(FACE_PLANES,) + plane] * 2,
        arguments,
        [held(6, *block), held(6, WELLS, LANES), held(*first_chunks), sent],
        cost=4 << 20,
        out=1,
    )
    parts = exchanged(after(part, came_x[0]))
    y_shape = (FACE_PLANES + CORNER_PLANES,) + plane
    y_first, y_second, fxl, fxh = call(
        corner_kernel,
        [y_shape] * 2 + [(FACE_PLANES + 1,) + plane] * 2,
        (y_low, y_high, *came_x),
        [held(*y_shape)] * 2,
    )
    came_y = swapped(y_first, y_second, "gy")
    ahead = call(
        block_kernel,
        [field, (4, 8) + plane] + [(LAYER_BLOCKS,) + plane] * 2,
        (couplings, diagonal, right, guess, y_first),
        cost=4 << 20,
    )

    residual, image, residual_faces, x_first, x_second, y_low, y_high, small, fyl, fyh = call(
        residual_kernel,
        [field, field, (4, 8) + plane]
        + [(IMAGE_PLANES,) + plane] * 4
        + [(8, LANES)]
        + [y_shape] * 2,
        (couplings, diagonal, wells, ids, fxl, fxh, *came_y, parts, *ahead),
        [held(IMAGE_PLANES, *plane)] * 2,
    )
    faces = (fxl, fxh, fyl, fyh)
    came_x = swapped(x_first, x_second, "gx")
    (part,) = call(
        moments_kernel,
        [chunks],
        (wells, ids, residual, image, present),
        [held(16, *block), held(16, WELLS, LANES), held(3, *plane), held(*chunks), sent],
        cost=4 << 20,
        out=1,
    )
    parts = exchanged(after(part, *came_x))
    y_shape = (IMAGE_PLANES + 2,) + plane
    y_first, y_second, gxl, gxh = call(
        image_corner_kernel,
        [y_shape] * 2 + [(IMAGE_PLANES,) + plane] * 2,
        (y_low, y_high, *came_x),
        [held(*y_shape)] * 2,
    )
    came_y = swapped(y_first, y_second, "gy")

    second, third, part, known = call(
        krylov_kernel,
        [field, field, (devices, 1, (RHS + 1) * LANES), (4 * RHS, LANES)],
        (couplings, diagonal, wells, ids) + faces + (gxl, gxh, *came_y)
        + (residual, image, residual_faces, parts, small, present),
        [held(12, WELLS, LANES), held(12, *block), held(10, *plane)]
        + [held(*y_shape)] * 2,
    )
    parts = exchanged(part)
    (result,) = call(
        solve_kernel,
        [field],
        (guess, residual, second, third, parts, known),
    )
    return result


def solution(mesh):
    in_specs = (
        P("member", None, "gx", "gy", None),
        P("member", "gx", "gy", None),
        P("member", "gx", "gy", None),
        P("gx", "gy", None),
        P("member", None, "gx", "gy", None),
        P("member", None, "gx", "gy", None),
    )
    out_specs = P("member", None, "gx", "gy", None)
    return jax.shard_map(body, mesh=mesh, in_specs=in_specs, out_specs=out_specs, check_vma=False)
```

```python
import jax
import jax.numpy as jnp
from jax import lax
from jax.experimental import pallas as pl
from jax.experimental.pallas import tpu as pltpu
from jax.sharding import PartitionSpec as P

WELLS = 40
RHS = 4
LANES = 128
WELL_EQ, WELL_ID, GUESS, REST = 4, 6, 7, 15
UP_WELL, DOWN_WELL, RISE_WELL, FALL_WELL, DIAGONAL_WELL = 23, 25, 27, 29, 31
BACK_WELL, BACK_ID = 33, 35
FACE_PLANES = 36
ENDS = 36
CORNER_PLANES = 5
LAT_UP, LAT_DOWN, RISE, FALL, DIAGONAL, BACK_IN = 0, 4, 8, 12, 16, 20
LAYER_BLOCKS = 24
IMAGE_PLANES = 16
TABLE_ROWS = 6
GRAM_ENTRIES = 10
CORNER_ROWS = 19
SIDE_IN, SIDE_EQ, SIDE_ID, SIDE_GUESS = 4, 8, 10, 11


def product(blocks, first, second):
    return [
        blocks(0) * first + blocks(2) * second,
        blocks(1) * first + blocks(3) * second,
    ]


def iota(shape, axis):
    return lax.broadcasted_iota(jnp.int32, shape, axis)


def roll_up(value, axis):
    return pltpu.roll(value, 1, axis)


def roll_down(value, axis):
    return pltpu.roll(value, value.shape[axis] - 1, axis)


def layer_moves(rising, falling):
    axis = rising.ndim - 1
    lane = iota(rising.shape, axis)
    up = jnp.where(lane == 0, 0.0, roll_up(rising, axis))
    down = jnp.where(lane == LANES - 1, 0.0, roll_down(falling, axis))
    return up + down


def block_stencil(couplings, diagonal, first, second, incoming):
    result = product(lambda e: diagonal[e], first, second)
    moved = [product(lambda e, d=d: couplings[d, e], first, second) for d in range(6)]
    row = iota(first.shape, 1)
    outgoing = [[], [], [], []]
    for b in range(2):
        east, west, north, south, rise, fall = (moved[d][b] for d in range(6))
        total = result[b] + jnp.concatenate([incoming[0][b][None], east[:-1]], axis=0)
        total = total + jnp.concatenate([west[1:], incoming[1][b][None]], axis=0)
        total = total + jnp.where(row == 0, incoming[2][b][:, None, :], roll_up(north, 1))
        total = total + jnp.where(
            row == row.shape[1] - 1, incoming[3][b][:, None, :], roll_down(south, 1)
        )
        result[b] = total + layer_moves(rise, fall)
        outgoing[0].append(west[0])
        outgoing[1].append(east[-1])
        outgoing[2].append(south[:, 0, :])
        outgoing[3].append(north[:, -1, :])
    return result, outgoing


def face_stencil(blocks, first, second, behind):
    def times(start):
        return product(lambda e: blocks(start + e), first, second)

    moves = [times(start) for start in (DIAGONAL, LAT_UP, LAT_DOWN, RISE, FALL)]
    return face_moves(*moves, behind)


def face_moves(kept, up, down, rise, fall, behind):
    result = list(kept)
    row = iota(kept[0].shape, 0)
    for b in range(2):
        total = result[b] + behind[b] + layer_moves(rise[b], fall[b])
        total = total + jnp.where(row == 0, 0.0, roll_up(up[b], 0))
        result[b] = total + jnp.where(row == row.shape[0] - 1, 0.0, roll_down(down[b], 0))
    return result


def face_entries(low_end, high_end, entering):
    row = iota(entering[0].shape, 0)
    return [
        entering[b]
        + jnp.where(row == 0, low_end[b], 0.0)
        + jnp.where(row == row.shape[0] - 1, high_end[b], 0.0)
        for b in range(2)
    ]


def spread(totals, ids):
    table = jnp.broadcast_to(totals, (8, LANES))
    if ids.ndim == 2:
        return jnp.take_along_axis(table, ids, axis=1)
    return jnp.stack(
        [jnp.take_along_axis(table, ids[x], axis=1) for x in range(ids.shape[0])], axis=0
    )


def as_ids(plane):
    return plane.astype(jnp.int32)


class Corner:
    def __init__(self, pack, which, base):
        self.pack, self.start = pack, base * 8 + which

    def row(self, number):
        at = self.start + number
        return self.pack[at // 8, at % 8 : at % 8 + 1, :]


def corners_of(faces, base, rows):
    found = []
    for y_face in (2, 3):
        for x_end in range(2):
            found.append(Corner(faces[y_face], x_end * rows, base))
    return found


def corner_inputs(corners, values):
    ends = {}
    for c in range(4):
        x_end, y_end = c % 2, c // 2
        over_x = product(corners[c].row, *values[c])
        over_y = product(lambda e, c=c: corners[c].row(SIDE_IN + e), *values[c])
        ends[(2 + y_end, x_end)] = over_x
        ends[(x_end, y_end)] = over_y
    return ends


def tile_sum(first, second):
    value = first[0] * second[0] + first[1] * second[1]
    return jnp.sum(jnp.sum(value, axis=0), axis=0, keepdims=True)


def list_wells(ids, present):
    planes = [ids[x].astype(jnp.float32) for x in range(ids.shape[0])]
    middle = WELLS // 2
    halves = ((0.0, float(middle)), (float(middle), float(WELLS)))

    def least(above, top):
        found = [jnp.where((p > above) & (p < top), p, top) for p in planes]
        value = found[0]
        for other in found[1:]:
            value = jnp.minimum(value, other)
        return jnp.min(value)

    def greatest(base, below):
        found = [jnp.where((p >= base) & (p < below), p, base - 1.0) for p in planes]
        value = found[0]
        for other in found[1:]:
            value = jnp.maximum(value, other)
        return jnp.max(value)

    def some_left(state):
        return (state[1] <= state[2]) | (state[3] <= state[4])

    def step(state):
        number, ends = state[0], state[1:]
        after = []
        for half, (base, top) in enumerate(halves):
            low, high = ends[2 * half], ends[2 * half + 1]
            present[number] = low.astype(jnp.int32)
            number = number + jnp.where(low <= high, 1, 0)
            present[number] = high.astype(jnp.int32)
            number = number + jnp.where(low < high, 1, 0)
            after += [least(low, top), greatest(base, high)]
        return (number, *after)

    ends = []
    for base, top in halves:
        ends += [least(base - 1.0, top), greatest(base, top)]
    state = lax.while_loop(some_left, step, (jnp.int32(1), *ends))
    present[0] = state[0] - 1


def segment_rows(ids, values, scratch, present):
    scratch[...] = jnp.zeros_like(scratch)
    count, depth = values.shape[0], ids.shape[0]

    def one_well(step, _):
        well = present[step + 1]
        masks = [ids[x] == well for x in range(depth)]
        for number in range(count):
            total = jnp.where(masks[0], values[number, 0], 0.0)
            for x in range(1, depth):
                total = total + jnp.where(masks[x], values[number, x], 0.0)
            scratch[number, pl.ds(well, 1), :] = jnp.sum(total, axis=0, keepdims=True)
        return 0

    lax.fori_loop(0, present[0], one_well, 0)
    rows = []
    for number in range(count):
        summed = jnp.sum(scratch[number], axis=1, keepdims=True)
        shape = scratch.shape[1:]
        on_lanes = jnp.where(iota(shape, 0) == iota(shape, 1), summed, 0.0)
        rows.append(jnp.sum(on_lanes, axis=0, keepdims=True))
    return rows


def pack_rows(rows, table):
    for number, row in enumerate(rows):
        placed = row if number % 3 == 0 else pltpu.roll(row, WELLS * (number % 3), 1)
        table = table + jnp.where(
            iota(table.shape, 0) == number // 3, jnp.broadcast_to(placed, table.shape), 0.0
        )
    return table


def unpack_row(table, number):
    row = table[number // 3 : number // 3 + 1, :]
    if number % 3:
        row = pltpu.roll(row, LANES - WELLS * (number % 3), 1)
    return jnp.where(iota(row.shape, 1) < WELLS, row, 0.0)


def place_rows(rows, table):
    for number, row in enumerate(rows):
        group, k = divmod(number, RHS)
        at = k + RHS * (group // 3)
        placed = pltpu.roll(row, WELLS * group, 1) if group in (1, 2) else row
        table = table + jnp.where(
            iota(table.shape, 0) == at, jnp.broadcast_to(placed, table.shape), 0.0
        )
    return table


def place_columns(dots, first_lane, table):
    for number in range(dots.shape[0]):
        column = jnp.sum(dots[number], axis=1, keepdims=True)
        table = table + jnp.where(iota(table.shape, 1) == first_lane + number, column, 0.0)
    return table


def take_group(table, group):
    if group in (1, 2):
        table = pltpu.roll(table, LANES - WELLS * group, 1)
    start = RHS * (group // 3)
    rows = table[start : start + RHS, :]
    return jnp.where(iota(rows.shape, 1) < WELLS, rows, 0.0)


def take_column(table, lane):
    return table[RHS : 2 * RHS, lane : lane + 1]


def lane_sum(row):
    return jnp.sum(row, axis=1, keepdims=True)


def on_even(axis):
    return lax.rem(lax.axis_index(axis), 2) == 0


def by_pair(axis, low, high, first, second):
    @pl.when(on_even(axis))
    def _():
        first[...] = high[...]
        second[...] = low[...]

    @pl.when(jnp.logical_not(on_even(axis)))
    def _():
        first[...] = low[...]
        second[...] = high[...]


def by_side(axis, first, second, low, high):
    by_pair(axis, second, first, high, low)


COUPLINGS, DIAGONALS, WELL_FIELDS, IDS, RIGHT_SIDE, START = range(6)


def layer_blocks(cut, inward, lateral):
    def plane(n):
        if n < DIAGONAL:
            return cut(COUPLINGS, ((lateral, lateral + 1, 4, 5)[n // 4], n % 4), 0)
        if n < BACK_IN:
            return cut(DIAGONALS, (n - DIAGONAL,), 0)
        return cut(COUPLINGS, (inward, n - BACK_IN), 1)

    return plane


def fill_pack(pack, inward, lateral, cut):
    blocks = layer_blocks(cut, inward, lateral)
    for e in range(4):
        pack[e] = cut(COUPLINGS, (inward, e), 0)
    wells = [cut(WELL_FIELDS, (2 + a,), 0) for a in range(2)]
    for a in range(2):
        pack[WELL_EQ + a] = wells[a]
    pack[WELL_ID] = cut(IDS, (), 0).astype(jnp.float32)
    pack[BACK_ID] = cut(IDS, (), 1).astype(jnp.float32)
    for start, at in (
        (LAT_UP, UP_WELL),
        (LAT_DOWN, DOWN_WELL),
        (RISE, RISE_WELL),
        (FALL, FALL_WELL),
        (DIAGONAL, DIAGONAL_WELL),
        (BACK_IN, BACK_WELL),
    ):
        if start == BACK_IN:
            wells = [cut(WELL_FIELDS, (2 + a,), 1) for a in range(2)]
        for b, value in enumerate(product(lambda e: blocks(start + e), *wells)):
            pack[at + b] = value
    for k in range(RHS):
        here = [cut(START, (k, a), 0) for a in range(2)]
        back = [cut(START, (k, a), 1) for a in range(2)]
        entering = product(lambda e: blocks(BACK_IN + e), *back)
        local = face_stencil(blocks, here[0], here[1], entering)
        for a in range(2):
            pack[GUESS + 2 * k + a] = here[a]
            pack[REST + 2 * k + a] = cut(RIGHT_SIDE, (k, a), 0) - local[a]
    if pack.shape[0] > ENDS:
        end = pack.shape[1] - 1
        for e in range(4):
            pack[ENDS, e : e + 1, :] = blocks(LAT_UP + e)[end : end + 1, :]
            pack[ENDS, 4 + e : 5 + e, :] = blocks(LAT_DOWN + e)[0:1, :]


def x_pack_kernel(*refs):
    sources, first, second, held_ends, arrived = refs[:6], refs[6], refs[7], refs[8:20], refs[20]
    packs = refs[21:23]
    copies = []
    for n, source in enumerate(sources):
        lead = (slice(None),) * (len(source.shape) - 3)
        depth = source.shape[-3]
        for end, start in enumerate((0, depth - 2)):
            copies.append(
                pltpu.make_async_copy(
                    source.at[lead + (pl.ds(start, 2),)],
                    held_ends[2 * n + end],
                    arrived.at[2 * n + end],
                )
            )
    for copy in copies:
        copy.start()
    for copy in copies:
        copy.wait()
    for end, pack in enumerate(packs):
        fill_pack(
            pack,
            1 - end,
            2,
            lambda n, index, layer: held_ends[2 * n + end][
                index + (1 - layer if end else layer,)
            ],
        )
    by_pair("gx", *packs, first, second)


def y_cut(arguments, end):
    last = arguments[0].shape[-2] - 1

    def cut(n, index, layer):
        return arguments[n][index + (slice(None), last - layer if end else layer, slice(None))]

    return cut


def send_out(table, chunks, part, sent):
    rows = min(chunks.shape[1], table.shape[0])
    chunks[:, :rows, :] = jnp.broadcast_to(table[None, :rows], (chunks.shape[0], rows, LANES))
    copy = pltpu.make_async_copy(chunks, part, sent.at[0])
    copy.start()
    return copy


def corner_kernel(y_low, y_high, came_first, came_second, first, second, fxl, fxh, *outs):
    by_side("gx", came_first, came_second, fxl, fxh)
    last = fxl.shape[1] - 1
    for own, out, at, side in ((y_low, outs[0], 0, 4), (y_high, outs[1], last, 0)):
        for n in range(FACE_PLANES):
            out[n] = own[n]
        row = FACE_PLANES * 8
        out[FACE_PLANES + CORNER_PLANES - 1] = jnp.zeros(out.shape[1:], jnp.float32)
        for face in (fxl, fxh):
            rows = [(n, at) for n in range(4)]
            rows += [(ENDS, side + e) for e in range(4)]
            rows += [(n, at) for n in range(WELL_EQ, REST)]
            for n, y in rows:
                out[row // 8, row % 8 : row % 8 + 1, :] = face[n, y : y + 1, :]
                row += 1
    by_pair("gy", *outs, first, second)


def diagonal_device(x_end, y_end):
    across, along = lax.axis_index("gx"), lax.axis_index("gy")
    there_x, there_y = across + 2 * x_end - 1, along + 2 * y_end - 1
    count_x, count_y = lax.axis_size("gx"), lax.axis_size("gy")
    exists = (there_x >= 0) & (there_x < count_x) & (there_y >= 0) & (there_y < count_y)
    return exists, jnp.where(exists, there_x * count_y + there_y, 0)


def guess_kernel(
    couplings, diagonal, wells, ids, right, guess,
    part, present, y_low, y_high, values, scratch, chunks, sent,
):
    list_wells(ids, present)
    for k in range(RHS):
        values[k] = wells[0] * guess[k, 0] + wells[1] * guess[k, 1]
    values[4] = wells[0] * wells[2] + wells[1] * wells[3]
    values[5] = wells[2] * wells[2] + wells[3] * wells[3]
    rows = segment_rows(ids, values, scratch, present)
    table = pack_rows(rows, jnp.zeros((8, LANES), jnp.float32))
    copy = send_out(table, chunks, part, sent)
    arguments = (couplings, diagonal, wells, ids, right, guess)
    for end, pack in enumerate((y_low, y_high)):
        fill_pack(pack, 3 - end, 0, y_cut(arguments, end))
    copy.wait()


def block_kernel(
    couplings, diagonal, right, guess, sent_face, rest, leaving
):
    nothing_enters = [[jnp.zeros(guess.shape[3:], jnp.float32)] * 2] * 4
    for k in range(RHS):
        inside, outgoing = block_stencil(
            couplings, diagonal, guess[k, 0], guess[k, 1], nothing_enters
        )
        for a in range(2):
            rest[k, a] = right[k, a] - inside[a]
            for f in range(4):
                leaving[f, 2 * k + a] = outgoing[f][a]


def residual_kernel(
    couplings, diagonal, wells, ids, fxl, fxh, came_first, came_second, parts,
    rest, leaving,
    residual, image, residual_faces, x_first, x_second, y_first, y_second, small, fyl, fyh,
    x_low, x_high, y_low, y_high,
):
    by_side("gy", came_first, came_second, fyl, fyh)
    faces = (fxl, fxh, fyl, fyh)
    totals = jnp.sum(parts[...], axis=0)
    corners = corners_of(faces, FACE_PLANES, CORNER_ROWS)
    all_ids = ids[...]
    face_ids = [as_ids(face[WELL_ID]) for face in faces]
    last = rest.shape[2] - 1
    row = iota(rest.shape[2:], 1)
    for k in range(RHS):
        s_row = unpack_row(totals, k)
        entering = [
            product(
                lambda e, f=f: faces[f][e],
                faces[f][GUESS + 2 * k],
                faces[f][GUESS + 2 * k + 1],
            )
            for f in range(4)
        ]
        outgoing = [[leaving[f, 2 * k + b] for b in range(2)] for f in range(4)]
        at_wells = spread(s_row, all_ids)
        now = []
        for a in range(2):
            value = rest[k, a] - wells[2 + a] * at_wells
            over_x = [
                (value[0] - entering[0][a])[None],
                value[1:last],
                (value[last] - entering[1][a])[None],
            ]
            value = jnp.concatenate(over_x, axis=0)
            value = value - jnp.where(row == 0, entering[2][a][:, None, :], 0.0)
            now.append(value - jnp.where(row == last, entering[3][a][:, None, :], 0.0))
        for a in range(2):
            residual[k, a] = now[a]
        ends = corner_inputs(
            corners,
            [[corners[c].row(SIDE_GUESS + 2 * k + a) for a in range(2)] for c in range(4)],
        )
        incoming = []
        for f in range(4):
            face = faces[f]
            there = face_entries(ends[(f, 0)], ends[(f, 1)], outgoing[f])
            face_wells = spread(s_row, face_ids[f])
            outer = [
                face[REST + 2 * k + a] - there[a] - face[WELL_EQ + a] * face_wells
                for a in range(2)
            ]
            for a in range(2):
                residual_faces[f, 2 * k + a] = outer[a]
            incoming.append(product(lambda e, f=f: faces[f][e], *outer))
        result, _ = block_stencil(couplings, diagonal, now[0], now[1], incoming)
        for a in range(2):
            image[k, a] = result[a]
    own = (couplings, diagonal)
    for axis, packs in enumerate(((x_low, x_high), (y_low, y_high))):
        for end, pack in enumerate(packs):

            def cut(ref, index, layer):
                at = last - layer if end else layer
                return ref[index + ((at,) if axis == 0 else (slice(None), at, slice(None)))]

            plane = layer_blocks(
                lambda n, index, layer: cut(own[n], index, layer),
                2 * axis + 1 - end,
                2 * (1 - axis),
            )
            blocks = [plane(n) for n in range(LAYER_BLOCKS)]
            for k in range(RHS):
                here = [cut(image, (k, a), 0) for a in range(2)]
                back = [cut(image, (k, a), 1) for a in range(2)]
                entering = product(lambda e: blocks[BACK_IN + e], *back)
                local = face_stencil(lambda n: blocks[n], here[0], here[1], entering)
                for a in range(2):
                    pack[2 * k + a] = here[a]
                    pack[8 + 2 * k + a] = local[a]
    by_pair("gx", x_low, x_high, x_first, x_second)
    by_pair("gy", y_low, y_high, y_first, y_second)
    small[...] = jnp.concatenate(
        [unpack_row(totals, 4), unpack_row(totals, 5), jnp.zeros((6, LANES), jnp.float32)], axis=0
    )


def moments_kernel(
    wells, ids, residual, image, present, part, values, scratch, dots, chunks, sent
):
    dots[...] = jnp.zeros_like(dots)
    for k in range(RHS):
        now = [residual[k, a] for a in range(2)]
        result = [image[k, a] for a in range(2)]
        for n, field in enumerate((now, result)):
            values[4 * n + k] = wells[0] * field[0] + wells[1] * field[1]
            values[8 + 4 * n + k] = wells[2] * field[0] + wells[3] * field[1]
        row = slice(RHS + k, RHS + k + 1)
        dots[0, row, :] = tile_sum(now, now)
        dots[1, row, :] = tile_sum(now, result)
        dots[2, row, :] = tile_sum(result, result)
    rows = segment_rows(ids, values, scratch, present)
    table = place_rows(rows, jnp.zeros((8, LANES), jnp.float32))
    chunks[:, 8:, :] = jnp.zeros_like(chunks[:, 8:, :])
    last = image.shape[2] - 1
    for x_end in range(2):
        for y_end in range(2):
            exists, place = diagonal_device(x_end, y_end)

            @pl.when(exists)
            def _():
                for k in range(RHS):
                    for a in range(2):
                        row, y = 8 + 2 * k + a, last * y_end
                        chunks[pl.ds(place, 1), row : row + 1, :] = image[
                            k, a, last * x_end, y : y + 1, :
                        ][None]

    send_out(place_columns(dots, WELLS, table), chunks, part, sent).wait()


def first_step(totals, small):
    s_row, us_row, p_row, ps_row = (take_group(totals, group) for group in range(4))
    within, equation = small[0:1, :], small[1:2, :]
    rr, rs, ss = (take_column(totals, WELLS + i) for i in range(3))
    height = (rs + lane_sum(p_row * s_row)) / rr
    square = ss + lane_sum(2.0 * ps_row * s_row + equation * s_row * s_row)
    left = jnp.maximum(square - height * height * rr, 1e-7 * square)
    scale = lax.rsqrt(left)
    s_image = us_row + within * s_row
    s_second = (s_image - height * s_row) * scale
    p_second = (ps_row + equation * s_row - height * p_row) * scale
    shift = rs / rr + lane_sum(p_second * s_second)
    unit = lax.rsqrt(rr)
    following = left * scale * unit
    return s_row, s_image, p_row, p_second, (unit, rr * unit, height, shift, following, scale)


def krylov_kernel(
    couplings, diagonal, wells, ids, fxl, fxh, fyl, fyh, x_first, x_second, y_first, y_second,
    residual, image, residual_faces, parts, small_in, present,
    second_out, third_out, part, known, scratch, values_scratch, dots, gxl, gxh, gyl, gyh,
):
    by_side("gx", x_first, x_second, gxl, gxh)
    by_side("gy", y_first, y_second, gyl, gyh)
    faces, sent = (fxl, fxh, fyl, fyh), (gxl, gxh, gyl, gyh)
    totals = jnp.sum(parts[:, 0:8, :], axis=0)
    small = small_in[...]
    s_rows, s_images, p_rows, p_seconds, scalars = first_step(totals, small)
    known[0:RHS, :] = p_rows
    known[RHS : 2 * RHS, :] = p_seconds
    columns = jnp.zeros((RHS, LANES), jnp.float32)
    for n, column in enumerate(scalars):
        columns = columns + jnp.where(iota(columns.shape, 1) == n, column, 0.0)
    known[2 * RHS : 3 * RHS, :] = columns
    known[3 * RHS :, :] = jnp.broadcast_to(small[1:2, :], (RHS, LANES))
    dots[...] = jnp.zeros_like(dots)
    corners = corners_of(faces, FACE_PLANES, CORNER_ROWS)
    places = [diagonal_device(c % 2, c // 2)[1] for c in range(4)]
    all_ids = ids[...]
    face_ids = [as_ids(face[WELL_ID]) for face in faces]
    back_ids = [as_ids(face[BACK_ID]) for face in faces]
    corner_ids = [
        as_ids(jnp.broadcast_to(corner.row(SIDE_ID), (8, LANES))) for corner in corners
    ]
    for k in range(RHS):
        unit, _, height, shift, _, scale = (column[k : k + 1, :] for column in scalars)
        s_row, s_image = s_rows[k : k + 1, :], s_images[k : k + 1, :]
        at_wells = spread(s_row, all_ids)
        now = [image[k, a] + wells[2 + a] * at_wells for a in range(2)]
        face_now, spread_now = [], []
        for f in range(4):
            here = spread(s_row, face_ids[f])
            spread_now.append((here, spread(s_row, back_ids[f])))
            face_now.append(
                [sent[f][2 * k + a] + faces[f][WELL_EQ + a] * here for a in range(2)]
            )
        corner_now = []
        for c in range(4):
            here = spread(s_row, corner_ids[c])[0:1, :]
            corner_now.append(
                [
                    parts[pl.ds(places[c], 1), 8 + 2 * k + a, :] + corners[c].row(SIDE_EQ + a) * here
                    for a in range(2)
                ]
            )
        incoming = [product(lambda e, f=f: faces[f][e], *face_now[f]) for f in range(4)]
        applied, outgoing = block_stencil(couplings, diagonal, now[0], now[1], incoming)
        at_wells = spread(s_image, all_ids)
        second, third = [], []
        for a in range(2):
            twice = applied[a] + wells[2 + a] * at_wells
            base = (now[a] - height * residual[k, a]) * scale
            second.append(base)
            third.append((twice - height * now[a]) * scale - shift * base)
            second_out[k, a] = second[a]
            third_out[k, a] = third[a]
        ends = corner_inputs(corners, corner_now)
        incoming = []
        for f in range(4):
            face = faces[f]
            here, behind = spread_now[f]
            moves = [
                [face[at + b] * here for b in range(2)]
                for at in (DIAGONAL_WELL, UP_WELL, DOWN_WELL, RISE_WELL, FALL_WELL)
            ]
            there = face_moves(*moves, [face[BACK_WELL + b] * behind for b in range(2)])
            local = [sent[f][8 + 2 * k + b] + there[b] for b in range(2)]
            over = face_entries(ends[(f, 0)], ends[(f, 1)], outgoing[f])
            here = spread(s_image, face_ids[f])
            outer = []
            for a in range(2):
                twice = local[a] + over[a] + face[WELL_EQ + a] * here
                base = (face_now[f][a] - height * residual_faces[f, 2 * k + a]) * scale
                outer.append((twice - height * face_now[f][a]) * scale - shift * base)
            incoming.append(product(lambda e, f=f: faces[f][e], *outer))
        result, _ = block_stencil(couplings, diagonal, third[0], third[1], incoming)
        fourth = [result[a] - shift * third[a] for a in range(2)]
        values_scratch[k] = wells[0] * third[0] + wells[1] * third[1]
        values_scratch[4 + k] = wells[2] * third[0] + wells[3] * third[1]
        values_scratch[8 + k] = wells[2] * fourth[0] + wells[3] * fourth[1]
        fields = [[residual[k, a] * unit for a in range(2)], second, third, fourth]
        number = 0
        for i in range(4):
            for j in range(i, 4):
                dots[number, RHS + k : RHS + k + 1, :] = tile_sum(fields[i], fields[j])
                number += 1
    rows = segment_rows(ids, values_scratch, scratch, present)
    table = place_rows(rows, jnp.zeros((8, LANES), jnp.float32))
    table = place_columns(dots, 0, table)
    gram = table[RHS : RHS + 1, :]
    for k in range(1, RHS):
        gram = gram + pltpu.roll(table[RHS + k : RHS + k + 1, :], GRAM_ENTRIES * k, 1)
    flat = jnp.concatenate([table[k : k + 1, :] for k in range(RHS)] + [gram], axis=1)
    part[...] = jnp.broadcast_to(flat[None], part.shape)


def solve_kernel(
    guess_in, residual, second, third, parts, known, solution, guess, arrived
):
    copy = pltpu.make_async_copy(guess_in, guess, arrived.at[0])
    copy.start()
    flat = jnp.sum(parts[...], axis=0)
    rows = [flat[:, LANES * n : LANES * (n + 1)] for n in range(RHS + 1)]
    for k in range(1, RHS):
        rows.append(pltpu.roll(rows[RHS], LANES - GRAM_ENTRIES * k, 1))
    totals = jnp.concatenate(rows, axis=0)
    s_third, p_third, p_fourth = (take_group(totals, group) for group in range(3))
    p_first, p_second = known[0:RHS, :], known[RHS : 2 * RHS, :]
    unit, beta, height, shift, following = (
        known[2 * RHS : 3 * RHS, n : n + 1] for n in range(5)
    )
    equation = known[3 * RHS :, :]
    gram = {}
    number = 0
    for i in range(4):
        for j in range(i, 4):
            gram[(i, j)] = take_column(totals, number)
            number += 1
    gram[(0, 3)] += lane_sum(p_first * s_third) * unit
    gram[(1, 3)] += lane_sum(p_second * s_third)
    gram[(2, 3)] += lane_sum(p_third * s_third)
    gram[(3, 3)] += lane_sum(2.0 * p_fourth * s_third + equation * s_third * s_third)
    tiny = 1e-30
    inverse = [lax.rsqrt(jnp.maximum(gram[(i, i)], tiny)) for i in range(4)]
    length = [jnp.maximum(gram[(i, i)], tiny) * inverse[i] for i in range(4)]
    upper = {}
    for i in range(4):
        for j in range(i, 4):
            entry = gram[(i, j)] * inverse[i] * inverse[j]
            for m in range(i):
                entry = entry - upper[(m, i)] * upper[(m, j)]
            if i == j:
                pivot = lax.rsqrt(jnp.maximum(entry, 1e-6))
                upper[(i, i)] = jnp.maximum(entry, 1e-6) * pivot
                over = pivot
            else:
                upper[(i, j)] = entry * over
    columns = [
        [(0, height * length[0]), (1, following * length[1])],
        [(1, shift * length[1]), (2, length[2])],
        [(2, shift * length[2]), (3, length[3])],
    ]
    zero = jnp.zeros_like(shift)
    hessenberg = [[zero] * 3 for _ in range(4)]
    for j in range(3):
        for i in range(j + 2):
            for m, factor in columns[j]:
                if m >= i:
                    hessenberg[i][j] = hessenberg[i][j] + upper[(i, m)] * factor
    target = [beta * length[0] * upper[(0, 0)], zero, zero, zero]
    turns = []
    for j in range(3):
        top, bottom = hessenberg[j][j], hessenberg[j + 1][j]
        turn = lax.rsqrt(top * top + bottom * bottom)
        turns.append(turn)
        cosine, sine = top * turn, bottom * turn
        for m in range(j, 3):
            high, low = hessenberg[j][m], hessenberg[j + 1][m]
            hessenberg[j][m] = cosine * high + sine * low
            hessenberg[j + 1][m] = cosine * low - sine * high
        high, low = target[j], target[j + 1]
        target[j] = cosine * high + sine * low
        target[j + 1] = cosine * low - sine * high
    weights = [zero] * 3
    for i in (2, 1, 0):
        value = target[i]
        for j in range(i + 1, 3):
            value = value - hessenberg[i][j] * weights[j]
        weights[i] = value * turns[i]
    copy.wait()
    for k in range(RHS):
        on_first, on_second, on_third = (
            column[k : k + 1, :] for column in (weights[0] * unit, weights[1], weights[2])
        )
        for a in range(2):
            solution[k, a] = (
                guess[k, a]
                + on_first * residual[k, a]
                + on_second * second[k, a]
                + on_third * third[k, a]
            )


def call(kernel, shapes, arguments, scratch=(), far_inputs=0, cost=0, grant=24 << 20, out=0):
    whole = pl.BlockSpec(memory_space=pltpu.VMEM)
    far = pl.BlockSpec(memory_space=pltpu.HBM)
    scalars = pl.BlockSpec(memory_space=pltpu.SMEM)

    def place(number, array):
        if len(array.shape) == 1:
            return scalars
        return far if number < far_inputs else whole

    outs = [
        jax.ShapeDtypeStruct(shape, jnp.float32 if len(shape) > 1 else jnp.int32)
        for shape in shapes
    ]
    outs[:out] = [pltpu.HBM(shape, jnp.float32) for shape in shapes[:out]]
    return pl.pallas_call(
        kernel,
        out_shape=outs,
        in_specs=[place(*numbered) for numbered in enumerate(arguments)],
        out_specs=[far] * out + [scalars if len(shape) == 1 else whole for shape in shapes[out:]],
        scratch_shapes=list(scratch),
        compiler_params=pltpu.CompilerParams(vmem_limit_bytes=grant),
        cost_estimate=pl.CostEstimate(flops=cost, bytes_accessed=cost, transcendentals=0)
        if cost
        else None,
    )(*arguments)


def nothing(value, *rest):
    pass


def after(value, *others):
    far = pl.BlockSpec(memory_space=pltpu.HBM)
    near = pl.BlockSpec(memory_space=pltpu.VMEM)
    return pl.pallas_call(
        nothing,
        out_shape=pltpu.HBM(value.shape, value.dtype),
        in_specs=[far] + [near] * len(others),
        out_specs=far,
        input_output_aliases={0: 0},
        compiler_params=pltpu.CompilerParams(vmem_limit_bytes=1 << 20),
    )(pltpu.with_memory_space_constraint(value, pltpu.HBM), *others)


def held(*shape):
    return pltpu.VMEM(shape, jnp.float32)


def swapped(first, second, axis):
    results = []
    for start, value in enumerate((first, second)):
        pairs = []
        for low in range(start, lax.axis_size(axis) - 1, 2):
            pairs += [(low, low + 1), (low + 1, low)]
        results.append(lax.ppermute(value, axis, pairs) if pairs else jnp.zeros_like(value))
    return results


def exchanged(part):
    return lax.all_to_all(part, ("gx", "gy"), 0, 0, tiled=True)


def body(couplings, diagonal, wells, ids, right, guess):
    devices = lax.axis_size("gx") * lax.axis_size("gy")
    plane = (8, LANES)
    field = guess.shape
    block = guess.shape[2:]
    arguments = (couplings, diagonal, wells, ids, right, guess)

    ends = []
    for argument in arguments:
        shape = argument.shape[:-3] + (2,) + argument.shape[-2:]
        ends += [pltpu.VMEM(shape, argument.dtype)] * 2
    x_first, x_second = call(
        x_pack_kernel,
        [(FACE_PLANES + 1,) + plane] * 2,
        [pltpu.with_memory_space_constraint(argument, pltpu.HBM) for argument in arguments],
        ends
        + [pltpu.SemaphoreType.DMA((len(ends),))]
        + [held(FACE_PLANES + 1, *plane)] * 2,
        far_inputs=len(arguments),
    )
    came_x = swapped(x_first, x_second, "gx")
    first_chunks, chunks = (devices, TABLE_ROWS, LANES), (devices, 16, LANES)
    sent = pltpu.SemaphoreType.DMA((1,))
    part, present, y_low, y_high = call(
        guess_kernel,
        [first_chunks, (WELLS + 8,)] + [(FACE_PLANES,) + plane] * 2,
        arguments,
        [held(6, *block), held(6, WELLS, LANES), held(*first_chunks), sent],
        cost=4 << 20,
        out=1,
    )
    parts = exchanged(after(part, came_x[0]))
    y_shape = (FACE_PLANES + CORNER_PLANES,) + plane
    y_first, y_second, fxl, fxh = call(
        corner_kernel,
        [y_shape] * 2 + [(FACE_PLANES + 1,) + plane] * 2,
        (y_low, y_high, *came_x),
        [held(*y_shape)] * 2,
    )
    came_y = swapped(y_first, y_second, "gy")
    ahead = call(
        block_kernel,
        [field, (4, 8) + plane],
        (couplings, diagonal, right, guess, y_first),
        cost=4 << 20,
    )

    residual, image, residual_faces, *packs, small, fyl, fyh = call(
        residual_kernel,
        [field, field, (4, 8) + plane]
        + [(IMAGE_PLANES,) + plane] * 4
        + [(8, LANES)]
        + [y_shape] * 2,
        (couplings, diagonal, wells, ids, fxl, fxh, *came_y, parts, *ahead),
        [held(IMAGE_PLANES, *plane)] * 4,
    )
    faces = (fxl, fxh, fyl, fyh)
    came_x, came_y = swapped(*packs[:2], "gx"), swapped(*packs[2:], "gy")
    (part,) = call(
        moments_kernel,
        [chunks],
        (wells, ids, residual, image, present),
        [held(16, *block), held(16, WELLS, LANES), held(3, *plane), held(*chunks), sent],
        cost=4 << 20,
        out=1,
    )
    parts = exchanged(part)
    second, third, part, known = call(
        krylov_kernel,
        [field, field, (devices, 1, (RHS + 1) * LANES), (4 * RHS, LANES)],
        (couplings, diagonal, wells, ids) + faces + (*came_x, *came_y)
        + (residual, image, residual_faces, parts, small, present),
        [held(12, WELLS, LANES), held(12, *block), held(10, *plane)]
        + [held(IMAGE_PLANES, *plane)] * 4,
    )
    parts = exchanged(part)
    (result,) = call(
        solve_kernel,
        [field],
        (
            pltpu.with_memory_space_constraint(guess, pltpu.HBM),
            residual, second, third, parts, known,
        ),
        [held(*field), pltpu.SemaphoreType.DMA((1,))],
        far_inputs=1,
    )
    return result


def solution(mesh):
    in_specs = (
        P("member", None, "gx", "gy", None),
        P("member", "gx", "gy", None),
        P("member", "gx", "gy", None),
        P("gx", "gy", None),
        P("member", None, "gx", "gy", None),
        P("member", None, "gx", "gy", None),
    )
    out_specs = P("member", None, "gx", "gy", None)
    return jax.shard_map(body, mesh=mesh, in_specs=in_specs, out_specs=out_specs, check_vma=False)
```

```python
import jax
import jax.numpy as jnp
from jax import lax
from jax.experimental import pallas as pl
from jax.experimental.pallas import tpu as pltpu
from jax.sharding import PartitionSpec as P

WELLS = 40
RHS = 4
LANES = 128
WELL_EQ, WELL_ID, GUESS, REST = 4, 6, 7, 15
UP_WELL, DOWN_WELL, RISE_WELL, FALL_WELL, DIAGONAL_WELL = 23, 25, 27, 29, 31
BACK_WELL, BACK_ID = 33, 35
FACE_PLANES = 36
ENDS = 36
CORNER_PLANES = 5
LAT_UP, LAT_DOWN, RISE, FALL, DIAGONAL, BACK_IN = 0, 4, 8, 12, 16, 20
LAYER_BLOCKS = 24
IMAGE_PLANES = 16
TABLE_ROWS = 6
GRAM_ENTRIES = 10
CORNER_ROWS = 19
SIDE_IN, SIDE_EQ, SIDE_ID, SIDE_GUESS = 4, 8, 10, 11


def product(blocks, first, second):
    return [
        blocks(0) * first + blocks(2) * second,
        blocks(1) * first + blocks(3) * second,
    ]


def iota(shape, axis):
    return lax.broadcasted_iota(jnp.int32, shape, axis)


def roll_up(value, axis):
    return pltpu.roll(value, 1, axis)


def roll_down(value, axis):
    return pltpu.roll(value, value.shape[axis] - 1, axis)


def layer_moves(rising, falling):
    axis = rising.ndim - 1
    lane = iota(rising.shape, axis)
    up = jnp.where(lane == 0, 0.0, roll_up(rising, axis))
    down = jnp.where(lane == LANES - 1, 0.0, roll_down(falling, axis))
    return up + down


def block_stencil(couplings, diagonal, first, second, incoming):
    result = product(lambda e: diagonal[e], first, second)
    moved = [product(lambda e, d=d: couplings[d, e], first, second) for d in range(6)]
    row = iota(first.shape, 1)
    outgoing = [[], [], [], []]
    for b in range(2):
        east, west, north, south, rise, fall = (moved[d][b] for d in range(6))
        total = result[b] + jnp.concatenate([incoming[0][b][None], east[:-1]], axis=0)
        total = total + jnp.concatenate([west[1:], incoming[1][b][None]], axis=0)
        total = total + jnp.where(row == 0, incoming[2][b][:, None, :], roll_up(north, 1))
        total = total + jnp.where(
            row == row.shape[1] - 1, incoming[3][b][:, None, :], roll_down(south, 1)
        )
        result[b] = total + layer_moves(rise, fall)
        outgoing[0].append(west[0])
        outgoing[1].append(east[-1])
        outgoing[2].append(south[:, 0, :])
        outgoing[3].append(north[:, -1, :])
    return result, outgoing


def face_stencil(blocks, first, second, behind):
    def times(start):
        return product(lambda e: blocks(start + e), first, second)

    moves = [times(start) for start in (DIAGONAL, LAT_UP, LAT_DOWN, RISE, FALL)]
    return face_moves(*moves, behind)


def face_moves(kept, up, down, rise, fall, behind):
    result = list(kept)
    row = iota(kept[0].shape, 0)
    for b in range(2):
        total = result[b] + behind[b] + layer_moves(rise[b], fall[b])
        total = total + jnp.where(row == 0, 0.0, roll_up(up[b], 0))
        result[b] = total + jnp.where(row == row.shape[0] - 1, 0.0, roll_down(down[b], 0))
    return result


def face_entries(low_end, high_end, entering):
    row = iota(entering[0].shape, 0)
    return [
        entering[b]
        + jnp.where(row == 0, low_end[b], 0.0)
        + jnp.where(row == row.shape[0] - 1, high_end[b], 0.0)
        for b in range(2)
    ]


def spread(totals, ids):
    table = jnp.broadcast_to(totals, (8, LANES))
    if ids.ndim == 2:
        return jnp.take_along_axis(table, ids, axis=1)
    return jnp.stack(
        [jnp.take_along_axis(table, ids[x], axis=1) for x in range(ids.shape[0])], axis=0
    )


def as_ids(plane):
    return plane.astype(jnp.int32)


class Corner:
    def __init__(self, pack, which, base):
        self.pack, self.start = pack, base * 8 + which

    def row(self, number):
        at = self.start + number
        return self.pack[at // 8, at % 8 : at % 8 + 1, :]


def corners_of(faces, base, rows):
    found = []
    for y_face in (2, 3):
        for x_end in range(2):
            found.append(Corner(faces[y_face], x_end * rows, base))
    return found


def corner_inputs(corners, values):
    ends = {}
    for c in range(4):
        x_end, y_end = c % 2, c // 2
        over_x = product(corners[c].row, *values[c])
        over_y = product(lambda e, c=c: corners[c].row(SIDE_IN + e), *values[c])
        ends[(2 + y_end, x_end)] = over_x
        ends[(x_end, y_end)] = over_y
    return ends


def tile_sum(first, second):
    value = first[0] * second[0] + first[1] * second[1]
    return jnp.sum(jnp.sum(value, axis=0), axis=0, keepdims=True)


def list_wells(ids, present):
    planes = [ids[x].astype(jnp.float32) for x in range(ids.shape[0])]
    middle = WELLS // 2
    halves = ((0.0, float(middle)), (float(middle), float(WELLS)))

    def least(above, top):
        found = [jnp.where((p > above) & (p < top), p, top) for p in planes]
        value = found[0]
        for other in found[1:]:
            value = jnp.minimum(value, other)
        return jnp.min(value)

    def greatest(base, below):
        found = [jnp.where((p >= base) & (p < below), p, base - 1.0) for p in planes]
        value = found[0]
        for other in found[1:]:
            value = jnp.maximum(value, other)
        return jnp.max(value)

    def some_left(state):
        return (state[1] <= state[2]) | (state[3] <= state[4])

    def step(state):
        number, ends = state[0], state[1:]
        after = []
        for half, (base, top) in enumerate(halves):
            low, high = ends[2 * half], ends[2 * half + 1]
            present[number] = low.astype(jnp.int32)
            number = number + jnp.where(low <= high, 1, 0)
            present[number] = high.astype(jnp.int32)
            number = number + jnp.where(low < high, 1, 0)
            after += [least(low, top), greatest(base, high)]
        return (number, *after)

    ends = []
    for base, top in halves:
        ends += [least(base - 1.0, top), greatest(base, top)]
    state = lax.while_loop(some_left, step, (jnp.int32(1), *ends))
    present[0] = state[0] - 1


def segment_rows(ids, values, scratch, present):
    scratch[...] = jnp.zeros_like(scratch)
    count, depth = values.shape[0], ids.shape[0]

    def one_well(step, _):
        well = present[step + 1]
        masks = [ids[x] == well for x in range(depth)]
        for number in range(count):
            total = jnp.where(masks[0], values[number, 0], 0.0)
            for x in range(1, depth):
                total = total + jnp.where(masks[x], values[number, x], 0.0)
            scratch[number, pl.ds(well, 1), :] = jnp.sum(total, axis=0, keepdims=True)
        return 0

    lax.fori_loop(0, present[0], one_well, 0)
    rows = []
    for number in range(count):
        summed = jnp.sum(scratch[number], axis=1, keepdims=True)
        shape = scratch.shape[1:]
        on_lanes = jnp.where(iota(shape, 0) == iota(shape, 1), summed, 0.0)
        rows.append(jnp.sum(on_lanes, axis=0, keepdims=True))
    return rows


def pack_rows(rows, table):
    for number, row in enumerate(rows):
        placed = row if number % 3 == 0 else pltpu.roll(row, WELLS * (number % 3), 1)
        table = table + jnp.where(
            iota(table.shape, 0) == number // 3, jnp.broadcast_to(placed, table.shape), 0.0
        )
    return table


def unpack_row(table, number):
    row = table[number // 3 : number // 3 + 1, :]
    if number % 3:
        row = pltpu.roll(row, LANES - WELLS * (number % 3), 1)
    return jnp.where(iota(row.shape, 1) < WELLS, row, 0.0)


def place_rows(rows, table):
    for number, row in enumerate(rows):
        group, k = divmod(number, RHS)
        at = k + RHS * (group // 3)
        placed = pltpu.roll(row, WELLS * group, 1) if group in (1, 2) else row
        table = table + jnp.where(
            iota(table.shape, 0) == at, jnp.broadcast_to(placed, table.shape), 0.0
        )
    return table


def place_columns(dots, first_lane, table):
    for number in range(dots.shape[0]):
        column = jnp.sum(dots[number], axis=1, keepdims=True)
        table = table + jnp.where(iota(table.shape, 1) == first_lane + number, column, 0.0)
    return table


def take_group(table, group):
    if group in (1, 2):
        table = pltpu.roll(table, LANES - WELLS * group, 1)
    start = RHS * (group // 3)
    rows = table[start : start + RHS, :]
    return jnp.where(iota(rows.shape, 1) < WELLS, rows, 0.0)


def take_column(table, lane):
    return table[RHS : 2 * RHS, lane : lane + 1]


def lane_sum(row):
    return jnp.sum(row, axis=1, keepdims=True)


def on_even(axis):
    return lax.rem(lax.axis_index(axis), 2) == 0


def by_pair(axis, low, high, first, second):
    @pl.when(on_even(axis))
    def _():
        first[...] = high[...]
        second[...] = low[...]

    @pl.when(jnp.logical_not(on_even(axis)))
    def _():
        first[...] = low[...]
        second[...] = high[...]


def by_side(axis, first, second, low, high):
    by_pair(axis, second, first, high, low)


COUPLINGS, DIAGONALS, WELL_FIELDS, IDS, RIGHT_SIDE, START = range(6)


def layer_blocks(cut, inward, lateral):
    def plane(n):
        if n < DIAGONAL:
            return cut(COUPLINGS, ((lateral, lateral + 1, 4, 5)[n // 4], n % 4), 0)
        if n < BACK_IN:
            return cut(DIAGONALS, (n - DIAGONAL,), 0)
        return cut(COUPLINGS, (inward, n - BACK_IN), 1)

    return plane


def fill_pack(pack, inward, lateral, cut):
    blocks = layer_blocks(cut, inward, lateral)
    for e in range(4):
        pack[e] = cut(COUPLINGS, (inward, e), 0)
    wells = [cut(WELL_FIELDS, (2 + a,), 0) for a in range(2)]
    for a in range(2):
        pack[WELL_EQ + a] = wells[a]
    pack[WELL_ID] = cut(IDS, (), 0).astype(jnp.float32)
    pack[BACK_ID] = cut(IDS, (), 1).astype(jnp.float32)
    for start, at in (
        (LAT_UP, UP_WELL),
        (LAT_DOWN, DOWN_WELL),
        (RISE, RISE_WELL),
        (FALL, FALL_WELL),
        (DIAGONAL, DIAGONAL_WELL),
        (BACK_IN, BACK_WELL),
    ):
        if start == BACK_IN:
            wells = [cut(WELL_FIELDS, (2 + a,), 1) for a in range(2)]
        for b, value in enumerate(product(lambda e: blocks(start + e), *wells)):
            pack[at + b] = value
    for k in range(RHS):
        here = [cut(START, (k, a), 0) for a in range(2)]
        back = [cut(START, (k, a), 1) for a in range(2)]
        entering = product(lambda e: blocks(BACK_IN + e), *back)
        local = face_stencil(blocks, here[0], here[1], entering)
        for a in range(2):
            pack[GUESS + 2 * k + a] = here[a]
            pack[REST + 2 * k + a] = cut(RIGHT_SIDE, (k, a), 0) - local[a]
    if pack.shape[0] > ENDS:
        end = pack.shape[1] - 1
        for e in range(4):
            pack[ENDS, e : e + 1, :] = blocks(LAT_UP + e)[end : end + 1, :]
            pack[ENDS, 4 + e : 5 + e, :] = blocks(LAT_DOWN + e)[0:1, :]


def x_pack_kernel(*refs):
    sources, first, second, held_ends, arrived = refs[:6], refs[6], refs[7], refs[8:20], refs[20]
    packs = refs[21:23]
    copies = []
    for n, source in enumerate(sources):
        lead = (slice(None),) * (len(source.shape) - 3)
        depth = source.shape[-3]
        for end, start in enumerate((0, depth - 2)):
            copies.append(
                pltpu.make_async_copy(
                    source.at[lead + (pl.ds(start, 2),)],
                    held_ends[2 * n + end],
                    arrived.at[2 * n + end],
                )
            )
    for copy in copies:
        copy.start()
    for copy in copies:
        copy.wait()
    for end, pack in enumerate(packs):
        fill_pack(
            pack,
            1 - end,
            2,
            lambda n, index, layer: held_ends[2 * n + end][
                index + (1 - layer if end else layer,)
            ],
        )
    by_pair("gx", *packs, first, second)


def y_cut(arguments, end):
    last = arguments[0].shape[-2] - 1

    def cut(n, index, layer):
        return arguments[n][index + (slice(None), last - layer if end else layer, slice(None))]

    return cut


def send_out(table, chunks, part, sent):
    rows = min(chunks.shape[1], table.shape[0])
    chunks[:, :rows, :] = jnp.broadcast_to(table[None, :rows], (chunks.shape[0], rows, LANES))
    copy = pltpu.make_async_copy(chunks, part, sent.at[0])
    copy.start()
    return copy


def corner_kernel(y_low, y_high, came_first, came_second, first, second, fxl, fxh, *outs):
    by_side("gx", came_first, came_second, fxl, fxh)
    last = fxl.shape[1] - 1
    for own, out, at, side in ((y_low, outs[0], 0, 4), (y_high, outs[1], last, 0)):
        for n in range(FACE_PLANES):
            out[n] = own[n]
        row = FACE_PLANES * 8
        out[FACE_PLANES + CORNER_PLANES - 1] = jnp.zeros(out.shape[1:], jnp.float32)
        for face in (fxl, fxh):
            rows = [(n, at) for n in range(4)]
            rows += [(ENDS, side + e) for e in range(4)]
            rows += [(n, at) for n in range(WELL_EQ, REST)]
            for n, y in rows:
                out[row // 8, row % 8 : row % 8 + 1, :] = face[n, y : y + 1, :]
                row += 1
    by_pair("gy", *outs, first, second)


def diagonal_device(x_end, y_end):
    across, along = lax.axis_index("gx"), lax.axis_index("gy")
    there_x, there_y = across + 2 * x_end - 1, along + 2 * y_end - 1
    count_x, count_y = lax.axis_size("gx"), lax.axis_size("gy")
    exists = (there_x >= 0) & (there_x < count_x) & (there_y >= 0) & (there_y < count_y)
    return exists, jnp.where(exists, there_x * count_y + there_y, 0)


def guess_kernel(
    couplings, diagonal, wells, ids, right, guess,
    part, present, y_low, y_high, values, scratch, chunks, sent,
):
    list_wells(ids, present)
    for k in range(RHS):
        values[k] = wells[0] * guess[k, 0] + wells[1] * guess[k, 1]
    values[4] = wells[0] * wells[2] + wells[1] * wells[3]
    values[5] = wells[2] * wells[2] + wells[3] * wells[3]
    rows = segment_rows(ids, values, scratch, present)
    table = pack_rows(rows, jnp.zeros((8, LANES), jnp.float32))
    copy = send_out(table, chunks, part, sent)
    arguments = (couplings, diagonal, wells, ids, right, guess)
    for end, pack in enumerate((y_low, y_high)):
        fill_pack(pack, 3 - end, 0, y_cut(arguments, end))
    copy.wait()


def block_kernel(
    couplings, diagonal, right, guess, sent_face, rest, leaving
):
    nothing_enters = [[jnp.zeros(guess.shape[3:], jnp.float32)] * 2] * 4
    for k in range(RHS):
        inside, outgoing = block_stencil(
            couplings, diagonal, guess[k, 0], guess[k, 1], nothing_enters
        )
        for a in range(2):
            rest[k, a] = right[k, a] - inside[a]
            for f in range(4):
                leaving[f, 2 * k + a] = outgoing[f][a]


def residual_kernel(
    couplings, diagonal, wells, ids, fxl, fxh, came_first, came_second, parts,
    rest, leaving,
    residual, image, residual_faces, x_first, x_second, y_first, y_second, small, fyl, fyh,
    x_low, x_high, y_low, y_high,
):
    by_side("gy", came_first, came_second, fyl, fyh)
    faces = (fxl, fxh, fyl, fyh)
    totals = jnp.sum(parts[...], axis=0)
    corners = corners_of(faces, FACE_PLANES, CORNER_ROWS)
    all_ids = ids[...]
    face_ids = [as_ids(face[WELL_ID]) for face in faces]
    last = rest.shape[2] - 1
    row = iota(rest.shape[2:], 1)
    for k in range(RHS):
        s_row = unpack_row(totals, k)
        entering = [
            product(
                lambda e, f=f: faces[f][e],
                faces[f][GUESS + 2 * k],
                faces[f][GUESS + 2 * k + 1],
            )
            for f in range(4)
        ]
        outgoing = [[leaving[f, 2 * k + b] for b in range(2)] for f in range(4)]
        at_wells = spread(s_row, all_ids)
        now = []
        for a in range(2):
            value = rest[k, a] - wells[2 + a] * at_wells
            over_x = [
                (value[0] - entering[0][a])[None],
                value[1:last],
                (value[last] - entering[1][a])[None],
            ]
            value = jnp.concatenate(over_x, axis=0)
            value = value - jnp.where(row == 0, entering[2][a][:, None, :], 0.0)
            now.append(value - jnp.where(row == last, entering[3][a][:, None, :], 0.0))
        for a in range(2):
            residual[k, a] = now[a]
        ends = corner_inputs(
            corners,
            [[corners[c].row(SIDE_GUESS + 2 * k + a) for a in range(2)] for c in range(4)],
        )
        incoming = []
        for f in range(4):
            face = faces[f]
            there = face_entries(ends[(f, 0)], ends[(f, 1)], outgoing[f])
            face_wells = spread(s_row, face_ids[f])
            outer = [
                face[REST + 2 * k + a] - there[a] - face[WELL_EQ + a] * face_wells
                for a in range(2)
            ]
            for a in range(2):
                residual_faces[f, 2 * k + a] = outer[a]
            incoming.append(product(lambda e, f=f: faces[f][e], *outer))
        result, _ = block_stencil(couplings, diagonal, now[0], now[1], incoming)
        for a in range(2):
            image[k, a] = result[a]
    own = (couplings, diagonal)
    for axis, packs in enumerate(((x_low, x_high), (y_low, y_high))):
        for end, pack in enumerate(packs):

            def cut(ref, index, layer):
                at = last - layer if end else layer
                return ref[index + ((at,) if axis == 0 else (slice(None), at, slice(None)))]

            plane = layer_blocks(
                lambda n, index, layer: cut(own[n], index, layer),
                2 * axis + 1 - end,
                2 * (1 - axis),
            )
            blocks = [plane(n) for n in range(LAYER_BLOCKS)]
            for k in range(RHS):
                here = [cut(image, (k, a), 0) for a in range(2)]
                back = [cut(image, (k, a), 1) for a in range(2)]
                entering = product(lambda e: blocks[BACK_IN + e], *back)
                local = face_stencil(lambda n: blocks[n], here[0], here[1], entering)
                for a in range(2):
                    pack[2 * k + a] = here[a]
                    pack[8 + 2 * k + a] = local[a]
    by_pair("gx", x_low, x_high, x_first, x_second)
    by_pair("gy", y_low, y_high, y_first, y_second)
    small[...] = jnp.concatenate(
        [unpack_row(totals, 4), unpack_row(totals, 5), jnp.zeros((6, LANES), jnp.float32)], axis=0
    )


def moments_kernel(
    wells, ids, residual, image, present, part, values, scratch, dots, chunks, sent
):
    dots[...] = jnp.zeros_like(dots)
    for k in range(RHS):
        now = [residual[k, a] for a in range(2)]
        result = [image[k, a] for a in range(2)]
        for n, field in enumerate((now, result)):
            values[4 * n + k] = wells[0] * field[0] + wells[1] * field[1]
            values[8 + 4 * n + k] = wells[2] * field[0] + wells[3] * field[1]
        row = slice(RHS + k, RHS + k + 1)
        dots[0, row, :] = tile_sum(now, now)
        dots[1, row, :] = tile_sum(now, result)
        dots[2, row, :] = tile_sum(result, result)
    rows = segment_rows(ids, values, scratch, present)
    table = place_rows(rows, jnp.zeros((8, LANES), jnp.float32))
    chunks[:, 8:, :] = jnp.zeros_like(chunks[:, 8:, :])
    last = image.shape[2] - 1
    for x_end in range(2):
        for y_end in range(2):
            exists, place = diagonal_device(x_end, y_end)

            @pl.when(exists)
            def _():
                for k in range(RHS):
                    for a in range(2):
                        row, y = 8 + 2 * k + a, last * y_end
                        chunks[pl.ds(place, 1), row : row + 1, :] = image[
                            k, a, last * x_end, y : y + 1, :
                        ][None]

    send_out(place_columns(dots, WELLS, table), chunks, part, sent).wait()


def first_step(totals, small):
    s_row, us_row, p_row, ps_row = (take_group(totals, group) for group in range(4))
    within, equation = small[0:1, :], small[1:2, :]
    rr, rs, ss = (take_column(totals, WELLS + i) for i in range(3))
    height = (rs + lane_sum(p_row * s_row)) / rr
    square = ss + lane_sum(2.0 * ps_row * s_row + equation * s_row * s_row)
    left = jnp.maximum(square - height * height * rr, 1e-7 * square)
    scale = lax.rsqrt(left)
    s_image = us_row + within * s_row
    s_second = (s_image - height * s_row) * scale
    p_second = (ps_row + equation * s_row - height * p_row) * scale
    shift = rs / rr + lane_sum(p_second * s_second)
    unit = lax.rsqrt(rr)
    following = left * scale * unit
    return s_row, s_image, p_row, p_second, (unit, rr * unit, height, shift, following, scale)


def krylov_kernel(
    couplings, diagonal, wells, ids, fxl, fxh, fyl, fyh, x_first, x_second, y_first, y_second,
    residual, image, residual_faces, parts, small_in, present,
    second_out, third_out, part, known, scratch, values_scratch, dots, gxl, gxh, gyl, gyh,
):
    by_side("gx", x_first, x_second, gxl, gxh)
    by_side("gy", y_first, y_second, gyl, gyh)
    faces, sent = (fxl, fxh, fyl, fyh), (gxl, gxh, gyl, gyh)
    totals = jnp.sum(parts[:, 0:8, :], axis=0)
    small = small_in[...]
    s_rows, s_images, p_rows, p_seconds, scalars = first_step(totals, small)
    known[0:RHS, :] = p_rows
    known[RHS : 2 * RHS, :] = p_seconds
    columns = jnp.zeros((RHS, LANES), jnp.float32)
    for n, column in enumerate(scalars):
        columns = columns + jnp.where(iota(columns.shape, 1) == n, column, 0.0)
    known[2 * RHS : 3 * RHS, :] = columns
    known[3 * RHS :, :] = jnp.broadcast_to(small[1:2, :], (RHS, LANES))
    dots[...] = jnp.zeros_like(dots)
    corners = corners_of(faces, FACE_PLANES, CORNER_ROWS)
    places = [diagonal_device(c % 2, c // 2)[1] for c in range(4)]
    all_ids = ids[...]
    face_ids = [as_ids(face[WELL_ID]) for face in faces]
    back_ids = [as_ids(face[BACK_ID]) for face in faces]
    corner_ids = [
        as_ids(jnp.broadcast_to(corner.row(SIDE_ID), (8, LANES))) for corner in corners
    ]
    for k in range(RHS):
        unit, _, height, shift, _, scale = (column[k : k + 1, :] for column in scalars)
        s_row, s_image = s_rows[k : k + 1, :], s_images[k : k + 1, :]
        at_wells = spread(s_row, all_ids)
        now = [image[k, a] + wells[2 + a] * at_wells for a in range(2)]
        face_now, spread_now = [], []
        for f in range(4):
            here = spread(s_row, face_ids[f])
            spread_now.append((here, spread(s_row, back_ids[f])))
            face_now.append(
                [sent[f][2 * k + a] + faces[f][WELL_EQ + a] * here for a in range(2)]
            )
        corner_now = []
        for c in range(4):
            here = spread(s_row, corner_ids[c])[0:1, :]
            corner_now.append(
                [
                    parts[pl.ds(places[c], 1), 8 + 2 * k + a, :] + corners[c].row(SIDE_EQ + a) * here
                    for a in range(2)
                ]
            )
        incoming = [product(lambda e, f=f: faces[f][e], *face_now[f]) for f in range(4)]
        applied, outgoing = block_stencil(couplings, diagonal, now[0], now[1], incoming)
        at_wells = spread(s_image, all_ids)
        second, third = [], []
        for a in range(2):
            twice = applied[a] + wells[2 + a] * at_wells
            base = (now[a] - height * residual[k, a]) * scale
            second.append(base)
            third.append((twice - height * now[a]) * scale - shift * base)
            second_out[k, a] = second[a]
            third_out[k, a] = third[a]
        ends = corner_inputs(corners, corner_now)
        incoming = []
        for f in range(4):
            face = faces[f]
            here, behind = spread_now[f]
            moves = [
                [face[at + b] * here for b in range(2)]
                for at in (DIAGONAL_WELL, UP_WELL, DOWN_WELL, RISE_WELL, FALL_WELL)
            ]
            there = face_moves(*moves, [face[BACK_WELL + b] * behind for b in range(2)])
            local = [sent[f][8 + 2 * k + b] + there[b] for b in range(2)]
            over = face_entries(ends[(f, 0)], ends[(f, 1)], outgoing[f])
            here = spread(s_image, face_ids[f])
            outer = []
            for a in range(2):
                twice = local[a] + over[a] + face[WELL_EQ + a] * here
                base = (face_now[f][a] - height * residual_faces[f, 2 * k + a]) * scale
                outer.append((twice - height * face_now[f][a]) * scale - shift * base)
            incoming.append(product(lambda e, f=f: faces[f][e], *outer))
        result, _ = block_stencil(couplings, diagonal, third[0], third[1], incoming)
        fourth = [result[a] - shift * third[a] for a in range(2)]
        values_scratch[k] = wells[0] * third[0] + wells[1] * third[1]
        values_scratch[4 + k] = wells[2] * third[0] + wells[3] * third[1]
        values_scratch[8 + k] = wells[2] * fourth[0] + wells[3] * fourth[1]
        fields = [[residual[k, a] * unit for a in range(2)], second, third, fourth]
        number = 0
        for i in range(4):
            for j in range(i, 4):
                dots[number, RHS + k : RHS + k + 1, :] = tile_sum(fields[i], fields[j])
                number += 1
    rows = segment_rows(ids, values_scratch, scratch, present)
    table = place_rows(rows, jnp.zeros((8, LANES), jnp.float32))
    table = place_columns(dots, 0, table)
    gram = table[RHS : RHS + 1, :]
    for k in range(1, RHS):
        gram = gram + pltpu.roll(table[RHS + k : RHS + k + 1, :], GRAM_ENTRIES * k, 1)
    flat = jnp.concatenate([table[k : k + 1, :] for k in range(RHS)] + [gram], axis=1)
    part[...] = jnp.broadcast_to(flat[None], part.shape)


def solve_kernel(
    guess_in, residual, second, third, parts, known, solution, guess, arrived
):
    copy = pltpu.make_async_copy(guess_in, guess, arrived.at[0])
    copy.start()
    flat = jnp.sum(parts[...], axis=0)
    rows = [flat[:, LANES * n : LANES * (n + 1)] for n in range(RHS + 1)]
    for k in range(1, RHS):
        rows.append(pltpu.roll(rows[RHS], LANES - GRAM_ENTRIES * k, 1))
    totals = jnp.concatenate(rows, axis=0)
    s_third, p_third, p_fourth = (take_group(totals, group) for group in range(3))
    p_first, p_second = known[0:RHS, :], known[RHS : 2 * RHS, :]
    unit, beta, height, shift, following = (
        known[2 * RHS : 3 * RHS, n : n + 1] for n in range(5)
    )
    equation = known[3 * RHS :, :]
    gram = {}
    number = 0
    for i in range(4):
        for j in range(i, 4):
            gram[(i, j)] = take_column(totals, number)
            number += 1
    gram[(0, 3)] += lane_sum(p_first * s_third) * unit
    gram[(1, 3)] += lane_sum(p_second * s_third)
    gram[(2, 3)] += lane_sum(p_third * s_third)
    gram[(3, 3)] += lane_sum(2.0 * p_fourth * s_third + equation * s_third * s_third)
    tiny = 1e-30
    inverse = [lax.rsqrt(jnp.maximum(gram[(i, i)], tiny)) for i in range(4)]
    length = [jnp.maximum(gram[(i, i)], tiny) * inverse[i] for i in range(4)]
    upper = {}
    for i in range(4):
        for j in range(i, 4):
            entry = gram[(i, j)] * inverse[i] * inverse[j]
            for m in range(i):
                entry = entry - upper[(m, i)] * upper[(m, j)]
            if i == j:
                pivot = lax.rsqrt(jnp.maximum(entry, 1e-6))
                upper[(i, i)] = jnp.maximum(entry, 1e-6) * pivot
                over = pivot
            else:
                upper[(i, j)] = entry * over
    columns = [
        [(0, height * length[0]), (1, following * length[1])],
        [(1, shift * length[1]), (2, length[2])],
        [(2, shift * length[2]), (3, length[3])],
    ]
    zero = jnp.zeros_like(shift)
    hessenberg = [[zero] * 3 for _ in range(4)]
    for j in range(3):
        for i in range(j + 2):
            for m, factor in columns[j]:
                if m >= i:
                    hessenberg[i][j] = hessenberg[i][j] + upper[(i, m)] * factor
    target = [beta * length[0] * upper[(0, 0)], zero, zero, zero]
    turns = []
    for j in range(3):
        top, bottom = hessenberg[j][j], hessenberg[j + 1][j]
        turn = lax.rsqrt(top * top + bottom * bottom)
        turns.append(turn)
        cosine, sine = top * turn, bottom * turn
        for m in range(j, 3):
            high, low = hessenberg[j][m], hessenberg[j + 1][m]
            hessenberg[j][m] = cosine * high + sine * low
            hessenberg[j + 1][m] = cosine * low - sine * high
        high, low = target[j], target[j + 1]
        target[j] = cosine * high + sine * low
        target[j + 1] = cosine * low - sine * high
    weights = [zero] * 3
    for i in (2, 1, 0):
        value = target[i]
        for j in range(i + 1, 3):
            value = value - hessenberg[i][j] * weights[j]
        weights[i] = value * turns[i]
    copy.wait()
    for k in range(RHS):
        on_first, on_second, on_third = (
            column[k : k + 1, :] for column in (weights[0] * unit, weights[1], weights[2])
        )
        for a in range(2):
            solution[k, a] = (
                guess[k, a]
                + on_first * residual[k, a]
                + on_second * second[k, a]
                + on_third * third[k, a]
            )


def call(kernel, shapes, arguments, scratch=(), far_inputs=0, cost=0, grant=24 << 20, out=0):
    whole = pl.BlockSpec(memory_space=pltpu.VMEM)
    far = pl.BlockSpec(memory_space=pltpu.HBM)
    scalars = pl.BlockSpec(memory_space=pltpu.SMEM)

    def place(number, array):
        if len(array.shape) == 1:
            return scalars
        return far if number < far_inputs else whole

    outs = [
        jax.ShapeDtypeStruct(shape, jnp.float32 if len(shape) > 1 else jnp.int32)
        for shape in shapes
    ]
    outs[:out] = [pltpu.HBM(shape, jnp.float32) for shape in shapes[:out]]
    return pl.pallas_call(
        kernel,
        out_shape=outs,
        in_specs=[place(*numbered) for numbered in enumerate(arguments)],
        out_specs=[far] * out + [scalars if len(shape) == 1 else whole for shape in shapes[out:]],
        scratch_shapes=list(scratch),
        compiler_params=pltpu.CompilerParams(vmem_limit_bytes=grant),
        cost_estimate=pl.CostEstimate(flops=cost, bytes_accessed=cost, transcendentals=0)
        if cost
        else None,
    )(*arguments)


def nothing(value, *rest):
    pass


def after(value, *others):
    far = pl.BlockSpec(memory_space=pltpu.HBM)
    near = pl.BlockSpec(memory_space=pltpu.VMEM)
    return pl.pallas_call(
        nothing,
        out_shape=pltpu.HBM(value.shape, value.dtype),
        in_specs=[far] + [near] * len(others),
        out_specs=far,
        input_output_aliases={0: 0},
        compiler_params=pltpu.CompilerParams(vmem_limit_bytes=1 << 20),
    )(pltpu.with_memory_space_constraint(value, pltpu.HBM), *others)


def held(*shape):
    return pltpu.VMEM(shape, jnp.float32)


def swap(value, axis, start):
    pairs = []
    for low in range(start, lax.axis_size(axis) - 1, 2):
        pairs += [(low, low + 1), (low + 1, low)]
    return lax.ppermute(value, axis, pairs) if pairs else jnp.zeros_like(value)


def swapped(first, second, axis):
    return swap(first, axis, 0), swap(second, axis, 1)


def exchanged(part):
    return lax.all_to_all(part, ("gx", "gy"), 0, 0, tiled=True)


def body(couplings, diagonal, wells, ids, right, guess):
    devices = lax.axis_size("gx") * lax.axis_size("gy")
    plane = (8, LANES)
    field = guess.shape
    block = guess.shape[2:]
    arguments = (couplings, diagonal, wells, ids, right, guess)

    ends = []
    for argument in arguments:
        shape = argument.shape[:-3] + (2,) + argument.shape[-2:]
        ends += [pltpu.VMEM(shape, argument.dtype)] * 2
    x_first, x_second = call(
        x_pack_kernel,
        [(FACE_PLANES + 1,) + plane] * 2,
        [pltpu.with_memory_space_constraint(argument, pltpu.HBM) for argument in arguments],
        ends
        + [pltpu.SemaphoreType.DMA((len(ends),))]
        + [held(FACE_PLANES + 1, *plane)] * 2,
        far_inputs=len(arguments),
    )
    came_x = swapped(x_first, x_second, "gx")
    first_chunks, chunks = (devices, TABLE_ROWS, LANES), (devices, 16, LANES)
    sent = pltpu.SemaphoreType.DMA((1,))
    part, present, y_low, y_high = call(
        guess_kernel,
        [first_chunks, (WELLS + 8,)] + [(FACE_PLANES,) + plane] * 2,
        arguments,
        [held(6, *block), held(6, WELLS, LANES), held(*first_chunks), sent],
        cost=4 << 20,
        out=1,
    )
    parts = exchanged(after(part, came_x[0]))
    y_shape = (FACE_PLANES + CORNER_PLANES,) + plane
    y_first, y_second, fxl, fxh = call(
        corner_kernel,
        [y_shape] * 2 + [(FACE_PLANES + 1,) + plane] * 2,
        (y_low, y_high, *came_x),
        [held(*y_shape)] * 2,
    )
    came_y = swapped(y_first, y_second, "gy")
    ahead = call(
        block_kernel,
        [field, (4, 8) + plane],
        (couplings, diagonal, right, guess, y_first),
        cost=4 << 20,
    )

    residual, image, residual_faces, *packs, small, fyl, fyh = call(
        residual_kernel,
        [field, field, (4, 8) + plane]
        + [(IMAGE_PLANES,) + plane] * 4
        + [(8, LANES)]
        + [y_shape] * 2,
        (couplings, diagonal, wells, ids, fxl, fxh, *came_y, parts, *ahead),
        [held(IMAGE_PLANES, *plane)] * 4,
    )
    faces = (fxl, fxh, fyl, fyh)
    came_y1 = swap(packs[3], "gy", 1)
    came_x1 = swap(packs[1], "gx", 1)
    came_x0 = swap(packs[0], "gx", 0)
    came_y0 = swap(packs[2], "gy", 0)
    (part,) = call(
        moments_kernel,
        [chunks],
        (wells, ids, residual, image, present),
        [held(16, *block), held(16, WELLS, LANES), held(3, *plane), held(*chunks), sent],
        cost=4 << 20,
        out=1,
    )
    parts = exchanged(part)
    second, third, part, known = call(
        krylov_kernel,
        [field, field, (devices, 1, (RHS + 1) * LANES), (4 * RHS, LANES)],
        (couplings, diagonal, wells, ids) + faces + (came_x0, came_x1, came_y0, came_y1)
        + (residual, image, residual_faces, parts, small, present),
        [held(12, WELLS, LANES), held(12, *block), held(10, *plane)]
        + [held(IMAGE_PLANES, *plane)] * 4,
    )
    parts = exchanged(part)
    (result,) = call(
        solve_kernel,
        [field],
        (
            pltpu.with_memory_space_constraint(guess, pltpu.HBM),
            residual, second, third, parts, known,
        ),
        [held(*field), pltpu.SemaphoreType.DMA((1,))],
        far_inputs=1,
    )
    return result


def solution(mesh):
    in_specs = (
        P("member", None, "gx", "gy", None),
        P("member", "gx", "gy", None),
        P("member", "gx", "gy", None),
        P("gx", "gy", None),
        P("member", None, "gx", "gy", None),
        P("member", None, "gx", "gy", None),
    )
    out_specs = P("member", None, "gx", "gy", None)
    return jax.shard_map(body, mesh=mesh, in_specs=in_specs, out_specs=out_specs, check_vma=False)
```

```python
import jax
import jax.numpy as jnp
from jax import lax
from jax.experimental import pallas as pl
from jax.experimental.pallas import tpu as pltpu
from jax.sharding import PartitionSpec as P

WELLS = 40
RHS = 4
LANES = 128
WELL_EQ, WELL_ID, GUESS, REST = 4, 6, 7, 15
UP_WELL, DOWN_WELL, RISE_WELL, FALL_WELL, DIAGONAL_WELL = 23, 25, 27, 29, 31
BACK_WELL, BACK_ID = 33, 35
FACE_PLANES = 36
ENDS = 36
CORNER_PLANES = 5
LAT_UP, LAT_DOWN, RISE, FALL, DIAGONAL, BACK_IN = 0, 4, 8, 12, 16, 20
LAYER_BLOCKS = 24
IMAGE_PLANES = 16
TABLE_ROWS = 6
GRAM_ENTRIES = 10
CORNER_ROWS = 19
SIDE_IN, SIDE_EQ, SIDE_ID, SIDE_GUESS = 4, 8, 10, 11


def product(blocks, first, second):
    return [
        blocks(0) * first + blocks(2) * second,
        blocks(1) * first + blocks(3) * second,
    ]


def iota(shape, axis):
    return lax.broadcasted_iota(jnp.int32, shape, axis)


def roll_up(value, axis):
    return pltpu.roll(value, 1, axis)


def roll_down(value, axis):
    return pltpu.roll(value, value.shape[axis] - 1, axis)


def layer_moves(rising, falling):
    axis = rising.ndim - 1
    lane = iota(rising.shape, axis)
    up = jnp.where(lane == 0, 0.0, roll_up(rising, axis))
    down = jnp.where(lane == LANES - 1, 0.0, roll_down(falling, axis))
    return up + down


def block_stencil(couplings, diagonal, first, second, incoming):
    result = product(lambda e: diagonal[e], first, second)
    moved = [product(lambda e, d=d: couplings[d, e], first, second) for d in range(6)]
    row = iota(first.shape, 1)
    outgoing = [[], [], [], []]
    for b in range(2):
        east, west, north, south, rise, fall = (moved[d][b] for d in range(6))
        total = result[b] + jnp.concatenate([incoming[0][b][None], east[:-1]], axis=0)
        total = total + jnp.concatenate([west[1:], incoming[1][b][None]], axis=0)
        total = total + jnp.where(row == 0, incoming[2][b][:, None, :], roll_up(north, 1))
        total = total + jnp.where(
            row == row.shape[1] - 1, incoming[3][b][:, None, :], roll_down(south, 1)
        )
        result[b] = total + layer_moves(rise, fall)
        outgoing[0].append(west[0])
        outgoing[1].append(east[-1])
        outgoing[2].append(south[:, 0, :])
        outgoing[3].append(north[:, -1, :])
    return result, outgoing


def face_stencil(blocks, first, second, behind):
    def times(start):
        return product(lambda e: blocks(start + e), first, second)

    moves = [times(start) for start in (DIAGONAL, LAT_UP, LAT_DOWN, RISE, FALL)]
    return face_moves(*moves, behind)


def face_moves(kept, up, down, rise, fall, behind):
    result = list(kept)
    row = iota(kept[0].shape, 0)
    for b in range(2):
        total = result[b] + behind[b] + layer_moves(rise[b], fall[b])
        total = total + jnp.where(row == 0, 0.0, roll_up(up[b], 0))
        result[b] = total + jnp.where(row == row.shape[0] - 1, 0.0, roll_down(down[b], 0))
    return result


def face_entries(low_end, high_end, entering):
    row = iota(entering[0].shape, 0)
    return [
        entering[b]
        + jnp.where(row == 0, low_end[b], 0.0)
        + jnp.where(row == row.shape[0] - 1, high_end[b], 0.0)
        for b in range(2)
    ]


def spread(totals, ids):
    table = jnp.broadcast_to(totals, (8, LANES))
    if ids.ndim == 2:
        return jnp.take_along_axis(table, ids, axis=1)
    return jnp.stack(
        [jnp.take_along_axis(table, ids[x], axis=1) for x in range(ids.shape[0])], axis=0
    )


def as_ids(plane):
    return plane.astype(jnp.int32)


class Corner:
    def __init__(self, pack, which, base):
        self.pack, self.start = pack, base * 8 + which

    def row(self, number):
        at = self.start + number
        return self.pack[at // 8, at % 8 : at % 8 + 1, :]


def corners_of(faces, base, rows):
    found = []
    for y_face in (2, 3):
        for x_end in range(2):
            found.append(Corner(faces[y_face], x_end * rows, base))
    return found


def corner_inputs(corners, values):
    ends = {}
    for c in range(4):
        x_end, y_end = c % 2, c // 2
        over_x = product(corners[c].row, *values[c])
        over_y = product(lambda e, c=c: corners[c].row(SIDE_IN + e), *values[c])
        ends[(2 + y_end, x_end)] = over_x
        ends[(x_end, y_end)] = over_y
    return ends


def tile_sum(first, second):
    value = first[0] * second[0] + first[1] * second[1]
    return jnp.sum(jnp.sum(value, axis=0), axis=0, keepdims=True)


def list_wells(ids, present):
    planes = [ids[x].astype(jnp.float32) for x in range(ids.shape[0])]
    middle = WELLS // 2
    halves = ((0.0, float(middle)), (float(middle), float(WELLS)))

    def least(above, top):
        found = [jnp.where((p > above) & (p < top), p, top) for p in planes]
        value = found[0]
        for other in found[1:]:
            value = jnp.minimum(value, other)
        return jnp.min(value)

    def greatest(base, below):
        found = [jnp.where((p >= base) & (p < below), p, base - 1.0) for p in planes]
        value = found[0]
        for other in found[1:]:
            value = jnp.maximum(value, other)
        return jnp.max(value)

    def some_left(state):
        return (state[1] <= state[2]) | (state[3] <= state[4])

    def step(state):
        number, ends = state[0], state[1:]
        after = []
        for half, (base, top) in enumerate(halves):
            low, high = ends[2 * half], ends[2 * half + 1]
            present[number] = low.astype(jnp.int32)
            number = number + jnp.where(low <= high, 1, 0)
            present[number] = high.astype(jnp.int32)
            number = number + jnp.where(low < high, 1, 0)
            after += [least(low, top), greatest(base, high)]
        return (number, *after)

    ends = []
    for base, top in halves:
        ends += [least(base - 1.0, top), greatest(base, top)]
    state = lax.while_loop(some_left, step, (jnp.int32(1), *ends))
    present[0] = state[0] - 1


def segment_rows(ids, values, scratch, present):
    scratch[...] = jnp.zeros_like(scratch)
    count, depth = values.shape[0], ids.shape[0]

    def one_well(step, _):
        well = present[step + 1]
        masks = [ids[x] == well for x in range(depth)]
        for number in range(count):
            total = jnp.where(masks[0], values[number, 0], 0.0)
            for x in range(1, depth):
                total = total + jnp.where(masks[x], values[number, x], 0.0)
            scratch[number, pl.ds(well, 1), :] = jnp.sum(total, axis=0, keepdims=True)
        return 0

    lax.fori_loop(0, present[0], one_well, 0)
    rows = []
    for number in range(count):
        summed = jnp.sum(scratch[number], axis=1, keepdims=True)
        shape = scratch.shape[1:]
        on_lanes = jnp.where(iota(shape, 0) == iota(shape, 1), summed, 0.0)
        rows.append(jnp.sum(on_lanes, axis=0, keepdims=True))
    return rows


def pack_rows(rows, table):
    for number, row in enumerate(rows):
        placed = row if number % 3 == 0 else pltpu.roll(row, WELLS * (number % 3), 1)
        table = table + jnp.where(
            iota(table.shape, 0) == number // 3, jnp.broadcast_to(placed, table.shape), 0.0
        )
    return table


def unpack_row(table, number):
    row = table[number // 3 : number // 3 + 1, :]
    if number % 3:
        row = pltpu.roll(row, LANES - WELLS * (number % 3), 1)
    return jnp.where(iota(row.shape, 1) < WELLS, row, 0.0)


def place_rows(rows, table):
    for number, row in enumerate(rows):
        group, k = divmod(number, RHS)
        at = k + RHS * (group // 3)
        placed = pltpu.roll(row, WELLS * group, 1) if group in (1, 2) else row
        table = table + jnp.where(
            iota(table.shape, 0) == at, jnp.broadcast_to(placed, table.shape), 0.0
        )
    return table


def place_columns(dots, first_lane, table):
    for number in range(dots.shape[0]):
        column = jnp.sum(dots[number], axis=1, keepdims=True)
        table = table + jnp.where(iota(table.shape, 1) == first_lane + number, column, 0.0)
    return table


def take_group(table, group):
    if group in (1, 2):
        table = pltpu.roll(table, LANES - WELLS * group, 1)
    start = RHS * (group // 3)
    rows = table[start : start + RHS, :]
    return jnp.where(iota(rows.shape, 1) < WELLS, rows, 0.0)


def take_column(table, lane):
    return table[RHS : 2 * RHS, lane : lane + 1]


def lane_sum(row):
    return jnp.sum(row, axis=1, keepdims=True)


def on_even(axis):
    return lax.rem(lax.axis_index(axis), 2) == 0


def copied(source, target):
    count = min(source.shape[0], target.shape[0])
    target[0:count] = source[0:count]
    if target.shape[0] > count:
        target[count:] = jnp.zeros_like(target[count:])


def by_pair(axis, low, high, first, second):
    @pl.when(on_even(axis))
    def _():
        copied(high, first)
        copied(low, second)

    @pl.when(jnp.logical_not(on_even(axis)))
    def _():
        copied(low, first)
        copied(high, second)


def by_side(axis, first, second, low, high):
    by_pair(axis, second, first, high, low)


COUPLINGS, DIAGONALS, WELL_FIELDS, IDS, RIGHT_SIDE, START = range(6)


def layer_blocks(cut, inward, lateral):
    def plane(n):
        if n < DIAGONAL:
            return cut(COUPLINGS, ((lateral, lateral + 1, 4, 5)[n // 4], n % 4), 0)
        if n < BACK_IN:
            return cut(DIAGONALS, (n - DIAGONAL,), 0)
        return cut(COUPLINGS, (inward, n - BACK_IN), 1)

    return plane


def fill_pack(pack, inward, lateral, cut):
    blocks = layer_blocks(cut, inward, lateral)
    for e in range(4):
        pack[e] = cut(COUPLINGS, (inward, e), 0)
    wells = [cut(WELL_FIELDS, (2 + a,), 0) for a in range(2)]
    for a in range(2):
        pack[WELL_EQ + a] = wells[a]
    pack[WELL_ID] = cut(IDS, (), 0).astype(jnp.float32)
    pack[BACK_ID] = cut(IDS, (), 1).astype(jnp.float32)
    for start, at in (
        (LAT_UP, UP_WELL),
        (LAT_DOWN, DOWN_WELL),
        (RISE, RISE_WELL),
        (FALL, FALL_WELL),
        (DIAGONAL, DIAGONAL_WELL),
        (BACK_IN, BACK_WELL),
    ):
        if start == BACK_IN:
            wells = [cut(WELL_FIELDS, (2 + a,), 1) for a in range(2)]
        for b, value in enumerate(product(lambda e: blocks(start + e), *wells)):
            pack[at + b] = value
    for k in range(RHS):
        here = [cut(START, (k, a), 0) for a in range(2)]
        back = [cut(START, (k, a), 1) for a in range(2)]
        entering = product(lambda e: blocks(BACK_IN + e), *back)
        local = face_stencil(blocks, here[0], here[1], entering)
        for a in range(2):
            pack[GUESS + 2 * k + a] = here[a]
            pack[REST + 2 * k + a] = cut(RIGHT_SIDE, (k, a), 0) - local[a]
    if pack.shape[0] > ENDS:
        end = pack.shape[1] - 1
        for e in range(4):
            pack[ENDS, e : e + 1, :] = blocks(LAT_UP + e)[end : end + 1, :]
            pack[ENDS, 4 + e : 5 + e, :] = blocks(LAT_DOWN + e)[0:1, :]


def x_pack_kernel(*refs):
    sources, first, second, held_ends, arrived = refs[:6], refs[6], refs[7], refs[8:20], refs[20]
    packs = refs[21:23]
    copies = []
    for n, source in enumerate(sources):
        lead = (slice(None),) * (len(source.shape) - 3)
        depth = source.shape[-3]
        for end, start in enumerate((0, depth - 2)):
            copies.append(
                pltpu.make_async_copy(
                    source.at[lead + (pl.ds(start, 2),)],
                    held_ends[2 * n + end],
                    arrived.at[2 * n + end],
                )
            )
    for copy in copies:
        copy.start()
    for copy in copies:
        copy.wait()
    for end, pack in enumerate(packs):
        fill_pack(
            pack,
            1 - end,
            2,
            lambda n, index, layer: held_ends[2 * n + end][
                index + (1 - layer if end else layer,)
            ],
        )
    by_pair("gx", *packs, first, second)


def y_cut(arguments, end):
    last = arguments[0].shape[-2] - 1

    def cut(n, index, layer):
        return arguments[n][index + (slice(None), last - layer if end else layer, slice(None))]

    return cut


def send_out(table, chunks, part, sent):
    rows = min(chunks.shape[1], table.shape[0])
    chunks[:, :rows, :] = jnp.broadcast_to(table[None, :rows], (chunks.shape[0], rows, LANES))
    copy = pltpu.make_async_copy(chunks, part, sent.at[0])
    copy.start()
    return copy


def corner_kernel(y_low, y_high, came_first, came_second, first, second, fxl, fxh, *outs):
    by_side("gx", came_first, came_second, fxl, fxh)
    last = fxl.shape[1] - 1
    for own, out, at, side in ((y_low, outs[0], 0, 4), (y_high, outs[1], last, 0)):
        for n in range(FACE_PLANES):
            out[n] = own[n]
        row = FACE_PLANES * 8
        out[FACE_PLANES + CORNER_PLANES - 1] = jnp.zeros(out.shape[1:], jnp.float32)
        for face in (fxl, fxh):
            rows = [(n, at) for n in range(4)]
            rows += [(ENDS, side + e) for e in range(4)]
            rows += [(n, at) for n in range(WELL_EQ, REST)]
            for n, y in rows:
                out[row // 8, row % 8 : row % 8 + 1, :] = face[n, y : y + 1, :]
                row += 1
    by_pair("gy", *outs, first, second)


def diagonal_device(x_end, y_end):
    across, along = lax.axis_index("gx"), lax.axis_index("gy")
    there_x, there_y = across + 2 * x_end - 1, along + 2 * y_end - 1
    count_x, count_y = lax.axis_size("gx"), lax.axis_size("gy")
    exists = (there_x >= 0) & (there_x < count_x) & (there_y >= 0) & (there_y < count_y)
    return exists, jnp.where(exists, there_x * count_y + there_y, 0)


def guess_kernel(
    couplings, diagonal, wells, ids, right, guess,
    part, present, y_low, y_high, values, scratch, chunks, sent,
):
    list_wells(ids, present)
    for k in range(RHS):
        values[k] = wells[0] * guess[k, 0] + wells[1] * guess[k, 1]
    values[4] = wells[0] * wells[2] + wells[1] * wells[3]
    values[5] = wells[2] * wells[2] + wells[3] * wells[3]
    rows = segment_rows(ids, values, scratch, present)
    table = pack_rows(rows, jnp.zeros((8, LANES), jnp.float32))
    copy = send_out(table, chunks, part, sent)
    arguments = (couplings, diagonal, wells, ids, right, guess)
    for end, pack in enumerate((y_low, y_high)):
        fill_pack(pack, 3 - end, 0, y_cut(arguments, end))
    copy.wait()


def block_kernel(
    couplings, diagonal, right, guess, sent_face, rest, leaving
):
    nothing_enters = [[jnp.zeros(guess.shape[3:], jnp.float32)] * 2] * 4
    for k in range(RHS):
        inside, outgoing = block_stencil(
            couplings, diagonal, guess[k, 0], guess[k, 1], nothing_enters
        )
        for a in range(2):
            rest[k, a] = right[k, a] - inside[a]
            for f in range(4):
                leaving[f, 2 * k + a] = outgoing[f][a]


def residual_kernel(
    couplings, diagonal, wells, ids, fxl, fxh, came_first, came_second, parts,
    rest, leaving,
    residual, image, residual_faces, x_first, x_second, y_first, y_second, small, fyl, fyh,
    x_low, x_high, y_low, y_high,
):
    by_side("gy", came_first, came_second, fyl, fyh)
    faces = (fxl, fxh, fyl, fyh)
    totals = jnp.sum(parts[...], axis=0)
    corners = corners_of(faces, FACE_PLANES, CORNER_ROWS)
    all_ids = ids[...]
    face_ids = [as_ids(face[WELL_ID]) for face in faces]
    last = rest.shape[2] - 1
    row = iota(rest.shape[2:], 1)
    for k in range(RHS):
        s_row = unpack_row(totals, k)
        entering = [
            product(
                lambda e, f=f: faces[f][e],
                faces[f][GUESS + 2 * k],
                faces[f][GUESS + 2 * k + 1],
            )
            for f in range(4)
        ]
        outgoing = [[leaving[f, 2 * k + b] for b in range(2)] for f in range(4)]
        at_wells = spread(s_row, all_ids)
        now = []
        for a in range(2):
            value = rest[k, a] - wells[2 + a] * at_wells
            over_x = [
                (value[0] - entering[0][a])[None],
                value[1:last],
                (value[last] - entering[1][a])[None],
            ]
            value = jnp.concatenate(over_x, axis=0)
            value = value - jnp.where(row == 0, entering[2][a][:, None, :], 0.0)
            now.append(value - jnp.where(row == last, entering[3][a][:, None, :], 0.0))
        for a in range(2):
            residual[k, a] = now[a]
        ends = corner_inputs(
            corners,
            [[corners[c].row(SIDE_GUESS + 2 * k + a) for a in range(2)] for c in range(4)],
        )
        incoming = []
        for f in range(4):
            face = faces[f]
            there = face_entries(ends[(f, 0)], ends[(f, 1)], outgoing[f])
            face_wells = spread(s_row, face_ids[f])
            outer = [
                face[REST + 2 * k + a] - there[a] - face[WELL_EQ + a] * face_wells
                for a in range(2)
            ]
            for a in range(2):
                residual_faces[f, 2 * k + a] = outer[a]
            incoming.append(product(lambda e, f=f: faces[f][e], *outer))
        result, _ = block_stencil(couplings, diagonal, now[0], now[1], incoming)
        for a in range(2):
            image[k, a] = result[a]
    own = (couplings, diagonal)
    for axis, packs in enumerate(((x_low, x_high), (y_low, y_high))):
        for end, pack in enumerate(packs):

            def cut(ref, index, layer):
                at = last - layer if end else layer
                return ref[index + ((at,) if axis == 0 else (slice(None), at, slice(None)))]

            plane = layer_blocks(
                lambda n, index, layer: cut(own[n], index, layer),
                2 * axis + 1 - end,
                2 * (1 - axis),
            )
            blocks = [plane(n) for n in range(LAYER_BLOCKS)]
            for k in range(RHS):
                here = [cut(image, (k, a), 0) for a in range(2)]
                back = [cut(image, (k, a), 1) for a in range(2)]
                entering = product(lambda e: blocks[BACK_IN + e], *back)
                local = face_stencil(lambda n: blocks[n], here[0], here[1], entering)
                for a in range(2):
                    pack[2 * k + a] = here[a]
                    pack[8 + 2 * k + a] = local[a]
    by_pair("gx", x_low, x_high, x_first, x_second)
    by_pair("gy", y_low, y_high, y_first, y_second)
    small[...] = jnp.concatenate(
        [unpack_row(totals, 4), unpack_row(totals, 5), jnp.zeros((6, LANES), jnp.float32)], axis=0
    )


def moments_kernel(
    wells, ids, residual, image, present, part, values, scratch, dots, chunks, sent
):
    dots[...] = jnp.zeros_like(dots)
    for k in range(RHS):
        now = [residual[k, a] for a in range(2)]
        result = [image[k, a] for a in range(2)]
        for n, field in enumerate((now, result)):
            values[4 * n + k] = wells[0] * field[0] + wells[1] * field[1]
            values[8 + 4 * n + k] = wells[2] * field[0] + wells[3] * field[1]
        row = slice(RHS + k, RHS + k + 1)
        dots[0, row, :] = tile_sum(now, now)
        dots[1, row, :] = tile_sum(now, result)
        dots[2, row, :] = tile_sum(result, result)
    rows = segment_rows(ids, values, scratch, present)
    table = place_rows(rows, jnp.zeros((8, LANES), jnp.float32))
    chunks[:, 8:, :] = jnp.zeros_like(chunks[:, 8:, :])
    last = image.shape[2] - 1
    for x_end in range(2):
        for y_end in range(2):
            exists, place = diagonal_device(x_end, y_end)

            @pl.when(exists)
            def _():
                for k in range(RHS):
                    for a in range(2):
                        row, y = 8 + 2 * k + a, last * y_end
                        chunks[pl.ds(place, 1), row : row + 1, :] = image[
                            k, a, last * x_end, y : y + 1, :
                        ][None]

    send_out(place_columns(dots, WELLS, table), chunks, part, sent).wait()


def first_step(totals, small):
    s_row, us_row, p_row, ps_row = (take_group(totals, group) for group in range(4))
    within, equation = small[0:1, :], small[1:2, :]
    rr, rs, ss = (take_column(totals, WELLS + i) for i in range(3))
    height = (rs + lane_sum(p_row * s_row)) / rr
    square = ss + lane_sum(2.0 * ps_row * s_row + equation * s_row * s_row)
    left = jnp.maximum(square - height * height * rr, 1e-7 * square)
    scale = lax.rsqrt(left)
    s_image = us_row + within * s_row
    s_second = (s_image - height * s_row) * scale
    p_second = (ps_row + equation * s_row - height * p_row) * scale
    shift = rs / rr + lane_sum(p_second * s_second)
    unit = lax.rsqrt(rr)
    following = left * scale * unit
    return s_row, s_image, p_row, p_second, (unit, rr * unit, height, shift, following, scale)


def krylov_kernel(
    couplings, diagonal, wells, ids, fxl, fxh, fyl, fyh, x_first, x_second, y_first, y_second,
    residual, image, residual_faces, parts, small_in, present,
    second_out, third_out, part, known, scratch, values_scratch, dots, gxl, gxh, gyl, gyh,
):
    by_side("gx", x_first, x_second, gxl, gxh)
    by_side("gy", y_first, y_second, gyl, gyh)
    faces, sent = (fxl, fxh, fyl, fyh), (gxl, gxh, gyl, gyh)
    totals = jnp.sum(parts[:, 0:8, :], axis=0)
    small = small_in[...]
    s_rows, s_images, p_rows, p_seconds, scalars = first_step(totals, small)
    known[0:RHS, :] = p_rows
    known[RHS : 2 * RHS, :] = p_seconds
    columns = jnp.zeros((RHS, LANES), jnp.float32)
    for n, column in enumerate(scalars):
        columns = columns + jnp.where(iota(columns.shape, 1) == n, column, 0.0)
    known[2 * RHS : 3 * RHS, :] = columns
    known[3 * RHS :, :] = jnp.broadcast_to(small[1:2, :], (RHS, LANES))
    dots[...] = jnp.zeros_like(dots)
    corners = corners_of(faces, FACE_PLANES, CORNER_ROWS)
    places = [diagonal_device(c % 2, c // 2)[1] for c in range(4)]
    all_ids = ids[...]
    face_ids = [as_ids(face[WELL_ID]) for face in faces]
    back_ids = [as_ids(face[BACK_ID]) for face in faces]
    corner_ids = [
        as_ids(jnp.broadcast_to(corner.row(SIDE_ID), (8, LANES))) for corner in corners
    ]
    for k in range(RHS):
        unit, _, height, shift, _, scale = (column[k : k + 1, :] for column in scalars)
        s_row, s_image = s_rows[k : k + 1, :], s_images[k : k + 1, :]
        at_wells = spread(s_row, all_ids)
        now = [image[k, a] + wells[2 + a] * at_wells for a in range(2)]
        face_now, spread_now = [], []
        for f in range(4):
            here = spread(s_row, face_ids[f])
            spread_now.append((here, spread(s_row, back_ids[f])))
            face_now.append(
                [sent[f][2 * k + a] + faces[f][WELL_EQ + a] * here for a in range(2)]
            )
        corner_now = []
        for c in range(4):
            here = spread(s_row, corner_ids[c])[0:1, :]
            corner_now.append(
                [
                    parts[pl.ds(places[c], 1), 8 + 2 * k + a, :] + corners[c].row(SIDE_EQ + a) * here
                    for a in range(2)
                ]
            )
        incoming = [product(lambda e, f=f: faces[f][e], *face_now[f]) for f in range(4)]
        applied, outgoing = block_stencil(couplings, diagonal, now[0], now[1], incoming)
        at_wells = spread(s_image, all_ids)
        second, third = [], []
        for a in range(2):
            twice = applied[a] + wells[2 + a] * at_wells
            base = (now[a] - height * residual[k, a]) * scale
            second.append(base)
            third.append((twice - height * now[a]) * scale - shift * base)
            second_out[k, a] = second[a]
            third_out[k, a] = third[a]
        ends = corner_inputs(corners, corner_now)
        incoming = []
        for f in range(4):
            face = faces[f]
            here, behind = spread_now[f]
            moves = [
                [face[at + b] * here for b in range(2)]
                for at in (DIAGONAL_WELL, UP_WELL, DOWN_WELL, RISE_WELL, FALL_WELL)
            ]
            there = face_moves(*moves, [face[BACK_WELL + b] * behind for b in range(2)])
            local = [sent[f][8 + 2 * k + b] + there[b] for b in range(2)]
            over = face_entries(ends[(f, 0)], ends[(f, 1)], outgoing[f])
            here = spread(s_image, face_ids[f])
            outer = []
            for a in range(2):
                twice = local[a] + over[a] + face[WELL_EQ + a] * here
                base = (face_now[f][a] - height * residual_faces[f, 2 * k + a]) * scale
                outer.append((twice - height * face_now[f][a]) * scale - shift * base)
            incoming.append(product(lambda e, f=f: faces[f][e], *outer))
        result, _ = block_stencil(couplings, diagonal, third[0], third[1], incoming)
        fourth = [result[a] - shift * third[a] for a in range(2)]
        values_scratch[k] = wells[0] * third[0] + wells[1] * third[1]
        values_scratch[4 + k] = wells[2] * third[0] + wells[3] * third[1]
        values_scratch[8 + k] = wells[2] * fourth[0] + wells[3] * fourth[1]
        fields = [[residual[k, a] * unit for a in range(2)], second, third, fourth]
        number = 0
        for i in range(4):
            for j in range(i, 4):
                dots[number, RHS + k : RHS + k + 1, :] = tile_sum(fields[i], fields[j])
                number += 1
    rows = segment_rows(ids, values_scratch, scratch, present)
    table = place_rows(rows, jnp.zeros((8, LANES), jnp.float32))
    table = place_columns(dots, 0, table)
    gram = table[RHS : RHS + 1, :]
    for k in range(1, RHS):
        gram = gram + pltpu.roll(table[RHS + k : RHS + k + 1, :], GRAM_ENTRIES * k, 1)
    flat = jnp.concatenate([table[k : k + 1, :] for k in range(RHS)] + [gram], axis=1)
    part[...] = jnp.broadcast_to(flat[None], part.shape)


def solve_kernel(
    guess_in, residual, second, third, parts, known, solution, guess, arrived
):
    copy = pltpu.make_async_copy(guess_in, guess, arrived.at[0])
    copy.start()
    flat = jnp.sum(parts[...], axis=0)
    rows = [flat[:, LANES * n : LANES * (n + 1)] for n in range(RHS + 1)]
    for k in range(1, RHS):
        rows.append(pltpu.roll(rows[RHS], LANES - GRAM_ENTRIES * k, 1))
    totals = jnp.concatenate(rows, axis=0)
    s_third, p_third, p_fourth = (take_group(totals, group) for group in range(3))
    p_first, p_second = known[0:RHS, :], known[RHS : 2 * RHS, :]
    unit, beta, height, shift, following = (
        known[2 * RHS : 3 * RHS, n : n + 1] for n in range(5)
    )
    equation = known[3 * RHS :, :]
    gram = {}
    number = 0
    for i in range(4):
        for j in range(i, 4):
            gram[(i, j)] = take_column(totals, number)
            number += 1
    gram[(0, 3)] += lane_sum(p_first * s_third) * unit
    gram[(1, 3)] += lane_sum(p_second * s_third)
    gram[(2, 3)] += lane_sum(p_third * s_third)
    gram[(3, 3)] += lane_sum(2.0 * p_fourth * s_third + equation * s_third * s_third)
    tiny = 1e-30
    inverse = [lax.rsqrt(jnp.maximum(gram[(i, i)], tiny)) for i in range(4)]
    length = [jnp.maximum(gram[(i, i)], tiny) * inverse[i] for i in range(4)]
    upper = {}
    for i in range(4):
        for j in range(i, 4):
            entry = gram[(i, j)] * inverse[i] * inverse[j]
            for m in range(i):
                entry = entry - upper[(m, i)] * upper[(m, j)]
            if i == j:
                pivot = lax.rsqrt(jnp.maximum(entry, 1e-6))
                upper[(i, i)] = jnp.maximum(entry, 1e-6) * pivot
                over = pivot
            else:
                upper[(i, j)] = entry * over
    columns = [
        [(0, height * length[0]), (1, following * length[1])],
        [(1, shift * length[1]), (2, length[2])],
        [(2, shift * length[2]), (3, length[3])],
    ]
    zero = jnp.zeros_like(shift)
    hessenberg = [[zero] * 3 for _ in range(4)]
    for j in range(3):
        for i in range(j + 2):
            for m, factor in columns[j]:
                if m >= i:
                    hessenberg[i][j] = hessenberg[i][j] + upper[(i, m)] * factor
    target = [beta * length[0] * upper[(0, 0)], zero, zero, zero]
    turns = []
    for j in range(3):
        top, bottom = hessenberg[j][j], hessenberg[j + 1][j]
        turn = lax.rsqrt(top * top + bottom * bottom)
        turns.append(turn)
        cosine, sine = top * turn, bottom * turn
        for m in range(j, 3):
            high, low = hessenberg[j][m], hessenberg[j + 1][m]
            hessenberg[j][m] = cosine * high + sine * low
            hessenberg[j + 1][m] = cosine * low - sine * high
        high, low = target[j], target[j + 1]
        target[j] = cosine * high + sine * low
        target[j + 1] = cosine * low - sine * high
    weights = [zero] * 3
    for i in (2, 1, 0):
        value = target[i]
        for j in range(i + 1, 3):
            value = value - hessenberg[i][j] * weights[j]
        weights[i] = value * turns[i]
    copy.wait()
    for k in range(RHS):
        on_first, on_second, on_third = (
            column[k : k + 1, :] for column in (weights[0] * unit, weights[1], weights[2])
        )
        for a in range(2):
            solution[k, a] = (
                guess[k, a]
                + on_first * residual[k, a]
                + on_second * second[k, a]
                + on_third * third[k, a]
            )


def call(kernel, shapes, arguments, scratch=(), far_inputs=0, cost=0, grant=24 << 20, out=0):
    whole = pl.BlockSpec(memory_space=pltpu.VMEM)
    far = pl.BlockSpec(memory_space=pltpu.HBM)
    scalars = pl.BlockSpec(memory_space=pltpu.SMEM)

    def place(number, array):
        if len(array.shape) == 1:
            return scalars
        return far if number < far_inputs else whole

    outs = [
        jax.ShapeDtypeStruct(shape, jnp.float32 if len(shape) > 1 else jnp.int32)
        for shape in shapes
    ]
    outs[:out] = [pltpu.HBM(shape, jnp.float32) for shape in shapes[:out]]
    return pl.pallas_call(
        kernel,
        out_shape=outs,
        in_specs=[place(*numbered) for numbered in enumerate(arguments)],
        out_specs=[far] * out + [scalars if len(shape) == 1 else whole for shape in shapes[out:]],
        scratch_shapes=list(scratch),
        compiler_params=pltpu.CompilerParams(vmem_limit_bytes=grant),
        cost_estimate=pl.CostEstimate(flops=cost, bytes_accessed=cost, transcendentals=0)
        if cost
        else None,
    )(*arguments)


def nothing(value, *rest):
    pass


def after(value, *others):
    far = pl.BlockSpec(memory_space=pltpu.HBM)
    near = pl.BlockSpec(memory_space=pltpu.VMEM)
    return pl.pallas_call(
        nothing,
        out_shape=pltpu.HBM(value.shape, value.dtype),
        in_specs=[far] + [near] * len(others),
        out_specs=far,
        input_output_aliases={0: 0},
        compiler_params=pltpu.CompilerParams(vmem_limit_bytes=1 << 20),
    )(pltpu.with_memory_space_constraint(value, pltpu.HBM), *others)


def held(*shape):
    return pltpu.VMEM(shape, jnp.float32)


def swap(value, axis, start):
    pairs = []
    for low in range(start, lax.axis_size(axis) - 1, 2):
        pairs += [(low, low + 1), (low + 1, low)]
    return lax.ppermute(value, axis, pairs) if pairs else jnp.zeros_like(value)


def swapped(first, second, axis):
    return swap(first, axis, 0), swap(second, axis, 1)


def exchanged(part):
    return lax.all_to_all(part, ("gx", "gy"), 0, 0, tiled=True)


def body(couplings, diagonal, wells, ids, right, guess):
    devices = lax.axis_size("gx") * lax.axis_size("gy")
    plane = (8, LANES)
    field = guess.shape
    block = guess.shape[2:]
    arguments = (couplings, diagonal, wells, ids, right, guess)

    ends = []
    for argument in arguments:
        shape = argument.shape[:-3] + (2,) + argument.shape[-2:]
        ends += [pltpu.VMEM(shape, argument.dtype)] * 2
    x_first, x_second = call(
        x_pack_kernel,
        [(FACE_PLANES + 1,) + plane] * 2,
        [pltpu.with_memory_space_constraint(argument, pltpu.HBM) for argument in arguments],
        ends
        + [pltpu.SemaphoreType.DMA((len(ends),))]
        + [held(FACE_PLANES + 1, *plane)] * 2,
        far_inputs=len(arguments),
    )
    came_x = swapped(x_first, x_second, "gx")
    first_chunks, chunks = (devices, TABLE_ROWS, LANES), (devices, 16, LANES)
    sent = pltpu.SemaphoreType.DMA((1,))
    part, present, y_low, y_high = call(
        guess_kernel,
        [first_chunks, (WELLS + 8,)] + [(FACE_PLANES,) + plane] * 2,
        arguments,
        [held(6, *block), held(6, WELLS, LANES), held(*first_chunks), sent],
        cost=4 << 20,
        out=1,
    )
    parts = exchanged(after(part, came_x[0]))
    y_shape = (FACE_PLANES + CORNER_PLANES,) + plane
    y_first, y_second, fxl, fxh = call(
        corner_kernel,
        [y_shape] * 2 + [(FACE_PLANES + 1,) + plane] * 2,
        (y_low, y_high, *came_x),
        [held(*y_shape)] * 2,
    )
    came_y = swapped(y_first, y_second, "gy")
    ahead = call(
        block_kernel,
        [field, (4, 8) + plane],
        (couplings, diagonal, right, guess, y_first),
        cost=4 << 20,
    )

    residual, image, residual_faces, *packs, small, fyl, fyh = call(
        residual_kernel,
        [field, field, (4, 8) + plane]
        + [(IMAGE_PLANES + spare,) + plane for spare in (1, 2, 0, 3)]
        + [(8, LANES)]
        + [y_shape] * 2,
        (couplings, diagonal, wells, ids, fxl, fxh, *came_y, parts, *ahead),
        [held(IMAGE_PLANES, *plane)] * 4,
    )
    faces = (fxl, fxh, fyl, fyh)
    came_y1 = swap(packs[3], "gy", 1)
    came_x1 = swap(packs[1], "gx", 1)
    came_x0 = swap(packs[0], "gx", 0)
    came_y0 = swap(packs[2], "gy", 0)
    (part,) = call(
        moments_kernel,
        [chunks],
        (wells, ids, residual, image, present),
        [held(16, *block), held(16, WELLS, LANES), held(3, *plane), held(*chunks), sent],
        cost=4 << 20,
        out=1,
    )
    parts = exchanged(part)
    second, third, part, known = call(
        krylov_kernel,
        [field, field, (devices, 1, (RHS + 1) * LANES), (4 * RHS, LANES)],
        (couplings, diagonal, wells, ids) + faces + (came_x0, came_x1, came_y0, came_y1)
        + (residual, image, residual_faces, parts, small, present),
        [held(12, WELLS, LANES), held(12, *block), held(10, *plane)]
        + [held(IMAGE_PLANES, *plane)] * 4,
    )
    parts = exchanged(part)
    (result,) = call(
        solve_kernel,
        [field],
        (
            pltpu.with_memory_space_constraint(guess, pltpu.HBM),
            residual, second, third, parts, known,
        ),
        [held(*field), pltpu.SemaphoreType.DMA((1,))],
        far_inputs=1,
    )
    return result


def solution(mesh):
    in_specs = (
        P("member", None, "gx", "gy", None),
        P("member", "gx", "gy", None),
        P("member", "gx", "gy", None),
        P("gx", "gy", None),
        P("member", None, "gx", "gy", None),
        P("member", None, "gx", "gy", None),
    )
    out_specs = P("member", None, "gx", "gy", None)
    return jax.shard_map(body, mesh=mesh, in_specs=in_specs, out_specs=out_specs, check_vma=False)
```

```python
import jax
import jax.numpy as jnp
from jax import lax
from jax.experimental import pallas as pl
from jax.experimental.pallas import tpu as pltpu
from jax.sharding import PartitionSpec as P

WELLS = 40
RHS = 4
LANES = 128
WELL_EQ, WELL_ID, GUESS, REST = 4, 6, 7, 15
UP_WELL, DOWN_WELL, RISE_WELL, FALL_WELL, DIAGONAL_WELL = 23, 25, 27, 29, 31
BACK_WELL, BACK_ID = 33, 35
FACE_PLANES = 36
ENDS = 36
CORNER_PLANES = 5
LAT_UP, LAT_DOWN, RISE, FALL, DIAGONAL, BACK_IN = 0, 4, 8, 12, 16, 20
LAYER_BLOCKS = 24
IMAGE_PLANES = 16
TABLE_ROWS = 6
GRAM_ENTRIES = 10
CORNER_ROWS = 19
SIDE_IN, SIDE_EQ, SIDE_ID, SIDE_GUESS = 4, 8, 10, 11


def product(blocks, first, second):
    return [
        blocks(0) * first + blocks(2) * second,
        blocks(1) * first + blocks(3) * second,
    ]


def iota(shape, axis):
    return lax.broadcasted_iota(jnp.int32, shape, axis)


def roll_up(value, axis):
    return pltpu.roll(value, 1, axis)


def roll_down(value, axis):
    return pltpu.roll(value, value.shape[axis] - 1, axis)


def layer_moves(rising, falling):
    axis = rising.ndim - 1
    lane = iota(rising.shape, axis)
    up = jnp.where(lane == 0, 0.0, roll_up(rising, axis))
    down = jnp.where(lane == LANES - 1, 0.0, roll_down(falling, axis))
    return up + down


def block_stencil(couplings, diagonal, first, second, incoming):
    result = product(lambda e: diagonal[e], first, second)
    moved = [product(lambda e, d=d: couplings[d, e], first, second) for d in range(6)]
    row = iota(first.shape, 1)
    outgoing = [[], [], [], []]
    for b in range(2):
        east, west, north, south, rise, fall = (moved[d][b] for d in range(6))
        total = result[b] + jnp.concatenate([incoming[0][b][None], east[:-1]], axis=0)
        total = total + jnp.concatenate([west[1:], incoming[1][b][None]], axis=0)
        total = total + jnp.where(row == 0, incoming[2][b][:, None, :], roll_up(north, 1))
        total = total + jnp.where(
            row == row.shape[1] - 1, incoming[3][b][:, None, :], roll_down(south, 1)
        )
        result[b] = total + layer_moves(rise, fall)
        outgoing[0].append(west[0])
        outgoing[1].append(east[-1])
        outgoing[2].append(south[:, 0, :])
        outgoing[3].append(north[:, -1, :])
    return result, outgoing


def face_stencil(blocks, first, second, behind):
    def times(start):
        return product(lambda e: blocks(start + e), first, second)

    moves = [times(start) for start in (DIAGONAL, LAT_UP, LAT_DOWN, RISE, FALL)]
    return face_moves(*moves, behind)


def face_moves(kept, up, down, rise, fall, behind):
    result = list(kept)
    row = iota(kept[0].shape, 0)
    for b in range(2):
        total = result[b] + behind[b] + layer_moves(rise[b], fall[b])
        total = total + jnp.where(row == 0, 0.0, roll_up(up[b], 0))
        result[b] = total + jnp.where(row == row.shape[0] - 1, 0.0, roll_down(down[b], 0))
    return result


def face_entries(low_end, high_end, entering):
    row = iota(entering[0].shape, 0)
    return [
        entering[b]
        + jnp.where(row == 0, low_end[b], 0.0)
        + jnp.where(row == row.shape[0] - 1, high_end[b], 0.0)
        for b in range(2)
    ]


def spread(totals, ids):
    table = jnp.broadcast_to(totals, (8, LANES))
    if ids.ndim == 2:
        return jnp.take_along_axis(table, ids, axis=1)
    return jnp.stack(
        [jnp.take_along_axis(table, ids[x], axis=1) for x in range(ids.shape[0])], axis=0
    )


def as_ids(plane):
    return plane.astype(jnp.int32)


class Corner:
    def __init__(self, pack, which, base):
        self.pack, self.start = pack, base * 8 + which

    def row(self, number):
        at = self.start + number
        return self.pack[at // 8, at % 8 : at % 8 + 1, :]


def corners_of(faces, base, rows):
    found = []
    for y_face in (2, 3):
        for x_end in range(2):
            found.append(Corner(faces[y_face], x_end * rows, base))
    return found


def corner_inputs(corners, values):
    ends = {}
    for c in range(4):
        x_end, y_end = c % 2, c // 2
        over_x = product(corners[c].row, *values[c])
        over_y = product(lambda e, c=c: corners[c].row(SIDE_IN + e), *values[c])
        ends[(2 + y_end, x_end)] = over_x
        ends[(x_end, y_end)] = over_y
    return ends


def tile_sum(first, second):
    value = first[0] * second[0] + first[1] * second[1]
    return jnp.sum(jnp.sum(value, axis=0), axis=0, keepdims=True)


def list_wells(ids, present):
    planes = [ids[x].astype(jnp.float32) for x in range(ids.shape[0])]
    middle = WELLS // 2
    halves = ((0.0, float(middle)), (float(middle), float(WELLS)))

    def least(above, top):
        found = [jnp.where((p > above) & (p < top), p, top) for p in planes]
        value = found[0]
        for other in found[1:]:
            value = jnp.minimum(value, other)
        return jnp.min(value)

    def greatest(base, below):
        found = [jnp.where((p >= base) & (p < below), p, base - 1.0) for p in planes]
        value = found[0]
        for other in found[1:]:
            value = jnp.maximum(value, other)
        return jnp.max(value)

    def some_left(state):
        return (state[1] <= state[2]) | (state[3] <= state[4])

    def step(state):
        number, ends = state[0], state[1:]
        after = []
        for half, (base, top) in enumerate(halves):
            low, high = ends[2 * half], ends[2 * half + 1]
            present[number] = low.astype(jnp.int32)
            number = number + jnp.where(low <= high, 1, 0)
            present[number] = high.astype(jnp.int32)
            number = number + jnp.where(low < high, 1, 0)
            after += [least(low, top), greatest(base, high)]
        return (number, *after)

    ends = []
    for base, top in halves:
        ends += [least(base - 1.0, top), greatest(base, top)]
    state = lax.while_loop(some_left, step, (jnp.int32(1), *ends))
    present[0] = state[0] - 1


def segment_rows(ids, values, scratch, present):
    scratch[...] = jnp.zeros_like(scratch)
    count, depth = values.shape[0], ids.shape[0]

    def one_well(step, _):
        well = present[step + 1]
        masks = [ids[x] == well for x in range(depth)]
        for number in range(count):
            total = jnp.where(masks[0], values[number, 0], 0.0)
            for x in range(1, depth):
                total = total + jnp.where(masks[x], values[number, x], 0.0)
            scratch[number, pl.ds(well, 1), :] = jnp.sum(total, axis=0, keepdims=True)
        return 0

    lax.fori_loop(0, present[0], one_well, 0)
    rows = []
    for number in range(count):
        summed = jnp.sum(scratch[number], axis=1, keepdims=True)
        shape = scratch.shape[1:]
        on_lanes = jnp.where(iota(shape, 0) == iota(shape, 1), summed, 0.0)
        rows.append(jnp.sum(on_lanes, axis=0, keepdims=True))
    return rows


def pack_rows(rows, table):
    for number, row in enumerate(rows):
        placed = row if number % 3 == 0 else pltpu.roll(row, WELLS * (number % 3), 1)
        table = table + jnp.where(
            iota(table.shape, 0) == number // 3, jnp.broadcast_to(placed, table.shape), 0.0
        )
    return table


def unpack_row(table, number):
    row = table[number // 3 : number // 3 + 1, :]
    if number % 3:
        row = pltpu.roll(row, LANES - WELLS * (number % 3), 1)
    return jnp.where(iota(row.shape, 1) < WELLS, row, 0.0)


def place_rows(rows, table):
    for number, row in enumerate(rows):
        group, k = divmod(number, RHS)
        at = k + RHS * (group // 3)
        placed = pltpu.roll(row, WELLS * group, 1) if group in (1, 2) else row
        table = table + jnp.where(
            iota(table.shape, 0) == at, jnp.broadcast_to(placed, table.shape), 0.0
        )
    return table


def place_columns(dots, first_lane, table):
    for number in range(dots.shape[0]):
        column = jnp.sum(dots[number], axis=1, keepdims=True)
        table = table + jnp.where(iota(table.shape, 1) == first_lane + number, column, 0.0)
    return table


def take_group(table, group):
    if group in (1, 2):
        table = pltpu.roll(table, LANES - WELLS * group, 1)
    start = RHS * (group // 3)
    rows = table[start : start + RHS, :]
    return jnp.where(iota(rows.shape, 1) < WELLS, rows, 0.0)


def take_column(table, lane):
    return table[RHS : 2 * RHS, lane : lane + 1]


def lane_sum(row):
    return jnp.sum(row, axis=1, keepdims=True)


def on_even(axis):
    return lax.rem(lax.axis_index(axis), 2) == 0


def copied(source, target):
    count = min(source.shape[0], target.shape[0])
    target[0:count] = source[0:count]
    if target.shape[0] > count:
        target[count:] = jnp.zeros_like(target[count:])


def by_pair(axis, low, high, first, second):
    @pl.when(on_even(axis))
    def _():
        copied(high, first)
        copied(low, second)

    @pl.when(jnp.logical_not(on_even(axis)))
    def _():
        copied(low, first)
        copied(high, second)


def by_side(axis, first, second, low, high):
    by_pair(axis, second, first, high, low)


COUPLINGS, DIAGONALS, WELL_FIELDS, IDS, RIGHT_SIDE, START = range(6)


def layer_blocks(cut, inward, lateral):
    def plane(n):
        if n < DIAGONAL:
            return cut(COUPLINGS, ((lateral, lateral + 1, 4, 5)[n // 4], n % 4), 0)
        if n < BACK_IN:
            return cut(DIAGONALS, (n - DIAGONAL,), 0)
        return cut(COUPLINGS, (inward, n - BACK_IN), 1)

    return plane


def fill_pack(pack, inward, lateral, cut):
    blocks = layer_blocks(cut, inward, lateral)
    for e in range(4):
        pack[e] = cut(COUPLINGS, (inward, e), 0)
    wells = [cut(WELL_FIELDS, (2 + a,), 0) for a in range(2)]
    for a in range(2):
        pack[WELL_EQ + a] = wells[a]
    pack[WELL_ID] = cut(IDS, (), 0).astype(jnp.float32)
    pack[BACK_ID] = cut(IDS, (), 1).astype(jnp.float32)
    for start, at in (
        (LAT_UP, UP_WELL),
        (LAT_DOWN, DOWN_WELL),
        (RISE, RISE_WELL),
        (FALL, FALL_WELL),
        (DIAGONAL, DIAGONAL_WELL),
        (BACK_IN, BACK_WELL),
    ):
        if start == BACK_IN:
            wells = [cut(WELL_FIELDS, (2 + a,), 1) for a in range(2)]
        for b, value in enumerate(product(lambda e: blocks(start + e), *wells)):
            pack[at + b] = value
    for k in range(RHS):
        here = [cut(START, (k, a), 0) for a in range(2)]
        back = [cut(START, (k, a), 1) for a in range(2)]
        entering = product(lambda e: blocks(BACK_IN + e), *back)
        local = face_stencil(blocks, here[0], here[1], entering)
        for a in range(2):
            pack[GUESS + 2 * k + a] = here[a]
            pack[REST + 2 * k + a] = cut(RIGHT_SIDE, (k, a), 0) - local[a]
    if pack.shape[0] > ENDS:
        end = pack.shape[1] - 1
        for e in range(4):
            pack[ENDS, e : e + 1, :] = blocks(LAT_UP + e)[end : end + 1, :]
            pack[ENDS, 4 + e : 5 + e, :] = blocks(LAT_DOWN + e)[0:1, :]


def x_pack_kernel(*refs):
    sources, first, second, held_ends, arrived = refs[:6], refs[6], refs[7], refs[8:20], refs[20]
    packs = refs[21:23]
    copies = []
    for n, source in enumerate(sources):
        lead = (slice(None),) * (len(source.shape) - 3)
        depth = source.shape[-3]
        for end, start in enumerate((0, depth - 2)):
            copies.append(
                pltpu.make_async_copy(
                    source.at[lead + (pl.ds(start, 2),)],
                    held_ends[2 * n + end],
                    arrived.at[2 * n + end],
                )
            )
    for copy in copies:
        copy.start()
    for copy in copies:
        copy.wait()
    for end, pack in enumerate(packs):
        fill_pack(
            pack,
            1 - end,
            2,
            lambda n, index, layer: held_ends[2 * n + end][
                index + (1 - layer if end else layer,)
            ],
        )
    by_pair("gx", *packs, first, second)


def y_cut(arguments, end):
    last = arguments[0].shape[-2] - 1

    def cut(n, index, layer):
        return arguments[n][index + (slice(None), last - layer if end else layer, slice(None))]

    return cut


def send_out(table, chunks, part, sent):
    rows = min(chunks.shape[1], table.shape[0])
    chunks[:, :rows, :] = jnp.broadcast_to(table[None, :rows], (chunks.shape[0], rows, LANES))
    copy = pltpu.make_async_copy(chunks, part, sent.at[0])
    copy.start()
    return copy


def corner_kernel(y_low, y_high, came_first, came_second, first, second, fxl, fxh, *outs):
    by_side("gx", came_first, came_second, fxl, fxh)
    last = fxl.shape[1] - 1
    for own, out, at, side in ((y_low, outs[0], 0, 4), (y_high, outs[1], last, 0)):
        for n in range(FACE_PLANES):
            out[n] = own[n]
        row = FACE_PLANES * 8
        out[FACE_PLANES + CORNER_PLANES - 1] = jnp.zeros(out.shape[1:], jnp.float32)
        for face in (fxl, fxh):
            rows = [(n, at) for n in range(4)]
            rows += [(ENDS, side + e) for e in range(4)]
            rows += [(n, at) for n in range(WELL_EQ, REST)]
            for n, y in rows:
                out[row // 8, row % 8 : row % 8 + 1, :] = face[n, y : y + 1, :]
                row += 1
    by_pair("gy", *outs, first, second)


def diagonal_device(x_end, y_end):
    across, along = lax.axis_index("gx"), lax.axis_index("gy")
    there_x, there_y = across + 2 * x_end - 1, along + 2 * y_end - 1
    count_x, count_y = lax.axis_size("gx"), lax.axis_size("gy")
    exists = (there_x >= 0) & (there_x < count_x) & (there_y >= 0) & (there_y < count_y)
    return exists, jnp.where(exists, there_x * count_y + there_y, 0)


def guess_kernel(
    couplings, diagonal, wells, ids, right, guess,
    part, present, y_low, y_high, values, scratch, chunks, sent,
):
    list_wells(ids, present)
    for k in range(RHS):
        values[k] = wells[0] * guess[k, 0] + wells[1] * guess[k, 1]
    values[4] = wells[0] * wells[2] + wells[1] * wells[3]
    values[5] = wells[2] * wells[2] + wells[3] * wells[3]
    rows = segment_rows(ids, values, scratch, present)
    table = pack_rows(rows, jnp.zeros((8, LANES), jnp.float32))
    copy = send_out(table, chunks, part, sent)
    arguments = (couplings, diagonal, wells, ids, right, guess)
    for end, pack in enumerate((y_low, y_high)):
        fill_pack(pack, 3 - end, 0, y_cut(arguments, end))
    copy.wait()


def block_kernel(
    couplings, diagonal, right, guess, sent_face, rest, leaving
):
    nothing_enters = [[jnp.zeros(guess.shape[3:], jnp.float32)] * 2] * 4
    for k in range(RHS):
        inside, outgoing = block_stencil(
            couplings, diagonal, guess[k, 0], guess[k, 1], nothing_enters
        )
        for a in range(2):
            rest[k, a] = right[k, a] - inside[a]
            for f in range(4):
                leaving[f, 2 * k + a] = outgoing[f][a]


def residual_kernel(
    couplings, diagonal, wells, ids, fxl, fxh, came_first, came_second, parts,
    rest, leaving,
    residual, image, residual_faces, x_first, x_second, y_first, y_second, small, fyl, fyh,
    x_low, x_high, y_low, y_high,
):
    by_side("gy", came_first, came_second, fyl, fyh)
    faces = (fxl, fxh, fyl, fyh)
    totals = jnp.sum(parts[...], axis=0)
    corners = corners_of(faces, FACE_PLANES, CORNER_ROWS)
    all_ids = ids[...]
    face_ids = [as_ids(face[WELL_ID]) for face in faces]
    last = rest.shape[2] - 1
    row = iota(rest.shape[2:], 1)
    for k in range(RHS):
        s_row = unpack_row(totals, k)
        entering = [
            product(
                lambda e, f=f: faces[f][e],
                faces[f][GUESS + 2 * k],
                faces[f][GUESS + 2 * k + 1],
            )
            for f in range(4)
        ]
        outgoing = [[leaving[f, 2 * k + b] for b in range(2)] for f in range(4)]
        at_wells = spread(s_row, all_ids)
        now = []
        for a in range(2):
            value = rest[k, a] - wells[2 + a] * at_wells
            over_x = [
                (value[0] - entering[0][a])[None],
                value[1:last],
                (value[last] - entering[1][a])[None],
            ]
            value = jnp.concatenate(over_x, axis=0)
            value = value - jnp.where(row == 0, entering[2][a][:, None, :], 0.0)
            now.append(value - jnp.where(row == last, entering[3][a][:, None, :], 0.0))
        for a in range(2):
            residual[k, a] = now[a]
        ends = corner_inputs(
            corners,
            [[corners[c].row(SIDE_GUESS + 2 * k + a) for a in range(2)] for c in range(4)],
        )
        incoming = []
        for f in range(4):
            face = faces[f]
            there = face_entries(ends[(f, 0)], ends[(f, 1)], outgoing[f])
            face_wells = spread(s_row, face_ids[f])
            outer = [
                face[REST + 2 * k + a] - there[a] - face[WELL_EQ + a] * face_wells
                for a in range(2)
            ]
            for a in range(2):
                residual_faces[f, 2 * k + a] = outer[a]
            incoming.append(product(lambda e, f=f: faces[f][e], *outer))
        result, _ = block_stencil(couplings, diagonal, now[0], now[1], incoming)
        for a in range(2):
            image[k, a] = result[a]
    own = (couplings, diagonal)
    for axis, packs in enumerate(((x_low, x_high), (y_low, y_high))):
        for end, pack in enumerate(packs):

            def cut(ref, index, layer):
                at = last - layer if end else layer
                return ref[index + ((at,) if axis == 0 else (slice(None), at, slice(None)))]

            plane = layer_blocks(
                lambda n, index, layer: cut(own[n], index, layer),
                2 * axis + 1 - end,
                2 * (1 - axis),
            )
            blocks = [plane(n) for n in range(LAYER_BLOCKS)]
            for k in range(RHS):
                here = [cut(image, (k, a), 0) for a in range(2)]
                back = [cut(image, (k, a), 1) for a in range(2)]
                entering = product(lambda e: blocks[BACK_IN + e], *back)
                local = face_stencil(lambda n: blocks[n], here[0], here[1], entering)
                for a in range(2):
                    pack[2 * k + a] = here[a]
                    pack[8 + 2 * k + a] = local[a]
    by_pair("gx", x_low, x_high, x_first, x_second)
    by_pair("gy", y_low, y_high, y_first, y_second)
    small[...] = jnp.concatenate(
        [unpack_row(totals, 4), unpack_row(totals, 5), jnp.zeros((6, LANES), jnp.float32)], axis=0
    )


def moments_kernel(
    wells, ids, residual, image, present, part, values, scratch, dots, chunks, sent
):
    dots[...] = jnp.zeros_like(dots)
    for k in range(RHS):
        now = [residual[k, a] for a in range(2)]
        result = [image[k, a] for a in range(2)]
        for n, field in enumerate((now, result)):
            values[4 * n + k] = wells[0] * field[0] + wells[1] * field[1]
            values[8 + 4 * n + k] = wells[2] * field[0] + wells[3] * field[1]
        row = slice(RHS + k, RHS + k + 1)
        dots[0, row, :] = tile_sum(now, now)
        dots[1, row, :] = tile_sum(now, result)
        dots[2, row, :] = tile_sum(result, result)
    rows = segment_rows(ids, values, scratch, present)
    table = place_rows(rows, jnp.zeros((8, LANES), jnp.float32))
    chunks[:, 8:, :] = jnp.zeros_like(chunks[:, 8:, :])
    last = image.shape[2] - 1
    for x_end in range(2):
        for y_end in range(2):
            exists, place = diagonal_device(x_end, y_end)

            @pl.when(exists)
            def _():
                for k in range(RHS):
                    for a in range(2):
                        row, y = 8 + 2 * k + a, last * y_end
                        chunks[pl.ds(place, 1), row : row + 1, :] = image[
                            k, a, last * x_end, y : y + 1, :
                        ][None]

    send_out(place_columns(dots, WELLS, table), chunks, part, sent).wait()


def first_step(totals, small):
    s_row, us_row, p_row, ps_row = (take_group(totals, group) for group in range(4))
    within, equation = small[0:1, :], small[1:2, :]
    rr, rs, ss = (take_column(totals, WELLS + i) for i in range(3))
    height = (rs + lane_sum(p_row * s_row)) / rr
    square = ss + lane_sum(2.0 * ps_row * s_row + equation * s_row * s_row)
    left = jnp.maximum(square - height * height * rr, 1e-7 * square)
    scale = lax.rsqrt(left)
    s_image = us_row + within * s_row
    s_second = (s_image - height * s_row) * scale
    p_second = (ps_row + equation * s_row - height * p_row) * scale
    shift = rs / rr + lane_sum(p_second * s_second)
    unit = lax.rsqrt(rr)
    following = left * scale * unit
    return s_row, s_image, p_row, p_second, (unit, rr * unit, height, shift, following, scale)


def krylov_kernel(
    couplings, diagonal, wells, ids, fxl, fxh, fyl, fyh, x_first, x_second, y_first, y_second,
    residual, image, residual_faces, parts, small_in, present,
    second_out, third_out, part, known, scratch, values_scratch, dots, gxl, gxh, gyl, gyh,
):
    by_side("gx", x_first, x_second, gxl, gxh)
    by_side("gy", y_first, y_second, gyl, gyh)
    faces, sent = (fxl, fxh, fyl, fyh), (gxl, gxh, gyl, gyh)
    totals = jnp.sum(parts[:, 0:8, :], axis=0)
    small = small_in[...]
    s_rows, s_images, p_rows, p_seconds, scalars = first_step(totals, small)
    known[0:RHS, :] = p_rows
    known[RHS : 2 * RHS, :] = p_seconds
    columns = jnp.zeros((RHS, LANES), jnp.float32)
    for n, column in enumerate(scalars):
        columns = columns + jnp.where(iota(columns.shape, 1) == n, column, 0.0)
    known[2 * RHS : 3 * RHS, :] = columns
    known[3 * RHS :, :] = jnp.broadcast_to(small[1:2, :], (RHS, LANES))
    dots[...] = jnp.zeros_like(dots)
    corners = corners_of(faces, FACE_PLANES, CORNER_ROWS)
    places = [diagonal_device(c % 2, c // 2)[1] for c in range(4)]
    all_ids = ids[...]
    face_ids = [as_ids(face[WELL_ID]) for face in faces]
    back_ids = [as_ids(face[BACK_ID]) for face in faces]
    corner_ids = [
        as_ids(jnp.broadcast_to(corner.row(SIDE_ID), (8, LANES))) for corner in corners
    ]
    for k in range(RHS):
        unit, _, height, shift, _, scale = (column[k : k + 1, :] for column in scalars)
        s_row, s_image = s_rows[k : k + 1, :], s_images[k : k + 1, :]
        at_wells = spread(s_row, all_ids)
        now = [image[k, a] + wells[2 + a] * at_wells for a in range(2)]
        face_now, spread_now = [], []
        for f in range(4):
            here = spread(s_row, face_ids[f])
            spread_now.append((here, spread(s_row, back_ids[f])))
            face_now.append(
                [sent[f][2 * k + a] + faces[f][WELL_EQ + a] * here for a in range(2)]
            )
        corner_now = []
        for c in range(4):
            here = spread(s_row, corner_ids[c])[0:1, :]
            corner_now.append(
                [
                    parts[pl.ds(places[c], 1), 8 + 2 * k + a, :] + corners[c].row(SIDE_EQ + a) * here
                    for a in range(2)
                ]
            )
        incoming = [product(lambda e, f=f: faces[f][e], *face_now[f]) for f in range(4)]
        applied, outgoing = block_stencil(couplings, diagonal, now[0], now[1], incoming)
        at_wells = spread(s_image, all_ids)
        second, third = [], []
        for a in range(2):
            twice = applied[a] + wells[2 + a] * at_wells
            base = (now[a] - height * residual[k, a]) * scale
            second.append(base)
            third.append((twice - height * now[a]) * scale - shift * base)
            second_out[k, a] = second[a]
            third_out[k, a] = third[a]
        ends = corner_inputs(corners, corner_now)
        incoming = []
        for f in range(4):
            face = faces[f]
            here, behind = spread_now[f]
            moves = [
                [face[at + b] * here for b in range(2)]
                for at in (DIAGONAL_WELL, UP_WELL, DOWN_WELL, RISE_WELL, FALL_WELL)
            ]
            there = face_moves(*moves, [face[BACK_WELL + b] * behind for b in range(2)])
            local = [sent[f][8 + 2 * k + b] + there[b] for b in range(2)]
            over = face_entries(ends[(f, 0)], ends[(f, 1)], outgoing[f])
            here = spread(s_image, face_ids[f])
            outer = []
            for a in range(2):
                twice = local[a] + over[a] + face[WELL_EQ + a] * here
                base = (face_now[f][a] - height * residual_faces[f, 2 * k + a]) * scale
                outer.append((twice - height * face_now[f][a]) * scale - shift * base)
            incoming.append(product(lambda e, f=f: faces[f][e], *outer))
        result, _ = block_stencil(couplings, diagonal, third[0], third[1], incoming)
        fourth = [result[a] - shift * third[a] for a in range(2)]
        values_scratch[k] = wells[0] * third[0] + wells[1] * third[1]
        values_scratch[4 + k] = wells[2] * third[0] + wells[3] * third[1]
        values_scratch[8 + k] = wells[2] * fourth[0] + wells[3] * fourth[1]
        fields = [[residual[k, a] * unit for a in range(2)], second, third, fourth]
        number = 0
        for i in range(4):
            for j in range(i, 4):
                dots[number, RHS + k : RHS + k + 1, :] = tile_sum(fields[i], fields[j])
                number += 1
    rows = segment_rows(ids, values_scratch, scratch, present)
    table = place_rows(rows, jnp.zeros((8, LANES), jnp.float32))
    table = place_columns(dots, 0, table)
    gram = table[RHS : RHS + 1, :]
    for k in range(1, RHS):
        gram = gram + pltpu.roll(table[RHS + k : RHS + k + 1, :], GRAM_ENTRIES * k, 1)
    flat = jnp.concatenate([table[k : k + 1, :] for k in range(RHS)] + [gram], axis=1)
    part[...] = jnp.broadcast_to(flat[None], part.shape)


def solve_kernel(
    guess_in, residual, second, third, parts, known, solution, guess, arrived
):
    copy = pltpu.make_async_copy(guess_in, guess, arrived.at[0])
    copy.start()
    flat = jnp.sum(parts[...], axis=0)
    rows = [flat[:, LANES * n : LANES * (n + 1)] for n in range(RHS + 1)]
    for k in range(1, RHS):
        rows.append(pltpu.roll(rows[RHS], LANES - GRAM_ENTRIES * k, 1))
    totals = jnp.concatenate(rows, axis=0)
    s_third, p_third, p_fourth = (take_group(totals, group) for group in range(3))
    p_first, p_second = known[0:RHS, :], known[RHS : 2 * RHS, :]
    unit, beta, height, shift, following = (
        known[2 * RHS : 3 * RHS, n : n + 1] for n in range(5)
    )
    equation = known[3 * RHS :, :]
    gram = {}
    number = 0
    for i in range(4):
        for j in range(i, 4):
            gram[(i, j)] = take_column(totals, number)
            number += 1
    gram[(0, 3)] += lane_sum(p_first * s_third) * unit
    gram[(1, 3)] += lane_sum(p_second * s_third)
    gram[(2, 3)] += lane_sum(p_third * s_third)
    gram[(3, 3)] += lane_sum(2.0 * p_fourth * s_third + equation * s_third * s_third)
    tiny = 1e-30
    inverse = [lax.rsqrt(jnp.maximum(gram[(i, i)], tiny)) for i in range(4)]
    length = [jnp.maximum(gram[(i, i)], tiny) * inverse[i] for i in range(4)]
    upper = {}
    for i in range(4):
        for j in range(i, 4):
            entry = gram[(i, j)] * inverse[i] * inverse[j]
            for m in range(i):
                entry = entry - upper[(m, i)] * upper[(m, j)]
            if i == j:
                pivot = lax.rsqrt(jnp.maximum(entry, 1e-6))
                upper[(i, i)] = jnp.maximum(entry, 1e-6) * pivot
                over = pivot
            else:
                upper[(i, j)] = entry * over
    columns = [
        [(0, height * length[0]), (1, following * length[1])],
        [(1, shift * length[1]), (2, length[2])],
        [(2, shift * length[2]), (3, length[3])],
    ]
    zero = jnp.zeros_like(shift)
    hessenberg = [[zero] * 3 for _ in range(4)]
    for j in range(3):
        for i in range(j + 2):
            for m, factor in columns[j]:
                if m >= i:
                    hessenberg[i][j] = hessenberg[i][j] + upper[(i, m)] * factor
    target = [beta * length[0] * upper[(0, 0)], zero, zero, zero]
    turns = []
    for j in range(3):
        top, bottom = hessenberg[j][j], hessenberg[j + 1][j]
        turn = lax.rsqrt(top * top + bottom * bottom)
        turns.append(turn)
        cosine, sine = top * turn, bottom * turn
        for m in range(j, 3):
            high, low = hessenberg[j][m], hessenberg[j + 1][m]
            hessenberg[j][m] = cosine * high + sine * low
            hessenberg[j + 1][m] = cosine * low - sine * high
        high, low = target[j], target[j + 1]
        target[j] = cosine * high + sine * low
        target[j + 1] = cosine * low - sine * high
    weights = [zero] * 3
    for i in (2, 1, 0):
        value = target[i]
        for j in range(i + 1, 3):
            value = value - hessenberg[i][j] * weights[j]
        weights[i] = value * turns[i]
    copy.wait()
    for k in range(RHS):
        on_first, on_second, on_third = (
            column[k : k + 1, :] for column in (weights[0] * unit, weights[1], weights[2])
        )
        for a in range(2):
            solution[k, a] = (
                guess[k, a]
                + on_first * residual[k, a]
                + on_second * second[k, a]
                + on_third * third[k, a]
            )


def call(kernel, shapes, arguments, scratch=(), far_inputs=0, cost=0, grant=24 << 20, out=0):
    whole = pl.BlockSpec(memory_space=pltpu.VMEM)
    far = pl.BlockSpec(memory_space=pltpu.HBM)
    scalars = pl.BlockSpec(memory_space=pltpu.SMEM)

    def place(number, array):
        if len(array.shape) == 1:
            return scalars
        return far if number < far_inputs else whole

    outs = [
        jax.ShapeDtypeStruct(shape, jnp.float32 if len(shape) > 1 else jnp.int32)
        for shape in shapes
    ]
    outs[:out] = [pltpu.HBM(shape, jnp.float32) for shape in shapes[:out]]
    return pl.pallas_call(
        kernel,
        out_shape=outs,
        in_specs=[place(*numbered) for numbered in enumerate(arguments)],
        out_specs=[far] * out + [scalars if len(shape) == 1 else whole for shape in shapes[out:]],
        scratch_shapes=list(scratch),
        compiler_params=pltpu.CompilerParams(vmem_limit_bytes=grant),
        cost_estimate=pl.CostEstimate(flops=cost, bytes_accessed=cost, transcendentals=0)
        if cost
        else None,
    )(*arguments)


def nothing(value, *rest):
    pass


def after(value, *others):
    far = pl.BlockSpec(memory_space=pltpu.HBM)
    near = pl.BlockSpec(memory_space=pltpu.VMEM)
    return pl.pallas_call(
        nothing,
        out_shape=pltpu.HBM(value.shape, value.dtype),
        in_specs=[far] + [near] * len(others),
        out_specs=far,
        input_output_aliases={0: 0},
        compiler_params=pltpu.CompilerParams(vmem_limit_bytes=1 << 20),
    )(pltpu.with_memory_space_constraint(value, pltpu.HBM), *others)


def held(*shape):
    return pltpu.VMEM(shape, jnp.float32)


def swap(value, axis, start):
    pairs = []
    for low in range(start, lax.axis_size(axis) - 1, 2):
        pairs += [(low, low + 1), (low + 1, low)]
    return lax.ppermute(value, axis, pairs) if pairs else jnp.zeros_like(value)


def swapped(first, second, axis):
    return swap(first, axis, 0), swap(second, axis, 1)


def exchanged(part):
    return lax.all_to_all(part, ("gx", "gy"), 0, 0, tiled=True)


def body(couplings, diagonal, wells, ids, right, guess):
    devices = lax.axis_size("gx") * lax.axis_size("gy")
    plane = (8, LANES)
    field = guess.shape
    block = guess.shape[2:]
    arguments = (couplings, diagonal, wells, ids, right, guess)

    ends = []
    for argument in arguments:
        shape = argument.shape[:-3] + (2,) + argument.shape[-2:]
        ends += [pltpu.VMEM(shape, argument.dtype)] * 2
    x_first, x_second = call(
        x_pack_kernel,
        [(FACE_PLANES + 1,) + plane, (FACE_PLANES + 2,) + plane],
        [pltpu.with_memory_space_constraint(argument, pltpu.HBM) for argument in arguments],
        ends
        + [pltpu.SemaphoreType.DMA((len(ends),))]
        + [held(FACE_PLANES + 1, *plane)] * 2,
        far_inputs=len(arguments),
    )
    came_x = swapped(x_first, x_second, "gx")
    first_chunks, chunks = (devices, TABLE_ROWS, LANES), (devices, 16, LANES)
    sent = pltpu.SemaphoreType.DMA((1,))
    part, present, y_low, y_high = call(
        guess_kernel,
        [first_chunks, (WELLS + 8,)] + [(FACE_PLANES,) + plane] * 2,
        arguments,
        [held(6, *block), held(6, WELLS, LANES), held(*first_chunks), sent],
        cost=4 << 20,
        out=1,
    )
    parts = exchanged(after(part, came_x[0]))
    y_shape = (FACE_PLANES + CORNER_PLANES,) + plane
    y_first, y_second, fxl, fxh = call(
        corner_kernel,
        [y_shape] * 2 + [(FACE_PLANES + 1,) + plane] * 2,
        (y_low, y_high, *came_x),
        [held(*y_shape)] * 2,
    )
    came_y = swapped(y_first, y_second, "gy")
    ahead = call(
        block_kernel,
        [field, (4, 8) + plane],
        (couplings, diagonal, right, guess, y_first),
        cost=4 << 20,
    )

    residual, image, residual_faces, *packs, small, fyl, fyh = call(
        residual_kernel,
        [field, field, (4, 8) + plane]
        + [(IMAGE_PLANES + spare,) + plane for spare in (1, 2, 0, 3)]
        + [(8, LANES)]
        + [y_shape] * 2,
        (couplings, diagonal, wells, ids, fxl, fxh, *came_y, parts, *ahead),
        [held(IMAGE_PLANES, *plane)] * 4,
    )
    faces = (fxl, fxh, fyl, fyh)
    came_y1 = swap(packs[3], "gy", 1)
    came_x1 = swap(packs[1], "gx", 1)
    came_x0 = swap(packs[0], "gx", 0)
    came_y0 = swap(packs[2], "gy", 0)
    (part,) = call(
        moments_kernel,
        [chunks],
        (wells, ids, residual, image, present),
        [held(16, *block), held(16, WELLS, LANES), held(3, *plane), held(*chunks), sent],
        cost=4 << 20,
        out=1,
    )
    parts = exchanged(part)
    second, third, part, known = call(
        krylov_kernel,
        [field, field, (devices, 1, (RHS + 1) * LANES), (4 * RHS, LANES)],
        (couplings, diagonal, wells, ids) + faces + (came_x0, came_x1, came_y0, came_y1)
        + (residual, image, residual_faces, parts, small, present),
        [held(12, WELLS, LANES), held(12, *block), held(10, *plane)]
        + [held(IMAGE_PLANES, *plane)] * 4,
    )
    parts = exchanged(part)
    (result,) = call(
        solve_kernel,
        [field],
        (
            pltpu.with_memory_space_constraint(guess, pltpu.HBM),
            residual, second, third, parts, known,
        ),
        [held(*field), pltpu.SemaphoreType.DMA((1,))],
        far_inputs=1,
    )
    return result


def solution(mesh):
    in_specs = (
        P("member", None, "gx", "gy", None),
        P("member", "gx", "gy", None),
        P("member", "gx", "gy", None),
        P("gx", "gy", None),
        P("member", None, "gx", "gy", None),
        P("member", None, "gx", "gy", None),
    )
    out_specs = P("member", None, "gx", "gy", None)
    return jax.shard_map(body, mesh=mesh, in_specs=in_specs, out_specs=out_specs, check_vma=False)
```

```python
import jax
import jax.numpy as jnp
from jax import lax
from jax.experimental import pallas as pl
from jax.experimental.pallas import tpu as pltpu
from jax.sharding import PartitionSpec as P

WELLS = 40
RHS = 4
LANES = 128
WELL_EQ, WELL_ID, GUESS, REST = 4, 6, 7, 15
UP_WELL, DOWN_WELL, RISE_WELL, FALL_WELL, DIAGONAL_WELL = 23, 25, 27, 29, 31
BACK_WELL, BACK_ID = 33, 35
FACE_PLANES = 36
ENDS = 36
CORNER_PLANES = 5
LAT_UP, LAT_DOWN, RISE, FALL, DIAGONAL, BACK_IN = 0, 4, 8, 12, 16, 20
LAYER_BLOCKS = 24
IMAGE_PLANES = 16
TABLE_ROWS = 6
GRAM_ENTRIES = 10
CORNER_ROWS = 19
SIDE_IN, SIDE_EQ, SIDE_ID, SIDE_GUESS = 4, 8, 10, 11


def product(blocks, first, second):
    return [
        blocks(0) * first + blocks(2) * second,
        blocks(1) * first + blocks(3) * second,
    ]


def iota(shape, axis):
    return lax.broadcasted_iota(jnp.int32, shape, axis)


def roll_up(value, axis):
    return pltpu.roll(value, 1, axis)


def roll_down(value, axis):
    return pltpu.roll(value, value.shape[axis] - 1, axis)


def layer_moves(rising, falling):
    axis = rising.ndim - 1
    lane = iota(rising.shape, axis)
    up = jnp.where(lane == 0, 0.0, roll_up(rising, axis))
    down = jnp.where(lane == LANES - 1, 0.0, roll_down(falling, axis))
    return up + down


def block_stencil(couplings, diagonal, first, second, incoming):
    result = product(lambda e: diagonal[e], first, second)
    moved = [product(lambda e, d=d: couplings[d, e], first, second) for d in range(6)]
    row = iota(first.shape, 1)
    outgoing = [[], [], [], []]
    for b in range(2):
        east, west, north, south, rise, fall = (moved[d][b] for d in range(6))
        total = result[b] + jnp.concatenate([incoming[0][b][None], east[:-1]], axis=0)
        total = total + jnp.concatenate([west[1:], incoming[1][b][None]], axis=0)
        total = total + jnp.where(row == 0, incoming[2][b][:, None, :], roll_up(north, 1))
        total = total + jnp.where(
            row == row.shape[1] - 1, incoming[3][b][:, None, :], roll_down(south, 1)
        )
        result[b] = total + layer_moves(rise, fall)
        outgoing[0].append(west[0])
        outgoing[1].append(east[-1])
        outgoing[2].append(south[:, 0, :])
        outgoing[3].append(north[:, -1, :])
    return result, outgoing


def face_stencil(blocks, first, second, behind):
    def times(start):
        return product(lambda e: blocks(start + e), first, second)

    moves = [times(start) for start in (DIAGONAL, LAT_UP, LAT_DOWN, RISE, FALL)]
    return face_moves(*moves, behind)


def face_moves(kept, up, down, rise, fall, behind):
    result = list(kept)
    row = iota(kept[0].shape, 0)
    for b in range(2):
        total = result[b] + behind[b] + layer_moves(rise[b], fall[b])
        total = total + jnp.where(row == 0, 0.0, roll_up(up[b], 0))
        result[b] = total + jnp.where(row == row.shape[0] - 1, 0.0, roll_down(down[b], 0))
    return result


def face_entries(low_end, high_end, entering):
    row = iota(entering[0].shape, 0)
    return [
        entering[b]
        + jnp.where(row == 0, low_end[b], 0.0)
        + jnp.where(row == row.shape[0] - 1, high_end[b], 0.0)
        for b in range(2)
    ]


def spread(totals, ids):
    table = jnp.broadcast_to(totals, (8, LANES))
    if ids.ndim == 2:
        return jnp.take_along_axis(table, ids, axis=1)
    return jnp.stack(
        [jnp.take_along_axis(table, ids[x], axis=1) for x in range(ids.shape[0])], axis=0
    )


def as_ids(plane):
    return plane.astype(jnp.int32)


class Corner:
    def __init__(self, pack, which, base):
        self.pack, self.start = pack, base * 8 + which

    def row(self, number):
        at = self.start + number
        return self.pack[at // 8, at % 8 : at % 8 + 1, :]


def corners_of(faces, base, rows):
    found = []
    for y_face in (2, 3):
        for x_end in range(2):
            found.append(Corner(faces[y_face], x_end * rows, base))
    return found


def corner_inputs(corners, values):
    ends = {}
    for c in range(4):
        x_end, y_end = c % 2, c // 2
        over_x = product(corners[c].row, *values[c])
        over_y = product(lambda e, c=c: corners[c].row(SIDE_IN + e), *values[c])
        ends[(2 + y_end, x_end)] = over_x
        ends[(x_end, y_end)] = over_y
    return ends


def tile_sum(first, second):
    value = first[0] * second[0] + first[1] * second[1]
    return jnp.sum(jnp.sum(value, axis=0), axis=0, keepdims=True)


def list_wells(ids, present):
    planes = [ids[x].astype(jnp.float32) for x in range(ids.shape[0])]
    middle = WELLS // 2
    halves = ((0.0, float(middle)), (float(middle), float(WELLS)))

    def least(above, top):
        found = [jnp.where((p > above) & (p < top), p, top) for p in planes]
        value = found[0]
        for other in found[1:]:
            value = jnp.minimum(value, other)
        return jnp.min(value)

    def greatest(base, below):
        found = [jnp.where((p >= base) & (p < below), p, base - 1.0) for p in planes]
        value = found[0]
        for other in found[1:]:
            value = jnp.maximum(value, other)
        return jnp.max(value)

    def some_left(state):
        return (state[1] <= state[2]) | (state[3] <= state[4])

    def step(state):
        number, ends = state[0], state[1:]
        after = []
        for half, (base, top) in enumerate(halves):
            low, high = ends[2 * half], ends[2 * half + 1]
            present[number] = low.astype(jnp.int32)
            number = number + jnp.where(low <= high, 1, 0)
            present[number] = high.astype(jnp.int32)
            number = number + jnp.where(low < high, 1, 0)
            after += [least(low, top), greatest(base, high)]
        return (number, *after)

    ends = []
    for base, top in halves:
        ends += [least(base - 1.0, top), greatest(base, top)]
    state = lax.while_loop(some_left, step, (jnp.int32(1), *ends))
    present[0] = state[0] - 1


def segment_rows(ids, values, scratch, present):
    scratch[...] = jnp.zeros_like(scratch)
    count, depth = values.shape[0], ids.shape[0]

    def one_well(step, _):
        well = present[step + 1]
        masks = [ids[x] == well for x in range(depth)]
        for number in range(count):
            total = jnp.where(masks[0], values[number, 0], 0.0)
            for x in range(1, depth):
                total = total + jnp.where(masks[x], values[number, x], 0.0)
            scratch[number, pl.ds(well, 1), :] = jnp.sum(total, axis=0, keepdims=True)
        return 0

    lax.fori_loop(0, present[0], one_well, 0)
    rows = []
    for number in range(count):
        summed = jnp.sum(scratch[number], axis=1, keepdims=True)
        shape = scratch.shape[1:]
        on_lanes = jnp.where(iota(shape, 0) == iota(shape, 1), summed, 0.0)
        rows.append(jnp.sum(on_lanes, axis=0, keepdims=True))
    return rows


def pack_rows(rows, table):
    for number, row in enumerate(rows):
        placed = row if number % 3 == 0 else pltpu.roll(row, WELLS * (number % 3), 1)
        table = table + jnp.where(
            iota(table.shape, 0) == number // 3, jnp.broadcast_to(placed, table.shape), 0.0
        )
    return table


def unpack_row(table, number):
    row = table[number // 3 : number // 3 + 1, :]
    if number % 3:
        row = pltpu.roll(row, LANES - WELLS * (number % 3), 1)
    return jnp.where(iota(row.shape, 1) < WELLS, row, 0.0)


def place_rows(rows, table):
    for number, row in enumerate(rows):
        group, k = divmod(number, RHS)
        at = k + RHS * (group // 3)
        placed = pltpu.roll(row, WELLS * group, 1) if group in (1, 2) else row
        table = table + jnp.where(
            iota(table.shape, 0) == at, jnp.broadcast_to(placed, table.shape), 0.0
        )
    return table


def place_columns(dots, first_lane, table):
    for number in range(dots.shape[0]):
        column = jnp.sum(dots[number], axis=1, keepdims=True)
        table = table + jnp.where(iota(table.shape, 1) == first_lane + number, column, 0.0)
    return table


def take_group(table, group):
    if group in (1, 2):
        table = pltpu.roll(table, LANES - WELLS * group, 1)
    start = RHS * (group // 3)
    rows = table[start : start + RHS, :]
    return jnp.where(iota(rows.shape, 1) < WELLS, rows, 0.0)


def take_column(table, lane):
    return table[RHS : 2 * RHS, lane : lane + 1]


def lane_sum(row):
    return jnp.sum(row, axis=1, keepdims=True)


def on_even(axis):
    return lax.rem(lax.axis_index(axis), 2) == 0


def copied(source, target):
    count = min(source.shape[0], target.shape[0])
    target[0:count] = source[0:count]
    if target.shape[0] > count:
        target[count:] = jnp.zeros_like(target[count:])


def by_pair(axis, low, high, first, second):
    @pl.when(on_even(axis))
    def _():
        copied(high, first)
        copied(low, second)

    @pl.when(jnp.logical_not(on_even(axis)))
    def _():
        copied(low, first)
        copied(high, second)


def by_side(axis, first, second, low, high):
    by_pair(axis, second, first, high, low)


COUPLINGS, DIAGONALS, WELL_FIELDS, IDS, RIGHT_SIDE, START = range(6)


def layer_blocks(cut, inward, lateral):
    def plane(n):
        if n < DIAGONAL:
            return cut(COUPLINGS, ((lateral, lateral + 1, 4, 5)[n // 4], n % 4), 0)
        if n < BACK_IN:
            return cut(DIAGONALS, (n - DIAGONAL,), 0)
        return cut(COUPLINGS, (inward, n - BACK_IN), 1)

    return plane


def fill_pack(pack, inward, lateral, cut):
    blocks = layer_blocks(cut, inward, lateral)
    for e in range(4):
        pack[e] = cut(COUPLINGS, (inward, e), 0)
    wells = [cut(WELL_FIELDS, (2 + a,), 0) for a in range(2)]
    for a in range(2):
        pack[WELL_EQ + a] = wells[a]
    pack[WELL_ID] = cut(IDS, (), 0).astype(jnp.float32)
    pack[BACK_ID] = cut(IDS, (), 1).astype(jnp.float32)
    for start, at in (
        (LAT_UP, UP_WELL),
        (LAT_DOWN, DOWN_WELL),
        (RISE, RISE_WELL),
        (FALL, FALL_WELL),
        (DIAGONAL, DIAGONAL_WELL),
        (BACK_IN, BACK_WELL),
    ):
        if start == BACK_IN:
            wells = [cut(WELL_FIELDS, (2 + a,), 1) for a in range(2)]
        for b, value in enumerate(product(lambda e: blocks(start + e), *wells)):
            pack[at + b] = value
    for k in range(RHS):
        here = [cut(START, (k, a), 0) for a in range(2)]
        back = [cut(START, (k, a), 1) for a in range(2)]
        entering = product(lambda e: blocks(BACK_IN + e), *back)
        local = face_stencil(blocks, here[0], here[1], entering)
        for a in range(2):
            pack[GUESS + 2 * k + a] = here[a]
            pack[REST + 2 * k + a] = cut(RIGHT_SIDE, (k, a), 0) - local[a]
    if pack.shape[0] > ENDS:
        end = pack.shape[1] - 1
        for e in range(4):
            pack[ENDS, e : e + 1, :] = blocks(LAT_UP + e)[end : end + 1, :]
            pack[ENDS, 4 + e : 5 + e, :] = blocks(LAT_DOWN + e)[0:1, :]


def x_pack_kernel(*refs):
    sources, first, second, held_ends, arrived = refs[:6], refs[6], refs[7], refs[8:20], refs[20]
    packs = refs[21:23]
    copies = []
    for n, source in enumerate(sources):
        lead = (slice(None),) * (len(source.shape) - 3)
        depth = source.shape[-3]
        for end, start in enumerate((0, depth - 2)):
            copies.append(
                pltpu.make_async_copy(
                    source.at[lead + (pl.ds(start, 2),)],
                    held_ends[2 * n + end],
                    arrived.at[2 * n + end],
                )
            )
    for copy in copies:
        copy.start()
    for copy in copies:
        copy.wait()
    for end, pack in enumerate(packs):
        fill_pack(
            pack,
            1 - end,
            2,
            lambda n, index, layer: held_ends[2 * n + end][
                index + (1 - layer if end else layer,)
            ],
        )
    by_pair("gx", *packs, first, second)


def y_cut(arguments, end):
    last = arguments[0].shape[-2] - 1

    def cut(n, index, layer):
        return arguments[n][index + (slice(None), last - layer if end else layer, slice(None))]

    return cut


def send_out(table, chunks, part, sent):
    rows = min(chunks.shape[1], table.shape[0])
    chunks[:, :rows, :] = jnp.broadcast_to(table[None, :rows], (chunks.shape[0], rows, LANES))
    copy = pltpu.make_async_copy(chunks, part, sent.at[0])
    copy.start()
    return copy


def corner_kernel(y_low, y_high, came_first, came_second, first, second, fxl, fxh, *outs):
    by_side("gx", came_first, came_second, fxl, fxh)
    last = fxl.shape[1] - 1
    for own, out, at, side in ((y_low, outs[0], 0, 4), (y_high, outs[1], last, 0)):
        for n in range(FACE_PLANES):
            out[n] = own[n]
        row = FACE_PLANES * 8
        out[FACE_PLANES + CORNER_PLANES - 1] = jnp.zeros(out.shape[1:], jnp.float32)
        for face in (fxl, fxh):
            rows = [(n, at) for n in range(4)]
            rows += [(ENDS, side + e) for e in range(4)]
            rows += [(n, at) for n in range(WELL_EQ, REST)]
            for n, y in rows:
                out[row // 8, row % 8 : row % 8 + 1, :] = face[n, y : y + 1, :]
                row += 1
    by_pair("gy", *outs, first, second)


def diagonal_device(x_end, y_end):
    across, along = lax.axis_index("gx"), lax.axis_index("gy")
    there_x, there_y = across + 2 * x_end - 1, along + 2 * y_end - 1
    count_x, count_y = lax.axis_size("gx"), lax.axis_size("gy")
    exists = (there_x >= 0) & (there_x < count_x) & (there_y >= 0) & (there_y < count_y)
    return exists, jnp.where(exists, there_x * count_y + there_y, 0)


def guess_kernel(
    couplings, diagonal, wells, ids, right, guess,
    part, present, y_low, y_high, values, scratch, chunks, sent,
):
    list_wells(ids, present)
    for k in range(RHS):
        values[k] = wells[0] * guess[k, 0] + wells[1] * guess[k, 1]
    values[4] = wells[0] * wells[2] + wells[1] * wells[3]
    values[5] = wells[2] * wells[2] + wells[3] * wells[3]
    rows = segment_rows(ids, values, scratch, present)
    table = pack_rows(rows, jnp.zeros((8, LANES), jnp.float32))
    copy = send_out(table, chunks, part, sent)
    arguments = (couplings, diagonal, wells, ids, right, guess)
    for end, pack in enumerate((y_low, y_high)):
        fill_pack(pack, 3 - end, 0, y_cut(arguments, end))
    copy.wait()


def block_kernel(
    couplings, diagonal, right, guess, sent_face, rest, leaving
):
    nothing_enters = [[jnp.zeros(guess.shape[3:], jnp.float32)] * 2] * 4
    for k in range(RHS):
        inside, outgoing = block_stencil(
            couplings, diagonal, guess[k, 0], guess[k, 1], nothing_enters
        )
        for a in range(2):
            rest[k, a] = right[k, a] - inside[a]
            for f in range(4):
                leaving[f, 2 * k + a] = outgoing[f][a]


def residual_kernel(
    couplings, diagonal, wells, ids, fxl, fxh, came_first, came_second, parts,
    rest, leaving,
    residual, image, residual_faces, x_first, x_second, y_first, y_second, small, fyl, fyh,
    x_low, x_high, y_low, y_high,
):
    by_side("gy", came_first, came_second, fyl, fyh)
    faces = (fxl, fxh, fyl, fyh)
    totals = jnp.sum(parts[...], axis=0)
    corners = corners_of(faces, FACE_PLANES, CORNER_ROWS)
    all_ids = ids[...]
    face_ids = [as_ids(face[WELL_ID]) for face in faces]
    last = rest.shape[2] - 1
    row = iota(rest.shape[2:], 1)
    for k in range(RHS):
        s_row = unpack_row(totals, k)
        entering = [
            product(
                lambda e, f=f: faces[f][e],
                faces[f][GUESS + 2 * k],
                faces[f][GUESS + 2 * k + 1],
            )
            for f in range(4)
        ]
        outgoing = [[leaving[f, 2 * k + b] for b in range(2)] for f in range(4)]
        at_wells = spread(s_row, all_ids)
        now = []
        for a in range(2):
            value = rest[k, a] - wells[2 + a] * at_wells
            over_x = [
                (value[0] - entering[0][a])[None],
                value[1:last],
                (value[last] - entering[1][a])[None],
            ]
            value = jnp.concatenate(over_x, axis=0)
            value = value - jnp.where(row == 0, entering[2][a][:, None, :], 0.0)
            now.append(value - jnp.where(row == last, entering[3][a][:, None, :], 0.0))
        for a in range(2):
            residual[k, a] = now[a]
        ends = corner_inputs(
            corners,
            [[corners[c].row(SIDE_GUESS + 2 * k + a) for a in range(2)] for c in range(4)],
        )
        incoming = []
        for f in range(4):
            face = faces[f]
            there = face_entries(ends[(f, 0)], ends[(f, 1)], outgoing[f])
            face_wells = spread(s_row, face_ids[f])
            outer = [
                face[REST + 2 * k + a] - there[a] - face[WELL_EQ + a] * face_wells
                for a in range(2)
            ]
            for a in range(2):
                residual_faces[f, 2 * k + a] = outer[a]
            incoming.append(product(lambda e, f=f: faces[f][e], *outer))
        result, _ = block_stencil(couplings, diagonal, now[0], now[1], incoming)
        for a in range(2):
            image[k, a] = result[a]
    own = (couplings, diagonal)
    for axis, packs in enumerate(((x_low, x_high), (y_low, y_high))):
        for end, pack in enumerate(packs):

            def cut(ref, index, layer):
                at = last - layer if end else layer
                return ref[index + ((at,) if axis == 0 else (slice(None), at, slice(None)))]

            plane = layer_blocks(
                lambda n, index, layer: cut(own[n], index, layer),
                2 * axis + 1 - end,
                2 * (1 - axis),
            )
            blocks = [plane(n) for n in range(LAYER_BLOCKS)]
            for k in range(RHS):
                here = [cut(image, (k, a), 0) for a in range(2)]
                back = [cut(image, (k, a), 1) for a in range(2)]
                entering = product(lambda e: blocks[BACK_IN + e], *back)
                local = face_stencil(lambda n: blocks[n], here[0], here[1], entering)
                for a in range(2):
                    pack[2 * k + a] = here[a]
                    pack[8 + 2 * k + a] = local[a]
    by_pair("gx", x_low, x_high, x_first, x_second)
    by_pair("gy", y_low, y_high, y_first, y_second)
    small[...] = jnp.concatenate(
        [unpack_row(totals, 4), unpack_row(totals, 5), jnp.zeros((6, LANES), jnp.float32)], axis=0
    )


def moments_kernel(
    wells, ids, residual, image, present, part, values, scratch, dots, chunks, sent
):
    dots[...] = jnp.zeros_like(dots)
    for k in range(RHS):
        now = [residual[k, a] for a in range(2)]
        result = [image[k, a] for a in range(2)]
        for n, field in enumerate((now, result)):
            values[4 * n + k] = wells[0] * field[0] + wells[1] * field[1]
            values[8 + 4 * n + k] = wells[2] * field[0] + wells[3] * field[1]
        row = slice(RHS + k, RHS + k + 1)
        dots[0, row, :] = tile_sum(now, now)
        dots[1, row, :] = tile_sum(now, result)
        dots[2, row, :] = tile_sum(result, result)
    rows = segment_rows(ids, values, scratch, present)
    table = place_rows(rows, jnp.zeros((8, LANES), jnp.float32))
    chunks[:, 8:, :] = jnp.zeros_like(chunks[:, 8:, :])
    last = image.shape[2] - 1
    for x_end in range(2):
        for y_end in range(2):
            exists, place = diagonal_device(x_end, y_end)

            @pl.when(exists)
            def _():
                for k in range(RHS):
                    for a in range(2):
                        row, y = 8 + 2 * k + a, last * y_end
                        chunks[pl.ds(place, 1), row : row + 1, :] = image[
                            k, a, last * x_end, y : y + 1, :
                        ][None]

    send_out(place_columns(dots, WELLS, table), chunks, part, sent).wait()


def first_step(totals, small):
    s_row, us_row, p_row, ps_row = (take_group(totals, group) for group in range(4))
    within, equation = small[0:1, :], small[1:2, :]
    rr, rs, ss = (take_column(totals, WELLS + i) for i in range(3))
    height = (rs + lane_sum(p_row * s_row)) / rr
    square = ss + lane_sum(2.0 * ps_row * s_row + equation * s_row * s_row)
    left = jnp.maximum(square - height * height * rr, 1e-7 * square)
    scale = lax.rsqrt(left)
    s_image = us_row + within * s_row
    s_second = (s_image - height * s_row) * scale
    p_second = (ps_row + equation * s_row - height * p_row) * scale
    shift = rs / rr + lane_sum(p_second * s_second)
    unit = lax.rsqrt(rr)
    following = left * scale * unit
    return s_row, s_image, p_row, p_second, (unit, rr * unit, height, shift, following, scale)


def krylov_kernel(
    couplings, diagonal, wells, ids, fxl, fxh, fyl, fyh, x_first, x_second, y_first, y_second,
    residual, image, residual_faces, parts, small_in, present,
    second_out, third_out, part, known, scratch, values_scratch, dots, gxl, gxh, gyl, gyh,
):
    by_side("gx", x_first, x_second, gxl, gxh)
    by_side("gy", y_first, y_second, gyl, gyh)
    faces, sent = (fxl, fxh, fyl, fyh), (gxl, gxh, gyl, gyh)
    totals = jnp.sum(parts[:, 0:8, :], axis=0)
    small = small_in[...]
    s_rows, s_images, p_rows, p_seconds, scalars = first_step(totals, small)
    known[0:RHS, :] = p_rows
    known[RHS : 2 * RHS, :] = p_seconds
    columns = jnp.zeros((RHS, LANES), jnp.float32)
    for n, column in enumerate(scalars):
        columns = columns + jnp.where(iota(columns.shape, 1) == n, column, 0.0)
    known[2 * RHS : 3 * RHS, :] = columns
    known[3 * RHS :, :] = jnp.broadcast_to(small[1:2, :], (RHS, LANES))
    dots[...] = jnp.zeros_like(dots)
    corners = corners_of(faces, FACE_PLANES, CORNER_ROWS)
    places = [diagonal_device(c % 2, c // 2)[1] for c in range(4)]
    all_ids = ids[...]
    face_ids = [as_ids(face[WELL_ID]) for face in faces]
    back_ids = [as_ids(face[BACK_ID]) for face in faces]
    corner_ids = [
        as_ids(jnp.broadcast_to(corner.row(SIDE_ID), (8, LANES))) for corner in corners
    ]
    for k in range(RHS):
        unit, _, height, shift, _, scale = (column[k : k + 1, :] for column in scalars)
        s_row, s_image = s_rows[k : k + 1, :], s_images[k : k + 1, :]
        at_wells = spread(s_row, all_ids)
        now = [image[k, a] + wells[2 + a] * at_wells for a in range(2)]
        face_now, spread_now = [], []
        for f in range(4):
            here = spread(s_row, face_ids[f])
            spread_now.append((here, spread(s_row, back_ids[f])))
            face_now.append(
                [sent[f][2 * k + a] + faces[f][WELL_EQ + a] * here for a in range(2)]
            )
        corner_now = []
        for c in range(4):
            here = spread(s_row, corner_ids[c])[0:1, :]
            corner_now.append(
                [
                    parts[pl.ds(places[c], 1), 8 + 2 * k + a, :] + corners[c].row(SIDE_EQ + a) * here
                    for a in range(2)
                ]
            )
        incoming = [product(lambda e, f=f: faces[f][e], *face_now[f]) for f in range(4)]
        applied, outgoing = block_stencil(couplings, diagonal, now[0], now[1], incoming)
        at_wells = spread(s_image, all_ids)
        second, third = [], []
        for a in range(2):
            twice = applied[a] + wells[2 + a] * at_wells
            base = (now[a] - height * residual[k, a]) * scale
            second.append(base)
            third.append((twice - height * now[a]) * scale - shift * base)
            second_out[k, a] = second[a]
            third_out[k, a] = third[a]
        ends = corner_inputs(corners, corner_now)
        incoming = []
        for f in range(4):
            face = faces[f]
            here, behind = spread_now[f]
            moves = [
                [face[at + b] * here for b in range(2)]
                for at in (DIAGONAL_WELL, UP_WELL, DOWN_WELL, RISE_WELL, FALL_WELL)
            ]
            there = face_moves(*moves, [face[BACK_WELL + b] * behind for b in range(2)])
            local = [sent[f][8 + 2 * k + b] + there[b] for b in range(2)]
            over = face_entries(ends[(f, 0)], ends[(f, 1)], outgoing[f])
            here = spread(s_image, face_ids[f])
            outer = []
            for a in range(2):
                twice = local[a] + over[a] + face[WELL_EQ + a] * here
                base = (face_now[f][a] - height * residual_faces[f, 2 * k + a]) * scale
                outer.append((twice - height * face_now[f][a]) * scale - shift * base)
            incoming.append(product(lambda e, f=f: faces[f][e], *outer))
        result, _ = block_stencil(couplings, diagonal, third[0], third[1], incoming)
        fourth = [result[a] - shift * third[a] for a in range(2)]
        values_scratch[k] = wells[0] * third[0] + wells[1] * third[1]
        values_scratch[4 + k] = wells[2] * third[0] + wells[3] * third[1]
        values_scratch[8 + k] = wells[2] * fourth[0] + wells[3] * fourth[1]
        fields = [[residual[k, a] * unit for a in range(2)], second, third, fourth]
        number = 0
        for i in range(4):
            for j in range(i, 4):
                dots[number, RHS + k : RHS + k + 1, :] = tile_sum(fields[i], fields[j])
                number += 1
    rows = segment_rows(ids, values_scratch, scratch, present)
    table = place_rows(rows, jnp.zeros((8, LANES), jnp.float32))
    table = place_columns(dots, 0, table)
    gram = table[RHS : RHS + 1, :]
    for k in range(1, RHS):
        gram = gram + pltpu.roll(table[RHS + k : RHS + k + 1, :], GRAM_ENTRIES * k, 1)
    flat = jnp.concatenate([table[k : k + 1, :] for k in range(RHS)] + [gram], axis=1)
    part[...] = jnp.broadcast_to(flat[None], part.shape)


def solve_kernel(
    guess_in, residual, second, third, parts, known, solution, guess, arrived
):
    copy = pltpu.make_async_copy(guess_in, guess, arrived.at[0])
    copy.start()
    flat = jnp.sum(parts[...], axis=0)
    rows = [flat[:, LANES * n : LANES * (n + 1)] for n in range(RHS + 1)]
    for k in range(1, RHS):
        rows.append(pltpu.roll(rows[RHS], LANES - GRAM_ENTRIES * k, 1))
    totals = jnp.concatenate(rows, axis=0)
    s_third, p_third, p_fourth = (take_group(totals, group) for group in range(3))
    p_first, p_second = known[0:RHS, :], known[RHS : 2 * RHS, :]
    unit, beta, height, shift, following = (
        known[2 * RHS : 3 * RHS, n : n + 1] for n in range(5)
    )
    equation = known[3 * RHS :, :]
    gram = {}
    number = 0
    for i in range(4):
        for j in range(i, 4):
            gram[(i, j)] = take_column(totals, number)
            number += 1
    gram[(0, 3)] += lane_sum(p_first * s_third) * unit
    gram[(1, 3)] += lane_sum(p_second * s_third)
    gram[(2, 3)] += lane_sum(p_third * s_third)
    gram[(3, 3)] += lane_sum(2.0 * p_fourth * s_third + equation * s_third * s_third)
    tiny = 1e-30
    inverse = [lax.rsqrt(jnp.maximum(gram[(i, i)], tiny)) for i in range(4)]
    length = [jnp.maximum(gram[(i, i)], tiny) * inverse[i] for i in range(4)]
    upper = {}
    for i in range(4):
        for j in range(i, 4):
            entry = gram[(i, j)] * inverse[i] * inverse[j]
            for m in range(i):
                entry = entry - upper[(m, i)] * upper[(m, j)]
            if i == j:
                pivot = lax.rsqrt(jnp.maximum(entry, 1e-6))
                upper[(i, i)] = jnp.maximum(entry, 1e-6) * pivot
                over = pivot
            else:
                upper[(i, j)] = entry * over
    columns = [
        [(0, height * length[0]), (1, following * length[1])],
        [(1, shift * length[1]), (2, length[2])],
        [(2, shift * length[2]), (3, length[3])],
    ]
    zero = jnp.zeros_like(shift)
    hessenberg = [[zero] * 3 for _ in range(4)]
    for j in range(3):
        for i in range(j + 2):
            for m, factor in columns[j]:
                if m >= i:
                    hessenberg[i][j] = hessenberg[i][j] + upper[(i, m)] * factor
    target = [beta * length[0] * upper[(0, 0)], zero, zero, zero]
    turns = []
    for j in range(3):
        top, bottom = hessenberg[j][j], hessenberg[j + 1][j]
        turn = lax.rsqrt(top * top + bottom * bottom)
        turns.append(turn)
        cosine, sine = top * turn, bottom * turn
        for m in range(j, 3):
            high, low = hessenberg[j][m], hessenberg[j + 1][m]
            hessenberg[j][m] = cosine * high + sine * low
            hessenberg[j + 1][m] = cosine * low - sine * high
        high, low = target[j], target[j + 1]
        target[j] = cosine * high + sine * low
        target[j + 1] = cosine * low - sine * high
    weights = [zero] * 3
    for i in (2, 1, 0):
        value = target[i]
        for j in range(i + 1, 3):
            value = value - hessenberg[i][j] * weights[j]
        weights[i] = value * turns[i]
    copy.wait()
    for k in range(RHS):
        on_first, on_second, on_third = (
            column[k : k + 1, :] for column in (weights[0] * unit, weights[1], weights[2])
        )
        for a in range(2):
            solution[k, a] = (
                guess[k, a]
                + on_first * residual[k, a]
                + on_second * second[k, a]
                + on_third * third[k, a]
            )


def call(kernel, shapes, arguments, scratch=(), far_inputs=0, cost=0, grant=24 << 20, out=0):
    whole = pl.BlockSpec(memory_space=pltpu.VMEM)
    far = pl.BlockSpec(memory_space=pltpu.HBM)
    scalars = pl.BlockSpec(memory_space=pltpu.SMEM)

    def place(number, array):
        if len(array.shape) == 1:
            return scalars
        return far if number < far_inputs else whole

    outs = [
        jax.ShapeDtypeStruct(shape, jnp.float32 if len(shape) > 1 else jnp.int32)
        for shape in shapes
    ]
    outs[:out] = [pltpu.HBM(shape, jnp.float32) for shape in shapes[:out]]
    return pl.pallas_call(
        kernel,
        out_shape=outs,
        in_specs=[place(*numbered) for numbered in enumerate(arguments)],
        out_specs=[far] * out + [scalars if len(shape) == 1 else whole for shape in shapes[out:]],
        scratch_shapes=list(scratch),
        compiler_params=pltpu.CompilerParams(vmem_limit_bytes=grant),
        cost_estimate=pl.CostEstimate(flops=cost, bytes_accessed=cost, transcendentals=0)
        if cost
        else None,
    )(*arguments)


def nothing(value, *rest):
    pass


def after(value, *others):
    far = pl.BlockSpec(memory_space=pltpu.HBM)
    near = pl.BlockSpec(memory_space=pltpu.VMEM)
    return pl.pallas_call(
        nothing,
        out_shape=pltpu.HBM(value.shape, value.dtype),
        in_specs=[far] + [near] * len(others),
        out_specs=far,
        input_output_aliases={0: 0},
        compiler_params=pltpu.CompilerParams(vmem_limit_bytes=1 << 20),
    )(pltpu.with_memory_space_constraint(value, pltpu.HBM), *others)


def held(*shape):
    return pltpu.VMEM(shape, jnp.float32)


def swap(value, axis, start):
    pairs = []
    for low in range(start, lax.axis_size(axis) - 1, 2):
        pairs += [(low, low + 1), (low + 1, low)]
    return lax.ppermute(value, axis, pairs) if pairs else jnp.zeros_like(value)


def swapped(first, second, axis):
    return swap(first, axis, 0), swap(second, axis, 1)


def exchanged(part):
    return lax.all_to_all(part, ("gx", "gy"), 0, 0, tiled=True)


def body(couplings, diagonal, wells, ids, right, guess):
    devices = lax.axis_size("gx") * lax.axis_size("gy")
    plane = (8, LANES)
    field = guess.shape
    block = guess.shape[2:]
    arguments = (couplings, diagonal, wells, ids, right, guess)

    ends = []
    for argument in arguments:
        shape = argument.shape[:-3] + (2,) + argument.shape[-2:]
        ends += [pltpu.VMEM(shape, argument.dtype)] * 2
    x_first, x_second = call(
        x_pack_kernel,
        [(FACE_PLANES + 1,) + plane] * 2,
        [pltpu.with_memory_space_constraint(argument, pltpu.HBM) for argument in arguments],
        ends
        + [pltpu.SemaphoreType.DMA((len(ends),))]
        + [held(FACE_PLANES + 1, *plane)] * 2,
        far_inputs=len(arguments),
    )
    came_x = swapped(x_first, x_second, "gx")
    first_chunks, chunks = (devices, TABLE_ROWS, LANES), (devices, 16, LANES)
    sent = pltpu.SemaphoreType.DMA((1,))
    part, present, y_low, y_high = call(
        guess_kernel,
        [first_chunks, (WELLS + 8,)] + [(FACE_PLANES,) + plane] * 2,
        arguments,
        [held(6, *block), held(6, WELLS, LANES), held(*first_chunks), sent],
        cost=4 << 20,
        out=1,
    )
    parts = exchanged(after(part, came_x[1]))
    y_shape = (FACE_PLANES + CORNER_PLANES,) + plane
    y_first, y_second, fxl, fxh = call(
        corner_kernel,
        [y_shape] * 2 + [(FACE_PLANES + 1,) + plane] * 2,
        (y_low, y_high, *came_x),
        [held(*y_shape)] * 2,
    )
    came_y = swapped(y_first, y_second, "gy")
    ahead = call(
        block_kernel,
        [field, (4, 8) + plane],
        (couplings, diagonal, right, guess, y_first),
        cost=4 << 20,
    )

    residual, image, residual_faces, *packs, small, fyl, fyh = call(
        residual_kernel,
        [field, field, (4, 8) + plane]
        + [(IMAGE_PLANES + spare,) + plane for spare in (1, 2, 0, 3)]
        + [(8, LANES)]
        + [y_shape] * 2,
        (couplings, diagonal, wells, ids, fxl, fxh, *came_y, parts, *ahead),
        [held(IMAGE_PLANES, *plane)] * 4,
    )
    faces = (fxl, fxh, fyl, fyh)
    came_y1 = swap(packs[3], "gy", 1)
    came_x1 = swap(packs[1], "gx", 1)
    came_x0 = swap(packs[0], "gx", 0)
    came_y0 = swap(packs[2], "gy", 0)
    (part,) = call(
        moments_kernel,
        [chunks],
        (wells, ids, residual, image, present),
        [held(16, *block), held(16, WELLS, LANES), held(3, *plane), held(*chunks), sent],
        cost=4 << 20,
        out=1,
    )
    parts = exchanged(part)
    second, third, part, known = call(
        krylov_kernel,
        [field, field, (devices, 1, (RHS + 1) * LANES), (4 * RHS, LANES)],
        (couplings, diagonal, wells, ids) + faces + (came_x0, came_x1, came_y0, came_y1)
        + (residual, image, residual_faces, parts, small, present),
        [held(12, WELLS, LANES), held(12, *block), held(10, *plane)]
        + [held(IMAGE_PLANES, *plane)] * 4,
    )
    parts = exchanged(part)
    (result,) = call(
        solve_kernel,
        [field],
        (
            pltpu.with_memory_space_constraint(guess, pltpu.HBM),
            residual, second, third, parts, known,
        ),
        [held(*field), pltpu.SemaphoreType.DMA((1,))],
        far_inputs=1,
    )
    return result


def solution(mesh):
    in_specs = (
        P("member", None, "gx", "gy", None),
        P("member", "gx", "gy", None),
        P("member", "gx", "gy", None),
        P("gx", "gy", None),
        P("member", None, "gx", "gy", None),
        P("member", None, "gx", "gy", None),
    )
    out_specs = P("member", None, "gx", "gy", None)
    return jax.shard_map(body, mesh=mesh, in_specs=in_specs, out_specs=out_specs, check_vma=False)
```

```python
import jax
import jax.numpy as jnp
from jax import lax
from jax.experimental import pallas as pl
from jax.experimental.pallas import tpu as pltpu
from jax.sharding import PartitionSpec as P

WELLS = 40
RHS = 4
LANES = 128
WELL_EQ, WELL_ID, GUESS, REST = 4, 6, 7, 15
UP_WELL, DOWN_WELL, RISE_WELL, FALL_WELL, DIAGONAL_WELL = 23, 25, 27, 29, 31
BACK_WELL, BACK_ID = 33, 35
FACE_PLANES = 36
ENDS = 36
CORNER_PLANES = 5
LAT_UP, LAT_DOWN, RISE, FALL, DIAGONAL, BACK_IN = 0, 4, 8, 12, 16, 20
LAYER_BLOCKS = 24
IMAGE_PLANES = 16
TABLE_ROWS = 6
GRAM_ENTRIES = 10
CORNER_ROWS = 19
SIDE_IN, SIDE_EQ, SIDE_ID, SIDE_GUESS = 4, 8, 10, 11


def product(blocks, first, second):
    return [
        blocks(0) * first + blocks(2) * second,
        blocks(1) * first + blocks(3) * second,
    ]


def iota(shape, axis):
    return lax.broadcasted_iota(jnp.int32, shape, axis)


def roll_up(value, axis):
    return pltpu.roll(value, 1, axis)


def roll_down(value, axis):
    return pltpu.roll(value, value.shape[axis] - 1, axis)


def layer_moves(rising, falling):
    axis = rising.ndim - 1
    lane = iota(rising.shape, axis)
    up = jnp.where(lane == 0, 0.0, roll_up(rising, axis))
    down = jnp.where(lane == LANES - 1, 0.0, roll_down(falling, axis))
    return up + down


def block_stencil(couplings, diagonal, first, second, incoming):
    result = product(lambda e: diagonal[e], first, second)
    moved = [product(lambda e, d=d: couplings[d, e], first, second) for d in range(6)]
    row = iota(first.shape, 1)
    outgoing = [[], [], [], []]
    for b in range(2):
        east, west, north, south, rise, fall = (moved[d][b] for d in range(6))
        total = result[b] + jnp.concatenate([incoming[0][b][None], east[:-1]], axis=0)
        total = total + jnp.concatenate([west[1:], incoming[1][b][None]], axis=0)
        total = total + jnp.where(row == 0, incoming[2][b][:, None, :], roll_up(north, 1))
        total = total + jnp.where(
            row == row.shape[1] - 1, incoming[3][b][:, None, :], roll_down(south, 1)
        )
        result[b] = total + layer_moves(rise, fall)
        outgoing[0].append(west[0])
        outgoing[1].append(east[-1])
        outgoing[2].append(south[:, 0, :])
        outgoing[3].append(north[:, -1, :])
    return result, outgoing


def face_stencil(blocks, first, second, behind):
    def times(start):
        return product(lambda e: blocks(start + e), first, second)

    moves = [times(start) for start in (DIAGONAL, LAT_UP, LAT_DOWN, RISE, FALL)]
    return face_moves(*moves, behind)


def face_moves(kept, up, down, rise, fall, behind):
    result = list(kept)
    row = iota(kept[0].shape, 0)
    for b in range(2):
        total = result[b] + behind[b] + layer_moves(rise[b], fall[b])
        total = total + jnp.where(row == 0, 0.0, roll_up(up[b], 0))
        result[b] = total + jnp.where(row == row.shape[0] - 1, 0.0, roll_down(down[b], 0))
    return result


def face_entries(low_end, high_end, entering):
    row = iota(entering[0].shape, 0)
    return [
        entering[b]
        + jnp.where(row == 0, low_end[b], 0.0)
        + jnp.where(row == row.shape[0] - 1, high_end[b], 0.0)
        for b in range(2)
    ]


def spread(totals, ids):
    table = jnp.broadcast_to(totals, (8, LANES))
    if ids.ndim == 2:
        return jnp.take_along_axis(table, ids, axis=1)
    return jnp.stack(
        [jnp.take_along_axis(table, ids[x], axis=1) for x in range(ids.shape[0])], axis=0
    )


def as_ids(plane):
    return plane.astype(jnp.int32)


class Corner:
    def __init__(self, pack, which, base):
        self.pack, self.start = pack, base * 8 + which

    def row(self, number):
        at = self.start + number
        return self.pack[at // 8, at % 8 : at % 8 + 1, :]


def corners_of(faces, base, rows):
    found = []
    for y_face in (2, 3):
        for x_end in range(2):
            found.append(Corner(faces[y_face], x_end * rows, base))
    return found


def corner_inputs(corners, values):
    ends = {}
    for c in range(4):
        x_end, y_end = c % 2, c // 2
        over_x = product(corners[c].row, *values[c])
        over_y = product(lambda e, c=c: corners[c].row(SIDE_IN + e), *values[c])
        ends[(2 + y_end, x_end)] = over_x
        ends[(x_end, y_end)] = over_y
    return ends


def tile_sum(first, second):
    value = first[0] * second[0] + first[1] * second[1]
    return jnp.sum(jnp.sum(value, axis=0), axis=0, keepdims=True)


def list_wells(ids, present):
    planes = [ids[x].astype(jnp.float32) for x in range(ids.shape[0])]
    middle = WELLS // 2
    halves = ((0.0, float(middle)), (float(middle), float(WELLS)))

    def least(above, top):
        found = [jnp.where((p > above) & (p < top), p, top) for p in planes]
        value = found[0]
        for other in found[1:]:
            value = jnp.minimum(value, other)
        return jnp.min(value)

    def greatest(base, below):
        found = [jnp.where((p >= base) & (p < below), p, base - 1.0) for p in planes]
        value = found[0]
        for other in found[1:]:
            value = jnp.maximum(value, other)
        return jnp.max(value)

    def some_left(state):
        return (state[1] <= state[2]) | (state[3] <= state[4])

    def step(state):
        number, ends = state[0], state[1:]
        after = []
        for half, (base, top) in enumerate(halves):
            low, high = ends[2 * half], ends[2 * half + 1]
            present[number] = low.astype(jnp.int32)
            number = number + jnp.where(low <= high, 1, 0)
            present[number] = high.astype(jnp.int32)
            number = number + jnp.where(low < high, 1, 0)
            after += [least(low, top), greatest(base, high)]
        return (number, *after)

    ends = []
    for base, top in halves:
        ends += [least(base - 1.0, top), greatest(base, top)]
    state = lax.while_loop(some_left, step, (jnp.int32(1), *ends))
    present[0] = state[0] - 1


def segment_rows(ids, values, scratch, present):
    scratch[...] = jnp.zeros_like(scratch)
    count, depth = values.shape[0], ids.shape[0]

    def one_well(step, _):
        well = present[step + 1]
        masks = [ids[x] == well for x in range(depth)]
        for number in range(count):
            total = jnp.where(masks[0], values[number, 0], 0.0)
            for x in range(1, depth):
                total = total + jnp.where(masks[x], values[number, x], 0.0)
            scratch[number, pl.ds(well, 1), :] = jnp.sum(total, axis=0, keepdims=True)
        return 0

    lax.fori_loop(0, present[0], one_well, 0)
    rows = []
    for number in range(count):
        summed = jnp.sum(scratch[number], axis=1, keepdims=True)
        shape = scratch.shape[1:]
        on_lanes = jnp.where(iota(shape, 0) == iota(shape, 1), summed, 0.0)
        rows.append(jnp.sum(on_lanes, axis=0, keepdims=True))
    return rows


def pack_rows(rows, table):
    for number, row in enumerate(rows):
        placed = row if number % 3 == 0 else pltpu.roll(row, WELLS * (number % 3), 1)
        table = table + jnp.where(
            iota(table.shape, 0) == number // 3, jnp.broadcast_to(placed, table.shape), 0.0
        )
    return table


def unpack_row(table, number):
    row = table[number // 3 : number // 3 + 1, :]
    if number % 3:
        row = pltpu.roll(row, LANES - WELLS * (number % 3), 1)
    return jnp.where(iota(row.shape, 1) < WELLS, row, 0.0)


def place_rows(rows, table):
    for number, row in enumerate(rows):
        group, k = divmod(number, RHS)
        at = k + RHS * (group // 3)
        placed = pltpu.roll(row, WELLS * group, 1) if group in (1, 2) else row
        table = table + jnp.where(
            iota(table.shape, 0) == at, jnp.broadcast_to(placed, table.shape), 0.0
        )
    return table


def place_columns(dots, first_lane, table):
    for number in range(dots.shape[0]):
        column = jnp.sum(dots[number], axis=1, keepdims=True)
        table = table + jnp.where(iota(table.shape, 1) == first_lane + number, column, 0.0)
    return table


def take_group(table, group):
    if group in (1, 2):
        table = pltpu.roll(table, LANES - WELLS * group, 1)
    start = RHS * (group // 3)
    rows = table[start : start + RHS, :]
    return jnp.where(iota(rows.shape, 1) < WELLS, rows, 0.0)


def take_column(table, lane):
    return table[RHS : 2 * RHS, lane : lane + 1]


def lane_sum(row):
    return jnp.sum(row, axis=1, keepdims=True)


def on_even(axis):
    return lax.rem(lax.axis_index(axis), 2) == 0


def copied(source, target):
    count = min(source.shape[0], target.shape[0])
    target[0:count] = source[0:count]
    if target.shape[0] > count:
        target[count:] = jnp.zeros_like(target[count:])


def by_pair(axis, low, high, first, second):
    @pl.when(on_even(axis))
    def _():
        copied(high, first)
        copied(low, second)

    @pl.when(jnp.logical_not(on_even(axis)))
    def _():
        copied(low, first)
        copied(high, second)


def by_side(axis, first, second, low, high):
    by_pair(axis, second, first, high, low)


COUPLINGS, DIAGONALS, WELL_FIELDS, IDS, RIGHT_SIDE, START = range(6)


def layer_blocks(cut, inward, lateral):
    def plane(n):
        if n < DIAGONAL:
            return cut(COUPLINGS, ((lateral, lateral + 1, 4, 5)[n // 4], n % 4), 0)
        if n < BACK_IN:
            return cut(DIAGONALS, (n - DIAGONAL,), 0)
        return cut(COUPLINGS, (inward, n - BACK_IN), 1)

    return plane


def fill_pack(pack, inward, lateral, cut):
    blocks = layer_blocks(cut, inward, lateral)
    for e in range(4):
        pack[e] = cut(COUPLINGS, (inward, e), 0)
    wells = [cut(WELL_FIELDS, (2 + a,), 0) for a in range(2)]
    for a in range(2):
        pack[WELL_EQ + a] = wells[a]
    pack[WELL_ID] = cut(IDS, (), 0).astype(jnp.float32)
    pack[BACK_ID] = cut(IDS, (), 1).astype(jnp.float32)
    for start, at in (
        (LAT_UP, UP_WELL),
        (LAT_DOWN, DOWN_WELL),
        (RISE, RISE_WELL),
        (FALL, FALL_WELL),
        (DIAGONAL, DIAGONAL_WELL),
        (BACK_IN, BACK_WELL),
    ):
        if start == BACK_IN:
            wells = [cut(WELL_FIELDS, (2 + a,), 1) for a in range(2)]
        for b, value in enumerate(product(lambda e: blocks(start + e), *wells)):
            pack[at + b] = value
    for k in range(RHS):
        here = [cut(START, (k, a), 0) for a in range(2)]
        back = [cut(START, (k, a), 1) for a in range(2)]
        entering = product(lambda e: blocks(BACK_IN + e), *back)
        local = face_stencil(blocks, here[0], here[1], entering)
        for a in range(2):
            pack[GUESS + 2 * k + a] = here[a]
            pack[REST + 2 * k + a] = cut(RIGHT_SIDE, (k, a), 0) - local[a]
    if pack.shape[0] > ENDS:
        end = pack.shape[1] - 1
        for e in range(4):
            pack[ENDS, e : e + 1, :] = blocks(LAT_UP + e)[end : end + 1, :]
            pack[ENDS, 4 + e : 5 + e, :] = blocks(LAT_DOWN + e)[0:1, :]


def x_pack_kernel(*refs):
    sources, first, second, held_ends, arrived = refs[:6], refs[6], refs[7], refs[8:20], refs[20]
    packs = refs[21:23]
    copies = []
    for n, source in enumerate(sources):
        lead = (slice(None),) * (len(source.shape) - 3)
        depth = source.shape[-3]
        for end, start in enumerate((0, depth - 2)):
            copies.append(
                pltpu.make_async_copy(
                    source.at[lead + (pl.ds(start, 2),)],
                    held_ends[2 * n + end],
                    arrived.at[2 * n + end],
                )
            )
    for copy in copies:
        copy.start()
    for copy in copies:
        copy.wait()
    for end, pack in enumerate(packs):
        fill_pack(
            pack,
            1 - end,
            2,
            lambda n, index, layer: held_ends[2 * n + end][
                index + (1 - layer if end else layer,)
            ],
        )
    by_pair("gx", *packs, first, second)


def y_cut(arguments, end):
    last = arguments[0].shape[-2] - 1

    def cut(n, index, layer):
        return arguments[n][index + (slice(None), last - layer if end else layer, slice(None))]

    return cut


def send_out(table, chunks, part, sent):
    rows = min(chunks.shape[1], table.shape[0])
    chunks[:, :rows, :] = jnp.broadcast_to(table[None, :rows], (chunks.shape[0], rows, LANES))
    copy = pltpu.make_async_copy(chunks, part, sent.at[0])
    copy.start()
    return copy


def corner_kernel(y_low, y_high, came_first, came_second, first, second, fxl, fxh, *outs):
    by_side("gx", came_first, came_second, fxl, fxh)
    last = fxl.shape[1] - 1
    for own, out, at, side in ((y_low, outs[0], 0, 4), (y_high, outs[1], last, 0)):
        for n in range(FACE_PLANES):
            out[n] = own[n]
        row = FACE_PLANES * 8
        out[FACE_PLANES + CORNER_PLANES - 1] = jnp.zeros(out.shape[1:], jnp.float32)
        for face in (fxl, fxh):
            rows = [(n, at) for n in range(4)]
            rows += [(ENDS, side + e) for e in range(4)]
            rows += [(n, at) for n in range(WELL_EQ, REST)]
            for n, y in rows:
                out[row // 8, row % 8 : row % 8 + 1, :] = face[n, y : y + 1, :]
                row += 1
    by_pair("gy", *outs, first, second)


def diagonal_device(x_end, y_end):
    across, along = lax.axis_index("gx"), lax.axis_index("gy")
    there_x, there_y = across + 2 * x_end - 1, along + 2 * y_end - 1
    count_x, count_y = lax.axis_size("gx"), lax.axis_size("gy")
    exists = (there_x >= 0) & (there_x < count_x) & (there_y >= 0) & (there_y < count_y)
    return exists, jnp.where(exists, there_x * count_y + there_y, 0)


def guess_kernel(
    couplings, diagonal, wells, ids, right, guess,
    part, present, y_low, y_high, values, scratch, chunks, sent,
):
    list_wells(ids, present)
    for k in range(RHS):
        values[k] = wells[0] * guess[k, 0] + wells[1] * guess[k, 1]
    values[4] = wells[0] * wells[2] + wells[1] * wells[3]
    values[5] = wells[2] * wells[2] + wells[3] * wells[3]
    rows = segment_rows(ids, values, scratch, present)
    table = pack_rows(rows, jnp.zeros((8, LANES), jnp.float32))
    copy = send_out(table, chunks, part, sent)
    arguments = (couplings, diagonal, wells, ids, right, guess)
    for end, pack in enumerate((y_low, y_high)):
        fill_pack(pack, 3 - end, 0, y_cut(arguments, end))
    copy.wait()


def block_kernel(
    couplings, diagonal, right, guess, sent_face, rest, leaving
):
    nothing_enters = [[jnp.zeros(guess.shape[3:], jnp.float32)] * 2] * 4
    for k in range(RHS):
        inside, outgoing = block_stencil(
            couplings, diagonal, guess[k, 0], guess[k, 1], nothing_enters
        )
        for a in range(2):
            rest[k, a] = right[k, a] - inside[a]
            for f in range(4):
                leaving[f, 2 * k + a] = outgoing[f][a]


def residual_kernel(
    couplings, diagonal, wells, ids, fxl, fxh, came_first, came_second, parts,
    rest, leaving,
    residual, image, residual_faces, x_first, x_second, y_first, y_second, small, fyl, fyh,
    x_low, x_high, y_low, y_high,
):
    by_side("gy", came_first, came_second, fyl, fyh)
    faces = (fxl, fxh, fyl, fyh)
    totals = jnp.sum(parts[...], axis=0)
    corners = corners_of(faces, FACE_PLANES, CORNER_ROWS)
    all_ids = ids[...]
    face_ids = [as_ids(face[WELL_ID]) for face in faces]
    last = rest.shape[2] - 1
    row = iota(rest.shape[2:], 1)
    for k in range(RHS):
        s_row = unpack_row(totals, k)
        entering = [
            product(
                lambda e, f=f: faces[f][e],
                faces[f][GUESS + 2 * k],
                faces[f][GUESS + 2 * k + 1],
            )
            for f in range(4)
        ]
        outgoing = [[leaving[f, 2 * k + b] for b in range(2)] for f in range(4)]
        at_wells = spread(s_row, all_ids)
        now = []
        for a in range(2):
            value = rest[k, a] - wells[2 + a] * at_wells
            over_x = [
                (value[0] - entering[0][a])[None],
                value[1:last],
                (value[last] - entering[1][a])[None],
            ]
            value = jnp.concatenate(over_x, axis=0)
            value = value - jnp.where(row == 0, entering[2][a][:, None, :], 0.0)
            now.append(value - jnp.where(row == last, entering[3][a][:, None, :], 0.0))
        for a in range(2):
            residual[k, a] = now[a]
        ends = corner_inputs(
            corners,
            [[corners[c].row(SIDE_GUESS + 2 * k + a) for a in range(2)] for c in range(4)],
        )
        incoming = []
        for f in range(4):
            face = faces[f]
            there = face_entries(ends[(f, 0)], ends[(f, 1)], outgoing[f])
            face_wells = spread(s_row, face_ids[f])
            outer = [
                face[REST + 2 * k + a] - there[a] - face[WELL_EQ + a] * face_wells
                for a in range(2)
            ]
            for a in range(2):
                residual_faces[f, 2 * k + a] = outer[a]
            incoming.append(product(lambda e, f=f: faces[f][e], *outer))
        result, _ = block_stencil(couplings, diagonal, now[0], now[1], incoming)
        for a in range(2):
            image[k, a] = result[a]
    own = (couplings, diagonal)
    for axis, packs in enumerate(((x_low, x_high), (y_low, y_high))):
        for end, pack in enumerate(packs):

            def cut(ref, index, layer):
                at = last - layer if end else layer
                return ref[index + ((at,) if axis == 0 else (slice(None), at, slice(None)))]

            plane = layer_blocks(
                lambda n, index, layer: cut(own[n], index, layer),
                2 * axis + 1 - end,
                2 * (1 - axis),
            )
            blocks = [plane(n) for n in range(LAYER_BLOCKS)]
            for k in range(RHS):
                here = [cut(image, (k, a), 0) for a in range(2)]
                back = [cut(image, (k, a), 1) for a in range(2)]
                entering = product(lambda e: blocks[BACK_IN + e], *back)
                local = face_stencil(lambda n: blocks[n], here[0], here[1], entering)
                for a in range(2):
                    pack[2 * k + a] = here[a]
                    pack[8 + 2 * k + a] = local[a]
    by_pair("gx", x_low, x_high, x_first, x_second)
    by_pair("gy", y_low, y_high, y_first, y_second)
    small[...] = jnp.concatenate(
        [unpack_row(totals, 4), unpack_row(totals, 5), jnp.zeros((6, LANES), jnp.float32)], axis=0
    )


def moments_kernel(
    wells, ids, residual, image, present, part, values, scratch, dots, chunks, sent
):
    dots[...] = jnp.zeros_like(dots)
    for k in range(RHS):
        now = [residual[k, a] for a in range(2)]
        result = [image[k, a] for a in range(2)]
        for n, field in enumerate((now, result)):
            values[4 * n + k] = wells[0] * field[0] + wells[1] * field[1]
            values[8 + 4 * n + k] = wells[2] * field[0] + wells[3] * field[1]
        row = slice(RHS + k, RHS + k + 1)
        dots[0, row, :] = tile_sum(now, now)
        dots[1, row, :] = tile_sum(now, result)
        dots[2, row, :] = tile_sum(result, result)
    rows = segment_rows(ids, values, scratch, present)
    table = place_rows(rows, jnp.zeros((8, LANES), jnp.float32))
    chunks[:, 8:, :] = jnp.zeros_like(chunks[:, 8:, :])
    last = image.shape[2] - 1
    for x_end in range(2):
        for y_end in range(2):
            exists, place = diagonal_device(x_end, y_end)

            @pl.when(exists)
            def _():
                for k in range(RHS):
                    for a in range(2):
                        row, y = 8 + 2 * k + a, last * y_end
                        chunks[pl.ds(place, 1), row : row + 1, :] = image[
                            k, a, last * x_end, y : y + 1, :
                        ][None]

    send_out(place_columns(dots, WELLS, table), chunks, part, sent).wait()


def first_step(totals, small):
    s_row, us_row, p_row, ps_row = (take_group(totals, group) for group in range(4))
    within, equation = small[0:1, :], small[1:2, :]
    rr, rs, ss = (take_column(totals, WELLS + i) for i in range(3))
    height = (rs + lane_sum(p_row * s_row)) / rr
    square = ss + lane_sum(2.0 * ps_row * s_row + equation * s_row * s_row)
    left = jnp.maximum(square - height * height * rr, 1e-7 * square)
    scale = lax.rsqrt(left)
    s_image = us_row + within * s_row
    s_second = (s_image - height * s_row) * scale
    p_second = (ps_row + equation * s_row - height * p_row) * scale
    shift = rs / rr + lane_sum(p_second * s_second)
    unit = lax.rsqrt(rr)
    following = left * scale * unit
    return s_row, s_image, p_row, p_second, (unit, rr * unit, height, shift, following, scale)


def krylov_kernel(
    couplings, diagonal, wells, ids, fxl, fxh, fyl, fyh, x_first, x_second, y_first, y_second,
    residual, image, residual_faces, parts, small_in, present,
    second_out, third_out, part, known, scratch, values_scratch, dots, gxl, gxh, gyl, gyh,
):
    by_side("gx", x_first, x_second, gxl, gxh)
    by_side("gy", y_first, y_second, gyl, gyh)
    faces, sent = (fxl, fxh, fyl, fyh), (gxl, gxh, gyl, gyh)
    totals = jnp.sum(parts[:, 0:8, :], axis=0)
    small = small_in[...]
    s_rows, s_images, p_rows, p_seconds, scalars = first_step(totals, small)
    known[0:RHS, :] = p_rows
    known[RHS : 2 * RHS, :] = p_seconds
    columns = jnp.zeros((RHS, LANES), jnp.float32)
    for n, column in enumerate(scalars):
        columns = columns + jnp.where(iota(columns.shape, 1) == n, column, 0.0)
    known[2 * RHS : 3 * RHS, :] = columns
    known[3 * RHS :, :] = jnp.broadcast_to(small[1:2, :], (RHS, LANES))
    dots[...] = jnp.zeros_like(dots)
    corners = corners_of(faces, FACE_PLANES, CORNER_ROWS)
    places = [diagonal_device(c % 2, c // 2)[1] for c in range(4)]
    all_ids = ids[...]
    face_ids = [as_ids(face[WELL_ID]) for face in faces]
    back_ids = [as_ids(face[BACK_ID]) for face in faces]
    corner_ids = [
        as_ids(jnp.broadcast_to(corner.row(SIDE_ID), (8, LANES))) for corner in corners
    ]
    for k in range(RHS):
        unit, _, height, shift, _, scale = (column[k : k + 1, :] for column in scalars)
        s_row, s_image = s_rows[k : k + 1, :], s_images[k : k + 1, :]
        at_wells = spread(s_row, all_ids)
        now = [image[k, a] + wells[2 + a] * at_wells for a in range(2)]
        face_now, spread_now = [], []
        for f in range(4):
            here = spread(s_row, face_ids[f])
            spread_now.append((here, spread(s_row, back_ids[f])))
            face_now.append(
                [sent[f][2 * k + a] + faces[f][WELL_EQ + a] * here for a in range(2)]
            )
        corner_now = []
        for c in range(4):
            here = spread(s_row, corner_ids[c])[0:1, :]
            corner_now.append(
                [
                    parts[pl.ds(places[c], 1), 8 + 2 * k + a, :] + corners[c].row(SIDE_EQ + a) * here
                    for a in range(2)
                ]
            )
        incoming = [product(lambda e, f=f: faces[f][e], *face_now[f]) for f in range(4)]
        applied, outgoing = block_stencil(couplings, diagonal, now[0], now[1], incoming)
        at_wells = spread(s_image, all_ids)
        second, third = [], []
        for a in range(2):
            twice = applied[a] + wells[2 + a] * at_wells
            base = (now[a] - height * residual[k, a]) * scale
            second.append(base)
            third.append((twice - height * now[a]) * scale - shift * base)
            second_out[k, a] = second[a]
            third_out[k, a] = third[a]
        ends = corner_inputs(corners, corner_now)
        incoming = []
        for f in range(4):
            face = faces[f]
            here, behind = spread_now[f]
            moves = [
                [face[at + b] * here for b in range(2)]
                for at in (DIAGONAL_WELL, UP_WELL, DOWN_WELL, RISE_WELL, FALL_WELL)
            ]
            there = face_moves(*moves, [face[BACK_WELL + b] * behind for b in range(2)])
            local = [sent[f][8 + 2 * k + b] + there[b] for b in range(2)]
            over = face_entries(ends[(f, 0)], ends[(f, 1)], outgoing[f])
            here = spread(s_image, face_ids[f])
            outer = []
            for a in range(2):
                twice = local[a] + over[a] + face[WELL_EQ + a] * here
                base = (face_now[f][a] - height * residual_faces[f, 2 * k + a]) * scale
                outer.append((twice - height * face_now[f][a]) * scale - shift * base)
            incoming.append(product(lambda e, f=f: faces[f][e], *outer))
        result, _ = block_stencil(couplings, diagonal, third[0], third[1], incoming)
        fourth = [result[a] - shift * third[a] for a in range(2)]
        values_scratch[k] = wells[0] * third[0] + wells[1] * third[1]
        values_scratch[4 + k] = wells[2] * third[0] + wells[3] * third[1]
        values_scratch[8 + k] = wells[2] * fourth[0] + wells[3] * fourth[1]
        fields = [[residual[k, a] * unit for a in range(2)], second, third, fourth]
        number = 0
        for i in range(4):
            for j in range(i, 4):
                dots[number, RHS + k : RHS + k + 1, :] = tile_sum(fields[i], fields[j])
                number += 1
    rows = segment_rows(ids, values_scratch, scratch, present)
    table = place_rows(rows, jnp.zeros((8, LANES), jnp.float32))
    table = place_columns(dots, 0, table)
    gram = table[RHS : RHS + 1, :]
    for k in range(1, RHS):
        gram = gram + pltpu.roll(table[RHS + k : RHS + k + 1, :], GRAM_ENTRIES * k, 1)
    flat = jnp.concatenate([table[k : k + 1, :] for k in range(RHS)] + [gram], axis=1)
    part[...] = jnp.broadcast_to(flat[None], part.shape)


def solve_kernel(
    guess_in, residual, second, third, parts, known, solution, guess, arrived
):
    copy = pltpu.make_async_copy(guess_in, guess, arrived.at[0])
    copy.start()
    flat = jnp.sum(parts[...], axis=0)
    rows = [flat[:, LANES * n : LANES * (n + 1)] for n in range(RHS + 1)]
    for k in range(1, RHS):
        rows.append(pltpu.roll(rows[RHS], LANES - GRAM_ENTRIES * k, 1))
    totals = jnp.concatenate(rows, axis=0)
    s_third, p_third, p_fourth = (take_group(totals, group) for group in range(3))
    p_first, p_second = known[0:RHS, :], known[RHS : 2 * RHS, :]
    unit, beta, height, shift, following = (
        known[2 * RHS : 3 * RHS, n : n + 1] for n in range(5)
    )
    equation = known[3 * RHS :, :]
    gram = {}
    number = 0
    for i in range(4):
        for j in range(i, 4):
            gram[(i, j)] = take_column(totals, number)
            number += 1
    gram[(0, 3)] += lane_sum(p_first * s_third) * unit
    gram[(1, 3)] += lane_sum(p_second * s_third)
    gram[(2, 3)] += lane_sum(p_third * s_third)
    gram[(3, 3)] += lane_sum(2.0 * p_fourth * s_third + equation * s_third * s_third)
    tiny = 1e-30
    inverse = [lax.rsqrt(jnp.maximum(gram[(i, i)], tiny)) for i in range(4)]
    length = [jnp.maximum(gram[(i, i)], tiny) * inverse[i] for i in range(4)]
    upper = {}
    for i in range(4):
        for j in range(i, 4):
            entry = gram[(i, j)] * inverse[i] * inverse[j]
            for m in range(i):
                entry = entry - upper[(m, i)] * upper[(m, j)]
            if i == j:
                pivot = lax.rsqrt(jnp.maximum(entry, 1e-6))
                upper[(i, i)] = jnp.maximum(entry, 1e-6) * pivot
                over = pivot
            else:
                upper[(i, j)] = entry * over
    columns = [
        [(0, height * length[0]), (1, following * length[1])],
        [(1, shift * length[1]), (2, length[2])],
        [(2, shift * length[2]), (3, length[3])],
    ]
    zero = jnp.zeros_like(shift)
    hessenberg = [[zero] * 3 for _ in range(4)]
    for j in range(3):
        for i in range(j + 2):
            for m, factor in columns[j]:
                if m >= i:
                    hessenberg[i][j] = hessenberg[i][j] + upper[(i, m)] * factor
    target = [beta * length[0] * upper[(0, 0)], zero, zero, zero]
    turns = []
    for j in range(3):
        top, bottom = hessenberg[j][j], hessenberg[j + 1][j]
        turn = lax.rsqrt(top * top + bottom * bottom)
        turns.append(turn)
        cosine, sine = top * turn, bottom * turn
        for m in range(j, 3):
            high, low = hessenberg[j][m], hessenberg[j + 1][m]
            hessenberg[j][m] = cosine * high + sine * low
            hessenberg[j + 1][m] = cosine * low - sine * high
        high, low = target[j], target[j + 1]
        target[j] = cosine * high + sine * low
        target[j + 1] = cosine * low - sine * high
    weights = [zero] * 3
    for i in (2, 1, 0):
        value = target[i]
        for j in range(i + 1, 3):
            value = value - hessenberg[i][j] * weights[j]
        weights[i] = value * turns[i]
    copy.wait()
    for k in range(RHS):
        on_first, on_second, on_third = (
            column[k : k + 1, :] for column in (weights[0] * unit, weights[1], weights[2])
        )
        for a in range(2):
            solution[k, a] = (
                guess[k, a]
                + on_first * residual[k, a]
                + on_second * second[k, a]
                + on_third * third[k, a]
            )


def call(kernel, shapes, arguments, scratch=(), far_inputs=0, cost=0, grant=24 << 20, out=0):
    whole = pl.BlockSpec(memory_space=pltpu.VMEM)
    far = pl.BlockSpec(memory_space=pltpu.HBM)
    scalars = pl.BlockSpec(memory_space=pltpu.SMEM)

    def place(number, array):
        if len(array.shape) == 1:
            return scalars
        return far if number < far_inputs else whole

    outs = [
        jax.ShapeDtypeStruct(shape, jnp.float32 if len(shape) > 1 else jnp.int32)
        for shape in shapes
    ]
    outs[:out] = [pltpu.HBM(shape, jnp.float32) for shape in shapes[:out]]
    return pl.pallas_call(
        kernel,
        out_shape=outs,
        in_specs=[place(*numbered) for numbered in enumerate(arguments)],
        out_specs=[far] * out + [scalars if len(shape) == 1 else whole for shape in shapes[out:]],
        scratch_shapes=list(scratch),
        compiler_params=pltpu.CompilerParams(vmem_limit_bytes=grant),
        cost_estimate=pl.CostEstimate(flops=cost, bytes_accessed=cost, transcendentals=0)
        if cost
        else None,
    )(*arguments)


def nothing(value, *rest):
    pass


def after(value, *others):
    far = pl.BlockSpec(memory_space=pltpu.HBM)
    near = pl.BlockSpec(memory_space=pltpu.VMEM)
    return pl.pallas_call(
        nothing,
        out_shape=pltpu.HBM(value.shape, value.dtype),
        in_specs=[far] + [near] * len(others),
        out_specs=far,
        input_output_aliases={0: 0},
        compiler_params=pltpu.CompilerParams(vmem_limit_bytes=1 << 20),
    )(pltpu.with_memory_space_constraint(value, pltpu.HBM), *others)


def held(*shape):
    return pltpu.VMEM(shape, jnp.float32)


def swap(value, axis, start):
    pairs = []
    for low in range(start, lax.axis_size(axis) - 1, 2):
        pairs += [(low, low + 1), (low + 1, low)]
    return lax.ppermute(value, axis, pairs) if pairs else jnp.zeros_like(value)


def swapped(first, second, axis):
    return swap(first, axis, 0), swap(second, axis, 1)


def exchanged(part):
    return lax.all_to_all(part, ("gx", "gy"), 0, 0, tiled=True)


def body(couplings, diagonal, wells, ids, right, guess):
    devices = lax.axis_size("gx") * lax.axis_size("gy")
    plane = (8, LANES)
    field = guess.shape
    block = guess.shape[2:]
    arguments = (couplings, diagonal, wells, ids, right, guess)

    ends = []
    for argument in arguments:
        shape = argument.shape[:-3] + (2,) + argument.shape[-2:]
        ends += [pltpu.VMEM(shape, argument.dtype)] * 2
    x_first, x_second = call(
        x_pack_kernel,
        [(FACE_PLANES + 1,) + plane] * 2,
        [pltpu.with_memory_space_constraint(argument, pltpu.HBM) for argument in arguments],
        ends
        + [pltpu.SemaphoreType.DMA((len(ends),))]
        + [held(FACE_PLANES + 1, *plane)] * 2,
        far_inputs=len(arguments),
    )
    came_x = swapped(x_first, x_second, "gx")
    first_chunks, chunks = (devices, TABLE_ROWS, LANES), (devices, 16, LANES)
    sent = pltpu.SemaphoreType.DMA((1,))
    part, present, y_low, y_high = call(
        guess_kernel,
        [first_chunks, (WELLS + 8,)] + [(FACE_PLANES,) + plane] * 2,
        arguments,
        [held(6, *block), held(6, WELLS, LANES), held(*first_chunks), sent],
        cost=4 << 20,
        out=1,
    )
    parts = exchanged(after(part, came_x[0]))
    y_shape = (FACE_PLANES + CORNER_PLANES,) + plane
    y_first, y_second, fxl, fxh = call(
        corner_kernel,
        [y_shape] * 2 + [(FACE_PLANES + 1,) + plane] * 2,
        (y_low, y_high, *came_x),
        [held(*y_shape)] * 2,
    )
    came_y = swapped(y_first, y_second, "gy")
    ahead = call(
        block_kernel,
        [field, (4, 8) + plane],
        (couplings, diagonal, right, guess, y_first),
        cost=4 << 20,
    )

    residual, image, residual_faces, *packs, small, fyl, fyh = call(
        residual_kernel,
        [field, field, (4, 8) + plane]
        + [(IMAGE_PLANES + spare,) + plane for spare in (2, 1, 0, 3)]
        + [(8, LANES)]
        + [y_shape] * 2,
        (couplings, diagonal, wells, ids, fxl, fxh, *came_y, parts, *ahead),
        [held(IMAGE_PLANES, *plane)] * 4,
    )
    faces = (fxl, fxh, fyl, fyh)
    came_y1 = swap(packs[3], "gy", 1)
    came_x1 = swap(packs[1], "gx", 1)
    came_x0 = swap(packs[0], "gx", 0)
    came_y0 = swap(packs[2], "gy", 0)
    (part,) = call(
        moments_kernel,
        [chunks],
        (wells, ids, residual, image, present),
        [held(16, *block), held(16, WELLS, LANES), held(3, *plane), held(*chunks), sent],
        cost=4 << 20,
        out=1,
    )
    parts = exchanged(part)
    second, third, part, known = call(
        krylov_kernel,
        [field, field, (devices, 1, (RHS + 1) * LANES), (4 * RHS, LANES)],
        (couplings, diagonal, wells, ids) + faces + (came_x0, came_x1, came_y0, came_y1)
        + (residual, image, residual_faces, parts, small, present),
        [held(12, WELLS, LANES), held(12, *block), held(10, *plane)]
        + [held(IMAGE_PLANES, *plane)] * 4,
    )
    parts = exchanged(part)
    (result,) = call(
        solve_kernel,
        [field],
        (
            pltpu.with_memory_space_constraint(guess, pltpu.HBM),
            residual, second, third, parts, known,
        ),
        [held(*field), pltpu.SemaphoreType.DMA((1,))],
        far_inputs=1,
    )
    return result


def solution(mesh):
    in_specs = (
        P("member", None, "gx", "gy", None),
        P("member", "gx", "gy", None),
        P("member", "gx", "gy", None),
        P("gx", "gy", None),
        P("member", None, "gx", "gy", None),
        P("member", None, "gx", "gy", None),
    )
    out_specs = P("member", None, "gx", "gy", None)
    return jax.shard_map(body, mesh=mesh, in_specs=in_specs, out_specs=out_specs, check_vma=False)
```

```python
import jax
import jax.numpy as jnp
from jax import lax
from jax.experimental import pallas as pl
from jax.experimental.pallas import tpu as pltpu
from jax.sharding import PartitionSpec as P

WELLS = 40
RHS = 4
LANES = 128
WELL_EQ, WELL_ID, GUESS, REST = 4, 6, 7, 15
UP_WELL, DOWN_WELL, RISE_WELL, FALL_WELL, DIAGONAL_WELL = 23, 25, 27, 29, 31
BACK_WELL, BACK_ID = 33, 35
FACE_PLANES = 36
ENDS = 36
CORNER_PLANES = 5
LAT_UP, LAT_DOWN, RISE, FALL, DIAGONAL, BACK_IN = 0, 4, 8, 12, 16, 20
LAYER_BLOCKS = 24
IMAGE_PLANES = 16
TABLE_ROWS = 4
GRAM_ENTRIES = 10
CORNER_ROWS = 19
SIDE_IN, SIDE_EQ, SIDE_ID, SIDE_GUESS = 4, 8, 10, 11


def product(blocks, first, second):
    return [
        blocks(0) * first + blocks(2) * second,
        blocks(1) * first + blocks(3) * second,
    ]


def iota(shape, axis):
    return lax.broadcasted_iota(jnp.int32, shape, axis)


def roll_up(value, axis):
    return pltpu.roll(value, 1, axis)


def roll_down(value, axis):
    return pltpu.roll(value, value.shape[axis] - 1, axis)


def layer_moves(rising, falling):
    axis = rising.ndim - 1
    lane = iota(rising.shape, axis)
    up = jnp.where(lane == 0, 0.0, roll_up(rising, axis))
    down = jnp.where(lane == LANES - 1, 0.0, roll_down(falling, axis))
    return up + down


def block_stencil(couplings, diagonal, first, second, incoming):
    result = product(lambda e: diagonal[e], first, second)
    moved = [product(lambda e, d=d: couplings[d, e], first, second) for d in range(6)]
    row = iota(first.shape, 1)
    outgoing = [[], [], [], []]
    for b in range(2):
        east, west, north, south, rise, fall = (moved[d][b] for d in range(6))
        total = result[b] + jnp.concatenate([incoming[0][b][None], east[:-1]], axis=0)
        total = total + jnp.concatenate([west[1:], incoming[1][b][None]], axis=0)
        total = total + jnp.where(row == 0, incoming[2][b][:, None, :], roll_up(north, 1))
        total = total + jnp.where(
            row == row.shape[1] - 1, incoming[3][b][:, None, :], roll_down(south, 1)
        )
        result[b] = total + layer_moves(rise, fall)
        outgoing[0].append(west[0])
        outgoing[1].append(east[-1])
        outgoing[2].append(south[:, 0, :])
        outgoing[3].append(north[:, -1, :])
    return result, outgoing


def face_stencil(blocks, first, second, behind):
    def times(start):
        return product(lambda e: blocks(start + e), first, second)

    moves = [times(start) for start in (DIAGONAL, LAT_UP, LAT_DOWN, RISE, FALL)]
    return face_moves(*moves, behind)


def face_moves(kept, up, down, rise, fall, behind):
    result = list(kept)
    row = iota(kept[0].shape, 0)
    for b in range(2):
        total = result[b] + behind[b] + layer_moves(rise[b], fall[b])
        total = total + jnp.where(row == 0, 0.0, roll_up(up[b], 0))
        result[b] = total + jnp.where(row == row.shape[0] - 1, 0.0, roll_down(down[b], 0))
    return result


def face_entries(low_end, high_end, entering):
    row = iota(entering[0].shape, 0)
    return [
        entering[b]
        + jnp.where(row == 0, low_end[b], 0.0)
        + jnp.where(row == row.shape[0] - 1, high_end[b], 0.0)
        for b in range(2)
    ]


def spread(totals, ids):
    table = jnp.broadcast_to(totals, (8, LANES))
    if ids.ndim == 2:
        return jnp.take_along_axis(table, ids, axis=1)
    return jnp.stack(
        [jnp.take_along_axis(table, ids[x], axis=1) for x in range(ids.shape[0])], axis=0
    )


def as_ids(plane):
    return plane.astype(jnp.int32)


class Corner:
    def __init__(self, pack, which, base):
        self.pack, self.start = pack, base * 8 + which

    def row(self, number):
        at = self.start + number
        return self.pack[at // 8, at % 8 : at % 8 + 1, :]


def corners_of(faces, base, rows):
    found = []
    for y_face in (2, 3):
        for x_end in range(2):
            found.append(Corner(faces[y_face], x_end * rows, base))
    return found


def corner_inputs(corners, values):
    ends = {}
    for c in range(4):
        x_end, y_end = c % 2, c // 2
        over_x = product(corners[c].row, *values[c])
        over_y = product(lambda e, c=c: corners[c].row(SIDE_IN + e), *values[c])
        ends[(2 + y_end, x_end)] = over_x
        ends[(x_end, y_end)] = over_y
    return ends


def tile_sum(first, second):
    value = first[0] * second[0] + first[1] * second[1]
    return jnp.sum(jnp.sum(value, axis=0), axis=0, keepdims=True)


def list_wells(ids, present):
    planes = [ids[x].astype(jnp.float32) for x in range(ids.shape[0])]
    middle = WELLS // 2
    halves = ((0.0, float(middle)), (float(middle), float(WELLS)))

    def least(above, top):
        found = [jnp.where((p > above) & (p < top), p, top) for p in planes]
        value = found[0]
        for other in found[1:]:
            value = jnp.minimum(value, other)
        return jnp.min(value)

    def greatest(base, below):
        found = [jnp.where((p >= base) & (p < below), p, base - 1.0) for p in planes]
        value = found[0]
        for other in found[1:]:
            value = jnp.maximum(value, other)
        return jnp.max(value)

    def some_left(state):
        return (state[1] <= state[2]) | (state[3] <= state[4])

    def step(state):
        number, ends = state[0], state[1:]
        after = []
        for half, (base, top) in enumerate(halves):
            low, high = ends[2 * half], ends[2 * half + 1]
            present[number] = low.astype(jnp.int32)
            number = number + jnp.where(low <= high, 1, 0)
            present[number] = high.astype(jnp.int32)
            number = number + jnp.where(low < high, 1, 0)
            after += [least(low, top), greatest(base, high)]
        return (number, *after)

    ends = []
    for base, top in halves:
        ends += [least(base - 1.0, top), greatest(base, top)]
    state = lax.while_loop(some_left, step, (jnp.int32(1), *ends))
    present[0] = state[0] - 1


def segment_rows(ids, values, scratch, present):
    scratch[...] = jnp.zeros_like(scratch)
    count, depth = values.shape[0], ids.shape[0]

    def one_well(step, _):
        well = present[step + 1]
        masks = [ids[x] == well for x in range(depth)]
        for number in range(count):
            total = jnp.where(masks[0], values[number, 0], 0.0)
            for x in range(1, depth):
                total = total + jnp.where(masks[x], values[number, x], 0.0)
            scratch[number, pl.ds(well, 1), :] = jnp.sum(total, axis=0, keepdims=True)
        return 0

    lax.fori_loop(0, present[0], one_well, 0)
    rows = []
    for number in range(count):
        summed = jnp.sum(scratch[number], axis=1, keepdims=True)
        shape = scratch.shape[1:]
        on_lanes = jnp.where(iota(shape, 0) == iota(shape, 1), summed, 0.0)
        rows.append(jnp.sum(on_lanes, axis=0, keepdims=True))
    return rows


def pack_rows(rows, table):
    for number, row in enumerate(rows):
        placed = row if number % 3 == 0 else pltpu.roll(row, WELLS * (number % 3), 1)
        table = table + jnp.where(
            iota(table.shape, 0) == number // 3, jnp.broadcast_to(placed, table.shape), 0.0
        )
    return table


def unpack_row(table, number):
    row = table[number // 3 : number // 3 + 1, :]
    if number % 3:
        row = pltpu.roll(row, LANES - WELLS * (number % 3), 1)
    return jnp.where(iota(row.shape, 1) < WELLS, row, 0.0)


def place_rows(rows, table):
    for number, row in enumerate(rows):
        group, k = divmod(number, RHS)
        at = k + RHS * (group // 3)
        placed = pltpu.roll(row, WELLS * group, 1) if group in (1, 2) else row
        table = table + jnp.where(
            iota(table.shape, 0) == at, jnp.broadcast_to(placed, table.shape), 0.0
        )
    return table


def place_columns(dots, first_lane, table):
    for number in range(dots.shape[0]):
        column = jnp.sum(dots[number], axis=1, keepdims=True)
        table = table + jnp.where(iota(table.shape, 1) == first_lane + number, column, 0.0)
    return table


def take_group(table, group):
    if group in (1, 2):
        table = pltpu.roll(table, LANES - WELLS * group, 1)
    start = RHS * (group // 3)
    rows = table[start : start + RHS, :]
    return jnp.where(iota(rows.shape, 1) < WELLS, rows, 0.0)


def take_column(table, lane):
    return table[RHS : 2 * RHS, lane : lane + 1]


def lane_sum(row):
    return jnp.sum(row, axis=1, keepdims=True)


def on_even(axis):
    return lax.rem(lax.axis_index(axis), 2) == 0


def copied(source, target):
    count = min(source.shape[0], target.shape[0])
    target[0:count] = source[0:count]
    if target.shape[0] > count:
        target[count:] = jnp.zeros_like(target[count:])


def by_pair(axis, low, high, first, second):
    @pl.when(on_even(axis))
    def _():
        copied(high, first)
        copied(low, second)

    @pl.when(jnp.logical_not(on_even(axis)))
    def _():
        copied(low, first)
        copied(high, second)


def by_side(axis, first, second, low, high):
    by_pair(axis, second, first, high, low)


COUPLINGS, DIAGONALS, WELL_FIELDS, IDS, RIGHT_SIDE, START = range(6)


def layer_blocks(cut, inward, lateral):
    def plane(n):
        if n < DIAGONAL:
            return cut(COUPLINGS, ((lateral, lateral + 1, 4, 5)[n // 4], n % 4), 0)
        if n < BACK_IN:
            return cut(DIAGONALS, (n - DIAGONAL,), 0)
        return cut(COUPLINGS, (inward, n - BACK_IN), 1)

    return plane


def fill_pack(pack, inward, lateral, cut):
    blocks = layer_blocks(cut, inward, lateral)
    for e in range(4):
        pack[e] = cut(COUPLINGS, (inward, e), 0)
    wells = [cut(WELL_FIELDS, (2 + a,), 0) for a in range(2)]
    for a in range(2):
        pack[WELL_EQ + a] = wells[a]
    pack[WELL_ID] = cut(IDS, (), 0).astype(jnp.float32)
    pack[BACK_ID] = cut(IDS, (), 1).astype(jnp.float32)
    for start, at in (
        (LAT_UP, UP_WELL),
        (LAT_DOWN, DOWN_WELL),
        (RISE, RISE_WELL),
        (FALL, FALL_WELL),
        (DIAGONAL, DIAGONAL_WELL),
        (BACK_IN, BACK_WELL),
    ):
        if start == BACK_IN:
            wells = [cut(WELL_FIELDS, (2 + a,), 1) for a in range(2)]
        for b, value in enumerate(product(lambda e: blocks(start + e), *wells)):
            pack[at + b] = value
    for k in range(RHS):
        here = [cut(START, (k, a), 0) for a in range(2)]
        back = [cut(START, (k, a), 1) for a in range(2)]
        entering = product(lambda e: blocks(BACK_IN + e), *back)
        local = face_stencil(blocks, here[0], here[1], entering)
        for a in range(2):
            pack[GUESS + 2 * k + a] = here[a]
            pack[REST + 2 * k + a] = cut(RIGHT_SIDE, (k, a), 0) - local[a]
    if pack.shape[0] > ENDS:
        end = pack.shape[1] - 1
        for e in range(4):
            pack[ENDS, e : e + 1, :] = blocks(LAT_UP + e)[end : end + 1, :]
            pack[ENDS, 4 + e : 5 + e, :] = blocks(LAT_DOWN + e)[0:1, :]


def x_pack_kernel(*refs):
    sources, first, second, held_ends, arrived = refs[:6], refs[6], refs[7], refs[8:20], refs[20]
    packs = refs[21:23]
    copies = []
    for n, source in enumerate(sources):
        lead = (slice(None),) * (len(source.shape) - 3)
        depth = source.shape[-3]
        for end, start in enumerate((0, depth - 2)):
            copies.append(
                pltpu.make_async_copy(
                    source.at[lead + (pl.ds(start, 2),)],
                    held_ends[2 * n + end],
                    arrived.at[2 * n + end],
                )
            )
    for copy in copies:
        copy.start()
    for copy in copies:
        copy.wait()
    for end, pack in enumerate(packs):
        fill_pack(
            pack,
            1 - end,
            2,
            lambda n, index, layer: held_ends[2 * n + end][
                index + (1 - layer if end else layer,)
            ],
        )
    by_pair("gx", *packs, first, second)


def y_cut(arguments, end):
    last = arguments[0].shape[-2] - 1

    def cut(n, index, layer):
        return arguments[n][index + (slice(None), last - layer if end else layer, slice(None))]

    return cut


def send_out(table, chunks, part, sent):
    rows = min(chunks.shape[1], table.shape[0])
    chunks[:, :rows, :] = jnp.broadcast_to(table[None, :rows], (chunks.shape[0], rows, LANES))
    copy = pltpu.make_async_copy(chunks, part, sent.at[0])
    copy.start()
    return copy


def corner_kernel(y_low, y_high, came_first, came_second, first, second, fxl, fxh, *outs):
    by_side("gx", came_first, came_second, fxl, fxh)
    last = fxl.shape[1] - 1
    for own, out, at, side in ((y_low, outs[0], 0, 4), (y_high, outs[1], last, 0)):
        for n in range(FACE_PLANES):
            out[n] = own[n]
        row = FACE_PLANES * 8
        out[FACE_PLANES + CORNER_PLANES - 1] = jnp.zeros(out.shape[1:], jnp.float32)
        for face in (fxl, fxh):
            rows = [(n, at) for n in range(4)]
            rows += [(ENDS, side + e) for e in range(4)]
            rows += [(n, at) for n in range(WELL_EQ, REST)]
            for n, y in rows:
                out[row // 8, row % 8 : row % 8 + 1, :] = face[n, y : y + 1, :]
                row += 1
    by_pair("gy", *outs, first, second)


def diagonal_device(x_end, y_end):
    across, along = lax.axis_index("gx"), lax.axis_index("gy")
    there_x, there_y = across + 2 * x_end - 1, along + 2 * y_end - 1
    count_x, count_y = lax.axis_size("gx"), lax.axis_size("gy")
    exists = (there_x >= 0) & (there_x < count_x) & (there_y >= 0) & (there_y < count_y)
    return exists, jnp.where(exists, there_x * count_y + there_y, 0)


def guess_kernel(
    couplings, diagonal, wells, ids, right, guess,
    part, present, y_low, y_high, values, scratch, chunks, sent,
):
    list_wells(ids, present)
    for k in range(RHS):
        values[k] = wells[0] * guess[k, 0] + wells[1] * guess[k, 1]
    values[4] = wells[0] * wells[2] + wells[1] * wells[3]
    values[5] = wells[2] * wells[2] + wells[3] * wells[3]
    rows = segment_rows(ids, values, scratch, present)
    table = pack_rows(rows, jnp.zeros((8, LANES), jnp.float32))
    copy = send_out(table, chunks, part, sent)
    arguments = (couplings, diagonal, wells, ids, right, guess)
    for end, pack in enumerate((y_low, y_high)):
        fill_pack(pack, 3 - end, 0, y_cut(arguments, end))
    copy.wait()


def block_kernel(
    couplings, diagonal, right, guess, sent_face, rest, leaving
):
    nothing_enters = [[jnp.zeros(guess.shape[3:], jnp.float32)] * 2] * 4
    for k in range(RHS):
        inside, outgoing = block_stencil(
            couplings, diagonal, guess[k, 0], guess[k, 1], nothing_enters
        )
        for a in range(2):
            rest[k, a] = right[k, a] - inside[a]
            for f in range(4):
                leaving[f, 2 * k + a] = outgoing[f][a]


def residual_kernel(
    couplings, diagonal, wells, ids, fxl, fxh, came_first, came_second, parts,
    rest, leaving,
    residual, image, residual_faces, x_first, x_second, y_first, y_second, small, fyl, fyh,
    x_low, x_high, y_low, y_high,
):
    by_side("gy", came_first, came_second, fyl, fyh)
    faces = (fxl, fxh, fyl, fyh)
    totals = jnp.sum(parts[...], axis=0)
    corners = corners_of(faces, FACE_PLANES, CORNER_ROWS)
    all_ids = ids[...]
    face_ids = [as_ids(face[WELL_ID]) for face in faces]
    last = rest.shape[2] - 1
    row = iota(rest.shape[2:], 1)
    for k in range(RHS):
        s_row = unpack_row(totals, k)
        entering = [
            product(
                lambda e, f=f: faces[f][e],
                faces[f][GUESS + 2 * k],
                faces[f][GUESS + 2 * k + 1],
            )
            for f in range(4)
        ]
        outgoing = [[leaving[f, 2 * k + b] for b in range(2)] for f in range(4)]
        at_wells = spread(s_row, all_ids)
        now = []
        for a in range(2):
            value = rest[k, a] - wells[2 + a] * at_wells
            over_x = [
                (value[0] - entering[0][a])[None],
                value[1:last],
                (value[last] - entering[1][a])[None],
            ]
            value = jnp.concatenate(over_x, axis=0)
            value = value - jnp.where(row == 0, entering[2][a][:, None, :], 0.0)
            now.append(value - jnp.where(row == last, entering[3][a][:, None, :], 0.0))
        for a in range(2):
            residual[k, a] = now[a]
        ends = corner_inputs(
            corners,
            [[corners[c].row(SIDE_GUESS + 2 * k + a) for a in range(2)] for c in range(4)],
        )
        incoming = []
        for f in range(4):
            face = faces[f]
            there = face_entries(ends[(f, 0)], ends[(f, 1)], outgoing[f])
            face_wells = spread(s_row, face_ids[f])
            outer = [
                face[REST + 2 * k + a] - there[a] - face[WELL_EQ + a] * face_wells
                for a in range(2)
            ]
            for a in range(2):
                residual_faces[f, 2 * k + a] = outer[a]
            incoming.append(product(lambda e, f=f: faces[f][e], *outer))
        result, _ = block_stencil(couplings, diagonal, now[0], now[1], incoming)
        for a in range(2):
            image[k, a] = result[a]
    own = (couplings, diagonal)
    for axis, packs in enumerate(((x_low, x_high), (y_low, y_high))):
        for end, pack in enumerate(packs):

            def cut(ref, index, layer):
                at = last - layer if end else layer
                return ref[index + ((at,) if axis == 0 else (slice(None), at, slice(None)))]

            plane = layer_blocks(
                lambda n, index, layer: cut(own[n], index, layer),
                2 * axis + 1 - end,
                2 * (1 - axis),
            )
            blocks = [plane(n) for n in range(LAYER_BLOCKS)]
            for k in range(RHS):
                here = [cut(image, (k, a), 0) for a in range(2)]
                back = [cut(image, (k, a), 1) for a in range(2)]
                entering = product(lambda e: blocks[BACK_IN + e], *back)
                local = face_stencil(lambda n: blocks[n], here[0], here[1], entering)
                for a in range(2):
                    pack[2 * k + a] = here[a]
                    pack[8 + 2 * k + a] = local[a]
    by_pair("gx", x_low, x_high, x_first, x_second)
    by_pair("gy", y_low, y_high, y_first, y_second)
    small[...] = jnp.concatenate(
        [unpack_row(totals, 4), unpack_row(totals, 5), jnp.zeros((6, LANES), jnp.float32)], axis=0
    )


def moments_kernel(
    wells, ids, residual, image, present, part, values, scratch, dots, chunks, sent
):
    dots[...] = jnp.zeros_like(dots)
    for k in range(RHS):
        now = [residual[k, a] for a in range(2)]
        result = [image[k, a] for a in range(2)]
        for n, field in enumerate((now, result)):
            values[4 * n + k] = wells[0] * field[0] + wells[1] * field[1]
            values[8 + 4 * n + k] = wells[2] * field[0] + wells[3] * field[1]
        row = slice(RHS + k, RHS + k + 1)
        dots[0, row, :] = tile_sum(now, now)
        dots[1, row, :] = tile_sum(now, result)
        dots[2, row, :] = tile_sum(result, result)
    rows = segment_rows(ids, values, scratch, present)
    table = place_rows(rows, jnp.zeros((8, LANES), jnp.float32))
    chunks[:, 8:, :] = jnp.zeros_like(chunks[:, 8:, :])
    last = image.shape[2] - 1
    for x_end in range(2):
        for y_end in range(2):
            exists, place = diagonal_device(x_end, y_end)

            @pl.when(exists)
            def _():
                for k in range(RHS):
                    for a in range(2):
                        row, y = 8 + 2 * k + a, last * y_end
                        chunks[pl.ds(place, 1), row : row + 1, :] = image[
                            k, a, last * x_end, y : y + 1, :
                        ][None]

    send_out(place_columns(dots, WELLS, table), chunks, part, sent).wait()


def first_step(totals, small):
    s_row, us_row, p_row, ps_row = (take_group(totals, group) for group in range(4))
    within, equation = small[0:1, :], small[1:2, :]
    rr, rs, ss = (take_column(totals, WELLS + i) for i in range(3))
    height = (rs + lane_sum(p_row * s_row)) / rr
    square = ss + lane_sum(2.0 * ps_row * s_row + equation * s_row * s_row)
    left = jnp.maximum(square - height * height * rr, 1e-7 * square)
    scale = lax.rsqrt(left)
    s_image = us_row + within * s_row
    s_second = (s_image - height * s_row) * scale
    p_second = (ps_row + equation * s_row - height * p_row) * scale
    shift = rs / rr + lane_sum(p_second * s_second)
    unit = lax.rsqrt(rr)
    following = left * scale * unit
    return s_row, s_image, p_row, p_second, (unit, rr * unit, height, shift, following, scale)


def krylov_kernel(
    couplings, diagonal, wells, ids, fxl, fxh, fyl, fyh, x_first, x_second, y_first, y_second,
    residual, image, residual_faces, parts, small_in, present,
    second_out, third_out, part, known, scratch, values_scratch, dots, gxl, gxh, gyl, gyh,
):
    by_side("gx", x_first, x_second, gxl, gxh)
    by_side("gy", y_first, y_second, gyl, gyh)
    faces, sent = (fxl, fxh, fyl, fyh), (gxl, gxh, gyl, gyh)
    totals = jnp.sum(parts[:, 0:8, :], axis=0)
    small = small_in[...]
    s_rows, s_images, p_rows, p_seconds, scalars = first_step(totals, small)
    known[0:RHS, :] = p_rows
    known[RHS : 2 * RHS, :] = p_seconds
    columns = jnp.zeros((RHS, LANES), jnp.float32)
    for n, column in enumerate(scalars):
        columns = columns + jnp.where(iota(columns.shape, 1) == n, column, 0.0)
    known[2 * RHS : 3 * RHS, :] = columns
    known[3 * RHS :, :] = jnp.broadcast_to(small[1:2, :], (RHS, LANES))
    dots[...] = jnp.zeros_like(dots)
    corners = corners_of(faces, FACE_PLANES, CORNER_ROWS)
    places = [diagonal_device(c % 2, c // 2)[1] for c in range(4)]
    all_ids = ids[...]
    face_ids = [as_ids(face[WELL_ID]) for face in faces]
    back_ids = [as_ids(face[BACK_ID]) for face in faces]
    corner_ids = [
        as_ids(jnp.broadcast_to(corner.row(SIDE_ID), (8, LANES))) for corner in corners
    ]
    for k in range(RHS):
        unit, _, height, shift, _, scale = (column[k : k + 1, :] for column in scalars)
        s_row, s_image = s_rows[k : k + 1, :], s_images[k : k + 1, :]
        at_wells = spread(s_row, all_ids)
        now = [image[k, a] + wells[2 + a] * at_wells for a in range(2)]
        face_now, spread_now = [], []
        for f in range(4):
            here = spread(s_row, face_ids[f])
            spread_now.append((here, spread(s_row, back_ids[f])))
            face_now.append(
                [sent[f][2 * k + a] + faces[f][WELL_EQ + a] * here for a in range(2)]
            )
        corner_now = []
        for c in range(4):
            here = spread(s_row, corner_ids[c])[0:1, :]
            corner_now.append(
                [
                    parts[pl.ds(places[c], 1), 8 + 2 * k + a, :] + corners[c].row(SIDE_EQ + a) * here
                    for a in range(2)
                ]
            )
        incoming = [product(lambda e, f=f: faces[f][e], *face_now[f]) for f in range(4)]
        applied, outgoing = block_stencil(couplings, diagonal, now[0], now[1], incoming)
        at_wells = spread(s_image, all_ids)
        second, third = [], []
        for a in range(2):
            twice = applied[a] + wells[2 + a] * at_wells
            base = (now[a] - height * residual[k, a]) * scale
            second.append(base)
            third.append((twice - height * now[a]) * scale - shift * base)
            second_out[k, a] = second[a]
            third_out[k, a] = third[a]
        ends = corner_inputs(corners, corner_now)
        incoming = []
        for f in range(4):
            face = faces[f]
            here, behind = spread_now[f]
            moves = [
                [face[at + b] * here for b in range(2)]
                for at in (DIAGONAL_WELL, UP_WELL, DOWN_WELL, RISE_WELL, FALL_WELL)
            ]
            there = face_moves(*moves, [face[BACK_WELL + b] * behind for b in range(2)])
            local = [sent[f][8 + 2 * k + b] + there[b] for b in range(2)]
            over = face_entries(ends[(f, 0)], ends[(f, 1)], outgoing[f])
            here = spread(s_image, face_ids[f])
            outer = []
            for a in range(2):
                twice = local[a] + over[a] + face[WELL_EQ + a] * here
                base = (face_now[f][a] - height * residual_faces[f, 2 * k + a]) * scale
                outer.append((twice - height * face_now[f][a]) * scale - shift * base)
            incoming.append(product(lambda e, f=f: faces[f][e], *outer))
        result, _ = block_stencil(couplings, diagonal, third[0], third[1], incoming)
        fourth = [result[a] - shift * third[a] for a in range(2)]
        values_scratch[k] = wells[0] * third[0] + wells[1] * third[1]
        values_scratch[4 + k] = wells[2] * third[0] + wells[3] * third[1]
        values_scratch[8 + k] = wells[2] * fourth[0] + wells[3] * fourth[1]
        fields = [[residual[k, a] * unit for a in range(2)], second, third, fourth]
        number = 0
        for i in range(4):
            for j in range(i, 4):
                dots[number, RHS + k : RHS + k + 1, :] = tile_sum(fields[i], fields[j])
                number += 1
    rows = segment_rows(ids, values_scratch, scratch, present)
    table = place_rows(rows, jnp.zeros((8, LANES), jnp.float32))
    table = place_columns(dots, 0, table)
    gram = table[RHS : RHS + 1, :]
    for k in range(1, RHS):
        gram = gram + pltpu.roll(table[RHS + k : RHS + k + 1, :], GRAM_ENTRIES * k, 1)
    flat = jnp.concatenate([table[k : k + 1, :] for k in range(RHS)] + [gram], axis=1)
    part[...] = jnp.broadcast_to(flat[None], part.shape)


def solve_kernel(
    guess_in, residual, second, third, parts, known, solution, guess, arrived
):
    copy = pltpu.make_async_copy(guess_in, guess, arrived.at[0])
    copy.start()
    flat = jnp.sum(parts[...], axis=0)
    rows = [flat[:, LANES * n : LANES * (n + 1)] for n in range(RHS + 1)]
    for k in range(1, RHS):
        rows.append(pltpu.roll(rows[RHS], LANES - GRAM_ENTRIES * k, 1))
    totals = jnp.concatenate(rows, axis=0)
    s_third, p_third, p_fourth = (take_group(totals, group) for group in range(3))
    p_first, p_second = known[0:RHS, :], known[RHS : 2 * RHS, :]
    unit, beta, height, shift, following = (
        known[2 * RHS : 3 * RHS, n : n + 1] for n in range(5)
    )
    equation = known[3 * RHS :, :]
    gram = {}
    number = 0
    for i in range(4):
        for j in range(i, 4):
            gram[(i, j)] = take_column(totals, number)
            number += 1
    gram[(0, 3)] += lane_sum(p_first * s_third) * unit
    gram[(1, 3)] += lane_sum(p_second * s_third)
    gram[(2, 3)] += lane_sum(p_third * s_third)
    gram[(3, 3)] += lane_sum(2.0 * p_fourth * s_third + equation * s_third * s_third)
    tiny = 1e-30
    inverse = [lax.rsqrt(jnp.maximum(gram[(i, i)], tiny)) for i in range(4)]
    length = [jnp.maximum(gram[(i, i)], tiny) * inverse[i] for i in range(4)]
    upper = {}
    for i in range(4):
        for j in range(i, 4):
            entry = gram[(i, j)] * inverse[i] * inverse[j]
            for m in range(i):
                entry = entry - upper[(m, i)] * upper[(m, j)]
            if i == j:
                pivot = lax.rsqrt(jnp.maximum(entry, 1e-6))
                upper[(i, i)] = jnp.maximum(entry, 1e-6) * pivot
                over = pivot
            else:
                upper[(i, j)] = entry * over
    columns = [
        [(0, height * length[0]), (1, following * length[1])],
        [(1, shift * length[1]), (2, length[2])],
        [(2, shift * length[2]), (3, length[3])],
    ]
    zero = jnp.zeros_like(shift)
    hessenberg = [[zero] * 3 for _ in range(4)]
    for j in range(3):
        for i in range(j + 2):
            for m, factor in columns[j]:
                if m >= i:
                    hessenberg[i][j] = hessenberg[i][j] + upper[(i, m)] * factor
    target = [beta * length[0] * upper[(0, 0)], zero, zero, zero]
    turns = []
    for j in range(3):
        top, bottom = hessenberg[j][j], hessenberg[j + 1][j]
        turn = lax.rsqrt(top * top + bottom * bottom)
        turns.append(turn)
        cosine, sine = top * turn, bottom * turn
        for m in range(j, 3):
            high, low = hessenberg[j][m], hessenberg[j + 1][m]
            hessenberg[j][m] = cosine * high + sine * low
            hessenberg[j + 1][m] = cosine * low - sine * high
        high, low = target[j], target[j + 1]
        target[j] = cosine * high + sine * low
        target[j + 1] = cosine * low - sine * high
    weights = [zero] * 3
    for i in (2, 1, 0):
        value = target[i]
        for j in range(i + 1, 3):
            value = value - hessenberg[i][j] * weights[j]
        weights[i] = value * turns[i]
    copy.wait()
    for k in range(RHS):
        on_first, on_second, on_third = (
            column[k : k + 1, :] for column in (weights[0] * unit, weights[1], weights[2])
        )
        for a in range(2):
            solution[k, a] = (
                guess[k, a]
                + on_first * residual[k, a]
                + on_second * second[k, a]
                + on_third * third[k, a]
            )


def call(kernel, shapes, arguments, scratch=(), far_inputs=0, cost=0, grant=24 << 20, out=0):
    whole = pl.BlockSpec(memory_space=pltpu.VMEM)
    far = pl.BlockSpec(memory_space=pltpu.HBM)
    scalars = pl.BlockSpec(memory_space=pltpu.SMEM)

    def place(number, array):
        if len(array.shape) == 1:
            return scalars
        return far if number < far_inputs else whole

    outs = [
        jax.ShapeDtypeStruct(shape, jnp.float32 if len(shape) > 1 else jnp.int32)
        for shape in shapes
    ]
    outs[:out] = [pltpu.HBM(shape, jnp.float32) for shape in shapes[:out]]
    return pl.pallas_call(
        kernel,
        out_shape=outs,
        in_specs=[place(*numbered) for numbered in enumerate(arguments)],
        out_specs=[far] * out + [scalars if len(shape) == 1 else whole for shape in shapes[out:]],
        scratch_shapes=list(scratch),
        compiler_params=pltpu.CompilerParams(vmem_limit_bytes=grant),
        cost_estimate=pl.CostEstimate(flops=cost, bytes_accessed=cost, transcendentals=0)
        if cost
        else None,
    )(*arguments)


def nothing(value, *rest):
    pass


def after(value, *others):
    far = pl.BlockSpec(memory_space=pltpu.HBM)
    near = pl.BlockSpec(memory_space=pltpu.VMEM)
    return pl.pallas_call(
        nothing,
        out_shape=pltpu.HBM(value.shape, value.dtype),
        in_specs=[far] + [near] * len(others),
        out_specs=far,
        input_output_aliases={0: 0},
        compiler_params=pltpu.CompilerParams(vmem_limit_bytes=1 << 20),
    )(pltpu.with_memory_space_constraint(value, pltpu.HBM), *others)


def held(*shape):
    return pltpu.VMEM(shape, jnp.float32)


def swap(value, axis, start):
    pairs = []
    for low in range(start, lax.axis_size(axis) - 1, 2):
        pairs += [(low, low + 1), (low + 1, low)]
    return lax.ppermute(value, axis, pairs) if pairs else jnp.zeros_like(value)


def swapped(first, second, axis):
    return swap(first, axis, 0), swap(second, axis, 1)


def exchanged(part):
    return lax.all_to_all(part, ("gx", "gy"), 0, 0, tiled=True)


def body(couplings, diagonal, wells, ids, right, guess):
    devices = lax.axis_size("gx") * lax.axis_size("gy")
    plane = (8, LANES)
    field = guess.shape
    block = guess.shape[2:]
    arguments = (couplings, diagonal, wells, ids, right, guess)

    ends = []
    for argument in arguments:
        shape = argument.shape[:-3] + (2,) + argument.shape[-2:]
        ends += [pltpu.VMEM(shape, argument.dtype)] * 2
    x_first, x_second = call(
        x_pack_kernel,
        [(FACE_PLANES + 1,) + plane, (FACE_PLANES + 2,) + plane],
        [pltpu.with_memory_space_constraint(argument, pltpu.HBM) for argument in arguments],
        ends
        + [pltpu.SemaphoreType.DMA((len(ends),))]
        + [held(FACE_PLANES + 1, *plane)] * 2,
        far_inputs=len(arguments),
    )
    came_x = swapped(x_first, x_second, "gx")
    first_chunks, chunks = (devices, TABLE_ROWS, LANES), (devices, 16, LANES)
    sent = pltpu.SemaphoreType.DMA((1,))
    part, present, y_low, y_high = call(
        guess_kernel,
        [first_chunks, (WELLS + 8,)] + [(FACE_PLANES,) + plane] * 2,
        arguments,
        [held(6, *block), held(6, WELLS, LANES), held(*first_chunks), sent],
        cost=4 << 20,
        out=1,
    )
    parts = exchanged(after(part, came_x[0]))
    y_shape = (FACE_PLANES + CORNER_PLANES,) + plane
    y_first, y_second, fxl, fxh = call(
        corner_kernel,
        [y_shape] * 2 + [(FACE_PLANES + 1,) + plane] * 2,
        (y_low, y_high, *came_x),
        [held(*y_shape)] * 2,
    )
    came_y = swapped(y_first, y_second, "gy")
    ahead = call(
        block_kernel,
        [field, (4, 8) + plane],
        (couplings, diagonal, right, guess, y_first),
        cost=4 << 20,
    )

    residual, image, residual_faces, *packs, small, fyl, fyh = call(
        residual_kernel,
        [field, field, (4, 8) + plane]
        + [(IMAGE_PLANES + spare,) + plane for spare in (1, 2, 0, 3)]
        + [(8, LANES)]
        + [y_shape] * 2,
        (couplings, diagonal, wells, ids, fxl, fxh, *came_y, parts, *ahead),
        [held(IMAGE_PLANES, *plane)] * 4,
    )
    faces = (fxl, fxh, fyl, fyh)
    came_y1 = swap(packs[3], "gy", 1)
    came_x1 = swap(packs[1], "gx", 1)
    came_x0 = swap(packs[0], "gx", 0)
    came_y0 = swap(packs[2], "gy", 0)
    (part,) = call(
        moments_kernel,
        [chunks],
        (wells, ids, residual, image, present),
        [held(16, *block), held(16, WELLS, LANES), held(3, *plane), held(*chunks), sent],
        cost=4 << 20,
        out=1,
    )
    parts = exchanged(part)
    second, third, part, known = call(
        krylov_kernel,
        [field, field, (devices, 1, (RHS + 1) * LANES), (4 * RHS, LANES)],
        (couplings, diagonal, wells, ids) + faces + (came_x0, came_x1, came_y0, came_y1)
        + (residual, image, residual_faces, parts, small, present),
        [held(12, WELLS, LANES), held(12, *block), held(10, *plane)]
        + [held(IMAGE_PLANES, *plane)] * 4,
    )
    parts = exchanged(part)
    (result,) = call(
        solve_kernel,
        [field],
        (
            pltpu.with_memory_space_constraint(guess, pltpu.HBM),
            residual, second, third, parts, known,
        ),
        [held(*field), pltpu.SemaphoreType.DMA((1,))],
        far_inputs=1,
    )
    return result


def solution(mesh):
    in_specs = (
        P("member", None, "gx", "gy", None),
        P("member", "gx", "gy", None),
        P("member", "gx", "gy", None),
        P("gx", "gy", None),
        P("member", None, "gx", "gy", None),
        P("member", None, "gx", "gy", None),
    )
    out_specs = P("member", None, "gx", "gy", None)
    return jax.shard_map(body, mesh=mesh, in_specs=in_specs, out_specs=out_specs, check_vma=False)
```

```python
import jax
import jax.numpy as jnp
from jax import lax
from jax.experimental import pallas as pl
from jax.experimental.pallas import tpu as pltpu
from jax.sharding import PartitionSpec as P

WELLS = 40
RHS = 4
LANES = 128
WELL_EQ, WELL_ID, GUESS, REST = 4, 6, 7, 15
UP_WELL, DOWN_WELL, RISE_WELL, FALL_WELL, DIAGONAL_WELL = 23, 25, 27, 29, 31
BACK_WELL, BACK_ID = 33, 35
FACE_PLANES = 36
ENDS = 36
CORNER_PLANES = 5
LAT_UP, LAT_DOWN, RISE, FALL, DIAGONAL, BACK_IN = 0, 4, 8, 12, 16, 20
LAYER_BLOCKS = 24
IMAGE_PLANES = 16
TABLE_ROWS = 2
GRAM_ENTRIES = 10
CORNER_ROWS = 19
SIDE_IN, SIDE_EQ, SIDE_ID, SIDE_GUESS = 4, 8, 10, 11


def product(blocks, first, second):
    return [
        blocks(0) * first + blocks(2) * second,
        blocks(1) * first + blocks(3) * second,
    ]


def iota(shape, axis):
    return lax.broadcasted_iota(jnp.int32, shape, axis)


def roll_up(value, axis):
    return pltpu.roll(value, 1, axis)


def roll_down(value, axis):
    return pltpu.roll(value, value.shape[axis] - 1, axis)


def layer_moves(rising, falling):
    axis = rising.ndim - 1
    lane = iota(rising.shape, axis)
    up = jnp.where(lane == 0, 0.0, roll_up(rising, axis))
    down = jnp.where(lane == LANES - 1, 0.0, roll_down(falling, axis))
    return up + down


def block_stencil(couplings, diagonal, first, second, incoming):
    result = product(lambda e: diagonal[e], first, second)
    moved = [product(lambda e, d=d: couplings[d, e], first, second) for d in range(6)]
    row = iota(first.shape, 1)
    outgoing = [[], [], [], []]
    for b in range(2):
        east, west, north, south, rise, fall = (moved[d][b] for d in range(6))
        total = result[b] + jnp.concatenate([incoming[0][b][None], east[:-1]], axis=0)
        total = total + jnp.concatenate([west[1:], incoming[1][b][None]], axis=0)
        total = total + jnp.where(row == 0, incoming[2][b][:, None, :], roll_up(north, 1))
        total = total + jnp.where(
            row == row.shape[1] - 1, incoming[3][b][:, None, :], roll_down(south, 1)
        )
        result[b] = total + layer_moves(rise, fall)
        outgoing[0].append(west[0])
        outgoing[1].append(east[-1])
        outgoing[2].append(south[:, 0, :])
        outgoing[3].append(north[:, -1, :])
    return result, outgoing


def face_stencil(blocks, first, second, behind):
    def times(start):
        return product(lambda e: blocks(start + e), first, second)

    moves = [times(start) for start in (DIAGONAL, LAT_UP, LAT_DOWN, RISE, FALL)]
    return face_moves(*moves, behind)


def face_moves(kept, up, down, rise, fall, behind):
    result = list(kept)
    row = iota(kept[0].shape, 0)
    for b in range(2):
        total = result[b] + behind[b] + layer_moves(rise[b], fall[b])
        total = total + jnp.where(row == 0, 0.0, roll_up(up[b], 0))
        result[b] = total + jnp.where(row == row.shape[0] - 1, 0.0, roll_down(down[b], 0))
    return result


def face_entries(low_end, high_end, entering):
    row = iota(entering[0].shape, 0)
    return [
        entering[b]
        + jnp.where(row == 0, low_end[b], 0.0)
        + jnp.where(row == row.shape[0] - 1, high_end[b], 0.0)
        for b in range(2)
    ]


def spread(totals, ids):
    table = jnp.broadcast_to(totals, (8, LANES))
    if ids.ndim == 2:
        return jnp.take_along_axis(table, ids, axis=1)
    return jnp.stack(
        [jnp.take_along_axis(table, ids[x], axis=1) for x in range(ids.shape[0])], axis=0
    )


def as_ids(plane):
    return plane.astype(jnp.int32)


class Corner:
    def __init__(self, pack, which, base):
        self.pack, self.start = pack, base * 8 + which

    def row(self, number):
        at = self.start + number
        return self.pack[at // 8, at % 8 : at % 8 + 1, :]


def corners_of(faces, base, rows):
    found = []
    for y_face in (2, 3):
        for x_end in range(2):
            found.append(Corner(faces[y_face], x_end * rows, base))
    return found


def corner_inputs(corners, values):
    ends = {}
    for c in range(4):
        x_end, y_end = c % 2, c // 2
        over_x = product(corners[c].row, *values[c])
        over_y = product(lambda e, c=c: corners[c].row(SIDE_IN + e), *values[c])
        ends[(2 + y_end, x_end)] = over_x
        ends[(x_end, y_end)] = over_y
    return ends


def tile_sum(first, second):
    value = first[0] * second[0] + first[1] * second[1]
    return jnp.sum(jnp.sum(value, axis=0), axis=0, keepdims=True)


def list_wells(ids, present):
    planes = [ids[x].astype(jnp.float32) for x in range(ids.shape[0])]
    middle = WELLS // 2
    halves = ((0.0, float(middle)), (float(middle), float(WELLS)))

    def least(above, top):
        found = [jnp.where((p > above) & (p < top), p, top) for p in planes]
        value = found[0]
        for other in found[1:]:
            value = jnp.minimum(value, other)
        return jnp.min(value)

    def greatest(base, below):
        found = [jnp.where((p >= base) & (p < below), p, base - 1.0) for p in planes]
        value = found[0]
        for other in found[1:]:
            value = jnp.maximum(value, other)
        return jnp.max(value)

    def some_left(state):
        return (state[1] <= state[2]) | (state[3] <= state[4])

    def step(state):
        number, ends = state[0], state[1:]
        after = []
        for half, (base, top) in enumerate(halves):
            low, high = ends[2 * half], ends[2 * half + 1]
            present[number] = low.astype(jnp.int32)
            number = number + jnp.where(low <= high, 1, 0)
            present[number] = high.astype(jnp.int32)
            number = number + jnp.where(low < high, 1, 0)
            after += [least(low, top), greatest(base, high)]
        return (number, *after)

    ends = []
    for base, top in halves:
        ends += [least(base - 1.0, top), greatest(base, top)]
    state = lax.while_loop(some_left, step, (jnp.int32(1), *ends))
    present[0] = state[0] - 1


def segment_rows(ids, values, scratch, present):
    scratch[...] = jnp.zeros_like(scratch)
    count, depth = values.shape[0], ids.shape[0]

    def one_well(step, _):
        well = present[step + 1]
        masks = [ids[x] == well for x in range(depth)]
        for number in range(count):
            total = jnp.where(masks[0], values[number, 0], 0.0)
            for x in range(1, depth):
                total = total + jnp.where(masks[x], values[number, x], 0.0)
            scratch[number, pl.ds(well, 1), :] = jnp.sum(total, axis=0, keepdims=True)
        return 0

    lax.fori_loop(0, present[0], one_well, 0)
    rows = []
    for number in range(count):
        summed = jnp.sum(scratch[number], axis=1, keepdims=True)
        shape = scratch.shape[1:]
        on_lanes = jnp.where(iota(shape, 0) == iota(shape, 1), summed, 0.0)
        rows.append(jnp.sum(on_lanes, axis=0, keepdims=True))
    return rows


def pack_rows(rows, table):
    for number, row in enumerate(rows):
        placed = row if number % 3 == 0 else pltpu.roll(row, WELLS * (number % 3), 1)
        table = table + jnp.where(
            iota(table.shape, 0) == number // 3, jnp.broadcast_to(placed, table.shape), 0.0
        )
    return table


def unpack_row(table, number):
    row = table[number // 3 : number // 3 + 1, :]
    if number % 3:
        row = pltpu.roll(row, LANES - WELLS * (number % 3), 1)
    return jnp.where(iota(row.shape, 1) < WELLS, row, 0.0)


def place_rows(rows, table):
    for number, row in enumerate(rows):
        group, k = divmod(number, RHS)
        at = k + RHS * (group // 3)
        placed = pltpu.roll(row, WELLS * group, 1) if group in (1, 2) else row
        table = table + jnp.where(
            iota(table.shape, 0) == at, jnp.broadcast_to(placed, table.shape), 0.0
        )
    return table


def place_columns(dots, first_lane, table):
    for number in range(dots.shape[0]):
        column = jnp.sum(dots[number], axis=1, keepdims=True)
        table = table + jnp.where(iota(table.shape, 1) == first_lane + number, column, 0.0)
    return table


def take_group(table, group):
    if group in (1, 2):
        table = pltpu.roll(table, LANES - WELLS * group, 1)
    start = RHS * (group // 3)
    rows = table[start : start + RHS, :]
    return jnp.where(iota(rows.shape, 1) < WELLS, rows, 0.0)


def take_column(table, lane):
    return table[RHS : 2 * RHS, lane : lane + 1]


def lane_sum(row):
    return jnp.sum(row, axis=1, keepdims=True)


def on_even(axis):
    return lax.rem(lax.axis_index(axis), 2) == 0


def copied(source, target):
    count = min(source.shape[0], target.shape[0])
    target[0:count] = source[0:count]
    if target.shape[0] > count:
        target[count:] = jnp.zeros_like(target[count:])


def by_pair(axis, low, high, first, second):
    @pl.when(on_even(axis))
    def _():
        copied(high, first)
        copied(low, second)

    @pl.when(jnp.logical_not(on_even(axis)))
    def _():
        copied(low, first)
        copied(high, second)


def by_side(axis, first, second, low, high):
    by_pair(axis, second, first, high, low)


COUPLINGS, DIAGONALS, WELL_FIELDS, IDS, RIGHT_SIDE, START = range(6)


def layer_blocks(cut, inward, lateral):
    def plane(n):
        if n < DIAGONAL:
            return cut(COUPLINGS, ((lateral, lateral + 1, 4, 5)[n // 4], n % 4), 0)
        if n < BACK_IN:
            return cut(DIAGONALS, (n - DIAGONAL,), 0)
        return cut(COUPLINGS, (inward, n - BACK_IN), 1)

    return plane


def fill_pack(pack, inward, lateral, cut):
    blocks = layer_blocks(cut, inward, lateral)
    for e in range(4):
        pack[e] = cut(COUPLINGS, (inward, e), 0)
    wells = [cut(WELL_FIELDS, (2 + a,), 0) for a in range(2)]
    for a in range(2):
        pack[WELL_EQ + a] = wells[a]
    pack[WELL_ID] = cut(IDS, (), 0).astype(jnp.float32)
    pack[BACK_ID] = cut(IDS, (), 1).astype(jnp.float32)
    for start, at in (
        (LAT_UP, UP_WELL),
        (LAT_DOWN, DOWN_WELL),
        (RISE, RISE_WELL),
        (FALL, FALL_WELL),
        (DIAGONAL, DIAGONAL_WELL),
        (BACK_IN, BACK_WELL),
    ):
        if start == BACK_IN:
            wells = [cut(WELL_FIELDS, (2 + a,), 1) for a in range(2)]
        for b, value in enumerate(product(lambda e: blocks(start + e), *wells)):
            pack[at + b] = value
    for k in range(RHS):
        here = [cut(START, (k, a), 0) for a in range(2)]
        back = [cut(START, (k, a), 1) for a in range(2)]
        entering = product(lambda e: blocks(BACK_IN + e), *back)
        local = face_stencil(blocks, here[0], here[1], entering)
        for a in range(2):
            pack[GUESS + 2 * k + a] = here[a]
            pack[REST + 2 * k + a] = cut(RIGHT_SIDE, (k, a), 0) - local[a]
    if pack.shape[0] > ENDS:
        end = pack.shape[1] - 1
        for e in range(4):
            pack[ENDS, e : e + 1, :] = blocks(LAT_UP + e)[end : end + 1, :]
            pack[ENDS, 4 + e : 5 + e, :] = blocks(LAT_DOWN + e)[0:1, :]


def x_pack_kernel(*refs):
    sources, first, second, held_ends, arrived = refs[:6], refs[6], refs[7], refs[8:20], refs[20]
    packs = refs[21:23]
    copies = []
    for n, source in enumerate(sources):
        lead = (slice(None),) * (len(source.shape) - 3)
        depth = source.shape[-3]
        for end, start in enumerate((0, depth - 2)):
            copies.append(
                pltpu.make_async_copy(
                    source.at[lead + (pl.ds(start, 2),)],
                    held_ends[2 * n + end],
                    arrived.at[2 * n + end],
                )
            )
    for copy in copies:
        copy.start()
    for copy in copies:
        copy.wait()
    for end, pack in enumerate(packs):
        fill_pack(
            pack,
            1 - end,
            2,
            lambda n, index, layer: held_ends[2 * n + end][
                index + (1 - layer if end else layer,)
            ],
        )
    by_pair("gx", *packs, first, second)


def y_cut(arguments, end):
    last = arguments[0].shape[-2] - 1

    def cut(n, index, layer):
        return arguments[n][index + (slice(None), last - layer if end else layer, slice(None))]

    return cut


def send_out(table, chunks, part, sent):
    rows = min(chunks.shape[1], table.shape[0])
    chunks[:, :rows, :] = jnp.broadcast_to(table[None, :rows], (chunks.shape[0], rows, LANES))
    copy = pltpu.make_async_copy(chunks, part, sent.at[0])
    copy.start()
    return copy


def corner_kernel(y_low, y_high, came_first, came_second, first, second, fxl, fxh, *outs):
    by_side("gx", came_first, came_second, fxl, fxh)
    last = fxl.shape[1] - 1
    for own, out, at, side in ((y_low, outs[0], 0, 4), (y_high, outs[1], last, 0)):
        for n in range(FACE_PLANES):
            out[n] = own[n]
        row = FACE_PLANES * 8
        out[FACE_PLANES + CORNER_PLANES - 1] = jnp.zeros(out.shape[1:], jnp.float32)
        for face in (fxl, fxh):
            rows = [(n, at) for n in range(4)]
            rows += [(ENDS, side + e) for e in range(4)]
            rows += [(n, at) for n in range(WELL_EQ, REST)]
            for n, y in rows:
                out[row // 8, row % 8 : row % 8 + 1, :] = face[n, y : y + 1, :]
                row += 1
    by_pair("gy", *outs, first, second)


def diagonal_device(x_end, y_end):
    across, along = lax.axis_index("gx"), lax.axis_index("gy")
    there_x, there_y = across + 2 * x_end - 1, along + 2 * y_end - 1
    count_x, count_y = lax.axis_size("gx"), lax.axis_size("gy")
    exists = (there_x >= 0) & (there_x < count_x) & (there_y >= 0) & (there_y < count_y)
    return exists, jnp.where(exists, there_x * count_y + there_y, 0)


def guess_kernel(
    couplings, diagonal, wells, ids, right, guess,
    part, present, y_low, y_high, values, scratch, chunks, sent,
):
    list_wells(ids, present)
    for k in range(RHS):
        values[k] = wells[0] * guess[k, 0] + wells[1] * guess[k, 1]
    values[4] = wells[0] * wells[2] + wells[1] * wells[3]
    values[5] = wells[2] * wells[2] + wells[3] * wells[3]
    rows = segment_rows(ids, values, scratch, present)
    table = pack_rows(rows, jnp.zeros((8, LANES), jnp.float32))
    copy = send_out(table, chunks, part, sent)
    arguments = (couplings, diagonal, wells, ids, right, guess)
    for end, pack in enumerate((y_low, y_high)):
        fill_pack(pack, 3 - end, 0, y_cut(arguments, end))
    copy.wait()


def block_kernel(
    couplings, diagonal, right, guess, sent_face, rest, leaving
):
    nothing_enters = [[jnp.zeros(guess.shape[3:], jnp.float32)] * 2] * 4
    for k in range(RHS):
        inside, outgoing = block_stencil(
            couplings, diagonal, guess[k, 0], guess[k, 1], nothing_enters
        )
        for a in range(2):
            rest[k, a] = right[k, a] - inside[a]
            for f in range(4):
                leaving[f, 2 * k + a] = outgoing[f][a]


def residual_kernel(
    couplings, diagonal, wells, ids, fxl, fxh, came_first, came_second, parts,
    rest, leaving,
    residual, image, residual_faces, x_first, x_second, y_first, y_second, small, fyl, fyh,
    x_low, x_high, y_low, y_high,
):
    by_side("gy", came_first, came_second, fyl, fyh)
    faces = (fxl, fxh, fyl, fyh)
    totals = jnp.sum(parts[...], axis=0)
    corners = corners_of(faces, FACE_PLANES, CORNER_ROWS)
    all_ids = ids[...]
    face_ids = [as_ids(face[WELL_ID]) for face in faces]
    last = rest.shape[2] - 1
    row = iota(rest.shape[2:], 1)
    for k in range(RHS):
        s_row = unpack_row(totals, k)
        entering = [
            product(
                lambda e, f=f: faces[f][e],
                faces[f][GUESS + 2 * k],
                faces[f][GUESS + 2 * k + 1],
            )
            for f in range(4)
        ]
        outgoing = [[leaving[f, 2 * k + b] for b in range(2)] for f in range(4)]
        at_wells = spread(s_row, all_ids)
        now = []
        for a in range(2):
            value = rest[k, a] - wells[2 + a] * at_wells
            over_x = [
                (value[0] - entering[0][a])[None],
                value[1:last],
                (value[last] - entering[1][a])[None],
            ]
            value = jnp.concatenate(over_x, axis=0)
            value = value - jnp.where(row == 0, entering[2][a][:, None, :], 0.0)
            now.append(value - jnp.where(row == last, entering[3][a][:, None, :], 0.0))
        for a in range(2):
            residual[k, a] = now[a]
        ends = corner_inputs(
            corners,
            [[corners[c].row(SIDE_GUESS + 2 * k + a) for a in range(2)] for c in range(4)],
        )
        incoming = []
        for f in range(4):
            face = faces[f]
            there = face_entries(ends[(f, 0)], ends[(f, 1)], outgoing[f])
            face_wells = spread(s_row, face_ids[f])
            outer = [
                face[REST + 2 * k + a] - there[a] - face[WELL_EQ + a] * face_wells
                for a in range(2)
            ]
            for a in range(2):
                residual_faces[f, 2 * k + a] = outer[a]
            incoming.append(product(lambda e, f=f: faces[f][e], *outer))
        result, _ = block_stencil(couplings, diagonal, now[0], now[1], incoming)
        for a in range(2):
            image[k, a] = result[a]
    own = (couplings, diagonal)
    for axis, packs in enumerate(((x_low, x_high), (y_low, y_high))):
        for end, pack in enumerate(packs):

            def cut(ref, index, layer):
                at = last - layer if end else layer
                return ref[index + ((at,) if axis == 0 else (slice(None), at, slice(None)))]

            plane = layer_blocks(
                lambda n, index, layer: cut(own[n], index, layer),
                2 * axis + 1 - end,
                2 * (1 - axis),
            )
            blocks = [plane(n) for n in range(LAYER_BLOCKS)]
            for k in range(RHS):
                here = [cut(image, (k, a), 0) for a in range(2)]
                back = [cut(image, (k, a), 1) for a in range(2)]
                entering = product(lambda e: blocks[BACK_IN + e], *back)
                local = face_stencil(lambda n: blocks[n], here[0], here[1], entering)
                for a in range(2):
                    pack[2 * k + a] = here[a]
                    pack[8 + 2 * k + a] = local[a]
    by_pair("gx", x_low, x_high, x_first, x_second)
    by_pair("gy", y_low, y_high, y_first, y_second)
    small[...] = jnp.concatenate(
        [unpack_row(totals, 4), unpack_row(totals, 5), jnp.zeros((6, LANES), jnp.float32)], axis=0
    )


def moments_kernel(
    wells, ids, residual, image, present, part, values, scratch, dots, chunks, sent
):
    dots[...] = jnp.zeros_like(dots)
    for k in range(RHS):
        now = [residual[k, a] for a in range(2)]
        result = [image[k, a] for a in range(2)]
        for n, field in enumerate((now, result)):
            values[4 * n + k] = wells[0] * field[0] + wells[1] * field[1]
            values[8 + 4 * n + k] = wells[2] * field[0] + wells[3] * field[1]
        row = slice(RHS + k, RHS + k + 1)
        dots[0, row, :] = tile_sum(now, now)
        dots[1, row, :] = tile_sum(now, result)
        dots[2, row, :] = tile_sum(result, result)
    rows = segment_rows(ids, values, scratch, present)
    table = place_rows(rows, jnp.zeros((8, LANES), jnp.float32))
    chunks[:, 8:, :] = jnp.zeros_like(chunks[:, 8:, :])
    last = image.shape[2] - 1
    for x_end in range(2):
        for y_end in range(2):
            exists, place = diagonal_device(x_end, y_end)

            @pl.when(exists)
            def _():
                for k in range(RHS):
                    for a in range(2):
                        row, y = 8 + 2 * k + a, last * y_end
                        chunks[pl.ds(place, 1), row : row + 1, :] = image[
                            k, a, last * x_end, y : y + 1, :
                        ][None]

    send_out(place_columns(dots, WELLS, table), chunks, part, sent).wait()


def first_step(totals, small):
    s_row, us_row, p_row, ps_row = (take_group(totals, group) for group in range(4))
    within, equation = small[0:1, :], small[1:2, :]
    rr, rs, ss = (take_column(totals, WELLS + i) for i in range(3))
    height = (rs + lane_sum(p_row * s_row)) / rr
    square = ss + lane_sum(2.0 * ps_row * s_row + equation * s_row * s_row)
    left = jnp.maximum(square - height * height * rr, 1e-7 * square)
    scale = lax.rsqrt(left)
    s_image = us_row + within * s_row
    s_second = (s_image - height * s_row) * scale
    p_second = (ps_row + equation * s_row - height * p_row) * scale
    shift = rs / rr + lane_sum(p_second * s_second)
    unit = lax.rsqrt(rr)
    following = left * scale * unit
    return s_row, s_image, p_row, p_second, (unit, rr * unit, height, shift, following, scale)


def krylov_kernel(
    couplings, diagonal, wells, ids, fxl, fxh, fyl, fyh, x_first, x_second, y_first, y_second,
    residual, image, residual_faces, parts, small_in, present,
    second_out, third_out, part, known, scratch, values_scratch, dots, gxl, gxh, gyl, gyh,
):
    by_side("gx", x_first, x_second, gxl, gxh)
    by_side("gy", y_first, y_second, gyl, gyh)
    faces, sent = (fxl, fxh, fyl, fyh), (gxl, gxh, gyl, gyh)
    totals = jnp.sum(parts[:, 0:8, :], axis=0)
    small = small_in[...]
    s_rows, s_images, p_rows, p_seconds, scalars = first_step(totals, small)
    known[0:RHS, :] = p_rows
    known[RHS : 2 * RHS, :] = p_seconds
    columns = jnp.zeros((RHS, LANES), jnp.float32)
    for n, column in enumerate(scalars):
        columns = columns + jnp.where(iota(columns.shape, 1) == n, column, 0.0)
    known[2 * RHS : 3 * RHS, :] = columns
    known[3 * RHS :, :] = jnp.broadcast_to(small[1:2, :], (RHS, LANES))
    dots[...] = jnp.zeros_like(dots)
    corners = corners_of(faces, FACE_PLANES, CORNER_ROWS)
    places = [diagonal_device(c % 2, c // 2)[1] for c in range(4)]
    all_ids = ids[...]
    face_ids = [as_ids(face[WELL_ID]) for face in faces]
    back_ids = [as_ids(face[BACK_ID]) for face in faces]
    corner_ids = [
        as_ids(jnp.broadcast_to(corner.row(SIDE_ID), (8, LANES))) for corner in corners
    ]
    for k in range(RHS):
        unit, _, height, shift, _, scale = (column[k : k + 1, :] for column in scalars)
        s_row, s_image = s_rows[k : k + 1, :], s_images[k : k + 1, :]
        at_wells = spread(s_row, all_ids)
        now = [image[k, a] + wells[2 + a] * at_wells for a in range(2)]
        face_now, spread_now = [], []
        for f in range(4):
            here = spread(s_row, face_ids[f])
            spread_now.append((here, spread(s_row, back_ids[f])))
            face_now.append(
                [sent[f][2 * k + a] + faces[f][WELL_EQ + a] * here for a in range(2)]
            )
        corner_now = []
        for c in range(4):
            here = spread(s_row, corner_ids[c])[0:1, :]
            corner_now.append(
                [
                    parts[pl.ds(places[c], 1), 8 + 2 * k + a, :] + corners[c].row(SIDE_EQ + a) * here
                    for a in range(2)
                ]
            )
        incoming = [product(lambda e, f=f: faces[f][e], *face_now[f]) for f in range(4)]
        applied, outgoing = block_stencil(couplings, diagonal, now[0], now[1], incoming)
        at_wells = spread(s_image, all_ids)
        second, third = [], []
        for a in range(2):
            twice = applied[a] + wells[2 + a] * at_wells
            base = (now[a] - height * residual[k, a]) * scale
            second.append(base)
            third.append((twice - height * now[a]) * scale - shift * base)
            second_out[k, a] = second[a]
            third_out[k, a] = third[a]
        ends = corner_inputs(corners, corner_now)
        incoming = []
        for f in range(4):
            face = faces[f]
            here, behind = spread_now[f]
            moves = [
                [face[at + b] * here for b in range(2)]
                for at in (DIAGONAL_WELL, UP_WELL, DOWN_WELL, RISE_WELL, FALL_WELL)
            ]
            there = face_moves(*moves, [face[BACK_WELL + b] * behind for b in range(2)])
            local = [sent[f][8 + 2 * k + b] + there[b] for b in range(2)]
            over = face_entries(ends[(f, 0)], ends[(f, 1)], outgoing[f])
            here = spread(s_image, face_ids[f])
            outer = []
            for a in range(2):
                twice = local[a] + over[a] + face[WELL_EQ + a] * here
                base = (face_now[f][a] - height * residual_faces[f, 2 * k + a]) * scale
                outer.append((twice - height * face_now[f][a]) * scale - shift * base)
            incoming.append(product(lambda e, f=f: faces[f][e], *outer))
        result, _ = block_stencil(couplings, diagonal, third[0], third[1], incoming)
        fourth = [result[a] - shift * third[a] for a in range(2)]
        values_scratch[k] = wells[0] * third[0] + wells[1] * third[1]
        values_scratch[4 + k] = wells[2] * third[0] + wells[3] * third[1]
        values_scratch[8 + k] = wells[2] * fourth[0] + wells[3] * fourth[1]
        fields = [[residual[k, a] * unit for a in range(2)], second, third, fourth]
        number = 0
        for i in range(4):
            for j in range(i, 4):
                dots[number, RHS + k : RHS + k + 1, :] = tile_sum(fields[i], fields[j])
                number += 1
    rows = segment_rows(ids, values_scratch, scratch, present)
    table = place_rows(rows, jnp.zeros((8, LANES), jnp.float32))
    table = place_columns(dots, 0, table)
    gram = table[RHS : RHS + 1, :]
    for k in range(1, RHS):
        gram = gram + pltpu.roll(table[RHS + k : RHS + k + 1, :], GRAM_ENTRIES * k, 1)
    flat = jnp.concatenate([table[k : k + 1, :] for k in range(RHS)] + [gram], axis=1)
    part[...] = jnp.broadcast_to(flat[None], part.shape)


def solve_kernel(
    guess_in, residual, second, third, parts, known, solution, guess, arrived
):
    copy = pltpu.make_async_copy(guess_in, guess, arrived.at[0])
    copy.start()
    flat = jnp.sum(parts[...], axis=0)
    rows = [flat[:, LANES * n : LANES * (n + 1)] for n in range(RHS + 1)]
    for k in range(1, RHS):
        rows.append(pltpu.roll(rows[RHS], LANES - GRAM_ENTRIES * k, 1))
    totals = jnp.concatenate(rows, axis=0)
    s_third, p_third, p_fourth = (take_group(totals, group) for group in range(3))
    p_first, p_second = known[0:RHS, :], known[RHS : 2 * RHS, :]
    unit, beta, height, shift, following = (
        known[2 * RHS : 3 * RHS, n : n + 1] for n in range(5)
    )
    equation = known[3 * RHS :, :]
    gram = {}
    number = 0
    for i in range(4):
        for j in range(i, 4):
            gram[(i, j)] = take_column(totals, number)
            number += 1
    gram[(0, 3)] += lane_sum(p_first * s_third) * unit
    gram[(1, 3)] += lane_sum(p_second * s_third)
    gram[(2, 3)] += lane_sum(p_third * s_third)
    gram[(3, 3)] += lane_sum(2.0 * p_fourth * s_third + equation * s_third * s_third)
    tiny = 1e-30
    inverse = [lax.rsqrt(jnp.maximum(gram[(i, i)], tiny)) for i in range(4)]
    length = [jnp.maximum(gram[(i, i)], tiny) * inverse[i] for i in range(4)]
    upper = {}
    for i in range(4):
        for j in range(i, 4):
            entry = gram[(i, j)] * inverse[i] * inverse[j]
            for m in range(i):
                entry = entry - upper[(m, i)] * upper[(m, j)]
            if i == j:
                pivot = lax.rsqrt(jnp.maximum(entry, 1e-6))
                upper[(i, i)] = jnp.maximum(entry, 1e-6) * pivot
                over = pivot
            else:
                upper[(i, j)] = entry * over
    columns = [
        [(0, height * length[0]), (1, following * length[1])],
        [(1, shift * length[1]), (2, length[2])],
        [(2, shift * length[2]), (3, length[3])],
    ]
    zero = jnp.zeros_like(shift)
    hessenberg = [[zero] * 3 for _ in range(4)]
    for j in range(3):
        for i in range(j + 2):
            for m, factor in columns[j]:
                if m >= i:
                    hessenberg[i][j] = hessenberg[i][j] + upper[(i, m)] * factor
    target = [beta * length[0] * upper[(0, 0)], zero, zero, zero]
    turns = []
    for j in range(3):
        top, bottom = hessenberg[j][j], hessenberg[j + 1][j]
        turn = lax.rsqrt(top * top + bottom * bottom)
        turns.append(turn)
        cosine, sine = top * turn, bottom * turn
        for m in range(j, 3):
            high, low = hessenberg[j][m], hessenberg[j + 1][m]
            hessenberg[j][m] = cosine * high + sine * low
            hessenberg[j + 1][m] = cosine * low - sine * high
        high, low = target[j], target[j + 1]
        target[j] = cosine * high + sine * low
        target[j + 1] = cosine * low - sine * high
    weights = [zero] * 3
    for i in (2, 1, 0):
        value = target[i]
        for j in range(i + 1, 3):
            value = value - hessenberg[i][j] * weights[j]
        weights[i] = value * turns[i]
    copy.wait()
    for k in range(RHS):
        on_first, on_second, on_third = (
            column[k : k + 1, :] for column in (weights[0] * unit, weights[1], weights[2])
        )
        for a in range(2):
            solution[k, a] = (
                guess[k, a]
                + on_first * residual[k, a]
                + on_second * second[k, a]
                + on_third * third[k, a]
            )


def call(kernel, shapes, arguments, scratch=(), far_inputs=0, cost=0, grant=24 << 20, out=0):
    whole = pl.BlockSpec(memory_space=pltpu.VMEM)
    far = pl.BlockSpec(memory_space=pltpu.HBM)
    scalars = pl.BlockSpec(memory_space=pltpu.SMEM)

    def place(number, array):
        if len(array.shape) == 1:
            return scalars
        return far if number < far_inputs else whole

    outs = [
        jax.ShapeDtypeStruct(shape, jnp.float32 if len(shape) > 1 else jnp.int32)
        for shape in shapes
    ]
    outs[:out] = [pltpu.HBM(shape, jnp.float32) for shape in shapes[:out]]
    return pl.pallas_call(
        kernel,
        out_shape=outs,
        in_specs=[place(*numbered) for numbered in enumerate(arguments)],
        out_specs=[far] * out + [scalars if len(shape) == 1 else whole for shape in shapes[out:]],
        scratch_shapes=list(scratch),
        compiler_params=pltpu.CompilerParams(vmem_limit_bytes=grant),
        cost_estimate=pl.CostEstimate(flops=cost, bytes_accessed=cost, transcendentals=0)
        if cost
        else None,
    )(*arguments)


def nothing(value, *rest):
    pass


def after(value, *others):
    far = pl.BlockSpec(memory_space=pltpu.HBM)
    near = pl.BlockSpec(memory_space=pltpu.VMEM)
    return pl.pallas_call(
        nothing,
        out_shape=pltpu.HBM(value.shape, value.dtype),
        in_specs=[far] + [near] * len(others),
        out_specs=far,
        input_output_aliases={0: 0},
        compiler_params=pltpu.CompilerParams(vmem_limit_bytes=1 << 20),
    )(pltpu.with_memory_space_constraint(value, pltpu.HBM), *others)


def held(*shape):
    return pltpu.VMEM(shape, jnp.float32)


def swap(value, axis, start):
    pairs = []
    for low in range(start, lax.axis_size(axis) - 1, 2):
        pairs += [(low, low + 1), (low + 1, low)]
    return lax.ppermute(value, axis, pairs) if pairs else jnp.zeros_like(value)


def swapped(first, second, axis):
    return swap(first, axis, 0), swap(second, axis, 1)


def exchanged(part):
    return lax.all_to_all(part, ("gx", "gy"), 0, 0, tiled=True)


def body(couplings, diagonal, wells, ids, right, guess):
    devices = lax.axis_size("gx") * lax.axis_size("gy")
    plane = (8, LANES)
    field = guess.shape
    block = guess.shape[2:]
    arguments = (couplings, diagonal, wells, ids, right, guess)

    ends = []
    for argument in arguments:
        shape = argument.shape[:-3] + (2,) + argument.shape[-2:]
        ends += [pltpu.VMEM(shape, argument.dtype)] * 2
    x_first, x_second = call(
        x_pack_kernel,
        [(FACE_PLANES + 1,) + plane, (FACE_PLANES + 2,) + plane],
        [pltpu.with_memory_space_constraint(argument, pltpu.HBM) for argument in arguments],
        ends
        + [pltpu.SemaphoreType.DMA((len(ends),))]
        + [held(FACE_PLANES + 1, *plane)] * 2,
        far_inputs=len(arguments),
    )
    came_x = swapped(x_first, x_second, "gx")
    first_chunks, chunks = (devices, TABLE_ROWS, LANES), (devices, 16, LANES)
    sent = pltpu.SemaphoreType.DMA((1,))
    part, present, y_low, y_high = call(
        guess_kernel,
        [first_chunks, (WELLS + 8,)] + [(FACE_PLANES,) + plane] * 2,
        arguments,
        [held(6, *block), held(6, WELLS, LANES), held(*first_chunks), sent],
        cost=4 << 20,
        out=1,
    )
    parts = exchanged(after(part, came_x[0]))
    y_shape = (FACE_PLANES + CORNER_PLANES,) + plane
    y_first, y_second, fxl, fxh = call(
        corner_kernel,
        [y_shape] * 2 + [(FACE_PLANES + 1,) + plane] * 2,
        (y_low, y_high, *came_x),
        [held(*y_shape)] * 2,
    )
    came_y = swapped(y_first, y_second, "gy")
    ahead = call(
        block_kernel,
        [field, (4, 8) + plane],
        (couplings, diagonal, right, guess, y_first),
        cost=4 << 20,
    )

    residual, image, residual_faces, *packs, small, fyl, fyh = call(
        residual_kernel,
        [field, field, (4, 8) + plane]
        + [(IMAGE_PLANES + spare,) + plane for spare in (1, 2, 0, 3)]
        + [(8, LANES)]
        + [y_shape] * 2,
        (couplings, diagonal, wells, ids, fxl, fxh, *came_y, parts, *ahead),
        [held(IMAGE_PLANES, *plane)] * 4,
    )
    faces = (fxl, fxh, fyl, fyh)
    came_y1 = swap(packs[3], "gy", 1)
    came_x1 = swap(packs[1], "gx", 1)
    came_x0 = swap(packs[0], "gx", 0)
    came_y0 = swap(packs[2], "gy", 0)
    (part,) = call(
        moments_kernel,
        [chunks],
        (wells, ids, residual, image, present),
        [held(16, *block), held(16, WELLS, LANES), held(3, *plane), held(*chunks), sent],
        cost=4 << 20,
        out=1,
    )
    parts = exchanged(part)
    second, third, part, known = call(
        krylov_kernel,
        [field, field, (devices, 1, (RHS + 1) * LANES), (4 * RHS, LANES)],
        (couplings, diagonal, wells, ids) + faces + (came_x0, came_x1, came_y0, came_y1)
        + (residual, image, residual_faces, parts, small, present),
        [held(12, WELLS, LANES), held(12, *block), held(10, *plane)]
        + [held(IMAGE_PLANES, *plane)] * 4,
    )
    parts = exchanged(part)
    (result,) = call(
        solve_kernel,
        [field],
        (
            pltpu.with_memory_space_constraint(guess, pltpu.HBM),
            residual, second, third, parts, known,
        ),
        [held(*field), pltpu.SemaphoreType.DMA((1,))],
        far_inputs=1,
    )
    return result


def solution(mesh):
    in_specs = (
        P("member", None, "gx", "gy", None),
        P("member", "gx", "gy", None),
        P("member", "gx", "gy", None),
        P("gx", "gy", None),
        P("member", None, "gx", "gy", None),
        P("member", None, "gx", "gy", None),
    )
    out_specs = P("member", None, "gx", "gy", None)
    return jax.shard_map(body, mesh=mesh, in_specs=in_specs, out_specs=out_specs, check_vma=False)
```

```python
import jax
import jax.numpy as jnp
from jax import lax
from jax.experimental import pallas as pl
from jax.experimental.pallas import tpu as pltpu
from jax.sharding import PartitionSpec as P

WELLS = 40
RHS = 4
LANES = 128
WELL_EQ, WELL_ID, GUESS, REST = 4, 6, 7, 15
UP_WELL, DOWN_WELL, RISE_WELL, FALL_WELL, DIAGONAL_WELL = 23, 25, 27, 29, 31
BACK_WELL, BACK_ID = 33, 35
FACE_PLANES = 36
ENDS = 36
CORNER_PLANES = 5
LAT_UP, LAT_DOWN, RISE, FALL, DIAGONAL, BACK_IN = 0, 4, 8, 12, 16, 20
LAYER_BLOCKS = 24
IMAGE_PLANES = 16
TABLE_ROWS = 4
GRAM_ENTRIES = 10
CORNER_ROWS = 19
SIDE_IN, SIDE_EQ, SIDE_ID, SIDE_GUESS = 4, 8, 10, 11


def product(blocks, first, second):
    return [
        blocks(0) * first + blocks(2) * second,
        blocks(1) * first + blocks(3) * second,
    ]


def iota(shape, axis):
    return lax.broadcasted_iota(jnp.int32, shape, axis)


def roll_up(value, axis):
    return pltpu.roll(value, 1, axis)


def roll_down(value, axis):
    return pltpu.roll(value, value.shape[axis] - 1, axis)


def layer_moves(rising, falling):
    axis = rising.ndim - 1
    lane = iota(rising.shape, axis)
    up = jnp.where(lane == 0, 0.0, roll_up(rising, axis))
    down = jnp.where(lane == LANES - 1, 0.0, roll_down(falling, axis))
    return up + down


def block_stencil(couplings, diagonal, first, second, incoming):
    result = product(lambda e: diagonal[e], first, second)
    moved = [product(lambda e, d=d: couplings[d, e], first, second) for d in range(6)]
    row = iota(first.shape, 1)
    outgoing = [[], [], [], []]
    for b in range(2):
        east, west, north, south, rise, fall = (moved[d][b] for d in range(6))
        total = result[b] + jnp.concatenate([incoming[0][b][None], east[:-1]], axis=0)
        total = total + jnp.concatenate([west[1:], incoming[1][b][None]], axis=0)
        total = total + jnp.where(row == 0, incoming[2][b][:, None, :], roll_up(north, 1))
        total = total + jnp.where(
            row == row.shape[1] - 1, incoming[3][b][:, None, :], roll_down(south, 1)
        )
        result[b] = total + layer_moves(rise, fall)
        outgoing[0].append(west[0])
        outgoing[1].append(east[-1])
        outgoing[2].append(south[:, 0, :])
        outgoing[3].append(north[:, -1, :])
    return result, outgoing


def face_stencil(blocks, first, second, behind):
    def times(start):
        return product(lambda e: blocks(start + e), first, second)

    moves = [times(start) for start in (DIAGONAL, LAT_UP, LAT_DOWN, RISE, FALL)]
    return face_moves(*moves, behind)


def face_moves(kept, up, down, rise, fall, behind):
    result = list(kept)
    row = iota(kept[0].shape, 0)
    for b in range(2):
        total = result[b] + behind[b] + layer_moves(rise[b], fall[b])
        total = total + jnp.where(row == 0, 0.0, roll_up(up[b], 0))
        result[b] = total + jnp.where(row == row.shape[0] - 1, 0.0, roll_down(down[b], 0))
    return result


def face_entries(low_end, high_end, entering):
    row = iota(entering[0].shape, 0)
    return [
        entering[b]
        + jnp.where(row == 0, low_end[b], 0.0)
        + jnp.where(row == row.shape[0] - 1, high_end[b], 0.0)
        for b in range(2)
    ]


def spread(totals, ids):
    table = jnp.broadcast_to(totals, (8, LANES))
    if ids.ndim == 2:
        return jnp.take_along_axis(table, ids, axis=1)
    return jnp.stack(
        [jnp.take_along_axis(table, ids[x], axis=1) for x in range(ids.shape[0])], axis=0
    )


def as_ids(plane):
    return plane.astype(jnp.int32)


class Corner:
    def __init__(self, pack, which, base):
        self.pack, self.start = pack, base * 8 + which

    def row(self, number):
        at = self.start + number
        return self.pack[at // 8, at % 8 : at % 8 + 1, :]


def corners_of(faces, base, rows):
    found = []
    for y_face in (2, 3):
        for x_end in range(2):
            found.append(Corner(faces[y_face], x_end * rows, base))
    return found


def corner_inputs(corners, values):
    ends = {}
    for c in range(4):
        x_end, y_end = c % 2, c // 2
        over_x = product(corners[c].row, *values[c])
        over_y = product(lambda e, c=c: corners[c].row(SIDE_IN + e), *values[c])
        ends[(2 + y_end, x_end)] = over_x
        ends[(x_end, y_end)] = over_y
    return ends


def tile_sum(first, second):
    value = first[0] * second[0] + first[1] * second[1]
    return jnp.sum(jnp.sum(value, axis=0), axis=0, keepdims=True)


def list_wells(ids, present):
    planes = [ids[x].astype(jnp.float32) for x in range(ids.shape[0])]
    middle = WELLS // 2
    halves = ((0.0, float(middle)), (float(middle), float(WELLS)))

    def least(above, top):
        found = [jnp.where((p > above) & (p < top), p, top) for p in planes]
        value = found[0]
        for other in found[1:]:
            value = jnp.minimum(value, other)
        return jnp.min(value)

    def greatest(base, below):
        found = [jnp.where((p >= base) & (p < below), p, base - 1.0) for p in planes]
        value = found[0]
        for other in found[1:]:
            value = jnp.maximum(value, other)
        return jnp.max(value)

    def some_left(state):
        return (state[1] <= state[2]) | (state[3] <= state[4])

    def step(state):
        number, ends = state[0], state[1:]
        after = []
        for half, (base, top) in enumerate(halves):
            low, high = ends[2 * half], ends[2 * half + 1]
            present[number] = low.astype(jnp.int32)
            number = number + jnp.where(low <= high, 1, 0)
            present[number] = high.astype(jnp.int32)
            number = number + jnp.where(low < high, 1, 0)
            after += [least(low, top), greatest(base, high)]
        return (number, *after)

    ends = []
    for base, top in halves:
        ends += [least(base - 1.0, top), greatest(base, top)]
    state = lax.while_loop(some_left, step, (jnp.int32(1), *ends))
    present[0] = state[0] - 1


def segment_rows(ids, values, scratch, present):
    scratch[...] = jnp.zeros_like(scratch)
    count, depth = values.shape[0], ids.shape[0]

    def one_well(step, _):
        well = present[step + 1]
        masks = [ids[x] == well for x in range(depth)]
        for number in range(count):
            total = jnp.where(masks[0], values[number, 0], 0.0)
            for x in range(1, depth):
                total = total + jnp.where(masks[x], values[number, x], 0.0)
            scratch[number, pl.ds(well, 1), :] = jnp.sum(total, axis=0, keepdims=True)
        return 0

    lax.fori_loop(0, present[0], one_well, 0)
    rows = []
    for number in range(count):
        summed = jnp.sum(scratch[number], axis=1, keepdims=True)
        shape = scratch.shape[1:]
        on_lanes = jnp.where(iota(shape, 0) == iota(shape, 1), summed, 0.0)
        rows.append(jnp.sum(on_lanes, axis=0, keepdims=True))
    return rows


def pack_rows(rows, table):
    for number, row in enumerate(rows):
        placed = row if number % 3 == 0 else pltpu.roll(row, WELLS * (number % 3), 1)
        table = table + jnp.where(
            iota(table.shape, 0) == number // 3, jnp.broadcast_to(placed, table.shape), 0.0
        )
    return table


def unpack_row(table, number):
    row = table[number // 3 : number // 3 + 1, :]
    if number % 3:
        row = pltpu.roll(row, LANES - WELLS * (number % 3), 1)
    return jnp.where(iota(row.shape, 1) < WELLS, row, 0.0)


def place_rows(rows, table):
    for number, row in enumerate(rows):
        group, k = divmod(number, RHS)
        at = k + RHS * (group // 3)
        placed = pltpu.roll(row, WELLS * group, 1) if group in (1, 2) else row
        table = table + jnp.where(
            iota(table.shape, 0) == at, jnp.broadcast_to(placed, table.shape), 0.0
        )
    return table


def place_columns(dots, first_lane, table):
    for number in range(dots.shape[0]):
        column = jnp.sum(dots[number], axis=1, keepdims=True)
        table = table + jnp.where(iota(table.shape, 1) == first_lane + number, column, 0.0)
    return table


def take_group(table, group):
    if group in (1, 2):
        table = pltpu.roll(table, LANES - WELLS * group, 1)
    start = RHS * (group // 3)
    rows = table[start : start + RHS, :]
    return jnp.where(iota(rows.shape, 1) < WELLS, rows, 0.0)


def take_column(table, lane):
    return table[RHS : 2 * RHS, lane : lane + 1]


def lane_sum(row):
    return jnp.sum(row, axis=1, keepdims=True)


def on_even(axis):
    return lax.rem(lax.axis_index(axis), 2) == 0


def copied(source, target):
    count = min(source.shape[0], target.shape[0])
    target[0:count] = source[0:count]
    if target.shape[0] > count:
        target[count:] = jnp.zeros_like(target[count:])


def by_pair(axis, low, high, first, second):
    @pl.when(on_even(axis))
    def _():
        copied(high, first)
        copied(low, second)

    @pl.when(jnp.logical_not(on_even(axis)))
    def _():
        copied(low, first)
        copied(high, second)


def by_side(axis, first, second, low, high):
    by_pair(axis, second, first, high, low)


COUPLINGS, DIAGONALS, WELL_FIELDS, IDS, RIGHT_SIDE, START = range(6)


def layer_blocks(cut, inward, lateral):
    def plane(n):
        if n < DIAGONAL:
            return cut(COUPLINGS, ((lateral, lateral + 1, 4, 5)[n // 4], n % 4), 0)
        if n < BACK_IN:
            return cut(DIAGONALS, (n - DIAGONAL,), 0)
        return cut(COUPLINGS, (inward, n - BACK_IN), 1)

    return plane


def fill_pack(pack, inward, lateral, cut):
    blocks = layer_blocks(cut, inward, lateral)
    for e in range(4):
        pack[e] = cut(COUPLINGS, (inward, e), 0)
    wells = [cut(WELL_FIELDS, (2 + a,), 0) for a in range(2)]
    for a in range(2):
        pack[WELL_EQ + a] = wells[a]
    pack[WELL_ID] = cut(IDS, (), 0).astype(jnp.float32)
    pack[BACK_ID] = cut(IDS, (), 1).astype(jnp.float32)
    for start, at in (
        (LAT_UP, UP_WELL),
        (LAT_DOWN, DOWN_WELL),
        (RISE, RISE_WELL),
        (FALL, FALL_WELL),
        (DIAGONAL, DIAGONAL_WELL),
        (BACK_IN, BACK_WELL),
    ):
        if start == BACK_IN:
            wells = [cut(WELL_FIELDS, (2 + a,), 1) for a in range(2)]
        for b, value in enumerate(product(lambda e: blocks(start + e), *wells)):
            pack[at + b] = value
    for k in range(RHS):
        here = [cut(START, (k, a), 0) for a in range(2)]
        back = [cut(START, (k, a), 1) for a in range(2)]
        entering = product(lambda e: blocks(BACK_IN + e), *back)
        local = face_stencil(blocks, here[0], here[1], entering)
        for a in range(2):
            pack[GUESS + 2 * k + a] = here[a]
            pack[REST + 2 * k + a] = cut(RIGHT_SIDE, (k, a), 0) - local[a]
    if pack.shape[0] > ENDS:
        end = pack.shape[1] - 1
        for e in range(4):
            pack[ENDS, e : e + 1, :] = blocks(LAT_UP + e)[end : end + 1, :]
            pack[ENDS, 4 + e : 5 + e, :] = blocks(LAT_DOWN + e)[0:1, :]


def x_pack_kernel(*refs):
    sources, first, second, held_ends, arrived = refs[:6], refs[6], refs[7], refs[8:20], refs[20]
    packs = refs[21:23]
    copies = []
    for n, source in enumerate(sources):
        lead = (slice(None),) * (len(source.shape) - 3)
        depth = source.shape[-3]
        for end, start in enumerate((0, depth - 2)):
            copies.append(
                pltpu.make_async_copy(
                    source.at[lead + (pl.ds(start, 2),)],
                    held_ends[2 * n + end],
                    arrived.at[2 * n + end],
                )
            )
    for copy in copies:
        copy.start()
    for copy in copies:
        copy.wait()
    for end, pack in enumerate(packs):
        fill_pack(
            pack,
            1 - end,
            2,
            lambda n, index, layer: held_ends[2 * n + end][
                index + (1 - layer if end else layer,)
            ],
        )
    by_pair("gx", *packs, first, second)


def y_cut(arguments, end):
    last = arguments[0].shape[-2] - 1

    def cut(n, index, layer):
        return arguments[n][index + (slice(None), last - layer if end else layer, slice(None))]

    return cut


def send_out(table, chunks, part, sent):
    rows = min(chunks.shape[1], table.shape[0])
    chunks[:, :rows, :] = jnp.broadcast_to(table[None, :rows], (chunks.shape[0], rows, LANES))
    copy = pltpu.make_async_copy(chunks, part, sent.at[0])
    copy.start()
    return copy


def corner_kernel(y_low, y_high, came_first, came_second, first, second, fxl, fxh, *outs):
    by_side("gx", came_first, came_second, fxl, fxh)
    last = fxl.shape[1] - 1
    for own, out, at, side in ((y_low, outs[0], 0, 4), (y_high, outs[1], last, 0)):
        for n in range(FACE_PLANES):
            out[n] = own[n]
        row = FACE_PLANES * 8
        out[FACE_PLANES + CORNER_PLANES - 1] = jnp.zeros(out.shape[1:], jnp.float32)
        for face in (fxl, fxh):
            rows = [(n, at) for n in range(4)]
            rows += [(ENDS, side + e) for e in range(4)]
            rows += [(n, at) for n in range(WELL_EQ, REST)]
            for n, y in rows:
                out[row // 8, row % 8 : row % 8 + 1, :] = face[n, y : y + 1, :]
                row += 1
    by_pair("gy", *outs, first, second)


def diagonal_device(x_end, y_end):
    across, along = lax.axis_index("gx"), lax.axis_index("gy")
    there_x, there_y = across + 2 * x_end - 1, along + 2 * y_end - 1
    count_x, count_y = lax.axis_size("gx"), lax.axis_size("gy")
    exists = (there_x >= 0) & (there_x < count_x) & (there_y >= 0) & (there_y < count_y)
    return exists, jnp.where(exists, there_x * count_y + there_y, 0)


def guess_kernel(
    couplings, diagonal, wells, ids, right, guess,
    part, present, y_low, y_high, values, scratch, chunks, sent,
):
    list_wells(ids, present)
    for k in range(RHS):
        values[k] = wells[0] * guess[k, 0] + wells[1] * guess[k, 1]
    values[4] = wells[0] * wells[2] + wells[1] * wells[3]
    values[5] = wells[2] * wells[2] + wells[3] * wells[3]
    rows = segment_rows(ids, values, scratch, present)
    table = pack_rows(rows, jnp.zeros((8, LANES), jnp.float32))
    copy = send_out(table, chunks, part, sent)
    arguments = (couplings, diagonal, wells, ids, right, guess)
    for end, pack in enumerate((y_low, y_high)):
        fill_pack(pack, 3 - end, 0, y_cut(arguments, end))
    copy.wait()


def block_kernel(
    couplings, diagonal, right, guess, sent_face, rest, leaving
):
    nothing_enters = [[jnp.zeros(guess.shape[3:], jnp.float32)] * 2] * 4
    for k in range(RHS):
        inside, outgoing = block_stencil(
            couplings, diagonal, guess[k, 0], guess[k, 1], nothing_enters
        )
        for a in range(2):
            rest[k, a] = right[k, a] - inside[a]
            for f in range(4):
                leaving[f, 2 * k + a] = outgoing[f][a]


def residual_kernel(
    couplings, diagonal, wells, ids, fxl, fxh, came_first, came_second, parts,
    rest, leaving,
    residual, image, residual_faces, x_first, x_second, y_first, y_second, small, fyl, fyh,
    x_low, x_high, y_low, y_high,
):
    by_side("gy", came_first, came_second, fyl, fyh)
    faces = (fxl, fxh, fyl, fyh)
    totals = jnp.sum(parts[...], axis=0)
    corners = corners_of(faces, FACE_PLANES, CORNER_ROWS)
    all_ids = ids[...]
    face_ids = [as_ids(face[WELL_ID]) for face in faces]
    last = rest.shape[2] - 1
    row = iota(rest.shape[2:], 1)
    for k in range(RHS):
        s_row = unpack_row(totals, k)
        entering = [
            product(
                lambda e, f=f: faces[f][e],
                faces[f][GUESS + 2 * k],
                faces[f][GUESS + 2 * k + 1],
            )
            for f in range(4)
        ]
        outgoing = [[leaving[f, 2 * k + b] for b in range(2)] for f in range(4)]
        at_wells = spread(s_row, all_ids)
        now = []
        for a in range(2):
            value = rest[k, a] - wells[2 + a] * at_wells
            over_x = [
                (value[0] - entering[0][a])[None],
                value[1:last],
                (value[last] - entering[1][a])[None],
            ]
            value = jnp.concatenate(over_x, axis=0)
            value = value - jnp.where(row == 0, entering[2][a][:, None, :], 0.0)
            now.append(value - jnp.where(row == last, entering[3][a][:, None, :], 0.0))
        for a in range(2):
            residual[k, a] = now[a]
        ends = corner_inputs(
            corners,
            [[corners[c].row(SIDE_GUESS + 2 * k + a) for a in range(2)] for c in range(4)],
        )
        incoming = []
        for f in range(4):
            face = faces[f]
            there = face_entries(ends[(f, 0)], ends[(f, 1)], outgoing[f])
            face_wells = spread(s_row, face_ids[f])
            outer = [
                face[REST + 2 * k + a] - there[a] - face[WELL_EQ + a] * face_wells
                for a in range(2)
            ]
            for a in range(2):
                residual_faces[f, 2 * k + a] = outer[a]
            incoming.append(product(lambda e, f=f: faces[f][e], *outer))
        result, _ = block_stencil(couplings, diagonal, now[0], now[1], incoming)
        for a in range(2):
            image[k, a] = result[a]
    own = (couplings, diagonal)
    for axis, packs in enumerate(((x_low, x_high), (y_low, y_high))):
        for end, pack in enumerate(packs):

            def cut(ref, index, layer):
                at = last - layer if end else layer
                return ref[index + ((at,) if axis == 0 else (slice(None), at, slice(None)))]

            plane = layer_blocks(
                lambda n, index, layer: cut(own[n], index, layer),
                2 * axis + 1 - end,
                2 * (1 - axis),
            )
            blocks = [plane(n) for n in range(LAYER_BLOCKS)]
            for k in range(RHS):
                here = [cut(image, (k, a), 0) for a in range(2)]
                back = [cut(image, (k, a), 1) for a in range(2)]
                entering = product(lambda e: blocks[BACK_IN + e], *back)
                local = face_stencil(lambda n: blocks[n], here[0], here[1], entering)
                for a in range(2):
                    pack[2 * k + a] = here[a]
                    pack[8 + 2 * k + a] = local[a]
    by_pair("gx", x_low, x_high, x_first, x_second)
    by_pair("gy", y_low, y_high, y_first, y_second)
    small[...] = jnp.concatenate(
        [unpack_row(totals, 4), unpack_row(totals, 5), jnp.zeros((6, LANES), jnp.float32)], axis=0
    )


def moments_kernel(
    wells, ids, residual, image, present, part, values, scratch, dots, chunks, sent
):
    dots[...] = jnp.zeros_like(dots)
    for k in range(RHS):
        now = [residual[k, a] for a in range(2)]
        result = [image[k, a] for a in range(2)]
        for n, field in enumerate((now, result)):
            values[4 * n + k] = wells[0] * field[0] + wells[1] * field[1]
            values[8 + 4 * n + k] = wells[2] * field[0] + wells[3] * field[1]
        row = slice(RHS + k, RHS + k + 1)
        dots[0, row, :] = tile_sum(now, now)
        dots[1, row, :] = tile_sum(now, result)
        dots[2, row, :] = tile_sum(result, result)
    rows = segment_rows(ids, values, scratch, present)
    table = place_rows(rows, jnp.zeros((8, LANES), jnp.float32))
    chunks[:, 8:, :] = jnp.zeros_like(chunks[:, 8:, :])
    last = image.shape[2] - 1
    for x_end in range(2):
        for y_end in range(2):
            exists, place = diagonal_device(x_end, y_end)

            @pl.when(exists)
            def _():
                for k in range(RHS):
                    for a in range(2):
                        row, y = 8 + 2 * k + a, last * y_end
                        chunks[pl.ds(place, 1), row : row + 1, :] = image[
                            k, a, last * x_end, y : y + 1, :
                        ][None]

    send_out(place_columns(dots, WELLS, table), chunks, part, sent).wait()


def first_step(totals, small):
    s_row, us_row, p_row, ps_row = (take_group(totals, group) for group in range(4))
    within, equation = small[0:1, :], small[1:2, :]
    rr, rs, ss = (take_column(totals, WELLS + i) for i in range(3))
    height = (rs + lane_sum(p_row * s_row)) / rr
    square = ss + lane_sum(2.0 * ps_row * s_row + equation * s_row * s_row)
    left = jnp.maximum(square - height * height * rr, 1e-7 * square)
    scale = lax.rsqrt(left)
    s_image = us_row + within * s_row
    s_second = (s_image - height * s_row) * scale
    p_second = (ps_row + equation * s_row - height * p_row) * scale
    shift = rs / rr + lane_sum(p_second * s_second)
    unit = lax.rsqrt(rr)
    following = left * scale * unit
    return s_row, s_image, p_row, p_second, (unit, rr * unit, height, shift, following, scale)


def krylov_kernel(
    couplings, diagonal, wells, ids, fxl, fxh, fyl, fyh, x_first, x_second, y_first, y_second,
    residual, image, residual_faces, parts, small_in, present,
    second_out, third_out, part, known, scratch, values_scratch, dots, gxl, gxh, gyl, gyh,
):
    by_side("gx", x_first, x_second, gxl, gxh)
    by_side("gy", y_first, y_second, gyl, gyh)
    faces, sent = (fxl, fxh, fyl, fyh), (gxl, gxh, gyl, gyh)
    totals = jnp.sum(parts[:, 0:8, :], axis=0)
    small = small_in[...]
    s_rows, s_images, p_rows, p_seconds, scalars = first_step(totals, small)
    known[0:RHS, :] = p_rows
    known[RHS : 2 * RHS, :] = p_seconds
    columns = jnp.zeros((RHS, LANES), jnp.float32)
    for n, column in enumerate(scalars):
        columns = columns + jnp.where(iota(columns.shape, 1) == n, column, 0.0)
    known[2 * RHS : 3 * RHS, :] = columns
    known[3 * RHS :, :] = jnp.broadcast_to(small[1:2, :], (RHS, LANES))
    dots[...] = jnp.zeros_like(dots)
    corners = corners_of(faces, FACE_PLANES, CORNER_ROWS)
    places = [diagonal_device(c % 2, c // 2)[1] for c in range(4)]
    all_ids = ids[...]
    face_ids = [as_ids(face[WELL_ID]) for face in faces]
    back_ids = [as_ids(face[BACK_ID]) for face in faces]
    corner_ids = [
        as_ids(jnp.broadcast_to(corner.row(SIDE_ID), (8, LANES))) for corner in corners
    ]
    for k in range(RHS):
        unit, _, height, shift, _, scale = (column[k : k + 1, :] for column in scalars)
        s_row, s_image = s_rows[k : k + 1, :], s_images[k : k + 1, :]
        at_wells = spread(s_row, all_ids)
        now = [image[k, a] + wells[2 + a] * at_wells for a in range(2)]
        face_now, spread_now = [], []
        for f in range(4):
            here = spread(s_row, face_ids[f])
            spread_now.append((here, spread(s_row, back_ids[f])))
            face_now.append(
                [sent[f][2 * k + a] + faces[f][WELL_EQ + a] * here for a in range(2)]
            )
        corner_now = []
        for c in range(4):
            here = spread(s_row, corner_ids[c])[0:1, :]
            corner_now.append(
                [
                    parts[pl.ds(places[c], 1), 8 + 2 * k + a, :] + corners[c].row(SIDE_EQ + a) * here
                    for a in range(2)
                ]
            )
        incoming = [product(lambda e, f=f: faces[f][e], *face_now[f]) for f in range(4)]
        applied, outgoing = block_stencil(couplings, diagonal, now[0], now[1], incoming)
        at_wells = spread(s_image, all_ids)
        second, third = [], []
        for a in range(2):
            twice = applied[a] + wells[2 + a] * at_wells
            base = (now[a] - height * residual[k, a]) * scale
            second.append(base)
            third.append((twice - height * now[a]) * scale - shift * base)
            second_out[k, a] = second[a]
            third_out[k, a] = third[a]
        ends = corner_inputs(corners, corner_now)
        incoming = []
        for f in range(4):
            face = faces[f]
            here, behind = spread_now[f]
            moves = [
                [face[at + b] * here for b in range(2)]
                for at in (DIAGONAL_WELL, UP_WELL, DOWN_WELL, RISE_WELL, FALL_WELL)
            ]
            there = face_moves(*moves, [face[BACK_WELL + b] * behind for b in range(2)])
            local = [sent[f][8 + 2 * k + b] + there[b] for b in range(2)]
            over = face_entries(ends[(f, 0)], ends[(f, 1)], outgoing[f])
            here = spread(s_image, face_ids[f])
            outer = []
            for a in range(2):
                twice = local[a] + over[a] + face[WELL_EQ + a] * here
                base = (face_now[f][a] - height * residual_faces[f, 2 * k + a]) * scale
                outer.append((twice - height * face_now[f][a]) * scale - shift * base)
            incoming.append(product(lambda e, f=f: faces[f][e], *outer))
        result, _ = block_stencil(couplings, diagonal, third[0], third[1], incoming)
        fourth = [result[a] - shift * third[a] for a in range(2)]
        values_scratch[k] = wells[0] * third[0] + wells[1] * third[1]
        values_scratch[4 + k] = wells[2] * third[0] + wells[3] * third[1]
        values_scratch[8 + k] = wells[2] * fourth[0] + wells[3] * fourth[1]
        fields = [[residual[k, a] * unit for a in range(2)], second, third, fourth]
        number = 0
        for i in range(4):
            for j in range(i, 4):
                dots[number, RHS + k : RHS + k + 1, :] = tile_sum(fields[i], fields[j])
                number += 1
    rows = segment_rows(ids, values_scratch, scratch, present)
    table = place_rows(rows, jnp.zeros((8, LANES), jnp.float32))
    table = place_columns(dots, 0, table)
    gram = table[RHS : RHS + 1, :]
    for k in range(1, RHS):
        gram = gram + pltpu.roll(table[RHS + k : RHS + k + 1, :], GRAM_ENTRIES * k, 1)
    flat = jnp.concatenate([table[k : k + 1, :] for k in range(RHS)] + [gram], axis=1)
    part[...] = jnp.broadcast_to(flat[None], part.shape)


def solve_kernel(
    guess_in, residual, second, third, parts, known, solution, guess, arrived
):
    copy = pltpu.make_async_copy(guess_in, guess, arrived.at[0])
    copy.start()
    flat = jnp.sum(parts[...], axis=0)
    rows = [flat[:, LANES * n : LANES * (n + 1)] for n in range(RHS + 1)]
    for k in range(1, RHS):
        rows.append(pltpu.roll(rows[RHS], LANES - GRAM_ENTRIES * k, 1))
    totals = jnp.concatenate(rows, axis=0)
    s_third, p_third, p_fourth = (take_group(totals, group) for group in range(3))
    p_first, p_second = known[0:RHS, :], known[RHS : 2 * RHS, :]
    unit, beta, height, shift, following = (
        known[2 * RHS : 3 * RHS, n : n + 1] for n in range(5)
    )
    equation = known[3 * RHS :, :]
    gram = {}
    number = 0
    for i in range(4):
        for j in range(i, 4):
            gram[(i, j)] = take_column(totals, number)
            number += 1
    gram[(0, 3)] += lane_sum(p_first * s_third) * unit
    gram[(1, 3)] += lane_sum(p_second * s_third)
    gram[(2, 3)] += lane_sum(p_third * s_third)
    gram[(3, 3)] += lane_sum(2.0 * p_fourth * s_third + equation * s_third * s_third)
    tiny = 1e-30
    inverse = [lax.rsqrt(jnp.maximum(gram[(i, i)], tiny)) for i in range(4)]
    length = [jnp.maximum(gram[(i, i)], tiny) * inverse[i] for i in range(4)]
    upper = {}
    for i in range(4):
        for j in range(i, 4):
            entry = gram[(i, j)] * inverse[i] * inverse[j]
            for m in range(i):
                entry = entry - upper[(m, i)] * upper[(m, j)]
            if i == j:
                pivot = lax.rsqrt(jnp.maximum(entry, 1e-6))
                upper[(i, i)] = jnp.maximum(entry, 1e-6) * pivot
                over = pivot
            else:
                upper[(i, j)] = entry * over
    columns = [
        [(0, height * length[0]), (1, following * length[1])],
        [(1, shift * length[1]), (2, length[2])],
        [(2, shift * length[2]), (3, length[3])],
    ]
    zero = jnp.zeros_like(shift)
    hessenberg = [[zero] * 3 for _ in range(4)]
    for j in range(3):
        for i in range(j + 2):
            for m, factor in columns[j]:
                if m >= i:
                    hessenberg[i][j] = hessenberg[i][j] + upper[(i, m)] * factor
    target = [beta * length[0] * upper[(0, 0)], zero, zero, zero]
    turns = []
    for j in range(3):
        top, bottom = hessenberg[j][j], hessenberg[j + 1][j]
        turn = lax.rsqrt(top * top + bottom * bottom)
        turns.append(turn)
        cosine, sine = top * turn, bottom * turn
        for m in range(j, 3):
            high, low = hessenberg[j][m], hessenberg[j + 1][m]
            hessenberg[j][m] = cosine * high + sine * low
            hessenberg[j + 1][m] = cosine * low - sine * high
        high, low = target[j], target[j + 1]
        target[j] = cosine * high + sine * low
        target[j + 1] = cosine * low - sine * high
    weights = [zero] * 3
    for i in (2, 1, 0):
        value = target[i]
        for j in range(i + 1, 3):
            value = value - hessenberg[i][j] * weights[j]
        weights[i] = value * turns[i]
    copy.wait()
    for k in range(RHS):
        on_first, on_second, on_third = (
            column[k : k + 1, :] for column in (weights[0] * unit, weights[1], weights[2])
        )
        for a in range(2):
            solution[k, a] = (
                guess[k, a]
                + on_first * residual[k, a]
                + on_second * second[k, a]
                + on_third * third[k, a]
            )


def call(kernel, shapes, arguments, scratch=(), far_inputs=0, cost=0, grant=24 << 20, out=0):
    whole = pl.BlockSpec(memory_space=pltpu.VMEM)
    far = pl.BlockSpec(memory_space=pltpu.HBM)
    scalars = pl.BlockSpec(memory_space=pltpu.SMEM)

    def place(number, array):
        if len(array.shape) == 1:
            return scalars
        return far if number < far_inputs else whole

    outs = [
        jax.ShapeDtypeStruct(shape, jnp.float32 if len(shape) > 1 else jnp.int32)
        for shape in shapes
    ]
    outs[:out] = [pltpu.HBM(shape, jnp.float32) for shape in shapes[:out]]
    return pl.pallas_call(
        kernel,
        out_shape=outs,
        in_specs=[place(*numbered) for numbered in enumerate(arguments)],
        out_specs=[far] * out + [scalars if len(shape) == 1 else whole for shape in shapes[out:]],
        scratch_shapes=list(scratch),
        compiler_params=pltpu.CompilerParams(vmem_limit_bytes=grant),
        cost_estimate=pl.CostEstimate(flops=cost, bytes_accessed=cost, transcendentals=0)
        if cost
        else None,
    )(*arguments)


def nothing(value, *rest):
    pass


def after(value, *others):
    far = pl.BlockSpec(memory_space=pltpu.HBM)
    near = pl.BlockSpec(memory_space=pltpu.VMEM)
    return pl.pallas_call(
        nothing,
        out_shape=pltpu.HBM(value.shape, value.dtype),
        in_specs=[far] + [near] * len(others),
        out_specs=far,
        input_output_aliases={0: 0},
        compiler_params=pltpu.CompilerParams(vmem_limit_bytes=1 << 20),
    )(pltpu.with_memory_space_constraint(value, pltpu.HBM), *others)


def held(*shape):
    return pltpu.VMEM(shape, jnp.float32)


def swap(value, axis, start):
    pairs = []
    for low in range(start, lax.axis_size(axis) - 1, 2):
        pairs += [(low, low + 1), (low + 1, low)]
    return lax.ppermute(value, axis, pairs) if pairs else jnp.zeros_like(value)


def swapped(first, second, axis):
    return swap(first, axis, 0), swap(second, axis, 1)


def exchanged(part):
    return lax.all_to_all(part, ("gx", "gy"), 0, 0, tiled=True)


def body(couplings, diagonal, wells, ids, right, guess):
    devices = lax.axis_size("gx") * lax.axis_size("gy")
    plane = (8, LANES)
    field = guess.shape
    block = guess.shape[2:]
    arguments = (couplings, diagonal, wells, ids, right, guess)

    ends = []
    for argument in arguments:
        shape = argument.shape[:-3] + (2,) + argument.shape[-2:]
        ends += [pltpu.VMEM(shape, argument.dtype)] * 2
    x_first, x_second = call(
        x_pack_kernel,
        [(FACE_PLANES + 1,) + plane, (FACE_PLANES + 2,) + plane],
        [pltpu.with_memory_space_constraint(argument, pltpu.HBM) for argument in arguments],
        ends
        + [pltpu.SemaphoreType.DMA((len(ends),))]
        + [held(FACE_PLANES + 1, *plane)] * 2,
        far_inputs=len(arguments),
    )
    came_x = swapped(x_first, x_second, "gx")
    first_chunks, chunks = (devices, TABLE_ROWS, LANES), (devices, 16, LANES)
    sent = pltpu.SemaphoreType.DMA((1,))
    part, present, y_low, y_high = call(
        guess_kernel,
        [first_chunks, (WELLS + 8,)] + [(FACE_PLANES,) + plane] * 2,
        arguments,
        [held(6, *block), held(6, WELLS, LANES), held(*first_chunks), sent],
        cost=4 << 20,
        out=1,
    )
    parts = exchanged(part)
    y_shape = (FACE_PLANES + CORNER_PLANES,) + plane
    y_first, y_second, fxl, fxh = call(
        corner_kernel,
        [y_shape] * 2 + [(FACE_PLANES + 1,) + plane] * 2,
        (y_low, y_high, *came_x),
        [held(*y_shape)] * 2,
    )
    came_y = swapped(y_first, y_second, "gy")
    ahead = call(
        block_kernel,
        [field, (4, 8) + plane],
        (couplings, diagonal, right, guess, y_first),
        cost=4 << 20,
    )

    residual, image, residual_faces, *packs, small, fyl, fyh = call(
        residual_kernel,
        [field, field, (4, 8) + plane]
        + [(IMAGE_PLANES + spare,) + plane for spare in (1, 2, 0, 3)]
        + [(8, LANES)]
        + [y_shape] * 2,
        (couplings, diagonal, wells, ids, fxl, fxh, *came_y, parts, *ahead),
        [held(IMAGE_PLANES, *plane)] * 4,
    )
    faces = (fxl, fxh, fyl, fyh)
    came_y1 = swap(packs[3], "gy", 1)
    came_x1 = swap(packs[1], "gx", 1)
    came_x0 = swap(packs[0], "gx", 0)
    came_y0 = swap(packs[2], "gy", 0)
    (part,) = call(
        moments_kernel,
        [chunks],
        (wells, ids, residual, image, present),
        [held(16, *block), held(16, WELLS, LANES), held(3, *plane), held(*chunks), sent],
        cost=4 << 20,
        out=1,
    )
    parts = exchanged(part)
    second, third, part, known = call(
        krylov_kernel,
        [field, field, (devices, 1, (RHS + 1) * LANES), (4 * RHS, LANES)],
        (couplings, diagonal, wells, ids) + faces + (came_x0, came_x1, came_y0, came_y1)
        + (residual, image, residual_faces, parts, small, present),
        [held(12, WELLS, LANES), held(12, *block), held(10, *plane)]
        + [held(IMAGE_PLANES, *plane)] * 4,
    )
    parts = exchanged(part)
    (result,) = call(
        solve_kernel,
        [field],
        (
            pltpu.with_memory_space_constraint(guess, pltpu.HBM),
            residual, second, third, parts, known,
        ),
        [held(*field), pltpu.SemaphoreType.DMA((1,))],
        far_inputs=1,
    )
    return result


def solution(mesh):
    in_specs = (
        P("member", None, "gx", "gy", None),
        P("member", "gx", "gy", None),
        P("member", "gx", "gy", None),
        P("gx", "gy", None),
        P("member", None, "gx", "gy", None),
        P("member", None, "gx", "gy", None),
    )
    out_specs = P("member", None, "gx", "gy", None)
    return jax.shard_map(body, mesh=mesh, in_specs=in_specs, out_specs=out_specs, check_vma=False)
```
